128 devices in a mesh: seq: 128 (over z, x, y, core).
Axes of the slice: x: 4, y: 4, z: 4, core: 2. Of those that a mesh axis runs over, the one named last changes fastest.
Arguments:
- tokens: bfloat16 [16384, 2048], P('seq'), may hold values from -6 to 6
- sequence_lengths: int32 [8], replicated, may hold values from 961 to 8192, as said below
- attention_gain: bfloat16 [2048], replicated, may hold values from 0.25 to 1.75
- query_weight: bfloat16 [2048, 2048], P('seq'), may hold values from -0.125 to 0.125
- key_weight: bfloat16 [2048, 256], P('seq'), may hold values from -0.125 to 0.125
- value_weight: bfloat16 [2048, 256], P('seq'), may hold values from -0.125 to 0.125
- output_weight_flipped: bfloat16 [2048, 2048], P('seq'), may hold values from -0.5 to 0.5
- query_adapter_down: bfloat16 [2048, 8], replicated, may hold values from -0.125 to 0.125
- query_adapter_up: bfloat16 [8, 2048], replicated, may hold values from -1 to 1
- key_adapter_down: bfloat16 [2048, 8], replicated, may hold values from -0.125 to 0.125
- key_adapter_up: bfloat16 [8, 256], replicated, may hold values from -1 to 1
- value_adapter_down: bfloat16 [2048, 8], replicated, may hold values from -0.125 to 0.125
- value_adapter_up: bfloat16 [8, 256], replicated, may hold values from -1 to 1
- output_adapter_down: bfloat16 [2048, 8], replicated, may hold values from -0.5 to 0.5
- output_adapter_up: bfloat16 [8, 2048], replicated, may hold values from -1 to 1
- query_feature_map: bfloat16 [32, 64, 64], replicated, may hold values from -3 to 3
- key_feature_map: bfloat16 [4, 64, 64], replicated, may hold values from -3 to 3
- feedforward_gain: bfloat16 [2048], replicated, may hold values from 0.25 to 1.75
- gate_weight: bfloat16 [2048, 5632], P('seq'), may hold values from -0.125 to 0.125
- up_weight: bfloat16 [2048, 5632], P('seq'), may hold values from -0.125 to 0.125
- down_weight_flipped: bfloat16 [2048, 5632], P('seq'), may hold values from -0.078125 to 0.078125
- output_gradient: bfloat16 [16384, 2048], P('seq'), may hold values from -6 to 6
Outputs:
- block_out: bfloat16 [16384, 2048], P('seq')
- grad_tokens: bfloat16 [16384, 2048], P('seq')
- grad_gain_attn: float32 [2048], replicated
- grad_lora_qa: float32 [2048, 8], replicated
- grad_lora_qb: float32 [8, 2048], replicated
- grad_lora_ka: float32 [2048, 8], replicated
- grad_lora_kb: float32 [8, 256], replicated
- grad_lora_va: float32 [2048, 8], replicated
- grad_lora_vb: float32 [8, 256], replicated
- grad_lora_oa: float32 [2048, 8], replicated
- grad_lora_ob: float32 [8, 2048], replicated
- grad_feat_query: float32 [32, 64, 64], replicated
- grad_feat_key: float32 [4, 64, 64], replicated
- grad_gain_mlp: float32 [2048], replicated
The draws below stay inside these ranges and needn't reach their ends.
Inputs may be any that keep to these rules, and one draw needn't show every extreme that they name: `sequence_lengths`: the sequences lie end to end in the order given, each starting at a stretch boundary; their stretch counts ceil(length / 64) add up to 256, and each spans 16 stretches or more. The longest spans exactly 128 stretches and fills them all.
All inputs are finite; a program needn't handle non-finite values.
Results may differ from the reference program's by a relative error of at most 0.024.
Values may be sent and summed in bfloat16 or wider, within the bound.
A program may use at most 256 MiB of HBM per device.

```python
import math
import jax
import jax.numpy as jnp
from jax import lax

MODEL_WIDTH = 2048
QUERY_HEADS = 32
KEY_VALUE_HEADS = 4
HEAD_SIZE = 64
FF = 5632
FEAT = 64
ADAPTER_RANK = 8
STRETCH = 64
MIN_STRETCHES = 16
TOKENS = 16384
NSEQ = 8
LONGEST = 128


def draw_sequence_lengths(key, part):
    key = jax.random.fold_in(key, 7)
    key_room, key_order, key_long, key_pad = jax.random.split(key, 4)
    stretch_total = TOKENS // STRETCH
    others = NSEQ - 1
    spare = stretch_total - LONGEST - others * MIN_STRETCHES
    base_share = spare // others
    positions = jnp.arange(others)
    extra = base_share + (positions < spare % others).astype(jnp.int32)
    room = max(0, min(base_share, LONGEST - MIN_STRETCHES - base_share - 1))
    moves = jax.random.randint(key_room, (others,), 0, room + 1)
    paired = positions < 2 * (others // 2)
    given = jnp.where(paired & (positions % 2 == 0), moves, 0)
    taken = jnp.roll(given, 1)
    counts = MIN_STRETCHES + extra + given - taken
    counts = counts[jax.random.permutation(key_order, others)]
    long_at = jax.random.randint(key_long, (), 0, NSEQ)
    slots = jnp.arange(NSEQ)
    padded = jnp.concatenate([counts, counts[-1:]])
    shifted = jnp.concatenate([counts[:1], counts])
    full_counts = jnp.where(slots < long_at, padded, jnp.where(slots == long_at, LONGEST, shifted))
    pads = jax.random.randint(key_pad, (NSEQ,), 0, STRETCH)
    pads = jnp.where(slots == long_at, 0, pads)
    return (full_counts * STRETCH - pads).astype(jnp.int32)


def level_of(own_key, dims, cuts, smallest, high):
    def one(axis_at, parts):
        steps = jax.random.uniform(jax.random.fold_in(jax.random.fold_in(own_key, 6), axis_at), (parts,), jnp.float32, smallest / len(cuts), high / len(cuts))
        return jnp.repeat(jnp.exp(steps), dims[axis_at] // parts).reshape((-1,) + (1,) * (len(dims) - axis_at - 1))

    level = one(*cuts[0])
    for cut in cuts[1:]:
        level = level * one(*cut)
    return level


def noise(rng, shape, width, limit, cuts=(), held_as=jnp.bfloat16):
    entries = jax.random.normal(rng, shape, jnp.float32) * width
    if len(cuts) > 0:
        entries = level_of(rng, shape, cuts, -0.22, 0.18) * entries
    return jnp.clip(entries, min=-limit, max=limit).astype(held_as)


def setup_inputs(seed: int = 0) -> dict:
    arg_keys = jax.random.split(jax.random.key(seed), 23)
    tokens = noise(arg_keys[0], (TOKENS, MODEL_WIDTH), 1.0, 6.0, ((0, 128),))
    sequence_lengths = draw_sequence_lengths(jax.random.fold_in(arg_keys[22], 71), 0)
    attention_gain = jnp.clip(1.0 + 0.15 * jax.random.normal(arg_keys[2], (MODEL_WIDTH,), jnp.float32), 0.25, 1.75).astype(jnp.bfloat16)
    query_weight = noise(arg_keys[3], (MODEL_WIDTH, QUERY_HEADS * HEAD_SIZE), MODEL_WIDTH ** -0.5, 0.125, ((0, 128),))
    key_weight = noise(arg_keys[4], (MODEL_WIDTH, KEY_VALUE_HEADS * HEAD_SIZE), MODEL_WIDTH ** -0.5, 0.125, ((0, 128),))
    value_weight = noise(arg_keys[5], (MODEL_WIDTH, KEY_VALUE_HEADS * HEAD_SIZE), MODEL_WIDTH ** -0.5, 0.125, ((0, 128),))
    output_weight_flipped = noise(arg_keys[6], (MODEL_WIDTH, QUERY_HEADS * HEAD_SIZE), (QUERY_HEADS * HEAD_SIZE // 16) ** -0.5, 0.5, ((0, 128),))
    query_adapter_down = noise(arg_keys[7], (MODEL_WIDTH, ADAPTER_RANK), MODEL_WIDTH ** -0.5, 0.125)
    query_adapter_up = noise(arg_keys[8], (ADAPTER_RANK, QUERY_HEADS * HEAD_SIZE), (4 * ADAPTER_RANK) ** -0.5, 1.0)
    key_adapter_down = noise(arg_keys[9], (MODEL_WIDTH, ADAPTER_RANK), MODEL_WIDTH ** -0.5, 0.125)
    key_adapter_up = noise(arg_keys[10], (ADAPTER_RANK, KEY_VALUE_HEADS * HEAD_SIZE), (4 * ADAPTER_RANK) ** -0.5, 1.0)
    value_adapter_down = noise(arg_keys[11], (MODEL_WIDTH, ADAPTER_RANK), MODEL_WIDTH ** -0.5, 0.125)
    value_adapter_up = noise(arg_keys[12], (ADAPTER_RANK, KEY_VALUE_HEADS * HEAD_SIZE), (4 * ADAPTER_RANK) ** -0.5, 1.0)
    output_adapter_down = noise(arg_keys[13], (QUERY_HEADS * HEAD_SIZE, ADAPTER_RANK), (QUERY_HEADS * HEAD_SIZE // 16) ** -0.5, 0.5)
    output_adapter_up = noise(arg_keys[14], (ADAPTER_RANK, MODEL_WIDTH), (4 * ADAPTER_RANK) ** -0.5, 1.0)
    query_feature_map = noise(arg_keys[15], (QUERY_HEADS, HEAD_SIZE, FEAT), (HEAD_SIZE // 16) ** -0.5, 3.0)
    key_feature_map = noise(arg_keys[16], (KEY_VALUE_HEADS, HEAD_SIZE, FEAT), (HEAD_SIZE // 16) ** -0.5, 3.0)
    feedforward_gain = jnp.clip(1.0 + 0.15 * jax.random.normal(arg_keys[17], (MODEL_WIDTH,), jnp.float32), 0.25, 1.75).astype(jnp.bfloat16)
    gate_weight = noise(arg_keys[18], (MODEL_WIDTH, FF), MODEL_WIDTH ** -0.5, 0.125, ((0, 128),))
    up_weight = noise(arg_keys[19], (MODEL_WIDTH, FF), MODEL_WIDTH ** -0.5, 0.125, ((0, 128),))
    down_weight_flipped = noise(arg_keys[20], (MODEL_WIDTH, FF), FF ** -0.5, 0.078125, ((0, 128),))
    output_gradient = noise(arg_keys[21], (TOKENS, MODEL_WIDTH), 1.0, 6.0, ((0, 128),))
    return {"tokens": tokens, "sequence_lengths": sequence_lengths, "attention_gain": attention_gain, "query_weight": query_weight, "key_weight": key_weight, "value_weight": value_weight, "output_weight_flipped": output_weight_flipped, "query_adapter_down": query_adapter_down, "query_adapter_up": query_adapter_up, "key_adapter_down": key_adapter_down, "key_adapter_up": key_adapter_up, "value_adapter_down": value_adapter_down, "value_adapter_up": value_adapter_up, "output_adapter_down": output_adapter_down, "output_adapter_up": output_adapter_up, "query_feature_map": query_feature_map, "key_feature_map": key_feature_map, "feedforward_gain": feedforward_gain, "gate_weight": gate_weight, "up_weight": up_weight, "down_weight_flipped": down_weight_flipped, "output_gradient": output_gradient}


@jax.custom_vjp
def low(v):
    return lax.optimization_barrier(v.astype(jnp.bfloat16)).astype(jnp.float32)

@jax.custom_vjp
def low_back(v):
    return v

def low_keep(v):
    return (low(v), None)

def low_pass(kept, grad):
    return (grad,)

def back_keep(v):
    return (v, None)

def back_low(kept, grad):
    return (low(grad),)
low.defvjp(low_keep, low_pass)
low_back.defvjp(back_keep, back_low)
EPSILON = 1e-05
HIGHEST = lax.Precision.HIGHEST

def matrix_product(left, right):
    return jnp.dot(left, right, precision=HIGHEST, preferred_element_type=jnp.float32)

def contract(form, left, right):
    return jnp.einsum(form, left, right, precision=HIGHEST, preferred_element_type=jnp.float32)

def rms_scale(values):
    return lax.rsqrt(lax.optimization_barrier(jnp.mean(values * values, -1, keepdims=True)) + EPSILON)

def layout(sequence_lengths, first_stretch, stretch_count):
    counts = (sequence_lengths + STRETCH - 1) // STRETCH
    seq_ends = jnp.cumsum(counts).astype(jnp.int32)
    starts = (seq_ends - counts).astype(jnp.int32)
    stretch_ids = (first_stretch + jnp.arange(stretch_count)).astype(jnp.int32)
    member = ((stretch_ids[:, None] >= starts[None]) & (stretch_ids[:, None] < seq_ends[None])).astype(jnp.int32)
    seq_begin = lax.optimization_barrier(jnp.sum(member * starts[None], 1))
    length = lax.optimization_barrier(jnp.sum(member * sequence_lengths[None], 1))
    stretch_gates = (stretch_ids != seq_begin).astype(jnp.float32)
    offset = jnp.arange(STRETCH).astype(jnp.int32)
    valid_mask = (stretch_ids - seq_begin)[:, None] * STRETCH + offset[None] < length[:, None]
    return (stretch_gates, valid_mask)

def attention(query_matrix, key_matrix, value_matrix, query_feature_map, key_feature_map, stretch_gates, valid_mask):
    stretches = TOKENS // STRETCH
    groups = QUERY_HEADS // KEY_VALUE_HEADS
    score_scale = 1.0 / math.sqrt(HEAD_SIZE)
    query5 = query_matrix.reshape(stretches, STRETCH, KEY_VALUE_HEADS, groups, HEAD_SIZE)
    key4 = key_matrix.reshape(stretches, STRETCH, KEY_VALUE_HEADS, HEAD_SIZE)
    value4 = value_matrix.reshape(stretches, STRETCH, KEY_VALUE_HEADS, HEAD_SIZE)
    valid_float = valid_mask.astype(jnp.float32)
    key_feat = jax.nn.softmax(low_back(contract('ctkd,kdf->ctkf', key4, key_feature_map)), -1) * valid_float[:, :, None, None]
    stretch_state = contract('ctkf,ctkd->ckfd', key_feat, value4)
    stretch_norm = lax.optimization_barrier(jnp.sum(key_feat, 1))

    def advance(carry, element):
        carry_state, carry_norm = carry
        block_state, block_norm, gate_value = element
        state_in = gate_value * carry_state
        norm_in = gate_value * carry_norm
        return ((state_in + block_state, norm_in + block_norm), (state_in, norm_in))
    initial = (jnp.zeros((KEY_VALUE_HEADS, FEAT, HEAD_SIZE), jnp.float32), jnp.zeros((KEY_VALUE_HEADS, FEAT), jnp.float32))
    _, (states_in, norms_in) = lax.scan(advance, initial, (stretch_state, stretch_norm, stretch_gates))
    query_feat = jax.nn.softmax(low_back(contract('ctkgd,kgdf->ctkgf', query5, query_feature_map.reshape(KEY_VALUE_HEADS, groups, HEAD_SIZE, FEAT))), -1)
    scores = low_back(contract('ctkgd,cukd->ckgtu', query5, key4) * score_scale)
    causal = jnp.tril(jnp.ones((STRETCH, STRETCH), bool))
    allowed = causal[None, None, None] & valid_mask[:, None, None, None, :]
    row_peak = lax.optimization_barrier(jnp.max(jnp.where(allowed, scores, -1e+30), -1))
    weights_p = jnp.exp(jnp.where(allowed, scores - row_peak[..., None], -1e+30))
    damping = jnp.exp(-row_peak)
    linear_num = damping[..., None] * contract('ctkgf,ckfd->ckgtd', query_feat, states_in)
    linear_den = damping * contract('ctkgf,ckf->ckgt', query_feat, norms_in)
    numerator = low_back(contract('ckgtu,cukd->ckgtd', low(weights_p), value4) + linear_num)
    denominator = lax.optimization_barrier(jnp.sum(weights_p, -1)) + linear_den
    heads_merged = numerator / denominator[..., None]
    return heads_merged.transpose(0, 3, 1, 2, 4).reshape(TOKENS, QUERY_HEADS * HEAD_SIZE)

def block(inputs, weight_collection, stretch_gates, valid_mask):
    attention_gain, query_weight, key_weight, value_weight, output_weight_flipped, query_adapter_down, query_adapter_up, key_adapter_down, key_adapter_up, value_adapter_down, value_adapter_up, output_adapter_down, output_adapter_up, query_feature_map, key_feature_map, feedforward_gain, gate_weight, up_weight, down_weight_flipped = weight_collection
    hidden_first = low(inputs * rms_scale(inputs) * attention_gain)
    query_adapter_rows = low_back(low(matrix_product(hidden_first, query_adapter_down)))
    key_adapter_rows = low_back(low(matrix_product(hidden_first, key_adapter_down)))
    value_adapter_rows = low_back(low(matrix_product(hidden_first, value_adapter_down)))
    query_matrix = low_back(low(matrix_product(hidden_first, query_weight) + 2.0 * matrix_product(query_adapter_rows, query_adapter_up)))
    key_matrix = low_back(low(matrix_product(hidden_first, key_weight) + 2.0 * matrix_product(key_adapter_rows, key_adapter_up)))
    value_matrix = low_back(low(matrix_product(hidden_first, value_weight) + 2.0 * matrix_product(value_adapter_rows, value_adapter_up)))
    heads_merged = attention(query_matrix, key_matrix, value_matrix, query_feature_map, key_feature_map, stretch_gates, valid_mask)
    heads_merged = low_back(low(heads_merged))
    output_adapter_rows = low_back(low(matrix_product(heads_merged, output_adapter_down)))
    branch_rows = low_back(matrix_product(heads_merged, output_weight_flipped.T) + 2.0 * matrix_product(output_adapter_rows, output_adapter_up))
    middle = inputs + branch_rows
    hidden_two = low(middle * rms_scale(middle) * feedforward_gain)
    gate_act = low_back(matrix_product(hidden_two, gate_weight))
    up_act = low_back(matrix_product(hidden_two, up_weight))
    inner_act = low_back(low(jax.nn.silu(gate_act) * up_act))
    return middle + matrix_product(inner_act, down_weight_flipped.T)

def reference(tokens, sequence_lengths, attention_gain, query_weight, key_weight, value_weight, output_weight_flipped, query_adapter_down, query_adapter_up, key_adapter_down, key_adapter_up, value_adapter_down, value_adapter_up, output_adapter_down, output_adapter_up, query_feature_map, key_feature_map, feedforward_gain, gate_weight, up_weight, down_weight_flipped, output_gradient):
    stretch_gates, valid_mask = layout(sequence_lengths, 0, TOKENS // STRETCH)
    weight_collection = tuple((element_value.astype(jnp.float32) for element_value in (attention_gain, query_weight, key_weight, value_weight, output_weight_flipped, query_adapter_down, query_adapter_up, key_adapter_down, key_adapter_up, value_adapter_down, value_adapter_up, output_adapter_down, output_adapter_up, query_feature_map, key_feature_map, feedforward_gain, gate_weight, up_weight, down_weight_flipped)))
    inputs = tokens.astype(jnp.float32)

    def forward(inputs, *weight_collection):
        return block(inputs, weight_collection, stretch_gates, valid_mask)
    result, pullback = jax.vjp(forward, inputs, *weight_collection)
    gradients = pullback(output_gradient.astype(jnp.float32))
    return (result.astype(jnp.bfloat16), gradients[0].astype(jnp.bfloat16), gradients[1], gradients[6], gradients[7], gradients[8], gradients[9], gradients[10], gradients[11], gradients[12], gradients[13], gradients[14], gradients[15], gradients[16])
```

```python
import math

import jax
import jax.numpy as jnp
from jax import lax
from jax.sharding import PartitionSpec as P

QUERY_HEADS = 32
KEY_VALUE_HEADS = 4
HEAD_SIZE = 64
FEAT = 64
STRETCH = 64


EPSILON = 1e-05
HIGHEST = lax.Precision.HIGHEST


def sequence_of(sequence_lengths, stretch_ids):
    counts = (sequence_lengths + STRETCH - 1) // STRETCH
    seq_ends = jnp.cumsum(counts)
    return jnp.sum((stretch_ids[:, None] >= seq_ends[None]).astype(jnp.int32), 1)


def entering(folded, sequence_lengths, stretches_dev, reverse):
    peers, position = (lax.axis_size("seq"), lax.axis_index("seq"))
    state, norm = (folded[0], folded[1])
    packed = jnp.concatenate([state, norm[:, :, None]], 2).astype(jnp.bfloat16)
    everything = lax.all_gather(packed.reshape(1, -1), "seq", axis=0, tiled=True)
    devices = jnp.arange(peers)
    firsts = sequence_of(sequence_lengths, devices * stretches_dev)
    lasts = sequence_of(sequence_lengths, devices * stretches_dev + stretches_dev - 1)
    if reverse:
        reached = (devices > position) & (firsts == lasts[position])
    else:
        reached = (devices < position) & (lasts == firsts[position])
    total = jnp.dot(
        reached.astype(jnp.bfloat16)[None], everything, preferred_element_type=jnp.float32
    ).reshape(packed.shape)
    return (total[:, :, :HEAD_SIZE], total[:, :, HEAD_SIZE])


def product_result(left, right):
    return jnp.dot(left, right, preferred_element_type=jnp.float32)


def flipped_product(left, right):
    return lax.dot_general(
        left, right, (((0,), (0,)), ((), ())), preferred_element_type=jnp.float32
    )


def product_flipped(left, right):
    return lax.dot_general(
        left, right, (((1,), (1,)), ((), ())), preferred_element_type=jnp.float32
    )


def layout(sequence_lengths, first_stretch, stretch_count):
    counts = (sequence_lengths + STRETCH - 1) // STRETCH
    seq_ends = jnp.cumsum(counts)
    starts = seq_ends - counts
    stretch_ids = first_stretch + jnp.arange(stretch_count)
    member = (
        (stretch_ids[:, None] >= starts[None]) & (stretch_ids[:, None] < seq_ends[None])
    ).astype(jnp.int32)
    seq_begin = jnp.sum(member * starts[None], 1)
    length = jnp.sum(member * sequence_lengths[None], 1)
    stretch_gates = (stretch_ids != seq_begin).astype(jnp.float32)
    offset = jnp.arange(STRETCH)
    valid_mask = (stretch_ids - seq_begin)[:, None] * STRETCH + offset[None] < length[:, None]
    return (stretch_gates, valid_mask)


def combine(earlier, later):
    return (
        later[0] + later[2] * earlier[0],
        later[1] + later[2] * earlier[1],
        later[2] * earlier[2],
    )


def identity_element():
    return (
        jnp.zeros((KEY_VALUE_HEADS, FEAT, HEAD_SIZE), jnp.float32),
        jnp.zeros((KEY_VALUE_HEADS, FEAT), jnp.float32),
        jnp.ones((), jnp.float32),
    )


def fold_local(block_states, block_norms, stretch_gates, backward):
    folded = identity_element()
    positions = list(range(stretch_gates.shape[0]))
    if backward:
        positions = positions[::-1]
    for position in positions:
        folded = combine(
            folded, (block_states[position], block_norms[position], stretch_gates[position])
        )
    return folded


def key_side(key4, value4, key_feature_map, valid_mask):
    logits = jnp.einsum("ctkd,kdf->ctkf", key4, key_feature_map, preferred_element_type=jnp.float32)
    key_feat = jax.nn.softmax(logits, -1)
    key_masked = key_feat * valid_mask.astype(jnp.float32)[:, :, None, None]
    stretch_state = jnp.einsum(
        "ctkf,ctkd->ckfd", key_masked, value4.astype(jnp.float32), precision=HIGHEST
    )
    stretch_norm = jnp.sum(key_masked, 1)
    return (key_feat, key_masked, stretch_state, stretch_norm)


def spread_states(prefix, stretch_state, stretch_norm, stretch_gates):
    carry_state, carry_norm = (prefix[0], prefix[1])
    states_in, norms_in = ([], [])
    for position in range(stretch_gates.shape[0]):
        carry_state = stretch_gates[position] * carry_state
        carry_norm = stretch_gates[position] * carry_norm
        states_in.append(carry_state)
        norms_in.append(carry_norm)
        carry_state = carry_state + stretch_state[position]
        carry_norm = carry_norm + stretch_norm[position]
    return (jnp.stack(states_in), jnp.stack(norms_in))


def query_side(query5, key4, value4, feat_q4, states_in, norms_in, allowed, score_scale):
    logits = jnp.einsum("ctkgd,kgdf->ctkgf", query5, feat_q4, preferred_element_type=jnp.float32)
    query_feat = jax.nn.softmax(logits, -1)
    scores = (
        jnp.einsum("ctkgd,cukd->ckgtu", query5, key4, preferred_element_type=jnp.float32)
        * score_scale
    )
    row_peak = jnp.max(jnp.where(allowed, scores, -1e30), -1)
    weights_p = jnp.exp(jnp.where(allowed, scores - row_peak[..., None], -1e30))
    damping = jnp.exp(-row_peak)
    linear_num = damping[..., None] * jnp.einsum(
        "ctkgf,ckfd->ckgtd", query_feat, states_in, precision=HIGHEST
    )
    linear_den = damping * jnp.einsum("ctkgf,ckf->ckgt", query_feat, norms_in, precision=HIGHEST)
    numerator = (
        jnp.einsum(
            "ckgtu,cukd->ckgtd",
            weights_p.astype(jnp.bfloat16),
            value4,
            preferred_element_type=jnp.float32,
        )
        + linear_num
    )
    denominator = jnp.sum(weights_p, -1) + linear_den
    return (query_feat, weights_p, damping, numerator, denominator)


def to_tokens(heads_first):
    return heads_first.transpose(0, 3, 1, 2, 4).reshape(-1, QUERY_HEADS * HEAD_SIZE)


def attention_back(
    heads_merged_gradient,
    query5,
    key4,
    value4,
    feat_q4,
    key_feature_map,
    key_feat,
    key_masked,
    query_feat,
    weights_p,
    damping,
    numerator,
    denominator,
    states_in,
    norms_in,
    stretch_gates,
    valid_mask,
    score_scale,
    sequence_lengths,
):
    stretches_dev = query5.shape[0]
    grad_heads = (
        heads_merged_gradient.astype(jnp.float32)
        .reshape(stretches_dev, STRETCH, KEY_VALUE_HEADS, QUERY_HEADS // KEY_VALUE_HEADS, HEAD_SIZE)
        .transpose(0, 2, 3, 1, 4)
    )
    mixed_full = numerator / denominator[..., None]
    numerator_grad = (grad_heads / denominator[..., None]).astype(jnp.bfloat16)
    denominator_grad = -jnp.sum(grad_heads * mixed_full, -1) / denominator
    prob_grad = (
        jnp.einsum("ckgtd,cukd->ckgtu", numerator_grad, value4, preferred_element_type=jnp.float32)
        + denominator_grad[..., None]
    )
    score_grad = (weights_p * prob_grad).astype(jnp.bfloat16)
    query_gradient = (
        jnp.einsum("ckgtu,cukd->ctkgd", score_grad, key4, preferred_element_type=jnp.float32)
        * score_scale
    )
    key_gradient = (
        jnp.einsum("ckgtu,ctkgd->cukd", score_grad, query5, preferred_element_type=jnp.float32)
        * score_scale
    )
    value_gradient = jnp.einsum(
        "ckgtu,ckgtd->cukd",
        weights_p.astype(jnp.bfloat16),
        numerator_grad,
        preferred_element_type=jnp.float32,
    )
    numer_wide = numerator_grad.astype(jnp.float32)
    damp_tokens = damping.transpose(0, 3, 1, 2)[..., None]
    denom_tokens = denominator_grad.transpose(0, 3, 1, 2)
    qfeat_grad = damp_tokens * (
        jnp.einsum("ckgtd,ckfd->ctkgf", numer_wide, states_in, precision=HIGHEST)
        + denom_tokens[..., None] * norms_in[:, None, :, None, :]
    )
    weighted = query_feat * damp_tokens
    state_in_grad = jnp.einsum("ctkgf,ckgtd->ckfd", weighted, numer_wide, precision=HIGHEST)
    norm_in_grad = jnp.einsum("ctkgf,ctkg->ckf", weighted, denom_tokens, precision=HIGHEST)
    suffix = entering(
        fold_local(
            state_in_grad,
            norm_in_grad,
            jnp.concatenate([stretch_gates[1:], stretch_gates[:1]]),
            True,
        ),
        sequence_lengths,
        stretches_dev,
        True,
    )
    carry_state, carry_norm = (suffix[0], suffix[1])
    state_grads, norm_grads = ([None] * stretches_dev, [None] * stretches_dev)
    for position in reversed(range(stretches_dev)):
        state_grads[position] = carry_state
        norm_grads[position] = carry_norm
        carry_state = stretch_gates[position] * (state_in_grad[position] + carry_state)
        carry_norm = stretch_gates[position] * (norm_in_grad[position] + carry_norm)
    stretch_state_grad = jnp.stack(state_grads)
    stretch_norm_grad = jnp.stack(norm_grads)
    kfeat_grad = (
        jnp.einsum(
            "ctkd,ckfd->ctkf", value4.astype(jnp.float32), stretch_state_grad, precision=HIGHEST
        )
        + stretch_norm_grad[:, None]
    ) * valid_mask.astype(jnp.float32)[:, :, None, None]
    value_gradient = value_gradient + jnp.einsum(
        "ctkf,ckfd->ctkd", key_masked, stretch_state_grad, precision=HIGHEST
    )
    key_logit_grad = (
        key_feat * (kfeat_grad - jnp.sum(key_feat * kfeat_grad, -1, keepdims=True))
    ).astype(jnp.bfloat16)
    query_logit_grad = (
        query_feat * (qfeat_grad - jnp.sum(query_feat * qfeat_grad, -1, keepdims=True))
    ).astype(jnp.bfloat16)
    key_gradient = key_gradient + jnp.einsum(
        "ctkf,kdf->ctkd", key_logit_grad, key_feature_map, preferred_element_type=jnp.float32
    )
    query_gradient = query_gradient + jnp.einsum(
        "ctkgf,kgdf->ctkgd", query_logit_grad, feat_q4, preferred_element_type=jnp.float32
    )
    feat_key_grad = jnp.einsum(
        "ctkd,ctkf->kdf", key4, key_logit_grad, preferred_element_type=jnp.float32
    )
    feat_query_grad = jnp.einsum(
        "ctkgd,ctkgf->kgdf", query5, query_logit_grad, preferred_element_type=jnp.float32
    ).reshape(QUERY_HEADS, HEAD_SIZE, FEAT)
    return (
        query_gradient.reshape(-1, QUERY_HEADS * HEAD_SIZE).astype(jnp.bfloat16),
        key_gradient.reshape(-1, KEY_VALUE_HEADS * HEAD_SIZE).astype(jnp.bfloat16),
        value_gradient.reshape(-1, KEY_VALUE_HEADS * HEAD_SIZE).astype(jnp.bfloat16),
        feat_query_grad,
        feat_key_grad,
    )


def body(
    tokens,
    sequence_lengths,
    attention_gain,
    query_weight,
    key_weight,
    value_weight,
    output_weight_flipped,
    query_adapter_down,
    query_adapter_up,
    key_adapter_down,
    key_adapter_up,
    value_adapter_down,
    value_adapter_up,
    output_adapter_down,
    output_adapter_up,
    query_feature_map,
    key_feature_map,
    feedforward_gain,
    gate_weight,
    up_weight,
    down_weight_flipped,
    output_gradient,
):
    rows_dev = tokens.shape[0]
    stretches_dev = rows_dev // STRETCH
    groups = QUERY_HEADS // KEY_VALUE_HEADS
    score_scale = 1.0 / math.sqrt(HEAD_SIZE)
    stretch_gates, valid_mask = layout(
        sequence_lengths, lax.axis_index("seq") * stretches_dev, stretches_dev
    )
    causal = jnp.tril(jnp.ones((STRETCH, STRETCH), bool))
    allowed = causal[None, None, None] & valid_mask[:, None, None, None, :]
    inputs = tokens.astype(jnp.float32)
    rms_one = lax.rsqrt(jnp.mean(inputs * inputs, -1, keepdims=True) + EPSILON)
    normed_one = inputs * rms_one
    gain_one = attention_gain.astype(jnp.float32)
    hidden_first = (normed_one * gain_one).astype(jnp.bfloat16)
    attention_rows = jnp.concatenate(
        [query_weight, key_weight, value_weight, output_weight_flipped], 1
    )
    attention_all = lax.all_gather(attention_rows, "seq", axis=0, tiled=True)
    width, narrow = (query_weight.shape[1], key_weight.shape[1])
    attention_whole = (
        attention_all[:, :width],
        attention_all[:, width : width + narrow],
        attention_all[:, width + narrow : width + 2 * narrow],
        attention_all[:, width + 2 * narrow :],
    )

    def apply_projection(weight_matrix, adapter_first_factor, adapter_second_factor):
        adapter_update = product_result(hidden_first, adapter_first_factor).astype(jnp.bfloat16)
        projection_result = product_result(hidden_first, weight_matrix) + 2.0 * product_result(
            adapter_update, adapter_second_factor
        )
        return (adapter_update, projection_result.astype(jnp.bfloat16))

    query_adapter_rows, query_matrix = apply_projection(
        attention_whole[0], query_adapter_down, query_adapter_up
    )
    key_adapter_rows, key_matrix = apply_projection(
        attention_whole[1], key_adapter_down, key_adapter_up
    )
    value_adapter_rows, value_matrix = apply_projection(
        attention_whole[2], value_adapter_down, value_adapter_up
    )
    query5 = query_matrix.reshape(stretches_dev, STRETCH, KEY_VALUE_HEADS, groups, HEAD_SIZE)
    key4 = key_matrix.reshape(stretches_dev, STRETCH, KEY_VALUE_HEADS, HEAD_SIZE)
    value4 = value_matrix.reshape(stretches_dev, STRETCH, KEY_VALUE_HEADS, HEAD_SIZE)
    feat_q4 = query_feature_map.reshape(KEY_VALUE_HEADS, groups, HEAD_SIZE, FEAT)
    key_feat, key_masked, stretch_state, stretch_norm = key_side(
        key4, value4, key_feature_map, valid_mask
    )
    prefix = entering(
        fold_local(stretch_state, stretch_norm, stretch_gates, False),
        sequence_lengths,
        stretches_dev,
        False,
    )
    states_in, norms_in = spread_states(prefix, stretch_state, stretch_norm, stretch_gates)
    query_feat, weights_p, damping, numerator, denominator = query_side(
        query5, key4, value4, feat_q4, states_in, norms_in, allowed, score_scale
    )
    heads_merged = to_tokens(numerator / denominator[..., None]).astype(jnp.bfloat16)
    output_adapter_rows = product_result(heads_merged, output_adapter_down).astype(jnp.bfloat16)
    branch_rows = product_flipped(heads_merged, attention_whole[3]) + 2.0 * product_result(
        output_adapter_rows, output_adapter_up
    )
    middle = inputs + branch_rows
    rms_two = lax.rsqrt(jnp.mean(middle * middle, -1, keepdims=True) + EPSILON)
    normed_two = middle * rms_two
    gain_two = feedforward_gain.astype(jnp.float32)
    hidden_two = (normed_two * gain_two).astype(jnp.bfloat16)
    mlp_full = (
        lax.all_gather(gate_weight, "seq", axis=0, tiled=True),
        lax.all_gather(up_weight, "seq", axis=0, tiled=True),
        lax.all_gather(down_weight_flipped, "seq", axis=0, tiled=True),
    )
    gate_act = product_result(hidden_two, mlp_full[0])
    up_act = product_result(hidden_two, mlp_full[1])
    sigmoid_gate = jax.nn.sigmoid(gate_act)
    swish_gate = gate_act * sigmoid_gate
    inner_act = (swish_gate * up_act).astype(jnp.bfloat16)
    block_out = (middle + product_flipped(inner_act, mlp_full[2])).astype(jnp.bfloat16)
    w_q_all, w_k_all, w_v_all, output_weight_whole = attention_whole
    w_g_all, w_u_all, w_d_all = mlp_full
    inner_grad = product_result(output_gradient, w_d_all).astype(jnp.bfloat16).astype(jnp.float32)
    gate_grad = (
        inner_grad * up_act * sigmoid_gate * (1.0 + gate_act * (1.0 - sigmoid_gate))
    ).astype(jnp.bfloat16)
    up_grad = (inner_grad * swish_gate).astype(jnp.bfloat16)
    two_grad = product_flipped(gate_grad, w_g_all) + product_flipped(up_grad, w_u_all)
    gain_mlp_grad = jnp.sum(two_grad * normed_two, 0)
    scaled_two = two_grad * gain_two
    middle_grad = output_gradient.astype(jnp.float32) + rms_two * (
        scaled_two - normed_two * jnp.mean(scaled_two * normed_two, -1, keepdims=True)
    )
    branch_gradient = middle_grad.astype(jnp.bfloat16)
    output_adapter_gradient = (2.0 * product_flipped(branch_gradient, output_adapter_up)).astype(
        jnp.bfloat16
    )
    output_adapter_up_gradient = 2.0 * flipped_product(output_adapter_rows, branch_gradient)
    output_adapter_down_gradient = flipped_product(heads_merged, output_adapter_gradient)
    heads_merged_gradient = (
        product_result(branch_gradient, output_weight_whole)
        + product_flipped(output_adapter_gradient, output_adapter_down)
    ).astype(jnp.bfloat16)
    kept_parts = (
        key_feat,
        key_masked,
        query_feat,
        weights_p,
        damping,
        numerator,
        denominator,
        states_in,
        norms_in,
    )
    query_gradient, key_gradient, value_gradient, feat_query_grad, feat_key_grad = attention_back(
        heads_merged_gradient,
        query5,
        key4,
        value4,
        feat_q4,
        key_feature_map,
        kept_parts[0],
        kept_parts[1],
        kept_parts[2],
        kept_parts[3],
        kept_parts[4],
        kept_parts[5],
        kept_parts[6],
        kept_parts[7],
        kept_parts[8],
        stretch_gates,
        valid_mask,
        score_scale,
        sequence_lengths,
    )
    query_adapter_gradient = (2.0 * product_flipped(query_gradient, query_adapter_up)).astype(
        jnp.bfloat16
    )
    key_adapter_gradient = (2.0 * product_flipped(key_gradient, key_adapter_up)).astype(
        jnp.bfloat16
    )
    value_adapter_gradient = (2.0 * product_flipped(value_gradient, value_adapter_up)).astype(
        jnp.bfloat16
    )
    query_adapter_up_gradient = 2.0 * flipped_product(query_adapter_rows, query_gradient)
    key_adapter_up_gradient = 2.0 * flipped_product(key_adapter_rows, key_gradient)
    value_adapter_up_gradient = 2.0 * flipped_product(value_adapter_rows, value_gradient)
    query_adapter_down_gradient = flipped_product(hidden_first, query_adapter_gradient)
    key_adapter_down_gradient = flipped_product(hidden_first, key_adapter_gradient)
    value_adapter_down_gradient = flipped_product(hidden_first, value_adapter_gradient)
    one_grad = (
        product_flipped(query_gradient, w_q_all)
        + product_flipped(key_gradient, w_k_all)
        + product_flipped(value_gradient, w_v_all)
        + product_flipped(query_adapter_gradient, query_adapter_down)
        + product_flipped(key_adapter_gradient, key_adapter_down)
        + product_flipped(value_adapter_gradient, value_adapter_down)
    )
    gain_attn_grad = jnp.sum(one_grad * normed_one, 0)
    scaled_one = one_grad * gain_one
    grad_tokens = (
        middle_grad
        + rms_one * (scaled_one - normed_one * jnp.mean(scaled_one * normed_one, -1, keepdims=True))
    ).astype(jnp.bfloat16)
    parts = (
        gain_attn_grad,
        query_adapter_down_gradient,
        query_adapter_up_gradient,
        key_adapter_down_gradient,
        key_adapter_up_gradient,
        value_adapter_down_gradient,
        value_adapter_up_gradient,
        output_adapter_down_gradient,
        output_adapter_up_gradient,
        feat_query_grad,
        feat_key_grad,
        gain_mlp_grad,
    )
    flat = jnp.concatenate([part.reshape(-1) for part in parts]).reshape(-1, 1024)
    flat = lax.psum(flat, "seq").reshape(-1)
    summed, at = ([], 0)
    for part in parts:
        summed.append(flat[at : at + part.size].reshape(part.shape))
        at += part.size
    return (
        block_out,
        grad_tokens,
        summed[0],
        summed[1],
        summed[2],
        summed[3],
        summed[4],
        summed[5],
        summed[6],
        summed[7],
        summed[8],
        summed[9],
        summed[10],
        summed[11],
    )


def solution(mesh):
    return jax.shard_map(
        body,
        mesh=mesh,
        in_specs=(
            P("seq", None),
            P(),
            P(),
            P("seq", None),
            P("seq", None),
            P("seq", None),
            P("seq", None),
            P(),
            P(),
            P(),
            P(),
            P(),
            P(),
            P(),
            P(),
            P(),
            P(),
            P(),
            P("seq", None),
            P("seq", None),
            P("seq", None),
            P("seq", None),
        ),
        out_specs=(
            P("seq", None),
            P("seq", None),
            P(),
            P(),
            P(),
            P(),
            P(),
            P(),
            P(),
            P(),
            P(),
            P(),
            P(),
            P(),
        ),
        check_vma=False,
    )
```

```python
import math

import jax
import jax.numpy as jnp
from jax import lax
from jax.experimental import pallas as pl
from jax.experimental.pallas import tpu as pltpu
from jax.sharding import PartitionSpec as P

QUERY_HEADS = 32
KEY_VALUE_HEADS = 4
HEAD = 64
STRETCH = 64
WIDTH = 2048
FF = 5632
ROWS = 128
CHIP = 256
HALF = 1024
NARROW = 128
QKV = HALF + 2 * NARROW
ATT = QKV + HALF
SLICE = FF // 4
AUG = 80
RANK = 8
PIECE = 1280
EPSILON = 1e-05
MESH = pl.DeviceIdType.MESH
F32 = jnp.float32
BF = jnp.bfloat16

SHARES = (
    (1, 0, 0, 64, 128),
    (3, 0, 64, 64, 192),
    (0, 1, 0, 64, 256),
    (0, 3, 64, 64, 320),
    (1, 1, 0, 32, 384),
    (1, 3, 32, 32, 416),
    (3, 1, 64, 32, 448),
    (3, 3, 96, 32, 480),
)


def nn(left, right):
    return jnp.dot(left, right, preferred_element_type=F32)


def nt(left, right):
    return lax.dot_general(left, right, (((1,), (1,)), ((), ())), preferred_element_type=F32)


def wrap(value):
    return lax.rem(value, 4)


class Copies:
    def __init__(self, send, recv):
        self.send, self.recv, self.count, self.open = send, recv, 0, []

    def start(self, src, dst, device):
        copy = pltpu.make_async_remote_copy(
            src_ref=src,
            dst_ref=dst,
            send_sem=self.send.at[self.count],
            recv_sem=self.recv.at[self.count],
            device_id=(device,),
            device_id_type=MESH,
        )
        self.count += 1
        copy.start()
        self.open.append(copy)
        return copy

    def sent(self, copies):
        for copy in copies:
            copy.wait_send()
            self.open = [k for k in self.open if k is not copy]

    def drain(self):
        for copy in self.open:
            copy.wait_send()


class Stream:
    def __init__(self, copies, view, where, device, parts, rings):
        self.copies, self.view, self.where, self.device = copies, view, where, device
        self.parts, self.rings = parts, rings
        self.flying = {}

    def block(self, order, phase, at, first, count):
        index = {}
        for k, axis in enumerate(order):
            if k < phase:
                index[axis] = slice(None)
            elif k == phase:
                index[axis] = at
            else:
                index[axis] = self.where[axis]
        return self.view(index, first, count)

    def begin(self, phase):
        for part, (order, first, count) in enumerate(self.parts):
            axis = order[phase]
            ring = self.rings[axis]
            own = self.block(order, phase, self.where[axis], first, count)
            if ring == 2:
                steps = (2,)
            else:
                steps = (1, 3)
            self.flying[phase, part] = [
                self.copies.start(own, own, self.device({axis: step})) for step in steps
            ]

    def middle(self, phase):
        for part, (order, first, count) in enumerate(self.parts):
            axis = order[phase]
            if self.rings[axis] == 2:
                continue
            flying = self.flying[phase, part]
            for copy in flying:
                copy.wait_recv()
            one = (count // 256) * 128
            left = self.block(order, phase, wrap(self.where[axis] + 3), first, one)
            right = self.block(order, phase, wrap(self.where[axis] + 1), first + one, count - one)
            self.flying[phase, part] = [
                self.copies.start(left, left, self.device({axis: 1})),
                self.copies.start(right, right, self.device({axis: 3})),
            ]

    def end(self, phase):
        for part in range(len(self.parts)):
            for copy in self.flying[phase, part]:
                copy.wait_recv()


def kernel(
    tok, og, qw, kw, vw, ow, gw, uw, dw, aall, ball, oac, ob2, fq_t, fq, fk_t, fk, gain1, gain2, bias, vrow, scal,
    blk_out, gtok_out, red_out,
    wa, wf, tok2, hid1, low, qt, kt, vt, knat, vnat, kfeat, st, comb, comb_t, wts, qfeat, mixf, damp, den, mixn, lowo,
    outs, outr, mid, ht, ogx, gg, inner, ug, rbt, rbb, mgrad, bg, ngt, dgr, sig, qlg, gt, gnat, lowg, ones,
    kacc, vacc, fsend, frecv, hsend, hrecv, red, rr, rz, fin, apart, asib, send, recv, loc,
):
    me = lax.axis_index("seq")
    c = lax.rem(me, 2)
    y = lax.rem(me // 2, 4)
    x = lax.rem(me // 8, 4)
    z = me // 32

    def device(steps):
        zz, xx, yy = (wrap(v + steps.get(n, 0)) for n, v in (("z", z), ("x", x), ("y", y)))
        return ((zz * 4 + xx) * 4 + yy) * 2 + c

    sibling = me + 1 - 2 * c
    plane = x * 4 + y
    xl, yl = lax.rem(x, 2), lax.rem(y, 2)
    xh, yh = x // 2, y // 2

    barrier = pltpu.get_barrier_semaphore()
    peers = [sibling]
    peers += [device({"x": i, "y": j}) for i in range(4) for j in range(4) if i + j > 0]
    peers += [device({"z": i}) for i in (1, 2, 3)]
    for peer in peers:
        pl.semaphore_signal(barrier, inc=1, device_id=(peer,), device_id_type=MESH)
    pl.semaphore_wait(barrier, len(peers))

    copies = Copies(send, recv)
    local = []

    def here(src, dst):
        copy = pltpu.make_async_copy(src, dst, loc.at[len(local)])
        copy.start()
        local.append(copy)

    first = []
    own = wa.at[z, x, y, c]
    for src, at, count in ((qw, 0, HALF), (kw, HALF, NARROW), (vw, HALF + NARROW, NARROW), (ow, QKV, HALF)):
        mine = src.at[:, pl.ds(pl.multiple_of(c * count, count), count)]
        other = src.at[:, pl.ds(pl.multiple_of((1 - c) * count, count), count)]
        dst = own.at[:, pl.ds(at, count)]
        here(mine, dst)
        first.append(copies.start(other, dst, sibling))
    start_ff = []
    ff_own = wf.at[z, xh, xl, yh, yl, c]
    for slot, src in enumerate((gw, uw, dw)):
        dst = ff_own.at[:, pl.ds(slot * SLICE, SLICE)]
        here(src.at[:, pl.ds(pl.multiple_of((xl * 2 + yl) * SLICE, 128), SLICE)], dst)
        for i, j in ((1, 0), (0, 1), (1, 1)):
            tx, ty = lax.rem(xl + i, 2), lax.rem(yl + j, 2)
            chip = (z * 4 + xh * 2 + tx) * 4 + yh * 2 + ty
            cols = pl.ds(pl.multiple_of((tx * 2 + ty) * SLICE, 128), SLICE)
            start_ff.append(copies.start(src.at[:, cols], dst, chip * 2 + c))
    tok_copy = copies.start(tok, tok2.at[c], sibling)
    here(tok, tok2.at[c])
    here(og, ogx.at[pl.ds(0, ROWS)])

    for copy in local:
        copy.wait()
    for copy in first:
        copy.wait_recv()

    def att_view(index, at, count):
        return wa.at[index["z"], index["x"], index["y"], :, :, pl.ds(at, count)]

    def ff_view(index, at, count):
        return wf.at[index["z"], index["x"], :, index["y"], :, c, :, pl.ds(at, count)]

    where_a = {"z": z, "x": x, "y": y}
    where_f = {"z": z, "x": xh, "y": yh}
    ring_a = {"z": 4, "x": 4, "y": 4}
    ring_f = {"z": 4, "x": 2, "y": 2}
    orders = (("y", "x", "z"), ("x", "z", "y"), ("z", "y", "x"))
    s_qkv = Stream(
        copies, att_view, where_a, device,
        ((orders[0], 0, 512), (orders[1], 512, 384), (orders[2], 896, 384)), ring_a,
    )
    s_o = Stream(
        copies, att_view, where_a, device,
        ((orders[0], 1280, 256), (orders[1], 1536, 384), (orders[2], 1920, 384)), ring_a,
    )
    s_d = Stream(
        copies, ff_view, where_f, device,
        ((orders[0], 2816, 512), (orders[1], 3328, 384), (orders[2], 3712, 512)), ring_f,
    )
    s_gu = Stream(
        copies, ff_view, where_f, device,
        ((orders[0], 0, 1024), (orders[1], 1024, 896), (orders[2], 1920, 896)), ring_f,
    )
    s_qkv.begin(0)
    s_qkv.middle(0)
    s_o.begin(0)
    s_qkv.end(0)
    s_qkv.begin(1)

    tok_copy.wait_recv()

    def norm_rows(i, carry):
        rows = pl.ds(i * 32, 32)
        for half in range(2):
            t = tok2[half, rows, :].astype(F32)
            r = lax.rsqrt(jnp.mean(t * t, -1, keepdims=True) + EPSILON)
            hid1[pl.ds(half * ROWS + i * 32, 32), :] = (t * r * gain1[...]).astype(BF)
        return carry

    lax.fori_loop(0, ROWS // 32, norm_rows, 0)
    low[...] = nn(hid1[...], aall[...]).astype(BF)

    s_o.middle(0)
    s_qkv.middle(1)
    s_o.end(0)
    s_qkv.end(1)
    s_qkv.begin(2)
    s_o.begin(1)
    s_o.middle(1)
    s_o.end(1)
    for copy in start_ff:
        copy.wait_recv()
    s_d.begin(0)
    s_qkv.middle(2)
    s_qkv.end(2)
    s_o.begin(2)
    s_d.middle(0)

    kv = nn(hid1[...], wa[:, :, :, :, :, HALF:QKV].reshape(WIDTH, 2 * NARROW))
    kv = (kv + nn(low[...], ball[:, HALF:QKV])).astype(BF)
    kv_t = kv.astype(F32).T.astype(BF)
    lane = lax.broadcasted_iota(jnp.int32, (1, 128), 1)
    low_lane = lane < 64
    for g in range(2):
        keep = low_lane if g == 0 else ~low_lane
        knat[g] = jnp.where(keep, kv[:, :NARROW], jnp.zeros((), BF))
        vnat[g] = jnp.where(keep, kv[:, NARROW:], jnp.zeros((), BF))
        kt[g] = kv_t[g * HEAD : (g + 1) * HEAD]
        tail = lax.broadcasted_iota(jnp.int32, (64, CHIP), 0) == 0
        vt[g, :HEAD] = kv_t[NARROW + g * HEAD : NARROW + (g + 1) * HEAD]
        vt[g, HEAD:] = tail.astype(F32).astype(BF)
    lanes4 = lax.broadcasted_iota(jnp.int32, (1, CHIP), 1) // STRETCH

    def softmax_rows(logits):
        e = jnp.exp(logits - jnp.max(logits, 0, keepdims=True))
        return e / jnp.sum(e, 0, keepdims=True)

    for g in range(2):
        kfeat[g * HEAD : (g + 1) * HEAD] = softmax_rows(nn(fk_t[g], kt[g])) * vrow[:1]
    kf = kfeat[...]
    kf_high = kf.astype(BF)
    kf_rest = (kf - kf_high.astype(F32)).astype(BF)
    for s in range(4):
        got = []
        for g in range(2):
            va = jnp.where(lanes4 == s, vt[g, :AUG], jnp.zeros((), BF))
            got.append(nt(va, kf_high) + nt(va, kf_rest))
        st[s] = jnp.where(low_lane, got[0], got[1])

    def gather_plane(base, folded, slots):
        fsend[base] = folded.astype(BF)
        fly = []
        for i in range(4):
            for j in range(4):
                if i + j > 0:
                    fly.append(copies.start(fsend.at[base], frecv.at[base, plane], device({"x": i, "y": j})))
        frecv[base, plane] = folded.astype(BF)
        return fly

    def fold_plane(base, fly, near, total):
        for copy in fly:
            copy.wait_recv()
        part = jnp.zeros((AUG, 128), F32)
        whole = jnp.zeros((AUG, 128), F32)
        for k in range(16):
            f = frecv[base, k].astype(F32)
            part += scal[near + k] * f
            whole += scal[total + k] * f
        hsend[base] = whole.astype(BF)
        fly = [copies.start(hsend.at[base], hrecv.at[base, i - 1], device({"z": i})) for i in (1, 2, 3)]
        return part, fly

    def fold_line(base, part, fly, far):
        for i, copy in zip((1, 2, 3), fly):
            copy.wait_recv()
            part += scal[far + wrap(z + 4 - i)] * hrecv[base, i - 1].astype(F32)
        return part

    gates = [scal[80 + s] for s in range(4)]
    folded = st[0]
    for s in (1, 2, 3):
        folded = st[s] + gates[s] * folded
    fly = gather_plane(0, folded, None)

    def query_columns(n, carry):
        cols = pl.ds(pl.multiple_of(n * 256, 256), 256)
        q = nn(hid1[...], wa[:, :, :, :, :, cols].reshape(WIDTH, 256)) + nn(low[...], ball[:, cols])
        qt[cols, :] = q.T.astype(BF)
        return carry

    lax.fori_loop(0, 4, query_columns, 0)
    part, fly = fold_plane(0, fly, 0, 16)
    s_o.middle(2)
    s_d.end(0)
    s_d.begin(1)
    prefix = fold_line(0, part, fly, 32)

    def combine(states):
        for g in range(2):
            for p in range(2):
                one, two = states[2 * p], states[2 * p + 1]
                if g == 0:
                    both = jnp.where(low_lane, one, pltpu.roll(two, 64, 1))
                else:
                    both = jnp.where(low_lane, pltpu.roll(one, 64, 1), two)
                yield g * 2 + p, both

    def put_states(states, base):
        for k, both in combine(states):
            comb[base + k] = both.astype(BF)
            tall = jnp.concatenate([both, jnp.zeros((128 - AUG, 128), F32)], 0)
            comb_t[base + k] = tall.T.astype(BF)

    states = [prefix]
    for s in (1, 2, 3):
        states.append(gates[s] * (states[s - 1] + st[s - 1]))
    put_states(states, 0)

    zero_low = jnp.zeros((), BF)

    def head_forward(h, carry):
        g = h // 8
        rows = pl.ds(pl.multiple_of(h * HEAD, HEAD), HEAD)
        logits = nn(fq_t[h], qt[rows, :])
        feat = softmax_rows(logits)
        qfeat[rows, :] = feat
        for p in range(2):
            cols = slice(p * 128, (p + 1) * 128)
            q = qt[rows, cols]
            scores = nn(knat[g, cols, :], jnp.concatenate([q, q], 0)) * 0.125 + bias[p]
            peak = jnp.max(scores, 0, keepdims=True)
            w = jnp.exp(scores - peak).astype(BF)
            wts[h * 2 + p] = w
            dm = jnp.exp(-peak)
            dq = (feat[:, cols] * dm).astype(BF)
            stack = jnp.concatenate(
                [w, jnp.where(low_lane, dq, zero_low), jnp.where(low_lane, zero_low, dq)], 0
            )
            lhs = jnp.concatenate([vt[g, :AUG, cols], comb[g * 2 + p]], 1)
            both = nn(lhs, stack)
            rden = 1.0 / both[HEAD : HEAD + 1]
            damp[h * 2 + p, :1] = dm
            den[h * 2 + p, :1] = rden
            mixf[rows, cols] = both[:HEAD] * rden
        return carry

    lax.fori_loop(0, 8, head_forward, 0)
    s_o.end(2)
    s_d.middle(1)
    s_d.end(1)
    s_d.begin(2)
    s_gu.begin(0)
    s_gu.middle(0)
    def share(src, dst):
        return [
            copies.start(src.at[pl.ds(r, n)], dst.at[pl.ds(at, n)], device({"x": i, "y": j}))
            for i, j, r, n, at in SHARES
        ]

    og_fly = share(og, ogx)
    lax.fori_loop(8, 16, head_forward, 0)
    s_gu.end(0)
    s_gu.begin(1)

    def mix_rows(n, carry):
        cols = pl.ds(pl.multiple_of(n * 256, 256), 256)
        mixn[:, cols] = mixf[cols, :].T.astype(BF)
        return carry

    lax.fori_loop(0, 4, mix_rows, 0)
    lowo[...] = nn(mixn[...], oac[...]).astype(BF)

    def out_columns(n, carry):
        cols = pl.ds(pl.multiple_of(n * 256, 256), 256)
        w = wa[n // 2, pl.ds(pl.multiple_of(lax.rem(n, 2) * 2, 2), 2), :, :, :, QKV:ATT].reshape(256, HALF)
        o = nt(mixn[...], w) + nn(lowo[...], ob2[:, cols])
        mine = jnp.where(c == 0, o[:ROWS], o[ROWS:])
        other = jnp.where(c == 0, o[ROWS:], o[:ROWS])
        mid[:, cols] = mine + tok[:, cols].astype(F32)
        outs[:, cols] = other.astype(BF)
        return carry

    lax.fori_loop(0, 8, out_columns, 0)
    out_copy = copies.start(outs, outr, sibling)
    s_d.middle(2)
    s_d.end(2)
    s_gu.middle(1)
    s_gu.end(1)
    s_gu.begin(2)
    out_copy.wait_recv()

    def middle_rows(i, carry):
        rows = pl.ds(i * 32, 32)
        m = mid[rows, :] + outr[rows, :].astype(F32)
        mid[rows, :] = m
        r = lax.rsqrt(jnp.mean(m * m, -1, keepdims=True) + EPSILON)
        ht[rows, :] = (m * r * gain2[...]).astype(BF)
        return carry

    lax.fori_loop(0, ROWS // 32, middle_rows, 0)
    ht_fly = share(ht, ht)

    def die(at, count):
        v = wf.at[:, :, :, :, :, c, :, pl.ds(at, count)]
        return copies.start(v, v, sibling)

    d_die = die(2 * SLICE, SLICE)
    for copy in og_fly:
        copy.wait_recv()
    d_die.wait_recv()

    def ff_cols(first, count):
        return wf[:, :, :, :, :, :, :, pl.ds(first, count)].reshape(WIDTH, count)

    def inner_columns(at, count):
        gg[:, pl.ds(at, count)] = nn(ogx[...], ff_cols(2 * SLICE + at, count)).astype(BF)

    def chunks(fn):
        def step(n, carry):
            fn(pl.multiple_of(n * 256, 256), 256)
            return carry

        lax.fori_loop(0, 5, step, 0)
        fn(1280, 128)

    chunks(inner_columns)
    s_gu.middle(2)
    s_gu.end(2)
    gu_die = die(0, 2 * SLICE)
    for copy in ht_fly:
        copy.wait_recv()
    gu_die.wait_recv()

    def gate_columns(at, count):
        cols = pl.ds(at, count)
        gate = nn(ht[...], ff_cols(at, count))
        up = nn(ht[...], ff_cols(SLICE + at, count))
        s = 1.0 / (1.0 + jnp.exp(-gate))
        swish = gate * s
        inner[:, cols] = (swish * up).astype(BF)
        d = gg[:, cols].astype(F32)
        gg[:, cols] = (d * up * s * (1.0 + gate * (1.0 - s))).astype(BF)
        ug[:, cols] = (d * swish).astype(BF)

    chunks(gate_columns)

    def ff_rows(n, at):
        return wf[n // 2, lax.rem(n, 2), :, :, :, :, :, pl.ds(at, SLICE)].reshape(256, SLICE)

    copies.sent(ht_fly)
    copies.sent(og_fly)

    def two_columns(n, carry):
        cols = pl.ds(pl.multiple_of(n * 256, 256), 256)
        ogx[:, cols] = (nt(gg[...], ff_rows(n, 0)) + nt(ug[...], ff_rows(n, SLICE))).astype(BF)
        return carry

    def give_back(src, dst, cols):
        return [
            copies.start(src.at[pl.ds(at, n), cols], dst.at[k // 2 - (k > 5), pl.ds(r, n), cols], device({"x": (4 - i) % 4, "y": (4 - j) % 4}))
            for k, (i, j, r, n, at) in enumerate(SHARES)
        ]

    two_fly = []
    for q in range(4):
        lax.fori_loop(2 * q, 2 * q + 2, two_columns, 0)
        two_fly += give_back(ogx, rbt, pl.ds(q * 512, 512))

    def block_columns(n, carry):
        cols = pl.ds(pl.multiple_of(n * 256, 256), 256)
        ht[:, cols] = nt(inner[...], ff_rows(n, 2 * SLICE)).astype(BF)
        return carry

    lax.fori_loop(0, 8, block_columns, 0)
    for copy in two_fly:
        copy.wait_recv()
    blk_fly = give_back(ht, rbb, pl.ds(0, WIDTH))

    def middle_back(i, acc):
        rows = pl.ds(i * 16, 16)
        t = ogx[rows, :].astype(F32)
        for k in range(3):
            t += rbt[k, rows, :].astype(F32)
        m = mid[rows, :]
        r = lax.rsqrt(jnp.mean(m * m, -1, keepdims=True) + EPSILON)
        n = m * r
        acc += jnp.sum(t * n, 0, keepdims=True)
        t = t * gain2[...]
        g = og[rows, :].astype(F32) + r * (t - n * jnp.mean(t * n, -1, keepdims=True))
        mgrad[rows, :] = g
        bg[c, rows, :] = g.astype(BF)
        return acc

    gain_mlp = lax.fori_loop(0, ROWS // 16, middle_back, jnp.zeros((1, WIDTH), F32))
    bg_copy = copies.start(bg.at[c], bg.at[c], sibling)
    bg_copy.wait_recv()
    bgv = bg.at[:, :, :]
    olg = nt(bgv[...].reshape(CHIP, WIDTH), ob2[...])
    olg_low = olg.astype(BF)

    def mixed_columns(n, carry):
        cols = pl.ds(pl.multiple_of(n * 256, 256), 256)
        wcols = pl.ds(pl.multiple_of(QKV + n * 256, 256), 256)
        m = nn(bg[...].reshape(CHIP, WIDTH), wa[:, :, :, :, :, wcols].reshape(WIDTH, 256))
        m += nt(olg_low, oac[cols, :])
        ngt[cols, :] = m.T.astype(BF)
        return carry

    lax.fori_loop(0, 4, mixed_columns, 0)
    lowo_t = lowo[...].astype(F32).T.astype(BF)
    olg_t = olg.T.astype(BF)
    apart[24:32] = 2.0 * nn(lowo_t[:16], bg[...].reshape(CHIP, WIDTH))[:8]
    red[72:80, :HALF] = nn(olg_t[:16], mixn[...])[:8]

    for k in range(4):
        sig[k] = jnp.zeros((AUG, 128), F32)

    def head_states(h, carry):
        g = h // 8
        rows = pl.ds(pl.multiple_of(h * HEAD, HEAD), HEAD)
        for p in range(2):
            cols = slice(p * 128, (p + 1) * 128)
            rden = den[h * 2 + p, :1]
            m = ngt[rows, cols].astype(F32)
            ng = (m * rden).astype(BF)
            dg = -jnp.sum(m * mixf[rows, cols], 0, keepdims=True) * rden
            ngt[rows, cols] = ng
            dgr[h * 2 + p, :1] = dg
            dq = (qfeat[rows, cols] * damp[h * 2 + p, :1]).astype(BF)
            stack = jnp.concatenate([jnp.where(low_lane, dq, zero_low), jnp.where(low_lane, zero_low, dq)], 0)
            tail = jnp.where(lax.broadcasted_iota(jnp.int32, (AUG - HEAD, 128), 0) == 0, dg, 0.0).astype(BF)
            sig[g * 2 + p] = sig[g * 2 + p] + nt(jnp.concatenate([ng, tail], 0), stack)
        return carry

    lax.fori_loop(0, 16, head_states, 0)
    sg_states = []
    for p in range(2):
        a, b = sig[p], sig[2 + p]
        sg_states.append(jnp.where(low_lane, a, pltpu.roll(b, 64, 1)))
        sg_states.append(jnp.where(low_lane, pltpu.roll(a, 64, 1), b))
    for s in range(4):
        st[s] = sg_states[s]
    folded = sg_states[3]
    for s in (2, 1, 0):
        folded = sg_states[s] + gates[s + 1] * folded
    fly = gather_plane(1, folded, None)

    for k in range(4):
        kacc[k] = jnp.zeros((HEAD, 128), F32)
        vacc[k] = jnp.zeros((HEAD, 128), F32)

    def head_back(h, carry):
        g = h // 8
        rows = pl.ds(pl.multiple_of(h * HEAD, HEAD), HEAD)
        for p in range(2):
            cols = slice(p * 128, (p + 1) * 128)
            ng = ngt[rows, cols]
            dg = dgr[h * 2 + p, :1]
            w = wts[h * 2 + p]
            pt = nn(vnat[g, cols, :], jnp.concatenate([ng, ng], 0)) + dg
            sgr = (w.astype(F32) * pt).astype(BF)
            tail = jnp.where(lax.broadcasted_iota(jnp.int32, (HEAD, 128), 0) == 0, dg, 0.0).astype(BF)
            both = nn(comb_t[g * 2 + p], jnp.concatenate([ng, tail], 0))
            qg = jnp.where(low_lane, both[:HEAD], both[HEAD:]) * damp[h * 2 + p, :1]
            f = qfeat[rows, cols]
            ql = (f * (qg - jnp.sum(f * qg, 0, keepdims=True))).astype(BF)
            qlg[rows, cols] = ql
            gt[rows, cols] = (nn(kt[g, :, cols], sgr) * 0.125 + nn(fq[h], ql)).astype(BF)
            kacc[g * 2 + p] = kacc[g * 2 + p] + nt(qt[rows, cols], sgr)
            vacc[g * 2 + p] = vacc[g * 2 + p] + nt(ng, w)
        return carry

    lax.fori_loop(0, 8, head_back, 0)
    part, fly = fold_plane(1, fly, 36, 52)
    lax.fori_loop(8, 16, head_back, 0)
    suffix = fold_line(1, part, fly, 68)
    states = [None, None, None, suffix]
    for s in (2, 1, 0):
        states[s] = gates[s + 1] * (states[s + 1] + st[s + 1])
    put_states(states, 4)

    valid = vrow[:1]
    for g in range(2):
        f_rows = slice(g * HEAD, (g + 1) * HEAD)
        for p in range(2):
            k = g * 2 + p
            cols = slice(p * 128, (p + 1) * 128)
            f = kfeat[f_rows, cols]
            both = nn(comb_t[4 + k], vt[g, :, cols])
            fg = jnp.where(low_lane, both[:HEAD], both[HEAD:]) * valid[:, cols]
            kl = (f * (fg - jnp.sum(f * fg, 0, keepdims=True))).astype(BF)
            qlg[HALF + g * HEAD : HALF + (g + 1) * HEAD, cols] = kl
            gt[HALF + g * HEAD : HALF + (g + 1) * HEAD, cols] = (kacc[k] * 0.125 + nn(fk[g], kl)).astype(BF)
            fl = f.astype(BF)
            stack = jnp.concatenate([jnp.where(low_lane, fl, zero_low), jnp.where(low_lane, zero_low, fl)], 0)
            gt[HALF + NARROW + g * HEAD : HALF + NARROW + (g + 1) * HEAD, cols] = (
                vacc[k] + nn(comb[4 + k, :HEAD], stack)
            ).astype(BF)

    def feat_pairs(n, carry):
        rows = pl.ds(pl.multiple_of(n * 128, 128), 128)
        r = nt(qt[rows, :], qlg[rows, :])
        red[0:64, rows] = jnp.where(low_lane, r[:HEAD], r[HEAD:])
        return carry

    lax.fori_loop(0, 8, feat_pairs, 0)
    r = nt(kt[...].reshape(128, CHIP), qlg[HALF:, :])
    red[0:64, HALF : HALF + 128] = jnp.where(low_lane, r[:HEAD], r[HEAD:])

    lowg_t = nn(ball[...], gt[...])
    lowg[...] = lowg_t.T.astype(BF)
    lowg_t = lowg_t.astype(BF)
    low_t = low[...].astype(F32).T.astype(BF)
    up = 2.0 * nt(low_t[:32], gt[...])
    red[64:72, :HALF] = up[0:8, :HALF]
    red[64:72, HALF : HALF + NARROW] = up[8:16, HALF : HALF + NARROW]
    red[64:72, HALF + NARROW :] = up[16:24, HALF + NARROW :]
    apart[0:24] = nn(lowg_t[:32], hid1[...])[:24]

    def grad_rows(n, carry):
        rows = pl.ds(pl.multiple_of(n * 256, 256), 256)
        gnat[:, rows] = gt[rows, :].astype(F32).T.astype(BF)
        return carry

    lax.fori_loop(0, 5, grad_rows, 0)

    def one_columns(n, carry):
        cols = pl.ds(pl.multiple_of(n * 256, 256), 256)
        w = wa[n // 2, pl.ds(pl.multiple_of(lax.rem(n, 2) * 2, 2), 2), :, :, :, 0:QKV].reshape(256, QKV)
        o = nt(gnat[...], w) + nt(lowg[...], aall[cols, :])
        ones[:, cols] = jnp.where(c == 0, o[:ROWS], o[ROWS:])
        outs[:, cols] = jnp.where(c == 0, o[ROWS:], o[:ROWS]).astype(BF)
        return carry

    copies.sent([out_copy])
    lax.fori_loop(0, 8, one_columns, 0)
    one_copy = copies.start(outs, outr, sibling)

    for copy in blk_fly:
        copy.wait_recv()

    def block_rows(i, carry):
        rows = pl.ds(i * 16, 16)
        t = mid[rows, :] + ht[rows, :].astype(F32)
        for k in range(3):
            t += rbb[k, rows, :].astype(F32)
        blk_out[rows, :] = t.astype(BF)
        return carry

    lax.fori_loop(0, ROWS // 16, block_rows, 0)
    one_copy.wait_recv()

    def token_rows(i, acc):
        rows = pl.ds(i * 16, 16)
        o = ones[rows, :] + outr[rows, :].astype(F32)
        t = tok[rows, :].astype(F32)
        r = lax.rsqrt(jnp.mean(t * t, -1, keepdims=True) + EPSILON)
        n = t * r
        acc += jnp.sum(o * n, 0, keepdims=True)
        o = o * gain1[...]
        gtok_out[rows, :] = (mgrad[rows, :] + r * (o - n * jnp.mean(o * n, -1, keepdims=True))).astype(BF)
        return acc

    gain_attn = lax.fori_loop(0, ROWS // 16, token_rows, jnp.zeros((1, WIDTH), F32))
    row8 = lax.broadcasted_iota(jnp.int32, (8, 1), 0)
    apart[32:40] = jnp.where(row8 == 0, gain_attn, 0.0) + jnp.where(row8 == 1, gain_mlp, 0.0)

    theirs = pl.ds(pl.multiple_of((1 - c) * HALF, HALF), HALF)
    mine = pl.ds(pl.multiple_of(c * HALF, HALF), HALF)
    a_copy = copies.start(apart.at[:, theirs], asib, sibling)
    red[72:80, HALF:] = jnp.zeros((8, PIECE - HALF), F32)
    red[0:64, HALF + 128 :] = jnp.zeros((64, 128), F32)
    red[80:128, HALF:] = jnp.zeros((48, PIECE - HALF), F32)
    red[120:128, :HALF] = jnp.zeros((8, HALF), F32)
    a_copy.wait_recv()
    red[80:120, :HALF] = apart[:, mine] + asib[...]
    fly = []
    for i in range(4):
        for j in range(4):
            if i + j > 0:
                to = wrap(x + i) * 4 + wrap(y + j)
                src = red.at[pl.ds(pl.multiple_of(to * 8, 8), 8)]
                fly.append(copies.start(src, rr.at[plane], device({"x": i, "y": j})))
    rr[plane] = red[pl.ds(pl.multiple_of(plane * 8, 8), 8), :]
    for copy in fly:
        copy.wait_recv()
    total = rr[0]
    for k in range(1, 16):
        total += rr[k]
    rz[z] = total
    fly = [copies.start(rz.at[z], rz.at[z], device({"z": i})) for i in (1, 2, 3)]
    for copy in fly:
        copy.wait_recv()
    total = (rz[0] + rz[1]) + (rz[2] + rz[3])
    fin[c, plane] = total
    piece = fin.at[c, plane]
    fly = [
        copies.start(piece, piece, device({"x": i, "y": j})) for i in range(4) for j in range(4) if i + j > 0
    ]
    for copy in fly:
        copy.wait_recv()
    f_copy = copies.start(fin.at[c], fin.at[c], sibling)
    f_copy.wait_recv()
    red_out[...] = fin[...]
    copies.drain()


N_COPIES = 400


def scratch():
    v = pltpu.VMEM
    return [
        v((4, 4, 4, 2, 16, ATT), BF),
        v((4, 2, 2, 2, 2, 2, 16, 3 * SLICE), BF),
        v((2, ROWS, WIDTH), BF),
        v((CHIP, WIDTH), BF),
        v((CHIP, 128), BF),
        v((HALF, CHIP), BF),
        v((2, HEAD, CHIP), BF),
        v((2, 128, CHIP), BF),
        v((2, CHIP, 128), BF),
        v((2, CHIP, 128), BF),
        v((128, CHIP), F32),
        v((4, AUG, 128), F32),
        v((8, AUG, 128), BF),
        v((8, 128, 128), BF),
        v((32, 128, 128), BF),
        v((HALF, CHIP), F32),
        v((HALF, CHIP), F32),
        v((32, 8, 128), F32),
        v((32, 8, 128), F32),
        v((CHIP, HALF), BF),
        v((CHIP, 128), BF),
        v((ROWS, WIDTH), BF),
        v((ROWS, WIDTH), BF),
        v((ROWS, WIDTH), F32),
        v((512, WIDTH), BF),
        v((512, WIDTH), BF),
        v((512, SLICE), BF),
        v((512, SLICE), BF),
        v((512, SLICE), BF),
        v((3, ROWS, WIDTH), BF),
        v((3, ROWS, WIDTH), BF),
        v((ROWS, WIDTH), F32),
        v((2, ROWS, WIDTH), BF),
        v((HALF, CHIP), BF),
        v((32, 8, 128), F32),
        v((4, AUG, 128), F32),
        v((HALF + 128, CHIP), BF),
        v((QKV, CHIP), BF),
        v((CHIP, QKV), BF),
        v((CHIP, 128), BF),
        v((ROWS, WIDTH), F32),
        v((4, HEAD, 128), F32),
        v((4, HEAD, 128), F32),
        v((2, AUG, 128), BF),
        v((2, 16, AUG, 128), BF),
        v((2, AUG, 128), BF),
        v((2, 3, AUG, 128), BF),
        v((128, PIECE), F32),
        v((16, 8, PIECE), F32),
        v((4, 8, PIECE), F32),
        v((2, 16, 8, PIECE), F32),
        v((40, WIDTH), F32),
        v((40, HALF), F32),
        pltpu.SemaphoreType.DMA((N_COPIES,)),
        pltpu.SemaphoreType.DMA((N_COPIES,)),
        pltpu.SemaphoreType.DMA((16,)),
    ]


def body(
    tokens, sequence_lengths, attention_gain, query_weight, key_weight, value_weight, output_weight_flipped,
    query_adapter_down, query_adapter_up, key_adapter_down, key_adapter_up, value_adapter_down, value_adapter_up,
    output_adapter_down, output_adapter_up, query_feature_map, key_feature_map, feedforward_gain,
    gate_weight, up_weight, down_weight_flipped, output_gradient,
):
    me = lax.axis_index("seq")
    c = me % 2
    chip = me // 2
    plane, z = chip % 16, chip // 16
    heads = QUERY_HEADS // 2

    counts = (sequence_lengths + STRETCH - 1) // STRETCH
    ends = jnp.cumsum(counts)
    starts = ends - counts

    def sid(stretch):
        return jnp.sum((stretch[..., None] >= ends).astype(jnp.int32), -1)

    own = chip * 4 + jnp.arange(4)
    own_sid = sid(own)
    member = (own_sid[:, None] == jnp.arange(8)[None]).astype(jnp.int32)
    begin = jnp.sum(member * starts[None], 1)
    length = jnp.sum(member * sequence_lengths[None], 1)
    valid = ((own - begin)[:, None] * STRETCH + jnp.arange(STRETCH)[None] < length[:, None]).reshape(CHIP)
    valid_f = valid.astype(F32)
    vrow = jnp.broadcast_to(valid_f[None], (8, CHIP))
    at = jnp.arange(128)
    allowed = (at[:, None] <= at[None]) & (at[:, None] // STRETCH == at[None] // STRETCH)
    bias = jnp.where(allowed[None] & valid.reshape(2, 128)[:, :, None], 0.0, -1e30).astype(F32)

    chips = z * 16 + jnp.arange(16)
    first_sid, last_sid = sid(chips * 4), sid(chips * 4 + 3)
    planes = jnp.arange(4)
    plane_first, plane_last = sid(planes * 64), sid(planes * 64 + 63)
    k16 = jnp.arange(16)
    s0, s3 = own_sid[0], own_sid[3]
    same = jnp.concatenate([jnp.zeros((1,), bool), own_sid[1:] == own_sid[:-1]])
    scal = jnp.concatenate([
        (k16 < plane) & (last_sid == s0),
        last_sid == plane_last[z],
        (planes < z) & (plane_last == s0),
        (k16 > plane) & (first_sid == s3),
        first_sid == plane_first[z],
        (planes > z) & (plane_first == s3),
        jnp.zeros((8,), bool),
        same,
    ]).astype(F32)

    def core(array, axis):
        count = array.shape[axis] // 2
        return lax.dynamic_slice_in_dim(array, c * count, count, axis)

    aall = jnp.concatenate([query_adapter_down, key_adapter_down, value_adapter_down], 1)
    aall = jnp.pad(aall, ((0, 0), (0, 128 - 3 * RANK)))
    ball = jnp.zeros((128, QKV), BF)
    ball = lax.dynamic_update_slice(ball, 2 * core(query_adapter_up, 1), (0, 0))
    ball = lax.dynamic_update_slice(ball, 2 * core(key_adapter_up, 1), (RANK, HALF))
    ball = lax.dynamic_update_slice(ball, 2 * core(value_adapter_up, 1), (2 * RANK, HALF + NARROW))
    oac = jnp.pad(core(output_adapter_down, 0), ((0, 0), (0, 128 - RANK)))
    ob2 = jnp.pad(2 * output_adapter_up, ((0, 128 - RANK), (0, 0)))
    fq = core(query_feature_map, 0)
    fk = core(key_feature_map, 0)

    vmem = pl.BlockSpec(memory_space=pltpu.VMEM)
    smem = pl.BlockSpec(memory_space=pltpu.SMEM)
    block_out, grad_tokens, red = pl.pallas_call(
        kernel,
        out_shape=(
            jax.ShapeDtypeStruct((ROWS, WIDTH), BF),
            jax.ShapeDtypeStruct((ROWS, WIDTH), BF),
            jax.ShapeDtypeStruct((2, 16, 8, PIECE), F32),
        ),
        in_specs=[vmem] * 21 + [smem],
        out_specs=(vmem, vmem, vmem),
        scratch_shapes=scratch(),
        compiler_params=pltpu.CompilerParams(
            collective_id=0, has_side_effects=True, vmem_limit_bytes=64 * 1024 * 1024
        ),
    )(
        tokens, output_gradient, query_weight, key_weight, value_weight, output_weight_flipped,
        gate_weight, up_weight, down_weight_flipped, aall, ball, oac, ob2,
        fq.swapaxes(1, 2), fq, fk.swapaxes(1, 2), fk,
        attention_gain.astype(F32)[None], feedforward_gain.astype(F32)[None], bias, vrow, scal,
    )
    red = red.reshape(2, 128, PIECE)
    both = jnp.concatenate([red[0, 80:120, :HALF], red[1, 80:120, :HALF]], 1)

    def columns(rows, first, count):
        return jnp.concatenate([red[0, rows, first : first + count], red[1, rows, first : first + count]], 1)

    feat_q = columns(slice(0, 64), 0, HALF).reshape(HEAD, QUERY_HEADS, HEAD).swapaxes(0, 1)
    feat_k = columns(slice(0, 64), HALF, NARROW).reshape(HEAD, KEY_VALUE_HEADS, HEAD).swapaxes(0, 1)
    return (
        block_out,
        grad_tokens,
        both[32],
        both[0:8].T,
        columns(slice(64, 72), 0, HALF),
        both[8:16].T,
        columns(slice(64, 72), HALF, NARROW),
        both[16:24].T,
        columns(slice(64, 72), HALF + NARROW, NARROW),
        columns(slice(72, 80), 0, HALF).T,
        both[24:32],
        feat_q,
        feat_k,
        both[33],
    )


def solution(mesh):
    split, whole = P("seq", None), P()
    return jax.shard_map(
        body,
        mesh=mesh,
        in_specs=(
            (split, whole, whole) + (split,) * 4 + (whole,) * 11 + (split,) * 4
        ),
        out_specs=(split, split) + (whole,) * 12,
        check_vma=False,
    )
```

```python
import math

import jax
import jax.numpy as jnp
from jax import lax
from jax.experimental import pallas as pl
from jax.experimental.pallas import tpu as pltpu
from jax.sharding import PartitionSpec as P

QUERY_HEADS = 32
KEY_VALUE_HEADS = 4
HEAD = 64
STRETCH = 64
WIDTH = 2048
FF = 5632
ROWS = 128
CHIP = 256
HALF = 1024
NARROW = 128
QKV = HALF + 2 * NARROW
ATT = QKV + HALF
SLICE = FF // 4
AUG = 80
RANK = 8
PIECE = 1280
EPSILON = 1e-05
MESH = pl.DeviceIdType.MESH
F32 = jnp.float32
BF = jnp.bfloat16

SHARES = (
    (1, 0, 0, 64, 128),
    (3, 0, 64, 64, 192),
    (0, 1, 0, 64, 256),
    (0, 3, 64, 64, 320),
    (1, 1, 0, 32, 384),
    (1, 3, 32, 32, 416),
    (3, 1, 64, 32, 448),
    (3, 3, 96, 32, 480),
)


def nn(left, right):
    return jnp.dot(left, right, preferred_element_type=F32)


def tn(left, right):
    return lax.dot_general(left, right, (((0,), (0,)), ((), ())), preferred_element_type=F32)


def nt(left, right):
    return lax.dot_general(left, right, (((1,), (1,)), ((), ())), preferred_element_type=F32)


def wrap(value):
    return lax.rem(value, 4)


class Copies:
    def __init__(self, send, recv):
        self.send, self.recv, self.count, self.open = send, recv, 0, {}

    def start(self, src, dst, device):
        slot = self.count % N_SENDS
        if slot in self.open:
            self.open.pop(slot).wait_send()
        copy = pltpu.make_async_remote_copy(
            src_ref=src,
            dst_ref=dst,
            send_sem=self.send.at[slot],
            recv_sem=self.recv.at[self.count],
            device_id=(device,),
            device_id_type=MESH,
        )
        self.count += 1
        copy.start()
        self.open[slot] = copy
        return copy

    def sent(self, copies):
        for slot in [k for k, copy in self.open.items() if any(copy is other for other in copies)]:
            self.open.pop(slot).wait_send()

    def drain(self):
        for copy in self.open.values():
            copy.wait_send()


class Heads:
    def __init__(self, copies, wa, where, device, parts, straight=False):
        self.copies, self.wa, self.where, self.device = copies, wa, where, device
        self.parts, self.straight = parts, straight
        self.flying = {}

    def block(self, order, phase, at, first, count):
        index = []
        for axis in "zxy":
            k = order.index(axis)
            index.append(slice(None) if k < phase else at if k == phase else self.where[axis])
        return self.wa.at[index[0], index[1], index[2], :, :, pl.ds(first, count)]

    def begin(self, phase):
        for part, (order, first, count) in enumerate(self.parts):
            axis = order[phase]
            own = self.block(order, phase, self.where[axis], first, count)
            steps = (1, 3) if phase == 2 and not self.straight else (1, 3, 2)
            self.flying[phase, part] = [self.copies.start(own, own, self.device({axis: step})) for step in steps]

    def middle(self, phase):
        for part, (order, first, count) in enumerate(self.parts):
            axis = order[phase]
            for copy in self.flying[phase, part]:
                copy.wait_recv()
            here = self.where[axis]
            one = (count // 256) * 128
            left = self.block(order, phase, wrap(here + 3), first, one)
            right = self.block(order, phase, wrap(here + 1), first + one, count - one)
            self.flying[phase, part] = [
                self.copies.start(left, left, self.device({axis: 1})),
                self.copies.start(right, right, self.device({axis: 3})),
            ]

    def end(self, phase):
        for part in range(len(self.parts)):
            for copy in self.flying[phase, part]:
                copy.wait_recv()


class Units:
    def __init__(self, copies, here, wf, stage, where, device, sibling, parts):
        self.copies, self.here, self.wf, self.stage = copies, here, wf, stage
        self.where, self.device, self.sibling, self.parts = where, device, sibling, parts
        self.flying, self.handed, self.own = {}, [], []

    def rows(self, order, along, across, cols):
        w = self.where
        a = (slice(None), slice(None)) if along is None else (along // 2, lax.rem(along, 2))
        b = (across // 2, lax.rem(across, 2))
        x, y = (a, b) if order == "xy" else (b, a)
        return self.wf.at[w["z"], x[0], x[1], y[0], y[1], w["c"], :, cols]

    def line(self, z, cols):
        return self.wf.at[z, :, :, :, :, self.where["c"], :, cols]

    def hand_on(self, block):
        self.handed.append(self.copies.start(block, block, self.sibling))

    def begin(self, phase):
        w = self.where
        for part, (order, src, at, first, count) in enumerate(self.parts):
            cols = pl.ds(first, count)
            a, b = order
            fly = []
            if phase == 0:
                for d in (1, 3, 2, 0):
                    for e in (0, 1):
                        pa, pb = lax.rem(w[a] + d, 2), lax.rem(w[b] + e, 2)
                        slot = pa * 2 + pb if order == "xy" else pb * 2 + pa
                        piece = src.at[:, pl.ds(pl.multiple_of(slot * SLICE + at, 128), count)]
                        if e == 0:
                            dst = self.rows(order, w[a], w[b], cols)
                        else:
                            dst = self.stage.at[w[a] // 2, lax.rem(w[a], 2), :, cols]
                        if d == 0:
                            self.own.append(self.here(piece, dst))
                        else:
                            fly.append(self.copies.start(piece, dst, self.device({a: d})))
            elif phase == 1:
                mine = self.rows(order, None, w[b], cols)
                other = self.stage.at[:, :, :, cols]
                fly = [
                    self.copies.start(other, mine, self.device({b: 1})),
                    self.copies.start(other, mine, self.device({b: 3})),
                    self.copies.start(mine, mine, self.device({b: 2})),
                ]
            else:
                block = self.line(w["z"], cols)
                self.hand_on(block)
                fly = [self.copies.start(block, block, self.device({"z": step})) for step in (1, 3)]
            self.flying[phase, part] = fly

    def middle(self, phase):
        z = self.where["z"]
        for part, (order, src, at, first, count) in enumerate(self.parts):
            for copy in self.flying[phase, part]:
                copy.wait_recv()
            one = (count // 256) * 128
            before, after = wrap(z + 3), wrap(z + 1)
            left = self.line(before, pl.ds(first, one))
            right = self.line(after, pl.ds(first + one, count - one))
            self.flying[phase, part] = [
                self.copies.start(left, left, self.device({"z": 1})),
                self.copies.start(right, right, self.device({"z": 3})),
            ]
            self.hand_on(self.line(before, pl.ds(first, count)))
            self.hand_on(self.line(after, pl.ds(first, count)))

    def end(self, phase):
        if phase == 0:
            for copy in self.own:
                copy.wait()
        for part, (order, src, at, first, count) in enumerate(self.parts):
            for copy in self.flying[phase, part]:
                copy.wait_recv()
            if phase == 2:
                self.hand_on(self.line(wrap(self.where["z"] + 2), pl.ds(first, count)))

    def settle(self):
        for copy in self.handed:
            copy.wait_recv()


EARLY = ("kv.b0", "q.b0", "o.b0", "d.b0", "g.b0",)
PLAN = (
    "kv.e0", "u.b0", "kv.b1", "q.e0", "o.e0", "q.b1", "d.e0", "d.b1", "u.e0", "g.e0", "o.b1", "d.e1",
    "q.e1", "g.b1", "kv.e1", "u.b1", "q.b2", "kv.b2", "d.b2", "g.e1", "d.m2", "q.m2", "o.e1", "g.b2",
    "kv.e2", "low", "kvc", "pls", "o.b2", "u.e1", "lns", "d.e2", "u.b2", "q.e2", "lnw", "qc",
    "o.m2", "ogs", "g.m2", "att", "o.e2", "ds", "oproj", "mid", "hts", "u.m2", "g.e2", "ogw",
    "ig", "u.e2", "gs", "us", "htw",
)


def kernel(
    tok, lens, gain_a, qw, kw, vw, ow, qa, qb, ka, kb, va, vb, oa, ob, fq, fk, gain_b, gw, uw, dw, og,
    blk_out, gtok_out, gain_a_out, qa_out, qb_out, ka_out, kb_out, va_out, vb_out, oa_out, ob_out, fq_out, fk_out,
    gain_b_out,
    wa, wf, stage, tok2, ogo, gains, r1, aall, ball, oac, ob2, masks, far_masks, bias, hid1, low, qt, kt, vt, knat, vnat,
    kfeat, st, comb, comb_t, wts, qfeat, mixf, damp, den, mixn, lowo, outs, outr, mid, ht, ogx, gg, inner, ug, rbt, rbb,
    mgrad, bg, ngt, dgr, sig, qlg, gt, gnat, lowg, ones, kacc, vacc, fsend, frecv, hsend, hrecv, red, redb, rr, rz, fin,
    apart, asib, send, recv, loc,
):
    me = lax.axis_index("seq")
    c = lax.rem(me, 2)
    y = lax.rem(me // 2, 4)
    x = lax.rem(me // 8, 4)
    z = me // 32

    def device(steps):
        zz, xx, yy = (wrap(v + steps.get(n, 0)) for n, v in (("z", z), ("x", x), ("y", y)))
        return ((zz * 4 + xx) * 4 + yy) * 2 + c

    sibling = me + 1 - 2 * c
    plane = x * 4 + y
    xl, yl = lax.rem(x, 2), lax.rem(y, 2)
    xh, yh = x // 2, y // 2

    barrier = pltpu.get_barrier_semaphore()
    peers = [sibling]
    peers += [device({"x": i, "y": j}) for i in range(4) for j in range(4) if i + j > 0]
    peers += [device({"z": i}) for i in (1, 2, 3)]
    for peer in peers:
        pl.semaphore_signal(barrier, inc=1, device_id=(peer,), device_id_type=MESH)
    pl.semaphore_wait(barrier, len(peers))

    copies = Copies(send, recv)
    local = []

    def here(src, dst):
        copy = pltpu.make_async_copy(src, dst, loc.at[len(local)])
        copy.start()
        local.append(copy)
        return copy

    tok_copy = copies.start(tok, tok2.at[c], sibling)
    first = []
    own = wa.at[z, x, y, c]
    for src, at, count in ((kw, HALF, NARROW), (vw, HALF + NARROW, NARROW), (qw, 0, HALF), (ow, QKV, HALF)):
        mine = src.at[:, pl.ds(pl.multiple_of(c * count, count), count)]
        other = src.at[:, pl.ds(pl.multiple_of((1 - c) * count, count), count)]
        dst = own.at[:, pl.ds(at, count)]
        here(mine, dst)
        first.append(copies.start(other, dst, sibling))
    here(tok, tok2.at[c])
    here(og, ogx.at[pl.ds(0, ROWS)])
    here(og, ogo)

    where = {"z": z, "x": x, "y": y, "c": c}
    streams = {
        "kv": Heads(copies, wa, where, device, (("xzy", 1024, 128), ("yzx", 1152, 128)), straight=True),
        "q": Heads(copies, wa, where, device, [(o, k * 256, 256) for k, o in enumerate(("xzy", "zyx", "zxy", "yzx"))]),
        "o": Heads(
            copies, wa, where, device, [(o, QKV + k * 256, 256) for k, o in enumerate(("xzy", "zyx", "zxy", "yzx"))]
        ),
        "d": Units(
            copies, here, wf, stage, where, device, sibling,
            (("xy", dw, 0, 2 * SLICE, 768), ("yx", dw, 768, 2 * SLICE + 768, 640)),
        ),
        "g": Units(copies, here, wf, stage, where, device, sibling, (("xy", gw, 0, 0, SLICE),)),
        "u": Units(copies, here, wf, stage, where, device, sibling, (("yx", uw, 0, SLICE, SLICE),)),
    }
    for k in range(4):
        local[k].wait()
        first[k].wait_recv()
    waiting = {}

    def advance(name):
        stream, step = name.split(".")
        stream = streams[stream]
        {"b": stream.begin, "m": stream.middle, "e": stream.end}[step[0]](int(step[1]))

    for name in EARLY:
        advance(name)

    for k, src in enumerate((gain_a, gain_b)):
        g = src[...].astype(F32)
        gains[k : k + 1, :] = jnp.concatenate([g[i : i + 1] for i in range(16)], 1)
    gain1, gain2 = gains.at[pl.ds(0, 1)], gains.at[pl.ds(1, 1)]

    def below(parts, rows, count):
        got = [part.astype(F32) for part in parts]
        used = RANK * len(parts)
        return jnp.concatenate(got + [jnp.zeros((rows - used, count), F32)], 0).astype(BF)

    aall[...] = below([qa[...], ka[...], va[...]], 128, WIDTH)
    half = pl.ds(pl.multiple_of(c * HALF, HALF), HALF)
    narrow = pl.ds(pl.multiple_of(c * NARROW, NARROW), NARROW)
    none = jnp.zeros((RANK, NARROW), F32)
    ball[:, :HALF] = below([2.0 * qb[:, half].astype(F32)], 128, HALF)
    ball[:, HALF : HALF + NARROW] = below([none, 2.0 * kb[:, narrow].astype(F32)], 128, NARROW)
    ball[:, HALF + NARROW :] = below([none, none, 2.0 * vb[:, narrow].astype(F32)], 128, NARROW)
    oac[...] = below([oa[:, half]], 128, HALF)
    ob2[...] = below([2.0 * ob[...].astype(F32)], 128, WIDTH)

    chip = me // 2
    starts, ends, total = [], [], jnp.int32(0)
    for k in range(8):
        starts.append(total)
        total = total + ((lens[k] + (STRETCH - 1)) >> 6)
        ends.append(total)

    def sequence(stretch):
        found = jnp.where(stretch >= ends[0], 1, 0)
        for k in range(1, 7):
            found = found + jnp.where(stretch >= ends[k], 1, 0)
        return found

    counts, gates = [], []
    for s in range(4):
        stretch = chip * 4 + s
        begin, length = starts[0], lens[0]
        for k in range(1, 8):
            inside = stretch >= starts[k]
            begin = jnp.where(inside, starts[k], begin)
            length = jnp.where(inside, lens[k], length)
        counts.append(length - (stretch - begin) * STRETCH)
        gates.append(jnp.where(stretch != begin, 1.0, 0.0))
    first_own, last_own = sequence(chip * 4), sequence(chip * 4 + 3)
    k16 = lax.broadcasted_iota(jnp.int32, (16, 128), 0)
    firsts = sequence((z * 16 + k16) * 4)
    lasts = sequence((z * 16 + k16) * 4 + 3)
    masks[0] = jnp.where((k16 < plane) & (lasts == first_own), 1.0, 0.0)
    masks[1] = jnp.where(lasts == sequence(z * 64 + 63), 1.0, 0.0)
    masks[2] = jnp.where((k16 > plane) & (firsts == last_own), 1.0, 0.0)
    masks[3] = jnp.where(firsts == sequence(z * 64), 1.0, 0.0)
    k8 = lax.broadcasted_iota(jnp.int32, (8, 128), 0)
    far_masks[0] = jnp.where((k8 < z) & (sequence(k8 * 64 + 63) == first_own), 1.0, 0.0)
    far_masks[1] = jnp.where((k8 > z) & (sequence(k8 * 64) == last_own), 1.0, 0.0)
    lane = lax.broadcasted_iota(jnp.int32, (1, 128), 1)
    low_lane = lane < 64
    in_stretch = lax.rem(lane, STRETCH)
    valid = jnp.concatenate(
        [jnp.where(in_stretch < jnp.where(low_lane, counts[2 * p], counts[2 * p + 1]), 1.0, 0.0) for p in range(2)], 1
    )
    iu = lax.broadcasted_iota(jnp.int32, (128, 128), 0)
    it = lax.broadcasted_iota(jnp.int32, (128, 128), 1)
    for p in range(2):
        room = jnp.where(iu < 64, counts[2 * p], counts[2 * p + 1])
        seen = (iu <= it) & ((iu < 64) == (it < 64)) & (lax.rem(iu, STRETCH) < room)
        bias[p] = jnp.where(seen, 0.0, -1e30)

    for copy in local[4:7]:
        copy.wait()
    tok_copy.wait_recv()

    def norm_rows(i, carry):
        rows = pl.ds(i * 32, 32)
        for side in range(2):
            t = tok2[side, rows, :].astype(F32)
            r = lax.rsqrt(jnp.mean(t * t, -1, keepdims=True) + EPSILON)
            r1[side, rows, :] = jnp.broadcast_to(r, (32, 128))
            hid1[pl.ds(side * ROWS + i * 32, 32), :] = (t * r * gain1[...]).astype(BF)
        return carry

    lax.fori_loop(0, ROWS // 32, norm_rows, 0)

    zero_low = jnp.zeros((), BF)

    def softmax_rows(logits):
        e = jnp.exp(logits - jnp.max(logits, 0, keepdims=True))
        return e / jnp.sum(e, 0, keepdims=True)

    def gather_plane(base, folded):
        fsend[base] = folded.astype(BF)
        fly = []
        for i in range(4):
            for j in range(4):
                if i + j > 0:
                    fly.append(copies.start(fsend.at[base], frecv.at[base, plane], device({"x": i, "y": j})))
        frecv[base, plane] = folded.astype(BF)
        return fly

    def fold_plane(base, fly):
        for copy in fly:
            copy.wait_recv()
        part = jnp.zeros((AUG, 128), F32)
        whole = jnp.zeros((AUG, 128), F32)
        for k in range(16):
            f = frecv[base, k].astype(F32)
            part += masks[2 * base, k : k + 1, :] * f
            whole += masks[2 * base + 1, k : k + 1, :] * f
        hsend[base] = whole.astype(BF)
        fly = [copies.start(hsend.at[base], hrecv.at[base, i - 1], device({"z": i})) for i in (1, 2, 3)]
        return part, fly

    def fold_line(base, part, fly):
        for i, copy in zip((1, 2, 3), fly):
            copy.wait_recv()
            part += far_masks[base, pl.ds(wrap(z + 4 - i), 1), :] * hrecv[base, i - 1].astype(F32)
        return part

    def combine(states):
        for g in range(2):
            for p in range(2):
                one, two = states[2 * p], states[2 * p + 1]
                if g == 0:
                    both = jnp.where(low_lane, one, pltpu.roll(two, 64, 1))
                else:
                    both = jnp.where(low_lane, pltpu.roll(one, 64, 1), two)
                yield g * 2 + p, both

    def put_states(states, base):
        for k, both in combine(states):
            comb[base + k] = both.astype(BF)
            tall = jnp.concatenate([both, jnp.zeros((128 - AUG, 128), F32)], 0)
            comb_t[base + k] = tall.T.astype(BF)

    def share(src, dst):
        return [
            copies.start(src.at[pl.ds(r, n)], dst.at[pl.ds(at, n)], device({"x": i, "y": j}))
            for i, j, r, n, at in SHARES
        ]

    def lower():
        low[...] = nt(hid1[...], aall[...]).astype(BF)

    def keys():
        kv = nn(hid1[...], wa[:, :, :, :, :, HALF:QKV].reshape(WIDTH, 2 * NARROW))
        kv = (kv + nn(low[...], ball[:, HALF:QKV])).astype(BF)
        kv_t = kv.astype(F32).T.astype(BF)
        for g in range(2):
            keep = low_lane if g == 0 else ~low_lane
            knat[g] = jnp.where(keep, kv[:, :NARROW], jnp.zeros((), BF))
            vnat[g] = jnp.where(keep, kv[:, NARROW:], jnp.zeros((), BF))
            kt[g] = kv_t[g * HEAD : (g + 1) * HEAD]
            tail = lax.broadcasted_iota(jnp.int32, (64, CHIP), 0) == 0
            vt[g, :HEAD] = kv_t[NARROW + g * HEAD : NARROW + (g + 1) * HEAD]
            vt[g, HEAD:] = tail.astype(F32).astype(BF)
        lanes4 = lax.broadcasted_iota(jnp.int32, (1, CHIP), 1) // STRETCH

        for g in range(2):
            kfeat[g * HEAD : (g + 1) * HEAD] = softmax_rows(tn(fk[c * 2 + g], kt[g])) * valid
        kf = kfeat[...]
        kf_high = kf.astype(BF)
        kf_rest = (kf - kf_high.astype(F32)).astype(BF)
        for s in range(4):
            got = []
            for g in range(2):
                va = jnp.where(lanes4 == s, vt[g, :AUG], jnp.zeros((), BF))
                got.append(nt(va, kf_high) + nt(va, kf_rest))
            st[s] = jnp.where(low_lane, got[0], got[1])


    def send_plane():
        folded = st[0]
        for s in (1, 2, 3):
            folded = st[s] + gates[s] * folded
        waiting["plane"] = gather_plane(0, folded)

    def send_line():
        waiting["part"], waiting["line"] = fold_plane(0, waiting["plane"])

    def take_line():
        prefix = fold_line(0, waiting["part"], waiting["line"])
        states = [prefix]
        for s in (1, 2, 3):
            states.append(gates[s] * (states[s - 1] + st[s - 1]))
        put_states(states, 0)

    def queries():
        def query_columns(n, carry):
            cols = pl.ds(pl.multiple_of(n * 256, 256), 256)
            q = nn(hid1[...], wa[:, :, :, :, :, cols].reshape(WIDTH, 256)) + nn(low[...], ball[:, cols])
            qt[cols, :] = q.T.astype(BF)
            return carry

        lax.fori_loop(0, 4, query_columns, 0)

    def lanes(parts):
        return jnp.concatenate(parts, 1)

    def split(wide):
        return [wide[:, k * 128 : (k + 1) * 128] for k in range(4)]

    def attend_four(n, carry):
        g = n // 2
        rows = [pl.ds(pl.multiple_of(n * 256 + k * HEAD, HEAD), HEAD) for k in range(4)]
        for k in range(4):
            qfeat[rows[k], :] = softmax_rows(tn(fq[c * 16 + n * 4 + k], qt[rows[k], :]))
        for p in range(2):
            cols = slice(p * 128, (p + 1) * 128)
            q = lanes([qt[r, cols] for r in rows])
            scores = split(nn(knat[g, cols, :], jnp.concatenate([q, q], 0)))
            stacks = []
            for k in range(4):
                sc = scores[k] * 0.125 + bias[p]
                peak = jnp.max(sc, 0, keepdims=True)
                w = jnp.exp(sc - peak).astype(BF)
                wts[(n * 4 + k) * 2 + p] = w
                dm = jnp.exp(-peak)
                damp[(n * 4 + k) * 2 + p, :1] = dm
                dq = (qfeat[rows[k], cols] * dm).astype(BF)
                stacks.append(
                    jnp.concatenate([w, jnp.where(low_lane, dq, zero_low), jnp.where(low_lane, zero_low, dq)], 0)
                )
            lhs = jnp.concatenate([vt[g, :AUG, cols], comb[g * 2 + p]], 1)
            both = split(nn(lhs, lanes(stacks)))
            for k in range(4):
                rden = 1.0 / both[k][HEAD : HEAD + 1]
                den[(n * 4 + k) * 2 + p, :1] = rden
                mixf[rows[k], cols] = both[k][:HEAD] * rden
        return carry

    def attend():
        lax.fori_loop(0, 4, attend_four, 0)


    def project():
        def mix_rows(n, carry):
            cols = pl.ds(pl.multiple_of(n * 256, 256), 256)
            mixn[:, cols] = mixf[cols, :].T.astype(BF)
            return carry

        lax.fori_loop(0, 4, mix_rows, 0)
        lowo[...] = nt(mixn[...], oac[...]).astype(BF)

        def out_columns(n, carry):
            cols = pl.ds(pl.multiple_of(n * 256, 256), 256)
            w = wa[n // 2, pl.ds(pl.multiple_of(lax.rem(n, 2) * 2, 2), 2), :, :, :, QKV:ATT].reshape(256, HALF)
            o = nt(mixn[...], w) + nn(lowo[...], ob2[:, cols])
            mine = jnp.where(c == 0, o[:ROWS], o[ROWS:])
            other = jnp.where(c == 0, o[ROWS:], o[:ROWS])
            mid[:, cols] = mine + tok2[c, :, cols].astype(F32)
            outs[:, cols] = other.astype(BF)
            return carry

        lax.fori_loop(0, 8, out_columns, 0)
        waiting["out"] = copies.start(outs, outr, sibling)

    def middle():
        waiting["out"].wait_recv()

        def middle_rows(i, carry):
            rows = pl.ds(i * 32, 32)
            m = mid[rows, :] + outr[rows, :].astype(F32)
            mid[rows, :] = m
            r = lax.rsqrt(jnp.mean(m * m, -1, keepdims=True) + EPSILON)
            ht[rows, :] = (m * r * gain2[...]).astype(BF)
            return carry

        lax.fori_loop(0, ROWS // 32, middle_rows, 0)

    def send_hidden():
        waiting["ht"] = share(ht, ht)

    def send_gradient():
        waiting["og"] = share(ogo, ogx)

    def arrived(name):
        for copy in waiting[name]:
            copy.wait_recv()

    def ff_cols(first, count):
        return wf[:, :, :, :, :, :, :, pl.ds(first, count)].reshape(WIDTH, count)

    def inner_columns(at, count):
        gg[:, pl.ds(at, count)] = nn(ogx[...], ff_cols(2 * SLICE + at, count)).astype(BF)

    def chunks(fn):
        def step(n, carry):
            fn(pl.multiple_of(n * 256, 256), 256)
            return carry

        lax.fori_loop(0, 5, step, 0)
        fn(1280, 128)

    def inner_gradient():
        chunks(inner_columns)

    steps = {
        "low": lower,
        "kvc": keys,
        "pls": send_plane,
        "lns": send_line,
        "lnw": take_line,
        "qc": queries,
        "att": attend,
        "oproj": project,
        "mid": middle,
        "hts": send_hidden,
        "htw": lambda: arrived("ht"),
        "ogs": send_gradient,
        "ogw": lambda: arrived("og"),
        "ds": streams["d"].settle,
        "gs": streams["g"].settle,
        "us": streams["u"].settle,
        "ig": inner_gradient,
    }
    for name in PLAN:
        if "." in name:
            advance(name)
        else:
            steps[name]()
    og_fly, ht_fly, out_copy = waiting["og"], waiting["ht"], waiting["out"]

    def gate_columns(at, count):
        cols = pl.ds(at, count)
        gate = nn(ht[...], ff_cols(at, count))
        up = nn(ht[...], ff_cols(SLICE + at, count))
        s = 1.0 / (1.0 + jnp.exp(-gate))
        swish = gate * s
        inner[:, cols] = (swish * up).astype(BF)
        d = gg[:, cols].astype(F32)
        gg[:, cols] = (d * up * s * (1.0 + gate * (1.0 - s))).astype(BF)
        ug[:, cols] = (d * swish).astype(BF)

    chunks(gate_columns)

    def ff_rows(n, at):
        return wf[n // 2, lax.rem(n, 2), :, :, :, :, :, pl.ds(at, SLICE)].reshape(256, SLICE)

    copies.sent(ht_fly)
    copies.sent(og_fly)

    def two_columns(n, carry):
        cols = pl.ds(pl.multiple_of(n * 256, 256), 256)
        ogx[:, cols] = (nt(gg[...], ff_rows(n, 0)) + nt(ug[...], ff_rows(n, SLICE))).astype(BF)
        return carry

    def give_back(src, dst, cols):
        return [
            copies.start(src.at[pl.ds(at, n), cols], dst.at[k // 2 - (k > 5), pl.ds(r, n), cols], device({"x": (4 - i) % 4, "y": (4 - j) % 4}))
            for k, (i, j, r, n, at) in enumerate(SHARES)
        ]

    two_fly = []
    for q in range(4):
        lax.fori_loop(2 * q, 2 * q + 2, two_columns, 0)
        two_fly += give_back(ogx, rbt, pl.ds(q * 512, 512))

    def block_columns(n, carry):
        cols = pl.ds(pl.multiple_of(n * 256, 256), 256)
        ht[:, cols] = nt(inner[...], ff_rows(n, 2 * SLICE)).astype(BF)
        return carry

    lax.fori_loop(0, 8, block_columns, 0)
    for copy in two_fly:
        copy.wait_recv()
    blk_fly = give_back(ht, rbb, pl.ds(0, WIDTH))

    def middle_back(i, acc):
        rows = pl.ds(i * 16, 16)
        t = ogx[rows, :].astype(F32)
        for k in range(3):
            t += rbt[k, rows, :].astype(F32)
        m = mid[rows, :]
        r = lax.rsqrt(jnp.mean(m * m, -1, keepdims=True) + EPSILON)
        n = m * r
        acc += jnp.sum(t * n, 0, keepdims=True)
        t = t * gain2[...]
        g = ogo[rows, :].astype(F32) + r * (t - n * jnp.mean(t * n, -1, keepdims=True))
        mgrad[rows, :] = g
        bg[c, rows, :] = g.astype(BF)
        return acc

    gain_mlp = lax.fori_loop(0, ROWS // 16, middle_back, jnp.zeros((1, WIDTH), F32))
    bg_copy = copies.start(bg.at[c], bg.at[c], sibling)
    bg_copy.wait_recv()
    bgv = bg.at[:, :, :]
    olg = nt(bgv[...].reshape(CHIP, WIDTH), ob2[...])
    olg_low = olg.astype(BF)

    def mixed_columns(n, carry):
        cols = pl.ds(pl.multiple_of(n * 256, 256), 256)
        wcols = pl.ds(pl.multiple_of(QKV + n * 256, 256), 256)
        m = nn(bg[...].reshape(CHIP, WIDTH), wa[:, :, :, :, :, wcols].reshape(WIDTH, 256))
        m += nn(olg_low, oac[:, cols])
        ngt[cols, :] = m.T.astype(BF)
        return carry

    lax.fori_loop(0, 4, mixed_columns, 0)
    lowo_t = lowo[...].astype(F32).T.astype(BF)
    olg_t = olg.T.astype(BF)
    apart[24:32] = 2.0 * nn(lowo_t[:16], bg[...].reshape(CHIP, WIDTH))[:8]
    red[72:80, :HALF] = nn(olg_t[:16], mixn[...])[:8]

    for k in range(4):
        sig[k] = jnp.zeros((AUG, 128), F32)

    def states_four(n, carry):
        g = n // 2
        rows = [pl.ds(pl.multiple_of(n * 256 + k * HEAD, HEAD), HEAD) for k in range(4)]
        for p in range(2):
            cols = slice(p * 128, (p + 1) * 128)
            left, right = [], []
            for k in range(4):
                h = (n * 4 + k) * 2 + p
                rden = den[h, :1]
                m = ngt[rows[k], cols].astype(F32)
                ng = (m * rden).astype(BF)
                dg = -jnp.sum(m * mixf[rows[k], cols], 0, keepdims=True) * rden
                ngt[rows[k], cols] = ng
                dgr[h, :1] = dg
                dq = (qfeat[rows[k], cols] * damp[h, :1]).astype(BF)
                right.append(jnp.concatenate([jnp.where(low_lane, dq, zero_low), jnp.where(low_lane, zero_low, dq)], 0))
                tail = jnp.where(lax.broadcasted_iota(jnp.int32, (AUG - HEAD, 128), 0) == 0, dg, 0.0).astype(BF)
                left.append(jnp.concatenate([ng, tail], 0))
            sig[g * 2 + p] = sig[g * 2 + p] + nt(lanes(left), lanes(right))
        return carry

    lax.fori_loop(0, 4, states_four, 0)
    sg_states = []
    for p in range(2):
        a, b = sig[p], sig[2 + p]
        sg_states.append(jnp.where(low_lane, a, pltpu.roll(b, 64, 1)))
        sg_states.append(jnp.where(low_lane, pltpu.roll(a, 64, 1), b))
    for s in range(4):
        st[s] = sg_states[s]
    folded = sg_states[3]
    for s in (2, 1, 0):
        folded = sg_states[s] + gates[s + 1] * folded
    fly = gather_plane(1, folded)

    for k in range(4):
        kacc[k] = jnp.zeros((HEAD, 128), F32)
        vacc[k] = jnp.zeros((HEAD, 128), F32)

    def back_four(n, carry):
        g = n // 2
        rows = [pl.ds(pl.multiple_of(n * 256 + k * HEAD, HEAD), HEAD) for k in range(4)]
        for p in range(2):
            cols = slice(p * 128, (p + 1) * 128)
            ngs = lanes([ngt[r, cols] for r in rows])
            dgs = [dgr[(n * 4 + k) * 2 + p, :1] for k in range(4)]
            dg = lanes(dgs)
            ws = lanes([wts[(n * 4 + k) * 2 + p] for k in range(4)])
            pt = nn(vnat[g, cols, :], jnp.concatenate([ngs, ngs], 0)) + dg
            sgr = (ws.astype(F32) * pt).astype(BF)
            tail = jnp.where(lax.broadcasted_iota(jnp.int32, (HEAD, 512), 0) == 0, dg, 0.0).astype(BF)
            both = split(nn(comb_t[g * 2 + p], jnp.concatenate([ngs, tail], 0)))
            for k in range(4):
                qg = jnp.where(low_lane, both[k][:HEAD], both[k][HEAD:]) * damp[(n * 4 + k) * 2 + p, :1]
                f = qfeat[rows[k], cols]
                qlg[rows[k], cols] = (f * (qg - jnp.sum(f * qg, 0, keepdims=True))).astype(BF)
            near = split(nn(kt[g, :, cols], sgr))
            for k in range(4):
                far = nn(fq[c * 16 + n * 4 + k], qlg[rows[k], cols])
                gt[rows[k], cols] = (near[k] * 0.125 + far).astype(BF)
            kacc[g * 2 + p] = kacc[g * 2 + p] + nt(lanes([qt[r, cols] for r in rows]), sgr)
            vacc[g * 2 + p] = vacc[g * 2 + p] + nt(ngs, ws)
        return carry

    lax.fori_loop(0, 2, back_four, 0)
    part, fly = fold_plane(1, fly)
    lax.fori_loop(2, 4, back_four, 0)
    suffix = fold_line(1, part, fly)
    states = [None, None, None, suffix]
    for s in (2, 1, 0):
        states[s] = gates[s + 1] * (states[s + 1] + st[s + 1])
    put_states(states, 4)

    for g in range(2):
        f_rows = slice(g * HEAD, (g + 1) * HEAD)
        for p in range(2):
            k = g * 2 + p
            cols = slice(p * 128, (p + 1) * 128)
            f = kfeat[f_rows, cols]
            both = nn(comb_t[4 + k], vt[g, :, cols])
            fg = jnp.where(low_lane, both[:HEAD], both[HEAD:]) * valid[:, cols]
            kl = (f * (fg - jnp.sum(f * fg, 0, keepdims=True))).astype(BF)
            qlg[HALF + g * HEAD : HALF + (g + 1) * HEAD, cols] = kl
            gt[HALF + g * HEAD : HALF + (g + 1) * HEAD, cols] = (kacc[k] * 0.125 + nn(fk[c * 2 + g], kl)).astype(BF)
            fl = f.astype(BF)
            stack = jnp.concatenate([jnp.where(low_lane, fl, zero_low), jnp.where(low_lane, zero_low, fl)], 0)
            gt[HALF + NARROW + g * HEAD : HALF + NARROW + (g + 1) * HEAD, cols] = (
                vacc[k] + nn(comb[4 + k, :HEAD], stack)
            ).astype(BF)

    def feat_pairs(n, carry):
        rows = pl.ds(pl.multiple_of(n * 128, 128), 128)
        r = nt(qt[rows, :], qlg[rows, :])
        red[0:64, rows] = jnp.where(low_lane, r[:HEAD], r[HEAD:])
        return carry

    lax.fori_loop(0, 8, feat_pairs, 0)
    r = nt(kt[...].reshape(128, CHIP), qlg[HALF:, :])
    red[0:64, HALF : HALF + 128] = jnp.where(low_lane, r[:HEAD], r[HEAD:])

    lowg_t = nn(ball[...], gt[...])
    lowg[...] = lowg_t.T.astype(BF)
    lowg_t = lowg_t.astype(BF)
    low_t = low[...].astype(F32).T.astype(BF)
    up = 2.0 * nt(low_t[:32], gt[...])
    red[64:72, :HALF] = up[0:8, :HALF]
    red[64:72, HALF : HALF + NARROW] = up[8:16, HALF : HALF + NARROW]
    red[64:72, HALF + NARROW :] = up[16:24, HALF + NARROW :]
    apart[0:24] = nn(lowg_t[:32], hid1[...])[:24]
    apart[32:40] = jnp.where(lax.broadcasted_iota(jnp.int32, (8, 1), 0) == 1, gain_mlp, 0.0)

    def grad_rows(n, carry):
        rows = pl.ds(pl.multiple_of(n * 256, 256), 256)
        gnat[:, rows] = gt[rows, :].astype(F32).T.astype(BF)
        return carry

    lax.fori_loop(0, 5, grad_rows, 0)

    def one_columns(n, carry):
        cols = pl.ds(pl.multiple_of(n * 256, 256), 256)
        w = wa[n // 2, pl.ds(pl.multiple_of(lax.rem(n, 2) * 2, 2), 2), :, :, :, 0:QKV].reshape(256, QKV)
        o = nt(gnat[...], w) + nn(lowg[...], aall[:, cols])
        normed = [tok2[side, :, cols].astype(F32) * r1[side, :, :1] for side in range(2)]
        apart[32:33, cols] = jnp.sum(o[:ROWS] * normed[0] + o[ROWS:] * normed[1], 0, keepdims=True)
        ones[:, cols] = jnp.where(c == 0, o[:ROWS], o[ROWS:])
        outs[:, cols] = jnp.where(c == 0, o[ROWS:], o[:ROWS]).astype(BF)
        return carry

    copies.sent([out_copy])
    lax.fori_loop(0, 8, one_columns, 0)
    one_copy = copies.start(outs, outr, sibling)

    theirs = pl.ds(pl.multiple_of((1 - c) * HALF, HALF), HALF)
    mine = pl.ds(pl.multiple_of(c * HALF, HALF), HALF)
    a_copy = copies.start(apart.at[:, theirs], asib, sibling)
    red[72:80, HALF:] = jnp.zeros((8, PIECE - HALF), F32)
    red[0:64, HALF + 128 :] = jnp.zeros((64, 128), F32)
    red[80:128, HALF:] = jnp.zeros((48, PIECE - HALF), F32)
    red[120:128, :HALF] = jnp.zeros((8, HALF), F32)
    a_copy.wait_recv()
    red[80:120, :HALF] = apart[:, mine] + asib[...]

    def fold_piece(k, carry):
        rows = pl.ds(pl.multiple_of(k * 8, 8), 8)
        redb[k] = jnp.concatenate([red[rows, : PIECE // 2], red[rows, PIECE // 2 :]], 0).astype(BF)
        return carry

    lax.fori_loop(0, 16, fold_piece, 0)
    fly = []
    for i in range(4):
        for j in range(4):
            if i + j > 0:
                to = wrap(x + i) * 4 + wrap(y + j)
                fly.append(copies.start(redb.at[to], rr.at[plane], device({"x": i, "y": j})))
    rr[plane] = redb[plane]
    for copy in blk_fly:
        copy.wait_recv()

    def block_rows(i, carry):
        rows = pl.ds(i * 16, 16)
        t = mid[rows, :] + ht[rows, :].astype(F32)
        for k in range(3):
            t += rbb[k, rows, :].astype(F32)
        blk_out[rows, :] = t.astype(BF)
        return carry

    lax.fori_loop(0, ROWS // 16, block_rows, 0)
    for copy in fly:
        copy.wait_recv()
    total = rr[0].astype(F32)
    for k in range(1, 16):
        total += rr[k].astype(F32)
    rz[z] = total
    line = [copies.start(rz.at[z], rz.at[z], device({"z": i})) for i in (1, 2, 3)]
    one_copy.wait_recv()

    def token_rows(i, carry):
        rows = pl.ds(i * 16, 16)
        o = ones[rows, :] + outr[rows, :].astype(F32)
        t = tok2[c, rows, :].astype(F32)
        r = r1[c, rows, :1]
        n = t * r
        o = o * gain1[...]
        gtok_out[rows, :] = (mgrad[rows, :] + r * (o - n * jnp.mean(o * n, -1, keepdims=True))).astype(BF)
        return carry

    lax.fori_loop(0, ROWS // 32, token_rows, 0)
    for copy in line:
        copy.wait_recv()
    total = (rz[0] + rz[1]) + (rz[2] + rz[3])
    fin[c, plane] = total.astype(BF)
    piece = fin.at[c, plane]
    fly = [
        copies.start(piece, piece, device({"x": i, "y": j})) for i in range(4) for j in range(4) if i + j > 0
    ]
    lax.fori_loop(ROWS // 32, ROWS // 16, token_rows, 0)
    for copy in fly:
        copy.wait_recv()
    f_copy = copies.start(fin.at[c], fin.at[c], sibling)
    f_copy.wait_recv()

    def wide(k, side):
        got = fin[side, k].astype(F32)
        return got[:8], got[8:]

    def feat_out(k, carry):
        rows = pl.ds(pl.multiple_of(k * 8, 8), 8)
        for side in range(2):
            left, right = wide(k, side)
            for j in range(9):
                v = left[:, j * 128 : (j + 1) * 128] if j < 5 else right[:, (j - 5) * 128 : (j - 4) * 128]
                out, head = (fq_out, side * 16 + 2 * j) if j < 8 else (fk_out, side * 2)
                out[head, rows, :] = v[:, :64]
                out[head + 1, rows, :] = pltpu.roll(v, 64, 1)[:, :64]
        return carry

    lax.fori_loop(0, 8, feat_out, 0)
    rest = HALF - PIECE // 2
    for side in range(2):
        for k, out in ((8, qb_out), (9, oa_out), (10, qa_out), (11, ka_out), (12, va_out), (13, ob_out)):
            left, right = wide(k, side)
            out[:, side * HALF : side * HALF + PIECE // 2] = left
            out[:, side * HALF + PIECE // 2 : (side + 1) * HALF] = right[:, :rest]
            if k == 8:
                kb_out[:, side * NARROW : (side + 1) * NARROW] = right[:, rest : rest + NARROW]
                vb_out[:, side * NARROW : (side + 1) * NARROW] = right[:, rest + NARROW :]
        left, right = wide(14, side)
        row = jnp.concatenate([left, right[:, :rest]], 1)
        for k, out in ((0, gain_a_out), (1, gain_b_out)):
            for i in range(8):
                out[side * 8 + i : side * 8 + i + 1, :] = row[k : k + 1, i * 128 : (i + 1) * 128]
    copies.drain()


N_COPIES = 301
N_SENDS = 64


def scratch():
    v = pltpu.VMEM
    return [
        v((4, 4, 4, 2, 16, ATT), BF),
        v((4, 2, 2, 2, 2, 2, 16, 3 * SLICE), BF),
        v((2, 2, 16, 3 * SLICE), BF),
        v((2, ROWS, WIDTH), BF),
        v((ROWS, WIDTH), BF),
        v((8, WIDTH), F32),
        v((2, ROWS, 128), F32),
        v((128, WIDTH), BF),
        v((128, QKV), BF),
        v((128, HALF), BF),
        v((128, WIDTH), BF),
        v((4, 16, 128), F32),
        v((2, 8, 128), F32),
        v((2, 128, 128), F32),
        v((CHIP, WIDTH), BF),
        v((CHIP, 128), BF),
        v((HALF, CHIP), BF),
        v((2, HEAD, CHIP), BF),
        v((2, 128, CHIP), BF),
        v((2, CHIP, 128), BF),
        v((2, CHIP, 128), BF),
        v((128, CHIP), F32),
        v((4, AUG, 128), F32),
        v((8, AUG, 128), BF),
        v((8, 128, 128), BF),
        v((32, 128, 128), BF),
        v((HALF, CHIP), F32),
        v((HALF, CHIP), F32),
        v((32, 8, 128), F32),
        v((32, 8, 128), F32),
        v((CHIP, HALF), BF),
        v((CHIP, 128), BF),
        v((ROWS, WIDTH), BF),
        v((ROWS, WIDTH), BF),
        v((ROWS, WIDTH), F32),
        v((512, WIDTH), BF),
        v((512, WIDTH), BF),
        v((512, SLICE), BF),
        v((512, SLICE), BF),
        v((512, SLICE), BF),
        v((3, ROWS, WIDTH), BF),
        v((3, ROWS, WIDTH), BF),
        v((ROWS, WIDTH), F32),
        v((2, ROWS, WIDTH), BF),
        v((HALF, CHIP), BF),
        v((32, 8, 128), F32),
        v((4, AUG, 128), F32),
        v((HALF + 128, CHIP), BF),
        v((QKV, CHIP), BF),
        v((CHIP, QKV), BF),
        v((CHIP, 128), BF),
        v((ROWS, WIDTH), F32),
        v((4, HEAD, 128), F32),
        v((4, HEAD, 128), F32),
        v((2, AUG, 128), BF),
        v((2, 16, AUG, 128), BF),
        v((2, AUG, 128), BF),
        v((2, 3, AUG, 128), BF),
        v((128, PIECE), F32),
        v((16, 16, PIECE // 2), BF),
        v((16, 16, PIECE // 2), BF),
        v((4, 16, PIECE // 2), F32),
        v((2, 16, 16, PIECE // 2), BF),
        v((40, WIDTH), F32),
        v((40, HALF), F32),
        pltpu.SemaphoreType.DMA((N_SENDS,)),
        pltpu.SemaphoreType.DMA((N_COPIES,)),
        pltpu.SemaphoreType.DMA((15,)),
    ]


def body(
    tokens, sequence_lengths, attention_gain, query_weight, key_weight, value_weight, output_weight_flipped,
    query_adapter_down, query_adapter_up, key_adapter_down, key_adapter_up, value_adapter_down, value_adapter_up,
    output_adapter_down, output_adapter_up, query_feature_map, key_feature_map, feedforward_gain,
    gate_weight, up_weight, down_weight_flipped, output_gradient,
):
    vmem = pl.BlockSpec(memory_space=pltpu.VMEM)
    smem = pl.BlockSpec(memory_space=pltpu.SMEM)
    anywhere = pl.BlockSpec(memory_space=pl.ANY)

    def array(*shape, dtype=F32):
        return jax.ShapeDtypeStruct(shape, dtype)

    out = pl.pallas_call(
        kernel,
        out_shape=(
            array(ROWS, WIDTH, dtype=BF), array(ROWS, WIDTH, dtype=BF), array(16, 128),
            array(RANK, WIDTH), array(RANK, WIDTH), array(RANK, WIDTH), array(RANK, 2 * NARROW),
            array(RANK, WIDTH), array(RANK, 2 * NARROW), array(RANK, WIDTH), array(RANK, WIDTH),
            array(QUERY_HEADS, HEAD, HEAD), array(KEY_VALUE_HEADS, HEAD, HEAD), array(16, 128),
        ),
        in_specs=[anywhere, smem, vmem] + [anywhere] * 4 + [vmem] * 11 + [anywhere] * 4,
        out_specs=(vmem,) * 14,
        scratch_shapes=scratch(),
        compiler_params=pltpu.CompilerParams(
            collective_id=0, has_side_effects=True, vmem_limit_bytes=64 * 1024 * 1024
        ),
    )(
        tokens, sequence_lengths, attention_gain.reshape(16, 128),
        query_weight, key_weight, value_weight, output_weight_flipped,
        query_adapter_down.T, query_adapter_up, key_adapter_down.T, key_adapter_up, value_adapter_down.T,
        value_adapter_up, output_adapter_down.T, output_adapter_up, query_feature_map, key_feature_map,
        feedforward_gain.reshape(16, 128), gate_weight, up_weight, down_weight_flipped, output_gradient,
    )
    (
        block_out, grad_tokens, gain_attn, qa, qb, ka, kb, va, vb, oa, ob, feat_q, feat_k, gain_mlp,
    ) = out
    return (
        block_out, grad_tokens, gain_attn.reshape(WIDTH), qa.T, qb, ka.T, kb, va.T, vb, oa.T, ob, feat_q, feat_k,
        gain_mlp.reshape(WIDTH),
    )


def solution(mesh):
    split, whole = P("seq", None), P()
    return jax.shard_map(
        body,
        mesh=mesh,
        in_specs=(
            (split, whole, whole) + (split,) * 4 + (whole,) * 11 + (split,) * 4
        ),
        out_specs=(split, split) + (whole,) * 12,
        check_vma=False,
    )
```

```python
import math

import jax
import jax.numpy as jnp
from jax import lax
from jax.experimental import pallas as pl
from jax.experimental.pallas import tpu as pltpu
from jax.sharding import PartitionSpec as P

QUERY_HEADS = 32
KEY_VALUE_HEADS = 4
HEAD = 64
STRETCH = 64
WIDTH = 2048
FF = 5632
ROWS = 128
CHIP = 256
HALF = 1024
NARROW = 128
QKV = HALF + 2 * NARROW
ATT = QKV + HALF
SLICE = FF // 4
AUG = 80
RANK = 8
PIECE = 1280
EPSILON = 1e-05
MESH = pl.DeviceIdType.MESH
F32 = jnp.float32
BF = jnp.bfloat16

SHARES = (
    (1, 0, 0, 64, 128),
    (3, 0, 64, 64, 192),
    (0, 1, 0, 64, 256),
    (0, 3, 64, 64, 320),
    (1, 1, 0, 32, 384),
    (1, 3, 32, 32, 416),
    (3, 1, 64, 32, 448),
    (3, 3, 96, 32, 480),
)


def nn(left, right):
    return jnp.dot(left, right, preferred_element_type=F32)


def tn(left, right):
    return lax.dot_general(left, right, (((0,), (0,)), ((), ())), preferred_element_type=F32)


def nt(left, right):
    return lax.dot_general(left, right, (((1,), (1,)), ((), ())), preferred_element_type=F32)


def wrap(value):
    return lax.rem(value, 4)


class Copies:
    def __init__(self, send, recv):
        self.send, self.recv, self.count, self.open = send, recv, 0, {}

    def start(self, src, dst, device):
        slot = self.count % N_SENDS
        if slot in self.open:
            self.open.pop(slot).wait_send()
        copy = pltpu.make_async_remote_copy(
            src_ref=src,
            dst_ref=dst,
            send_sem=self.send.at[slot],
            recv_sem=self.recv.at[self.count],
            device_id=(device,),
            device_id_type=MESH,
        )
        self.count += 1
        copy.start()
        self.open[slot] = copy
        return copy

    def sent(self, copies):
        for slot in [k for k, copy in self.open.items() if any(copy is other for other in copies)]:
            self.open.pop(slot).wait_send()

    def drain(self):
        for copy in self.open.values():
            copy.wait_send()


class Heads:
    def __init__(self, copies, wa, where, device, parts, straight=False):
        self.copies, self.wa, self.where, self.device = copies, wa, where, device
        self.parts, self.straight = parts, straight
        self.flying = {}

    def block(self, order, phase, at, first, count):
        index = []
        for axis in "zxy":
            k = order.index(axis)
            index.append(slice(None) if k < phase else at if k == phase else self.where[axis])
        return self.wa.at[index[0], index[1], index[2], :, :, pl.ds(first, count)]

    def begin(self, phase):
        for part, (order, first, count) in enumerate(self.parts):
            axis = order[phase]
            own = self.block(order, phase, self.where[axis], first, count)
            steps = (1, 3) if phase > 0 and not self.straight else (1, 3, 2)
            self.flying[phase, part] = [self.copies.start(own, own, self.device({axis: step})) for step in steps]

    def middle(self, phase):
        for part, (order, first, count) in enumerate(self.parts):
            axis = order[phase]
            for copy in self.flying[phase, part]:
                copy.wait_recv()
            here = self.where[axis]
            one = (count // 256) * 128
            left = self.block(order, phase, wrap(here + 3), first, one)
            right = self.block(order, phase, wrap(here + 1), first + one, count - one)
            self.flying[phase, part] = [
                self.copies.start(left, left, self.device({axis: 1})),
                self.copies.start(right, right, self.device({axis: 3})),
            ]

    def end(self, phase):
        for part in range(len(self.parts)):
            for copy in self.flying[phase, part]:
                copy.wait_recv()


class Units:
    def __init__(self, copies, here, wf, stage, where, device, sibling, parts):
        self.copies, self.here, self.wf, self.stage = copies, here, wf, stage
        self.where, self.device, self.sibling, self.parts = where, device, sibling, parts
        self.flying, self.handed, self.own = {}, [], []

    def rows(self, order, along, across, cols):
        w = self.where
        a = (slice(None), slice(None)) if along is None else (along // 2, lax.rem(along, 2))
        b = (across // 2, lax.rem(across, 2))
        x, y = (a, b) if order == "xy" else (b, a)
        return self.wf.at[w["z"], x[0], x[1], y[0], y[1], w["c"], :, cols]

    def line(self, z, cols):
        return self.wf.at[z, :, :, :, :, self.where["c"], :, cols]

    def hand_on(self, block):
        self.handed.append(self.copies.start(block, block, self.sibling))

    def begin(self, phase):
        w = self.where
        for part, (order, src, at, first, count) in enumerate(self.parts):
            cols = pl.ds(first, count)
            a, b = order
            fly = []
            if phase == 0:
                for d in (1, 3, 2, 0):
                    for e in (0, 1):
                        pa, pb = lax.rem(w[a] + d, 2), lax.rem(w[b] + e, 2)
                        slot = pa * 2 + pb if order == "xy" else pb * 2 + pa
                        piece = src.at[:, pl.ds(pl.multiple_of(slot * SLICE + at, 128), count)]
                        if e == 0:
                            dst = self.rows(order, w[a], w[b], cols)
                        else:
                            dst = self.stage.at[w[a] // 2, lax.rem(w[a], 2), :, cols]
                        if d == 0:
                            self.own.append(self.here(piece, dst))
                        else:
                            fly.append(self.copies.start(piece, dst, self.device({a: d})))
            elif phase == 1:
                mine = self.rows(order, None, w[b], cols)
                other = self.stage.at[:, :, :, cols]
                fly = [
                    self.copies.start(other, mine, self.device({b: 1})),
                    self.copies.start(other, mine, self.device({b: 3})),
                    self.copies.start(mine, mine, self.device({b: 2})),
                ]
            else:
                block = self.line(w["z"], cols)
                self.hand_on(block)
                fly = [self.copies.start(block, block, self.device({"z": step})) for step in (1, 3)]
            self.flying[phase, part] = fly

    def middle(self, phase):
        z = self.where["z"]
        for part, (order, src, at, first, count) in enumerate(self.parts):
            for copy in self.flying[phase, part]:
                copy.wait_recv()
            one = (count // 256) * 128
            before, after = wrap(z + 3), wrap(z + 1)
            left = self.line(before, pl.ds(first, one))
            right = self.line(after, pl.ds(first + one, count - one))
            self.flying[phase, part] = [
                self.copies.start(left, left, self.device({"z": 1})),
                self.copies.start(right, right, self.device({"z": 3})),
            ]
            self.hand_on(self.line(before, pl.ds(first, count)))
            self.hand_on(self.line(after, pl.ds(first, count)))

    def end(self, phase):
        if phase == 0:
            for copy in self.own:
                copy.wait()
        for part, (order, src, at, first, count) in enumerate(self.parts):
            for copy in self.flying[phase, part]:
                copy.wait_recv()
            if phase == 2:
                self.hand_on(self.line(wrap(self.where["z"] + 2), pl.ds(first, count)))

    def settle(self):
        for copy in self.handed:
            copy.wait_recv()


EARLY = ("kv.b0", "o.b0", "q.b0",)
PLAN = (
    "d.b0", "kv.e0", "kv.b1", "g.b0", "u.b0", "q.e0", "low", "o.e0", "d.e0", "d.b1", "q.b1", "o.b1",
    "q.m1", "d.e1", "u.e0", "d.b2", "kv.e1", "g.e0", "g.b1", "kv.b2", "u.b1", "q.e1", "q.b2", "o.m1",
    "g.e1", "u.e1", "d.m2", "kv.e2", "g.b2", "kvc", "pls", "o.e1", "o.b2", "lns", "d.e2", "q.m2",
    "u.b2", "o.m2", "lnw", "q.e2", "ogs", "qc", "g.m2", "att", "o.e2", "ds", "oproj", "mid",
    "hts", "u.m2", "ogw", "ig", "g.e2", "u.e2", "gs", "us", "htw",
)


def kernel(
    tok, lens, gain_a, qw, kw, vw, ow, qa, qb, ka, kb, va, vb, oa, ob, fq, fk, gain_b, gw, uw, dw, og,
    blk_out, gtok_out, red_out,
    wa, wf, stage, tok2, ogo, gains, r1, aall, ball, oac, ob2, masks, far_masks, bias, hid1, low, qt, kt, vt, knat, vnat,
    kfeat, st, comb, comb_t, wts, qfeat, mixf, damp, den, mixn, lowo, outs, outr, mid, ht, ogx, gg, inner, ug, rbt, rbb,
    mgrad, bg, ngt, dgr, sig, qlg, gt, gnat, lowg, ones, kacc, vacc, fsend, frecv, hsend, hrecv, red, redb, rr, rz, fin,
    apart, asib, send, recv, loc,
):
    me = lax.axis_index("seq")
    c = lax.rem(me, 2)
    y = lax.rem(me // 2, 4)
    x = lax.rem(me // 8, 4)
    z = me // 32

    def device(steps):
        zz, xx, yy = (wrap(v + steps.get(n, 0)) for n, v in (("z", z), ("x", x), ("y", y)))
        return ((zz * 4 + xx) * 4 + yy) * 2 + c

    sibling = me + 1 - 2 * c
    plane = x * 4 + y
    xl, yl = lax.rem(x, 2), lax.rem(y, 2)
    xh, yh = x // 2, y // 2

    barrier = pltpu.get_barrier_semaphore()
    peers = [sibling]
    peers += [device({"x": i, "y": j}) for i in range(4) for j in range(4) if i + j > 0]
    peers += [device({"z": i}) for i in (1, 2, 3)]
    for peer in peers:
        pl.semaphore_signal(barrier, inc=1, device_id=(peer,), device_id_type=MESH)
    copies = Copies(send, recv)
    local = []

    def here(src, dst):
        copy = pltpu.make_async_copy(src, dst, loc.at[len(local)])
        copy.start()
        local.append(copy)
        return copy

    own = wa.at[z, x, y, c]
    pieces = ((kw, HALF, NARROW), (vw, HALF + NARROW, NARROW), (qw, 0, HALF), (ow, QKV, HALF))
    for src, at, count in pieces:
        mine = src.at[:, pl.ds(pl.multiple_of(c * count, count), count)]
        here(mine, own.at[:, pl.ds(at, count)])
    here(tok, tok2.at[c])
    here(og, ogx.at[pl.ds(0, ROWS)])
    here(og, ogo)

    for k, src in enumerate((gain_a, gain_b)):
        g = src[...].astype(F32)
        gains[k : k + 1, :] = jnp.concatenate([g[i : i + 1] for i in range(16)], 1)
    gain1, gain2 = gains.at[pl.ds(0, 1)], gains.at[pl.ds(1, 1)]

    def below(parts, rows, count):
        got = [part.astype(F32) for part in parts]
        used = RANK * len(parts)
        return jnp.concatenate(got + [jnp.zeros((rows - used, count), F32)], 0).astype(BF)

    aall[...] = below([qa[...], ka[...], va[...]], 128, WIDTH)
    half = pl.ds(pl.multiple_of(c * HALF, HALF), HALF)
    narrow = pl.ds(pl.multiple_of(c * NARROW, NARROW), NARROW)
    none = jnp.zeros((RANK, NARROW), F32)
    ball[:, :HALF] = below([2.0 * qb[:, half].astype(F32)], 128, HALF)
    ball[:, HALF : HALF + NARROW] = below([none, 2.0 * kb[:, narrow].astype(F32)], 128, NARROW)
    ball[:, HALF + NARROW :] = below([none, none, 2.0 * vb[:, narrow].astype(F32)], 128, NARROW)
    oac[...] = below([oa[:, half]], 128, HALF)
    ob2[...] = below([2.0 * ob[...].astype(F32)], 128, WIDTH)

    chip = me // 2
    starts, ends, total = [], [], jnp.int32(0)
    for k in range(8):
        starts.append(total)
        total = total + ((lens[k] + (STRETCH - 1)) >> 6)
        ends.append(total)

    def sequence(stretch):
        found = jnp.where(stretch >= ends[0], 1, 0)
        for k in range(1, 7):
            found = found + jnp.where(stretch >= ends[k], 1, 0)
        return found

    counts, gates = [], []
    for s in range(4):
        stretch = chip * 4 + s
        begin, length = starts[0], lens[0]
        for k in range(1, 8):
            inside = stretch >= starts[k]
            begin = jnp.where(inside, starts[k], begin)
            length = jnp.where(inside, lens[k], length)
        counts.append(length - (stretch - begin) * STRETCH)
        gates.append(jnp.where(stretch != begin, 1.0, 0.0))
    first_own, last_own = sequence(chip * 4), sequence(chip * 4 + 3)
    k16 = lax.broadcasted_iota(jnp.int32, (16, 128), 0)
    firsts = sequence((z * 16 + k16) * 4)
    lasts = sequence((z * 16 + k16) * 4 + 3)
    masks[0] = jnp.where((k16 < plane) & (lasts == first_own), 1.0, 0.0)
    masks[1] = jnp.where(lasts == sequence(z * 64 + 63), 1.0, 0.0)
    masks[2] = jnp.where((k16 > plane) & (firsts == last_own), 1.0, 0.0)
    masks[3] = jnp.where(firsts == sequence(z * 64), 1.0, 0.0)
    k8 = lax.broadcasted_iota(jnp.int32, (8, 128), 0)
    far_masks[0] = jnp.where((k8 < z) & (sequence(k8 * 64 + 63) == first_own), 1.0, 0.0)
    far_masks[1] = jnp.where((k8 > z) & (sequence(k8 * 64) == last_own), 1.0, 0.0)
    lane = lax.broadcasted_iota(jnp.int32, (1, 128), 1)
    low_lane = lane < 64
    in_stretch = lax.rem(lane, STRETCH)
    valid = jnp.concatenate(
        [jnp.where(in_stretch < jnp.where(low_lane, counts[2 * p], counts[2 * p + 1]), 1.0, 0.0) for p in range(2)], 1
    )
    iu = lax.broadcasted_iota(jnp.int32, (128, 128), 0)
    it = lax.broadcasted_iota(jnp.int32, (128, 128), 1)
    for p in range(2):
        room = jnp.where(iu < 64, counts[2 * p], counts[2 * p + 1])
        seen = (iu <= it) & ((iu < 64) == (it < 64)) & (lax.rem(iu, STRETCH) < room)
        bias[p] = jnp.where(seen, 0.0, -1e30)

    pl.semaphore_wait(barrier, len(peers))
    first = []
    for src, at, count in pieces:
        other = src.at[:, pl.ds(pl.multiple_of((1 - c) * count, count), count)]
        first.append(copies.start(other, own.at[:, pl.ds(at, count)], sibling))
    tok_copy = copies.start(tok, tok2.at[c], sibling)
    where = {"z": z, "x": x, "y": y, "c": c}
    streams = {
        "kv": Heads(copies, wa, where, device, (("xzy", 1024, 128), ("yzx", 1152, 128)), straight=True),
        "q": Heads(copies, wa, where, device, (("xzy", 0, 512), ("yzx", 512, 512))),
        "o": Heads(copies, wa, where, device, (("zxy", QKV, 512), ("zyx", QKV + 512, 512))),
        "d": Units(
            copies, here, wf, stage, where, device, sibling,
            (("xy", dw, 0, 2 * SLICE, 768), ("yx", dw, 768, 2 * SLICE + 768, 640)),
        ),
        "g": Units(copies, here, wf, stage, where, device, sibling, (("xy", gw, 0, 0, SLICE),)),
        "u": Units(copies, here, wf, stage, where, device, sibling, (("yx", uw, 0, SLICE, SLICE),)),
    }
    for k in range(4):
        local[k].wait()
        first[k].wait_recv()
    waiting = {}

    def advance(name):
        stream, step = name.split(".")
        stream = streams[stream]
        {"b": stream.begin, "m": stream.middle, "e": stream.end}[step[0]](int(step[1]))

    for name in EARLY:
        advance(name)

    for copy in local[4:7]:
        copy.wait()
    tok_copy.wait_recv()

    def norm_rows(i, carry):
        rows = pl.ds(i * 32, 32)
        for side in range(2):
            t = tok2[side, rows, :].astype(F32)
            r = lax.rsqrt(jnp.mean(t * t, -1, keepdims=True) + EPSILON)
            r1[side, rows, :] = jnp.broadcast_to(r, (32, 128))
            hid1[pl.ds(side * ROWS + i * 32, 32), :] = (t * r * gain1[...]).astype(BF)
        return carry

    lax.fori_loop(0, ROWS // 32, norm_rows, 0)

    zero_low = jnp.zeros((), BF)

    def softmax_rows(logits):
        e = jnp.exp(logits - jnp.max(logits, 0, keepdims=True))
        return e / jnp.sum(e, 0, keepdims=True)

    def gather_plane(base, folded):
        fsend[base] = folded.astype(BF)
        fly = []
        for i in range(4):
            for j in range(4):
                if i + j > 0:
                    fly.append(copies.start(fsend.at[base], frecv.at[base, plane], device({"x": i, "y": j})))
        frecv[base, plane] = folded.astype(BF)
        return fly

    def fold_plane(base, fly):
        for copy in fly:
            copy.wait_recv()
        part = jnp.zeros((AUG, 128), F32)
        whole = jnp.zeros((AUG, 128), F32)
        for k in range(16):
            f = frecv[base, k].astype(F32)
            part += masks[2 * base, k : k + 1, :] * f
            whole += masks[2 * base + 1, k : k + 1, :] * f
        hsend[base] = whole.astype(BF)
        fly = [copies.start(hsend.at[base], hrecv.at[base, i - 1], device({"z": i})) for i in (1, 2, 3)]
        return part, fly

    def fold_line(base, part, fly):
        for i, copy in zip((1, 2, 3), fly):
            copy.wait_recv()
            part += far_masks[base, pl.ds(wrap(z + 4 - i), 1), :] * hrecv[base, i - 1].astype(F32)
        return part

    def combine(states):
        for g in range(2):
            for p in range(2):
                one, two = states[2 * p], states[2 * p + 1]
                if g == 0:
                    both = jnp.where(low_lane, one, pltpu.roll(two, 64, 1))
                else:
                    both = jnp.where(low_lane, pltpu.roll(one, 64, 1), two)
                yield g * 2 + p, both

    def put_states(states, base):
        for k, both in combine(states):
            comb[base + k] = both.astype(BF)
            tall = jnp.concatenate([both, jnp.zeros((128 - AUG, 128), F32)], 0)
            comb_t[base + k] = tall.T.astype(BF)

    def share(src, dst):
        return [
            copies.start(src.at[pl.ds(r, n)], dst.at[pl.ds(at, n)], device({"x": i, "y": j}))
            for i, j, r, n, at in SHARES
        ]

    def lower():
        low[...] = nt(hid1[...], aall[...]).astype(BF)

    def keys():
        kv = nn(hid1[...], wa[:, :, :, :, :, HALF:QKV].reshape(WIDTH, 2 * NARROW))
        kv = (kv + nn(low[...], ball[:, HALF:QKV])).astype(BF)
        kv_t = kv.astype(F32).T.astype(BF)
        for g in range(2):
            keep = low_lane if g == 0 else ~low_lane
            knat[g] = jnp.where(keep, kv[:, :NARROW], jnp.zeros((), BF))
            vnat[g] = jnp.where(keep, kv[:, NARROW:], jnp.zeros((), BF))
            kt[g] = kv_t[g * HEAD : (g + 1) * HEAD]
            tail = lax.broadcasted_iota(jnp.int32, (64, CHIP), 0) == 0
            vt[g, :HEAD] = kv_t[NARROW + g * HEAD : NARROW + (g + 1) * HEAD]
            vt[g, HEAD:] = tail.astype(F32).astype(BF)
        lanes4 = lax.broadcasted_iota(jnp.int32, (1, CHIP), 1) // STRETCH

        for g in range(2):
            kfeat[g * HEAD : (g + 1) * HEAD] = softmax_rows(tn(fk[c * 2 + g], kt[g])) * valid
        kf = kfeat[...]
        kf_high = kf.astype(BF)
        kf_rest = (kf - kf_high.astype(F32)).astype(BF)
        for s in range(4):
            got = []
            for g in range(2):
                va = jnp.where(lanes4 == s, vt[g, :AUG], jnp.zeros((), BF))
                got.append(nt(va, kf_high) + nt(va, kf_rest))
            st[s] = jnp.where(low_lane, got[0], got[1])


    def send_plane():
        folded = st[0]
        for s in (1, 2, 3):
            folded = st[s] + gates[s] * folded
        waiting["plane"] = gather_plane(0, folded)

    def send_line():
        waiting["part"], waiting["line"] = fold_plane(0, waiting["plane"])

    def take_line():
        prefix = fold_line(0, waiting["part"], waiting["line"])
        states = [prefix]
        for s in (1, 2, 3):
            states.append(gates[s] * (states[s - 1] + st[s - 1]))
        put_states(states, 0)

    def queries():
        def query_columns(n, carry):
            cols = pl.ds(pl.multiple_of(n * 256, 256), 256)
            q = nn(hid1[...], wa[:, :, :, :, :, cols].reshape(WIDTH, 256)) + nn(low[...], ball[:, cols])
            qt[cols, :] = q.T.astype(BF)
            return carry

        lax.fori_loop(0, 4, query_columns, 0)

    def lanes(parts):
        return jnp.concatenate(parts, 1)

    def split(wide):
        return [wide[:, k * 128 : (k + 1) * 128] for k in range(4)]

    def attend_four(n, carry):
        g = n // 2
        rows = [pl.ds(pl.multiple_of(n * 256 + k * HEAD, HEAD), HEAD) for k in range(4)]
        for k in range(4):
            qfeat[rows[k], :] = softmax_rows(tn(fq[c * 16 + n * 4 + k], qt[rows[k], :]))
        for p in range(2):
            cols = slice(p * 128, (p + 1) * 128)
            q = lanes([qt[r, cols] for r in rows])
            scores = split(nn(knat[g, cols, :], jnp.concatenate([q, q], 0)))
            stacks = []
            for k in range(4):
                sc = scores[k] * 0.125 + bias[p]
                peak = jnp.max(sc, 0, keepdims=True)
                w = jnp.exp(sc - peak).astype(BF)
                wts[(n * 4 + k) * 2 + p] = w
                dm = jnp.exp(-peak)
                damp[(n * 4 + k) * 2 + p, :1] = dm
                dq = (qfeat[rows[k], cols] * dm).astype(BF)
                stacks.append(
                    jnp.concatenate([w, jnp.where(low_lane, dq, zero_low), jnp.where(low_lane, zero_low, dq)], 0)
                )
            lhs = jnp.concatenate([vt[g, :AUG, cols], comb[g * 2 + p]], 1)
            both = split(nn(lhs, lanes(stacks)))
            for k in range(4):
                rden = 1.0 / both[k][HEAD : HEAD + 1]
                den[(n * 4 + k) * 2 + p, :1] = rden
                mixf[rows[k], cols] = both[k][:HEAD] * rden
        return carry

    def attend():
        lax.fori_loop(0, 4, attend_four, 0)


    def project():
        def mix_rows(n, carry):
            cols = pl.ds(pl.multiple_of(n * 256, 256), 256)
            mixn[:, cols] = mixf[cols, :].T.astype(BF)
            return carry

        lax.fori_loop(0, 4, mix_rows, 0)
        lowo[...] = nt(mixn[...], oac[...]).astype(BF)

        def out_columns(n, carry):
            cols = pl.ds(pl.multiple_of(n * 256, 256), 256)
            w = wa[n // 2, pl.ds(pl.multiple_of(lax.rem(n, 2) * 2, 2), 2), :, :, :, QKV:ATT].reshape(256, HALF)
            o = nt(mixn[...], w) + nn(lowo[...], ob2[:, cols])
            mine = jnp.where(c == 0, o[:ROWS], o[ROWS:])
            other = jnp.where(c == 0, o[ROWS:], o[:ROWS])
            mid[:, cols] = mine + tok2[c, :, cols].astype(F32)
            outs[:, cols] = other.astype(BF)
            return carry

        lax.fori_loop(0, 8, out_columns, 0)
        waiting["out"] = copies.start(outs, outr, sibling)

    def middle():
        waiting["out"].wait_recv()

        def middle_rows(i, carry):
            rows = pl.ds(i * 32, 32)
            m = mid[rows, :] + outr[rows, :].astype(F32)
            mid[rows, :] = m
            r = lax.rsqrt(jnp.mean(m * m, -1, keepdims=True) + EPSILON)
            ht[rows, :] = (m * r * gain2[...]).astype(BF)
            return carry

        lax.fori_loop(0, ROWS // 32, middle_rows, 0)

    def send_hidden():
        waiting["ht"] = share(ht, ht)

    def send_gradient():
        waiting["og"] = share(ogo, ogx)

    def arrived(name):
        for copy in waiting[name]:
            copy.wait_recv()

    def ff_cols(first, count):
        return wf[:, :, :, :, :, :, :, pl.ds(first, count)].reshape(WIDTH, count)

    def inner_gradient():
        gg[...] = nn(ogx[...], ff_cols(2 * SLICE, SLICE)).astype(BF)

    steps = {
        "low": lower,
        "kvc": keys,
        "pls": send_plane,
        "lns": send_line,
        "lnw": take_line,
        "qc": queries,
        "att": attend,
        "oproj": project,
        "mid": middle,
        "hts": send_hidden,
        "htw": lambda: arrived("ht"),
        "ogs": send_gradient,
        "ogw": lambda: arrived("og"),
        "ds": streams["d"].settle,
        "gs": streams["g"].settle,
        "us": streams["u"].settle,
        "ig": inner_gradient,
    }
    for name in PLAN:
        if "." in name:
            advance(name)
        else:
            steps[name]()
    og_fly, ht_fly, out_copy = waiting["og"], waiting["ht"], waiting["out"]

    def activate(gate, up, cols):
        s = 0.5 * jnp.tanh(0.5 * gate) + 0.5
        swish = gate * s
        inner[:, cols] = (swish * up).astype(BF)
        d = gg[:, cols].astype(F32)
        gg[:, cols] = (d * up * s * (1.0 + gate * (1.0 - s))).astype(BF)
        ug[:, cols] = (d * swish).astype(BF)

    for n in range(5):
        cols = slice(n * 256, (n + 1) * 256)
        activate(nn(ht[...], ff_cols(n * 256, 256)), nn(ht[...], ff_cols(SLICE + n * 256, 256)), cols)
    both = nn(ht[...], jnp.concatenate([ff_cols(1280, 128), ff_cols(SLICE + 1280, 128)], 1))
    activate(both[:, :128], both[:, 128:], slice(1280, SLICE))

    def ff_rows(n, at):
        return wf[n // 2, lax.rem(n, 2), :, :, :, :, :, pl.ds(at, SLICE)].reshape(256, SLICE)

    copies.sent(ht_fly)
    copies.sent(og_fly)

    def two_columns(n, carry):
        cols = pl.ds(pl.multiple_of(n * 256, 256), 256)
        ogx[:, cols] = (nt(gg[...], ff_rows(n, 0)) + nt(ug[...], ff_rows(n, SLICE))).astype(BF)
        return carry

    def give_back(src, dst, cols):
        return [
            copies.start(src.at[pl.ds(at, n), cols], dst.at[k // 2 - (k > 5), pl.ds(r, n), cols], device({"x": (4 - i) % 4, "y": (4 - j) % 4}))
            for k, (i, j, r, n, at) in enumerate(SHARES)
        ]

    two_fly = []
    for at, end in ((0, 1), (1, 3), (3, 5), (5, 8)):
        lax.fori_loop(at, end, two_columns, 0)
        two_fly += give_back(ogx, rbt, pl.ds(at * 256, (end - at) * 256))

    def block_columns(n, carry):
        cols = pl.ds(pl.multiple_of(n * 256, 256), 256)
        ht[:, cols] = nt(inner[...], ff_rows(n, 2 * SLICE)).astype(BF)
        return carry

    lax.fori_loop(0, 4, block_columns, 0)
    blk_fly = give_back(ht, rbb, pl.ds(0, HALF))
    lax.fori_loop(4, 8, block_columns, 0)
    for copy in two_fly:
        copy.wait_recv()

    def middle_back(i, acc):
        rows = pl.ds(i * 16, 16)
        t = ogx[rows, :].astype(F32)
        for k in range(3):
            t += rbt[k, rows, :].astype(F32)
        m = mid[rows, :]
        r = lax.rsqrt(jnp.mean(m * m, -1, keepdims=True) + EPSILON)
        n = m * r
        acc += jnp.sum(t * n, 0, keepdims=True)
        t = t * gain2[...]
        g = ogo[rows, :].astype(F32) + r * (t - n * jnp.mean(t * n, -1, keepdims=True))
        mgrad[rows, :] = g
        bg[c, rows, :] = g.astype(BF)
        return acc

    gain_mlp = lax.fori_loop(0, ROWS // 16, middle_back, jnp.zeros((1, WIDTH), F32))
    bg_copy = copies.start(bg.at[c], bg.at[c], sibling)
    bg_copy.wait_recv()
    bgv = bg.at[:, :, :]
    olg = nt(bgv[...].reshape(CHIP, WIDTH), ob2[...])
    olg_low = olg.astype(BF)

    def mixed_columns(n, carry):
        cols = pl.ds(pl.multiple_of(n * 256, 256), 256)
        wcols = pl.ds(pl.multiple_of(QKV + n * 256, 256), 256)
        m = nn(bg[...].reshape(CHIP, WIDTH), wa[:, :, :, :, :, wcols].reshape(WIDTH, 256))
        m += nn(olg_low, oac[:, cols])
        ngt[cols, :] = m.T.astype(BF)
        return carry

    lax.fori_loop(0, 4, mixed_columns, 0)
    for k in range(4):
        sig[k] = jnp.zeros((AUG, 128), F32)

    def states_four(n, carry):
        g = n // 2
        rows = [pl.ds(pl.multiple_of(n * 256 + k * HEAD, HEAD), HEAD) for k in range(4)]
        for p in range(2):
            cols = slice(p * 128, (p + 1) * 128)
            left, right = [], []
            for k in range(4):
                h = (n * 4 + k) * 2 + p
                rden = den[h, :1]
                m = ngt[rows[k], cols].astype(F32)
                ng = (m * rden).astype(BF)
                dg = -jnp.sum(m * mixf[rows[k], cols], 0, keepdims=True) * rden
                ngt[rows[k], cols] = ng
                dgr[h, :1] = dg
                dq = (qfeat[rows[k], cols] * damp[h, :1]).astype(BF)
                right.append(jnp.concatenate([jnp.where(low_lane, dq, zero_low), jnp.where(low_lane, zero_low, dq)], 0))
                tail = jnp.where(lax.broadcasted_iota(jnp.int32, (AUG - HEAD, 128), 0) == 0, dg, 0.0).astype(BF)
                left.append(jnp.concatenate([ng, tail], 0))
            sig[g * 2 + p] = sig[g * 2 + p] + nt(lanes(left), lanes(right))
        return carry

    lax.fori_loop(0, 4, states_four, 0)
    sg_states = []
    for p in range(2):
        a, b = sig[p], sig[2 + p]
        sg_states.append(jnp.where(low_lane, a, pltpu.roll(b, 64, 1)))
        sg_states.append(jnp.where(low_lane, pltpu.roll(a, 64, 1), b))
    for s in range(4):
        st[s] = sg_states[s]
    folded = sg_states[3]
    for s in (2, 1, 0):
        folded = sg_states[s] + gates[s + 1] * folded
    fly = gather_plane(1, folded)
    blk_fly += give_back(ht, rbb, pl.ds(HALF, HALF))

    for k in range(4):
        kacc[k] = jnp.zeros((HEAD, 128), F32)
        vacc[k] = jnp.zeros((HEAD, 128), F32)

    def back_four(n, carry):
        g = n // 2
        rows = [pl.ds(pl.multiple_of(n * 256 + k * HEAD, HEAD), HEAD) for k in range(4)]
        for p in range(2):
            cols = slice(p * 128, (p + 1) * 128)
            ngs = lanes([ngt[r, cols] for r in rows])
            dgs = [dgr[(n * 4 + k) * 2 + p, :1] for k in range(4)]
            dg = lanes(dgs)
            ws = lanes([wts[(n * 4 + k) * 2 + p] for k in range(4)])
            pt = nn(vnat[g, cols, :], jnp.concatenate([ngs, ngs], 0)) + dg
            sgr = (ws.astype(F32) * pt).astype(BF)
            tail = jnp.where(lax.broadcasted_iota(jnp.int32, (HEAD, 512), 0) == 0, dg, 0.0).astype(BF)
            both = split(nn(comb_t[g * 2 + p], jnp.concatenate([ngs, tail], 0)))
            for k in range(4):
                qg = jnp.where(low_lane, both[k][:HEAD], both[k][HEAD:]) * damp[(n * 4 + k) * 2 + p, :1]
                f = qfeat[rows[k], cols]
                qlg[rows[k], cols] = (f * (qg - jnp.sum(f * qg, 0, keepdims=True))).astype(BF)
            near = split(nn(kt[g, :, cols], sgr))
            for k in range(4):
                far = nn(fq[c * 16 + n * 4 + k], qlg[rows[k], cols])
                gt[rows[k], cols] = (near[k] * 0.125 + far).astype(BF)
            kacc[g * 2 + p] = kacc[g * 2 + p] + nt(lanes([qt[r, cols] for r in rows]), sgr)
            vacc[g * 2 + p] = vacc[g * 2 + p] + nt(ngs, ws)
        return carry

    lax.fori_loop(0, 4, back_four, 0)
    lowo_t = lowo[...].astype(F32).T.astype(BF)
    olg_t = olg.T.astype(BF)
    apart[24:32] = 2.0 * nn(lowo_t[:16], bg[...].reshape(CHIP, WIDTH))[:8]
    red[72:80, :HALF] = nn(olg_t[:16], mixn[...])[:8]


    def grad_rows(n, carry):
        rows = pl.ds(pl.multiple_of(n * 256, 256), 256)
        gnat[:, rows] = gt[rows, :].astype(F32).T.astype(BF)
        return carry

    lax.fori_loop(0, 4, grad_rows, 0)

    def feat_pairs(n, carry):
        rows = pl.ds(pl.multiple_of(n * 128, 128), 128)
        r = nt(qt[rows, :], qlg[rows, :])
        red[0:64, rows] = jnp.where(low_lane, r[:HEAD], r[HEAD:])
        return carry

    lax.fori_loop(0, 8, feat_pairs, 0)

    part, fly = fold_plane(1, fly)

    def one_queries(n, carry):
        w = wa[n // 2, pl.ds(pl.multiple_of(lax.rem(n, 2) * 2, 2), 2), :, :, :, 0:HALF].reshape(256, HALF)
        o = nt(gnat[:, :HALF], w)
        rows = pl.ds(pl.multiple_of(lax.rem(n, 4) * 256, 256), 256)

        @pl.when(n < 4)
        def _():
            qfeat[rows, :] = o

        @pl.when(n >= 4)
        def _():
            mixf[rows, :] = o

        return carry

    lax.fori_loop(0, 8, one_queries, 0)
    suffix = fold_line(1, part, fly)
    states = [None, None, None, suffix]
    for s in (2, 1, 0):
        states[s] = gates[s + 1] * (states[s + 1] + st[s + 1])
    put_states(states, 4)

    for g in range(2):
        f_rows = slice(g * HEAD, (g + 1) * HEAD)
        for p in range(2):
            k = g * 2 + p
            cols = slice(p * 128, (p + 1) * 128)
            f = kfeat[f_rows, cols]
            both = nn(comb_t[4 + k], vt[g, :, cols])
            fg = jnp.where(low_lane, both[:HEAD], both[HEAD:]) * valid[:, cols]
            kl = (f * (fg - jnp.sum(f * fg, 0, keepdims=True))).astype(BF)
            qlg[HALF + g * HEAD : HALF + (g + 1) * HEAD, cols] = kl
            gt[HALF + g * HEAD : HALF + (g + 1) * HEAD, cols] = (kacc[k] * 0.125 + nn(fk[c * 2 + g], kl)).astype(BF)
            fl = f.astype(BF)
            stack = jnp.concatenate([jnp.where(low_lane, fl, zero_low), jnp.where(low_lane, zero_low, fl)], 0)
            gt[HALF + NARROW + g * HEAD : HALF + NARROW + (g + 1) * HEAD, cols] = (
                vacc[k] + nn(comb[4 + k, :HEAD], stack)
            ).astype(BF)

    lowg_t = nn(ball[...], gt[...])
    lowg[...] = lowg_t.T.astype(BF)
    lowg_t = lowg_t.astype(BF)

    grad_rows(4, 0)

    def one_columns(n, had):
        cols = pl.ds(pl.multiple_of(n * 256, 256), 256)
        w = wa[n // 2, pl.ds(pl.multiple_of(lax.rem(n, 2) * 2, 2), 2), :, :, :, HALF:QKV].reshape(256, 2 * NARROW)
        o = had[pl.ds(pl.multiple_of(lax.rem(n, 4) * 256, 256), 256), :]
        o = o + nt(gnat[:, HALF:], w) + nn(lowg[...], aall[:, cols])
        normed = [tok2[side, :, cols].astype(F32) * r1[side, :, :1] for side in range(2)]
        apart[32:33, cols] = jnp.sum(o[:ROWS] * normed[0] + o[ROWS:] * normed[1], 0, keepdims=True)
        ones[:, cols] = jnp.where(c == 0, o[:ROWS], o[ROWS:])
        outs[:, cols] = jnp.where(c == 0, o[ROWS:], o[:ROWS]).astype(BF)

    def one_first(n, carry):
        one_columns(n, qfeat)
        return carry

    def one_second(n, carry):
        one_columns(n, mixf)
        return carry

    apart[0:24] = nn(lowg_t[:32], hid1[...])[:24]
    apart[32:40] = jnp.where(lax.broadcasted_iota(jnp.int32, (8, 1), 0) == 1, gain_mlp, 0.0)
    copies.sent([out_copy])
    lax.fori_loop(0, 4, one_first, 0)
    lax.fori_loop(4, 8, one_second, 0)
    one_copy = copies.start(outs, outr, sibling)

    theirs = pl.ds(pl.multiple_of((1 - c) * HALF, HALF), HALF)
    mine = pl.ds(pl.multiple_of(c * HALF, HALF), HALF)
    a_copy = copies.start(apart.at[:, theirs], asib, sibling)

    r = nt(kt[...].reshape(128, CHIP), qlg[HALF:, :])
    red[0:64, HALF : HALF + 128] = jnp.where(low_lane, r[:HEAD], r[HEAD:])

    low_t = low[...].astype(F32).T.astype(BF)
    up = 2.0 * nt(low_t[:32], gt[...])
    red[64:72, :HALF] = up[0:8, :HALF]
    red[64:72, HALF : HALF + NARROW] = up[8:16, HALF : HALF + NARROW]
    red[64:72, HALF + NARROW :] = up[16:24, HALF + NARROW :]

    red[72:80, HALF:] = jnp.zeros((8, PIECE - HALF), F32)
    red[0:64, HALF + 128 :] = jnp.zeros((64, 128), F32)
    red[80:128, HALF:] = jnp.zeros((48, PIECE - HALF), F32)
    red[120:128, :HALF] = jnp.zeros((8, HALF), F32)
    a_copy.wait_recv()
    red[80:120, :HALF] = apart[:, mine] + asib[...]

    def fold_piece(k, carry):
        rows = pl.ds(pl.multiple_of(k * 8, 8), 8)
        redb[k] = jnp.concatenate([red[rows, : PIECE // 2], red[rows, PIECE // 2 :]], 0).astype(BF)
        return carry

    lax.fori_loop(0, 16, fold_piece, 0)
    fly = []
    for i in range(4):
        for j in range(4):
            if i + j > 0:
                to = wrap(x + i) * 4 + wrap(y + j)
                fly.append(copies.start(redb.at[to], rr.at[plane], device({"x": i, "y": j})))
    rr[plane] = redb[plane]
    for copy in blk_fly:
        copy.wait_recv()

    def block_rows(i, carry):
        rows = pl.ds(i * 16, 16)
        t = mid[rows, :] + ht[rows, :].astype(F32)
        for k in range(3):
            t += rbb[k, rows, :].astype(F32)
        ht[rows, :] = t.astype(BF)
        return carry

    copies.sent(blk_fly)
    lax.fori_loop(0, ROWS // 16, block_rows, 0)
    here(ht.at[pl.ds(0, ROWS)], blk_out)
    for copy in fly:
        copy.wait_recv()
    total = rr[0].astype(F32)
    for k in range(1, 16):
        total += rr[k].astype(F32)
    rz[z] = total
    line = [copies.start(rz.at[z], rz.at[z], device({"z": i})) for i in (1, 2, 3)]
    one_copy.wait_recv()
    copies.sent([one_copy])

    def token_rows(i, carry):
        rows = pl.ds(i * 16, 16)
        o = ones[rows, :] + outr[rows, :].astype(F32)
        t = tok2[c, rows, :].astype(F32)
        r = r1[c, rows, :1]
        n = t * r
        o = o * gain1[...]
        outs[rows, :] = (mgrad[rows, :] + r * (o - n * jnp.mean(o * n, -1, keepdims=True))).astype(BF)
        return carry

    lax.fori_loop(0, ROWS // 32, token_rows, 0)
    for copy in line:
        copy.wait_recv()
    total = (rz[0] + rz[1]) + (rz[2] + rz[3])
    fin[c, plane] = total.astype(BF)
    piece = fin.at[c, plane]
    fly = [
        copies.start(piece, piece, device({"x": i, "y": j})) for i in range(4) for j in range(4) if i + j > 0
    ]
    lax.fori_loop(ROWS // 32, ROWS // 16, token_rows, 0)
    here(outs, gtok_out)
    for copy in fly:
        copy.wait_recv()
    f_copy = copies.start(fin.at[c], fin.at[c], sibling)
    f_copy.wait_recv()

    here(fin, red_out)
    for copy in local[-3:]:
        copy.wait()
    copies.drain()


def finish(
    blk, gtok, fin,
    blk_out, gtok_out, gain_a_out, qa_out, qb_out, ka_out, kb_out, va_out, vb_out, oa_out, ob_out, fq_out, fk_out,
    gain_b_out,
):
    blk_out[...] = blk[...]
    gtok_out[...] = gtok[...]

    def wide(k, side):
        got = fin[side, k].astype(F32)
        return got[:8], got[8:]

    def feat_out(k, carry):
        rows = pl.ds(pl.multiple_of(k * 8, 8), 8)
        for side in range(2):
            left, right = wide(k, side)
            for j in range(9):
                v = left[:, j * 128 : (j + 1) * 128] if j < 5 else right[:, (j - 5) * 128 : (j - 4) * 128]
                out, head = (fq_out, side * 16 + 2 * j) if j < 8 else (fk_out, side * 2)
                out[head, rows, :] = v[:, :64]
                out[head + 1, rows, :] = pltpu.roll(v, 64, 1)[:, :64]
        return carry

    lax.fori_loop(0, 8, feat_out, 0)
    rest = HALF - PIECE // 2
    for side in range(2):
        for k, out in ((8, qb_out), (9, oa_out), (10, qa_out), (11, ka_out), (12, va_out), (13, ob_out)):
            left, right = wide(k, side)
            out[:, side * HALF : side * HALF + PIECE // 2] = left
            out[:, side * HALF + PIECE // 2 : (side + 1) * HALF] = right[:, :rest]
            if k == 8:
                kb_out[:, side * NARROW : (side + 1) * NARROW] = right[:, rest : rest + NARROW]
                vb_out[:, side * NARROW : (side + 1) * NARROW] = right[:, rest + NARROW :]
        left, right = wide(14, side)
        row = jnp.concatenate([left, right[:, :rest]], 1)
        for k, out in ((0, gain_a_out), (1, gain_b_out)):
            for i in range(8):
                out[side * 8 + i : side * 8 + i + 1, :] = row[k : k + 1, i * 128 : (i + 1) * 128]


N_COPIES = 273
N_SENDS = 64


def scratch():
    v = pltpu.VMEM
    return [
        v((4, 4, 4, 2, 16, ATT), BF),
        v((4, 2, 2, 2, 2, 2, 16, 3 * SLICE), BF),
        v((2, 2, 16, 3 * SLICE), BF),
        v((2, ROWS, WIDTH), BF),
        v((ROWS, WIDTH), BF),
        v((8, WIDTH), F32),
        v((2, ROWS, 128), F32),
        v((128, WIDTH), BF),
        v((128, QKV), BF),
        v((128, HALF), BF),
        v((128, WIDTH), BF),
        v((4, 16, 128), F32),
        v((2, 8, 128), F32),
        v((2, 128, 128), F32),
        v((CHIP, WIDTH), BF),
        v((CHIP, 128), BF),
        v((HALF, CHIP), BF),
        v((2, HEAD, CHIP), BF),
        v((2, 128, CHIP), BF),
        v((2, CHIP, 128), BF),
        v((2, CHIP, 128), BF),
        v((128, CHIP), F32),
        v((4, AUG, 128), F32),
        v((8, AUG, 128), BF),
        v((8, 128, 128), BF),
        v((32, 128, 128), BF),
        v((HALF, CHIP), F32),
        v((HALF, CHIP), F32),
        v((32, 8, 128), F32),
        v((32, 8, 128), F32),
        v((CHIP, HALF), BF),
        v((CHIP, 128), BF),
        v((ROWS, WIDTH), BF),
        v((ROWS, WIDTH), BF),
        v((ROWS, WIDTH), F32),
        v((512, WIDTH), BF),
        v((512, WIDTH), BF),
        v((512, SLICE), BF),
        v((512, SLICE), BF),
        v((512, SLICE), BF),
        v((3, ROWS, WIDTH), BF),
        v((3, ROWS, WIDTH), BF),
        v((ROWS, WIDTH), F32),
        v((2, ROWS, WIDTH), BF),
        v((HALF, CHIP), BF),
        v((32, 8, 128), F32),
        v((4, AUG, 128), F32),
        v((HALF + 128, CHIP), BF),
        v((QKV, CHIP), BF),
        v((CHIP, QKV), BF),
        v((CHIP, 128), BF),
        v((ROWS, WIDTH), F32),
        v((4, HEAD, 128), F32),
        v((4, HEAD, 128), F32),
        v((2, AUG, 128), BF),
        v((2, 16, AUG, 128), BF),
        v((2, AUG, 128), BF),
        v((2, 3, AUG, 128), BF),
        v((128, PIECE), F32),
        v((16, 16, PIECE // 2), BF),
        v((16, 16, PIECE // 2), BF),
        v((4, 16, PIECE // 2), F32),
        v((2, 16, 16, PIECE // 2), BF),
        v((40, WIDTH), F32),
        v((40, HALF), F32),
        pltpu.SemaphoreType.DMA((N_SENDS,)),
        pltpu.SemaphoreType.DMA((N_COPIES,)),
        pltpu.SemaphoreType.DMA((18,)),
    ]


def body(
    tokens, sequence_lengths, attention_gain, query_weight, key_weight, value_weight, output_weight_flipped,
    query_adapter_down, query_adapter_up, key_adapter_down, key_adapter_up, value_adapter_down, value_adapter_up,
    output_adapter_down, output_adapter_up, query_feature_map, key_feature_map, feedforward_gain,
    gate_weight, up_weight, down_weight_flipped, output_gradient,
):
    vmem = pl.BlockSpec(memory_space=pltpu.VMEM)
    smem = pl.BlockSpec(memory_space=pltpu.SMEM)
    anywhere = pl.BlockSpec(memory_space=pl.ANY)

    def array(*shape, dtype=F32):
        return jax.ShapeDtypeStruct(shape, dtype)

    parts = pl.pallas_call(
        kernel,
        out_shape=(
            array(ROWS, WIDTH, dtype=BF), array(ROWS, WIDTH, dtype=BF), array(2, 16, 16, PIECE // 2, dtype=BF),
        ),
        in_specs=[anywhere, smem, vmem] + [anywhere] * 4 + [vmem] * 11 + [anywhere] * 4,
        out_specs=(anywhere,) * 3,
        scratch_shapes=scratch(),
        compiler_params=pltpu.CompilerParams(
            collective_id=0, has_side_effects=True, vmem_limit_bytes=64 * 1024 * 1024
        ),
    )(
        tokens, sequence_lengths, attention_gain.reshape(16, 128),
        query_weight, key_weight, value_weight, output_weight_flipped,
        query_adapter_down.T, query_adapter_up, key_adapter_down.T, key_adapter_up, value_adapter_down.T,
        value_adapter_up, output_adapter_down.T, output_adapter_up, query_feature_map, key_feature_map,
        feedforward_gain.reshape(16, 128), gate_weight, up_weight, down_weight_flipped, output_gradient,
    )
    out = pl.pallas_call(
        finish,
        out_shape=(
            array(ROWS, WIDTH, dtype=BF), array(ROWS, WIDTH, dtype=BF), array(16, 128),
            array(RANK, WIDTH), array(RANK, WIDTH), array(RANK, WIDTH), array(RANK, 2 * NARROW),
            array(RANK, WIDTH), array(RANK, 2 * NARROW), array(RANK, WIDTH), array(RANK, WIDTH),
            array(QUERY_HEADS, HEAD, HEAD), array(KEY_VALUE_HEADS, HEAD, HEAD), array(16, 128),
        ),
        in_specs=[vmem] * 3,
        out_specs=(vmem,) * 14,
    )(*parts)
    (
        block_out, grad_tokens, gain_attn, qa, qb, ka, kb, va, vb, oa, ob, feat_q, feat_k, gain_mlp,
    ) = out
    return (
        block_out, grad_tokens, gain_attn.reshape(WIDTH), qa.T, qb, ka.T, kb, va.T, vb, oa.T, ob, feat_q, feat_k,
        gain_mlp.reshape(WIDTH),
    )


def solution(mesh):
    split, whole = P("seq", None), P()
    return jax.shard_map(
        body,
        mesh=mesh,
        in_specs=(
            (split, whole, whole) + (split,) * 4 + (whole,) * 11 + (split,) * 4
        ),
        out_specs=(split, split) + (whole,) * 12,
        check_vma=False,
    )
```

```python
import math

import jax
import jax.numpy as jnp
from jax import lax
from jax.experimental import pallas as pl
from jax.experimental.pallas import tpu as pltpu
from jax.sharding import PartitionSpec as P

QUERY_HEADS = 32
KEY_VALUE_HEADS = 4
HEAD = 64
STRETCH = 64
WIDTH = 2048
FF = 5632
ROWS = 128
CHIP = 256
HALF = 1024
NARROW = 128
QKV = HALF + 2 * NARROW
ATT = QKV + HALF
SLICE = FF // 4
AUG = 80
RANK = 8
PIECE = 512
EPSILON = 1e-05
MESH = pl.DeviceIdType.MESH
F32 = jnp.float32
BF = jnp.bfloat16

SHARES = (
    (1, 0, 0, 64, 128),
    (3, 0, 64, 64, 192),
    (0, 1, 0, 64, 256),
    (0, 3, 64, 64, 320),
    (1, 1, 0, 32, 384),
    (1, 3, 32, 32, 416),
    (3, 1, 64, 32, 448),
    (3, 3, 96, 32, 480),
)


def nn(left, right):
    return jnp.dot(left, right, preferred_element_type=F32)


def tn(left, right):
    return lax.dot_general(left, right, (((0,), (0,)), ((), ())), preferred_element_type=F32)


def nt(left, right):
    return lax.dot_general(left, right, (((1,), (1,)), ((), ())), preferred_element_type=F32)


def wrap(value):
    return lax.rem(value, 4)


class Copy:
    def __init__(self, copy, index):
        self.copy, self.index, self.landed = copy, index, False
        self.wait_send = copy.wait_send

    def wait_recv(self):
        self.copy.wait_recv()
        self.landed = True


class Copies:
    def __init__(self, send, recv):
        self.send, self.recv, self.count, self.open = send, recv, 0, {}
        self.all, self.heard, self.free, self.indices = [], [], [], 0

    def start(self, src, dst, device):
        slot = self.count % N_SENDS
        if slot in self.open:
            self.open.pop(slot).wait_send()
        if self.free:
            index = self.free.pop()
        else:
            index = self.indices
            self.indices += 1
        copy = pltpu.make_async_remote_copy(
            src_ref=src,
            dst_ref=dst,
            send_sem=self.send.at[slot],
            recv_sem=self.recv.at[index],
            device_id=(device,),
            device_id_type=MESH,
        )
        self.count += 1
        copy.start()
        copy = Copy(copy, index)
        self.open[slot] = copy
        self.all.append(copy)
        return copy

    def note(self):
        self.heard = [copy.index for copy in self.all if copy.landed]

    def reuse(self):
        self.free = self.heard

    def sent(self, copies):
        for slot in [k for k, copy in self.open.items() if any(copy is other for other in copies)]:
            self.open.pop(slot).wait_send()

    def drain(self):
        for copy in self.open.values():
            copy.wait_send()


class Heads:
    def __init__(self, copies, wa, where, device, settled, parts):
        self.copies, self.wa, self.where, self.device = copies, wa, where, device
        self.settled, self.parts = settled, parts
        self.flying = {}

    def block(self, order, phase, at, cols, core=slice(None)):
        index = []
        for axis in "zxy":
            k = order.index(axis)
            index.append(slice(None) if k < phase else at if k == phase else self.where[axis])
        return self.wa.at[index[0], index[1], index[2], core, :, cols]

    def begin(self, phase):
        c = self.where["c"]
        for part, (order, src, at, first, count) in enumerate(self.parts):
            axis = order[phase]
            cols = pl.ds(first, count)
            fly = []
            if phase == 0:
                for step in (1, 3, 2):
                    for cross in (0, 1):
                        core = 1 - c if cross else c
                        piece = src.at[:, pl.ds(pl.multiple_of(core * (src.shape[1] // 2) + at, 128), count)]
                        dst = self.wa.at[self.where["z"], self.where["x"], self.where["y"], c, :, cols]
                        fly.append(self.copies.start(piece, dst, self.device({axis: step}, cross)))
            else:
                own = self.block(order, phase, self.where[axis], cols)
                fly = [self.copies.start(own, own, self.device({axis: step})) for step in (1, 3)]
            self.flying[phase, part] = fly

    def middle(self, phase):
        for part, (order, src, at, first, count) in enumerate(self.parts):
            axis = order[phase]
            for copy in self.flying[phase, part]:
                copy.wait_recv()
            here = self.where[axis]
            left = self.block(order, phase, wrap(here + 3), pl.ds(first, count), 0)
            right = self.block(order, phase, wrap(here + 1), pl.ds(first, count), 1)
            self.flying[phase, part] = [
                self.copies.start(left, left, self.device({axis: 1})),
                self.copies.start(right, right, self.device({axis: 3})),
            ]

    def end(self, phase):
        self.settled()
        for part in range(len(self.parts)):
            for copy in self.flying[phase, part]:
                copy.wait_recv()


class Units:
    def __init__(self, copies, here, wf, stage, where, device, sibling, parts):
        self.copies, self.here, self.wf, self.stage = copies, here, wf, stage
        self.where, self.device, self.sibling, self.parts = where, device, sibling, parts
        self.flying, self.handed, self.own = {}, [], []

    def rows(self, order, along, across, cols):
        w = self.where
        a = (slice(None), slice(None)) if along is None else (along // 2, lax.rem(along, 2))
        b = (across // 2, lax.rem(across, 2))
        x, y = (a, b) if order == "xy" else (b, a)
        return self.wf.at[w["z"], x[0], x[1], y[0], y[1], w["c"], :, cols]

    def line(self, z, cols):
        return self.wf.at[z, :, :, :, :, self.where["c"], :, cols]

    def hand_on(self, block):
        self.handed.append(self.copies.start(block, block, self.sibling))

    def begin(self, phase):
        w = self.where
        for part, (order, src, at, first, count) in enumerate(self.parts):
            cols = pl.ds(first, count)
            a, b = order
            fly = []
            if phase == 0:
                for d in (1, 3, 2, 0):
                    for e in (0, 1):
                        pa, pb = lax.rem(w[a] + d, 2), lax.rem(w[b] + e, 2)
                        slot = pa * 2 + pb if order == "xy" else pb * 2 + pa
                        piece = src.at[:, pl.ds(pl.multiple_of(slot * SLICE + at, 128), count)]
                        if e == 0:
                            dst = self.rows(order, w[a], w[b], cols)
                        else:
                            dst = self.stage.at[w[a] // 2, lax.rem(w[a], 2), :, cols]
                        if d == 0:
                            self.own.append(self.here(piece, dst))
                        else:
                            fly.append(self.copies.start(piece, dst, self.device({a: d})))
            elif phase == 1:
                mine = self.rows(order, None, w[b], cols)
                other = self.stage.at[:, :, :, cols]
                fly = [
                    self.copies.start(other, mine, self.device({b: 1})),
                    self.copies.start(other, mine, self.device({b: 3})),
                    self.copies.start(mine, mine, self.device({b: 2})),
                ]
            else:
                block = self.line(w["z"], cols)
                self.hand_on(block)
                fly = [self.copies.start(block, block, self.device({"z": step})) for step in (1, 3)]
            self.flying[phase, part] = fly

    def middle(self, phase):
        z = self.where["z"]
        for part, (order, src, at, first, count) in enumerate(self.parts):
            for copy in self.flying[phase, part]:
                copy.wait_recv()
            one = (count // 256) * 128
            before, after = wrap(z + 3), wrap(z + 1)
            left = self.line(before, pl.ds(first, one))
            right = self.line(after, pl.ds(first + one, count - one))
            self.flying[phase, part] = [
                self.copies.start(left, left, self.device({"z": 1})),
                self.copies.start(right, right, self.device({"z": 3})),
            ]
            self.hand_on(self.line(before, pl.ds(first, count)))
            self.hand_on(self.line(after, pl.ds(first, count)))

    def end(self, phase):
        if phase == 0:
            for copy in self.own:
                copy.wait()
        for part, (order, src, at, first, count) in enumerate(self.parts):
            for copy in self.flying[phase, part]:
                copy.wait_recv()
            if phase == 2:
                self.hand_on(self.line(wrap(self.where["z"] + 2), pl.ds(first, count)))

    def settle(self):
        for copy in self.handed:
            copy.wait_recv()


EARLY = ("kv.b0", "q.b0", "o.b0", "d.b0", "kv.e0", "u.b0", "g.b0", "kv.b1",)
PLAN = (
    "o.e0", "q.e0", "q.b1", "d.e0", "kv.m1", "d.b1", "o.b1", "q.m1", "kv.e1", "g.e0", "u.e0", "kv.b2",
    "d.e1", "d.b2", "q.e1", "o.m1", "g.b1", "u.b1", "kv.m2", "q.b2", "g.e1", "g.b2", "o.e1", "kv.e2",
    "low", "d.m2", "u.e1", "kvc", "pls", "o.b2", "lns", "q.m2", "u.b2", "o.m2", "g.m2", "d.e2",
    "lnw", "q.e2", "qc", "ogs", "att", "o.e2", "oproj", "mid", "u.m2", "hts", "g.e2", "ogw",
    "ds", "ig", "u.e2", "gs", "us", "htw",
)


def kernel(
    tok, lens, gain_a, qw, kw, vw, ow, qa, qb, ka, kb, va, vb, oa, ob, fq, fk, gain_b, gw, uw, dw, og,
    blk_out, gtok_out, red_out,
    wa, wf, stage, tok2, ogo, gains, r1, aall, ball, oac, ob2, masks, far_masks, bias, hid1, low, qt, kt, vt, knat, vnat,
    kfeat, st, comb, comb_t, wts, qfeat, mixf, damp, den, mixn, lowo, outs, outr, mid, ht, ogx, gg, inner, ug, rbt, rbb,
    mgrad, bg, ngt, dgr, sig, qlg, gt, gnat, lowg, ones, kacc, vacc, fsend, frecv, hsend, hrecv, red, redb, rr, rz, fin,
    apart, asib, gsum, send, recv, loc,
):
    me = lax.axis_index("seq")
    c = lax.rem(me, 2)
    y = lax.rem(me // 2, 4)
    x = lax.rem(me // 8, 4)
    z = me // 32

    def device(steps, cross=0):
        zz, xx, yy = (wrap(v + steps.get(n, 0)) for n, v in (("z", z), ("x", x), ("y", y)))
        return ((zz * 4 + xx) * 4 + yy) * 2 + (1 - c if cross else c)

    sibling = me + 1 - 2 * c
    plane = x * 4 + y
    xl, yl = lax.rem(x, 2), lax.rem(y, 2)
    xh, yh = x // 2, y // 2

    barrier = pltpu.get_barrier_semaphore()
    peers = [sibling]
    peers += [device({"x": i, "y": j}) for i in range(4) for j in range(4) if i + j > 0]
    peers += [device({"z": i}) for i in (1, 2, 3)]
    peers += [device({axis: i}, 1) for axis in "xyz" for i in (1, 2, 3)]
    for peer in peers:
        pl.semaphore_signal(barrier, inc=1, device_id=(peer,), device_id_type=MESH)
    copies = Copies(send, recv)
    local = []

    def here(src, dst):
        copy = pltpu.make_async_copy(src, dst, loc.at[len(local)])
        copy.start()
        local.append(copy)
        return copy

    own = wa.at[z, x, y, c]
    pieces = ((kw, HALF, NARROW), (vw, HALF + NARROW, NARROW), (qw, 0, HALF), (ow, QKV, HALF))
    for src, at, count in pieces:
        mine = src.at[:, pl.ds(pl.multiple_of(c * count, count), count)]
        here(mine, own.at[:, pl.ds(at, count)])
    here(tok, tok2.at[c])
    here(og, ogx.at[pl.ds(0, ROWS)])
    here(og, ogo)

    pl.semaphore_wait(barrier, len(peers))
    first = []
    for src, at, count in pieces:
        other = src.at[:, pl.ds(pl.multiple_of((1 - c) * count, count), count)]
        first.append(copies.start(other, own.at[:, pl.ds(at, count)], sibling))
    tok_copy = copies.start(tok, tok2.at[c], sibling)
    where = {"z": z, "x": x, "y": y, "c": c}
    pending = [local[:4] + first]

    def settled():
        if pending:
            done = pending.pop()
            for copy in done[:4]:
                copy.wait()
            for copy in done[4:]:
                copy.wait_recv()

    streams = {
        "kv": Heads(copies, wa, where, device, settled, (("xzy", kw, 0, HALF, NARROW), ("yzx", vw, 0, HALF + NARROW, NARROW))),
        "q": Heads(copies, wa, where, device, settled, (("xzy", qw, 0, 0, 512), ("yzx", qw, 512, 0 + 512, 512))),
        "o": Heads(copies, wa, where, device, settled, (("zxy", ow, 0, QKV, 512), ("zyx", ow, 512, QKV + 512, 512))),
        "d": Units(
            copies, here, wf, stage, where, device, sibling,
            (("xy", dw, 0, 2 * SLICE, 768), ("yx", dw, 768, 2 * SLICE + 768, 640)),
        ),
        "g": Units(copies, here, wf, stage, where, device, sibling, (("xy", gw, 0, 0, SLICE),)),
        "u": Units(copies, here, wf, stage, where, device, sibling, (("yx", uw, 0, SLICE, SLICE),)),
    }
    waiting = {}

    def advance(name):
        stream, step = name.split(".")
        stream = streams[stream]
        {"b": stream.begin, "m": stream.middle, "e": stream.end}[step[0]](int(step[1]))

    for name in EARLY:
        advance(name)

    for k, src in enumerate((gain_a, gain_b)):
        g = src[...].astype(F32)
        gains[k : k + 1, :] = jnp.concatenate([g[i : i + 1] for i in range(16)], 1)
    gain1, gain2 = gains.at[pl.ds(0, 1)], gains.at[pl.ds(1, 1)]

    def below(parts, rows, count):
        got = [part.astype(F32) for part in parts]
        used = RANK * len(parts)
        return jnp.concatenate(got + [jnp.zeros((rows - used, count), F32)], 0).astype(BF)

    aall[...] = below([qa[...], ka[...], va[...]], 128, WIDTH)
    half = pl.ds(pl.multiple_of(c * HALF, HALF), HALF)
    narrow = pl.ds(pl.multiple_of(c * NARROW, NARROW), NARROW)
    none = jnp.zeros((RANK, NARROW), F32)
    ball[:, :HALF] = below([2.0 * qb[:, half].astype(F32)], 128, HALF)
    ball[:, HALF : HALF + NARROW] = below([none, 2.0 * kb[:, narrow].astype(F32)], 128, NARROW)
    ball[:, HALF + NARROW :] = below([none, none, 2.0 * vb[:, narrow].astype(F32)], 128, NARROW)
    oac[...] = below([oa[:, half]], 128, HALF)
    ob2[...] = below([2.0 * ob[...].astype(F32)], 128, WIDTH)

    chip = me // 2
    starts, ends, total = [], [], jnp.int32(0)
    for k in range(8):
        starts.append(total)
        total = total + ((lens[k] + (STRETCH - 1)) >> 6)
        ends.append(total)

    def sequence(stretch):
        found = jnp.where(stretch >= ends[0], 1, 0)
        for k in range(1, 7):
            found = found + jnp.where(stretch >= ends[k], 1, 0)
        return found

    counts, gates = [], []
    for s in range(4):
        stretch = chip * 4 + s
        begin, length = starts[0], lens[0]
        for k in range(1, 8):
            inside = stretch >= starts[k]
            begin = jnp.where(inside, starts[k], begin)
            length = jnp.where(inside, lens[k], length)
        counts.append(length - (stretch - begin) * STRETCH)
        gates.append(jnp.where(stretch != begin, 1.0, 0.0))
    first_own, last_own = sequence(chip * 4), sequence(chip * 4 + 3)
    k16 = lax.broadcasted_iota(jnp.int32, (16, 128), 0)
    firsts = sequence((z * 16 + k16) * 4)
    lasts = sequence((z * 16 + k16) * 4 + 3)
    masks[0] = jnp.where((k16 < plane) & (lasts == first_own), 1.0, 0.0)
    masks[1] = jnp.where(lasts == sequence(z * 64 + 63), 1.0, 0.0)
    masks[2] = jnp.where((k16 > plane) & (firsts == last_own), 1.0, 0.0)
    masks[3] = jnp.where(firsts == sequence(z * 64), 1.0, 0.0)
    k8 = lax.broadcasted_iota(jnp.int32, (8, 128), 0)
    far_masks[0] = jnp.where((k8 < z) & (sequence(k8 * 64 + 63) == first_own), 1.0, 0.0)
    far_masks[1] = jnp.where((k8 > z) & (sequence(k8 * 64) == last_own), 1.0, 0.0)
    lane = lax.broadcasted_iota(jnp.int32, (1, 128), 1)
    low_lane = lane < 64
    in_stretch = lax.rem(lane, STRETCH)
    valid = jnp.concatenate(
        [jnp.where(in_stretch < jnp.where(low_lane, counts[2 * p], counts[2 * p + 1]), 1.0, 0.0) for p in range(2)], 1
    )
    iu = lax.broadcasted_iota(jnp.int32, (128, 128), 0)
    it = lax.broadcasted_iota(jnp.int32, (128, 128), 1)
    for p in range(2):
        room = jnp.where(iu < 64, counts[2 * p], counts[2 * p + 1])
        seen = (iu <= it) & ((iu < 64) == (it < 64)) & (lax.rem(iu, STRETCH) < room)
        bias[p] = jnp.where(seen, 0.0, -1e30)

    for copy in local[4:7]:
        copy.wait()
    tok_copy.wait_recv()

    def norm_rows(i, carry):
        rows = pl.ds(i * 32, 32)
        for side in range(2):
            t = tok2[side, rows, :].astype(F32)
            r = lax.rsqrt(jnp.mean(t * t, -1, keepdims=True) + EPSILON)
            r1[side, rows, :] = jnp.broadcast_to(r, (32, 128))
            hid1[pl.ds(side * ROWS + i * 32, 32), :] = (t * r * gain1[...]).astype(BF)
        return carry

    lax.fori_loop(0, ROWS // 32, norm_rows, 0)

    zero_low = jnp.zeros((), BF)

    def softmax_rows(logits):
        e = jnp.exp(logits - jnp.max(logits, 0, keepdims=True))
        return e / jnp.sum(e, 0, keepdims=True)

    def gather_plane(base, folded):
        fsend[base] = folded.astype(BF)
        fly = []
        for i in range(4):
            for j in range(4):
                if i + j > 0:
                    fly.append(copies.start(fsend.at[base], frecv.at[base, plane], device({"x": i, "y": j})))
        frecv[base, plane] = folded.astype(BF)
        return fly

    def fold_plane(base, fly):
        for copy in fly:
            copy.wait_recv()
        part = jnp.zeros((AUG, 128), F32)
        whole = jnp.zeros((AUG, 128), F32)
        for k in range(16):
            f = frecv[base, k].astype(F32)
            part += masks[2 * base, k : k + 1, :] * f
            whole += masks[2 * base + 1, k : k + 1, :] * f
        hsend[base] = whole.astype(BF)
        fly = [copies.start(hsend.at[base], hrecv.at[base, i - 1], device({"z": i})) for i in (1, 2, 3)]
        return part, fly

    def fold_line(base, part, fly):
        for i, copy in zip((1, 2, 3), fly):
            copy.wait_recv()
            part += far_masks[base, pl.ds(wrap(z + 4 - i), 1), :] * hrecv[base, i - 1].astype(F32)
        return part

    def combine(states):
        for g in range(2):
            for p in range(2):
                one, two = states[2 * p], states[2 * p + 1]
                if g == 0:
                    both = jnp.where(low_lane, one, pltpu.roll(two, 64, 1))
                else:
                    both = jnp.where(low_lane, pltpu.roll(one, 64, 1), two)
                yield g * 2 + p, both

    def put_states(states, base):
        for k, both in combine(states):
            comb[base + k] = both.astype(BF)
            tall = jnp.concatenate([both, jnp.zeros((128 - AUG, 128), F32)], 0)
            comb_t[base + k] = tall.T.astype(BF)

    def share(src, dst):
        return [
            copies.start(src.at[pl.ds(r, n)], dst.at[pl.ds(at, n)], device({"x": i, "y": j}))
            for i, j, r, n, at in SHARES
        ]

    def lower():
        low[...] = nt(hid1[...], aall[...]).astype(BF)

    def keys():
        kv = nn(hid1[...], wa[:, :, :, :, :, HALF:QKV].reshape(WIDTH, 2 * NARROW))
        kv = (kv + nn(low[...], ball[:, HALF:QKV])).astype(BF)
        kv_t = kv.astype(F32).T.astype(BF)
        for g in range(2):
            keep = low_lane if g == 0 else ~low_lane
            knat[g] = jnp.where(keep, kv[:, :NARROW], jnp.zeros((), BF))
            vnat[g] = jnp.where(keep, kv[:, NARROW:], jnp.zeros((), BF))
            kt[g] = kv_t[g * HEAD : (g + 1) * HEAD]
            tail = lax.broadcasted_iota(jnp.int32, (64, CHIP), 0) == 0
            vt[g, :HEAD] = kv_t[NARROW + g * HEAD : NARROW + (g + 1) * HEAD]
            vt[g, HEAD:] = tail.astype(F32).astype(BF)
        lanes4 = lax.broadcasted_iota(jnp.int32, (1, CHIP), 1) // STRETCH

        for g in range(2):
            kfeat[g * HEAD : (g + 1) * HEAD] = softmax_rows(tn(fk[c * 2 + g], kt[g])) * valid
        kf = kfeat[...]
        kf_high = kf.astype(BF)
        kf_rest = (kf - kf_high.astype(F32)).astype(BF)
        for s in range(4):
            got = []
            for g in range(2):
                va = jnp.where(lanes4 == s, vt[g, :AUG], jnp.zeros((), BF))
                got.append(nt(va, kf_high) + nt(va, kf_rest))
            st[s] = jnp.where(low_lane, got[0], got[1])


    def send_plane():
        folded = st[0]
        for s in (1, 2, 3):
            folded = st[s] + gates[s] * folded
        copies.note()
        waiting["plane"] = gather_plane(0, folded)

    def send_line():
        waiting["part"], waiting["line"] = fold_plane(0, waiting["plane"])

    def take_line():
        prefix = fold_line(0, waiting["part"], waiting["line"])
        states = [prefix]
        for s in (1, 2, 3):
            states.append(gates[s] * (states[s - 1] + st[s - 1]))
        put_states(states, 0)

    def queries():
        def query_columns(n, carry):
            cols = pl.ds(pl.multiple_of(n * 256, 256), 256)
            q = nn(hid1[...], wa[:, :, :, :, :, cols].reshape(WIDTH, 256)) + nn(low[...], ball[:, cols])
            qt[cols, :] = q.T.astype(BF)
            return carry

        lax.fori_loop(0, 4, query_columns, 0)

    def lanes(parts):
        return jnp.concatenate(parts, 1)

    def split(wide):
        return [wide[:, k * 128 : (k + 1) * 128] for k in range(4)]

    def attend_four(n, carry):
        g = n // 2
        rows = [pl.ds(pl.multiple_of(n * 256 + k * HEAD, HEAD), HEAD) for k in range(4)]
        for k in range(4):
            qfeat[rows[k], :] = softmax_rows(tn(fq[c * 16 + n * 4 + k], qt[rows[k], :]))
        for p in range(2):
            cols = slice(p * 128, (p + 1) * 128)
            q = lanes([qt[r, cols] for r in rows])
            scores = split(nn(knat[g, cols, :], jnp.concatenate([q, q], 0)))
            stacks = []
            for k in range(4):
                sc = scores[k] * 0.125 + bias[p]
                peak = jnp.max(sc, 0, keepdims=True)
                w = jnp.exp(sc - peak).astype(BF)
                wts[(n * 4 + k) * 2 + p] = w
                dm = jnp.exp(-peak)
                damp[(n * 4 + k) * 2 + p, :1] = dm
                dq = (qfeat[rows[k], cols] * dm).astype(BF)
                stacks.append(
                    jnp.concatenate([w, jnp.where(low_lane, dq, zero_low), jnp.where(low_lane, zero_low, dq)], 0)
                )
            lhs = jnp.concatenate([vt[g, :AUG, cols], comb[g * 2 + p]], 1)
            both = split(nn(lhs, lanes(stacks)))
            for k in range(4):
                rden = 1.0 / both[k][HEAD : HEAD + 1]
                den[(n * 4 + k) * 2 + p, :1] = rden
                mixf[rows[k], cols] = both[k][:HEAD] * rden
        return carry

    def attend():
        lax.fori_loop(0, 4, attend_four, 0)


    def project():
        def mix_rows(n, carry):
            cols = pl.ds(pl.multiple_of(n * 256, 256), 256)
            mixn[:, cols] = mixf[cols, :].T.astype(BF)
            return carry

        lax.fori_loop(0, 4, mix_rows, 0)
        lowo[...] = nt(mixn[...], oac[...]).astype(BF)

        def out_columns(n, carry):
            cols = pl.ds(pl.multiple_of(n * 256, 256), 256)
            w = wa[n // 2, pl.ds(pl.multiple_of(lax.rem(n, 2) * 2, 2), 2), :, :, :, QKV:ATT].reshape(256, HALF)
            o = nt(mixn[...], w) + nn(lowo[...], ob2[:, cols])
            mine = jnp.where(c == 0, o[:ROWS], o[ROWS:])
            other = jnp.where(c == 0, o[ROWS:], o[:ROWS])
            mid[:, cols] = mine + tok2[c, :, cols].astype(F32)
            outs[:, cols] = other.astype(BF)
            return carry

        waiting["out"] = []
        for at in (0, 4):
            lax.fori_loop(at, at + 4, out_columns, 0)
            cols = pl.ds(at * 256, HALF)
            waiting["out"].append(copies.start(outs.at[:, cols], outr.at[:, cols], sibling))

    def middle():
        arrived("out")

        def middle_rows(i, carry):
            rows = pl.ds(i * 32, 32)
            m = mid[rows, :] + outr[rows, :].astype(F32)
            mid[rows, :] = m
            r = lax.rsqrt(jnp.mean(m * m, -1, keepdims=True) + EPSILON)
            ht[rows, :] = (m * r * gain2[...]).astype(BF)
            return carry

        lax.fori_loop(0, ROWS // 32, middle_rows, 0)

    def send_hidden():
        waiting["ht"] = share(ht, ht)

    def send_gradient():
        waiting["og"] = share(ogo, ogx)

    def arrived(name):
        for copy in waiting[name]:
            copy.wait_recv()

    def ff_cols(first, count):
        return wf[:, :, :, :, :, :, :, pl.ds(first, count)].reshape(WIDTH, count)

    def inner_gradient():
        gg[...] = nn(ogx[...], ff_cols(2 * SLICE, SLICE)).astype(BF)

    steps = {
        "low": lower,
        "kvc": keys,
        "pls": send_plane,
        "lns": send_line,
        "lnw": take_line,
        "qc": queries,
        "att": attend,
        "oproj": project,
        "mid": middle,
        "hts": send_hidden,
        "htw": lambda: arrived("ht"),
        "ogs": send_gradient,
        "ogw": lambda: arrived("og"),
        "ds": streams["d"].settle,
        "gs": streams["g"].settle,
        "us": streams["u"].settle,
        "ig": inner_gradient,
    }
    for name in PLAN:
        if "." in name:
            advance(name)
        else:
            steps[name]()
    copies.reuse()
    og_fly, ht_fly, out_copy = waiting["og"], waiting["ht"], waiting["out"]

    def activate(gate, up, cols):
        s = 0.5 * jnp.tanh(0.5 * gate) + 0.5
        swish = gate * s
        inner[:, cols] = (swish * up).astype(BF)
        d = gg[:, cols].astype(F32)
        gg[:, cols] = (d * up * s * (1.0 + gate * (1.0 - s))).astype(BF)
        ug[:, cols] = (d * swish).astype(BF)

    for n in range(5):
        cols = slice(n * 256, (n + 1) * 256)
        activate(nn(ht[...], ff_cols(n * 256, 256)), nn(ht[...], ff_cols(SLICE + n * 256, 256)), cols)
    both = nn(ht[...], jnp.concatenate([ff_cols(1280, 128), ff_cols(SLICE + 1280, 128)], 1))
    activate(both[:, :128], both[:, 128:], slice(1280, SLICE))

    def ff_rows(n, at):
        return wf[n // 2, lax.rem(n, 2), :, :, :, :, :, pl.ds(at, SLICE)].reshape(256, SLICE)

    copies.sent(ht_fly)
    copies.sent(og_fly)

    def two_columns(n, carry):
        cols = pl.ds(pl.multiple_of(n * 256, 256), 256)
        ogx[:, cols] = (nt(gg[...], ff_rows(n, 0)) + nt(ug[...], ff_rows(n, SLICE))).astype(BF)
        return carry

    def give_back(src, dst, cols):
        return [
            copies.start(src.at[pl.ds(at, n), cols], dst.at[k // 2 - (k > 5), pl.ds(r, n), cols], device({"x": (4 - i) % 4, "y": (4 - j) % 4}))
            for k, (i, j, r, n, at) in enumerate(SHARES)
        ]

    two_fly = []
    for at, end in ((0, 2), (2, 4), (4, 6), (6, 8)):
        lax.fori_loop(at, end, two_columns, 0)
        two_fly += give_back(ogx, rbt, pl.ds(at * 256, (end - at) * 256))

    def block_columns(n, carry):
        cols = pl.ds(pl.multiple_of(n * 256, 256), 256)
        ht[:, cols] = nt(inner[...], ff_rows(n, 2 * SLICE)).astype(BF)
        return carry

    lax.fori_loop(0, 4, block_columns, 0)
    blk_fly = give_back(ht, rbb, pl.ds(0, HALF))
    lax.fori_loop(4, 8, block_columns, 0)
    for copy in two_fly:
        copy.wait_recv()

    def middle_back(i, acc):
        rows = pl.ds(i * 16, 16)
        t = ogx[rows, :].astype(F32)
        for k in range(3):
            t += rbt[k, rows, :].astype(F32)
        m = mid[rows, :]
        r = lax.rsqrt(jnp.mean(m * m, -1, keepdims=True) + EPSILON)
        n = m * r
        acc += jnp.sum(t * n, 0, keepdims=True)
        t = t * gain2[...]
        g = ogo[rows, :].astype(F32) + r * (t - n * jnp.mean(t * n, -1, keepdims=True))
        mgrad[rows, :] = g
        bg[c, rows, :] = g.astype(BF)
        return acc

    gain_mlp = jnp.zeros((1, WIDTH), F32)
    bg_fly = []
    for at in (0, ROWS // 2):
        gain_mlp = lax.fori_loop(at // 16, at // 16 + ROWS // 32, middle_back, gain_mlp)
        part = bg.at[c, pl.ds(at, ROWS // 2)]
        bg_fly.append(copies.start(part, part, sibling))
    for copy in bg_fly:
        copy.wait_recv()
    bgv = bg.at[:, :, :]
    olg = nt(bgv[...].reshape(CHIP, WIDTH), ob2[...])
    olg_low = olg.astype(BF)

    def mixed_columns(n, carry):
        cols = pl.ds(pl.multiple_of(n * 256, 256), 256)
        wcols = pl.ds(pl.multiple_of(QKV + n * 256, 256), 256)
        m = nn(bg[...].reshape(CHIP, WIDTH), wa[:, :, :, :, :, wcols].reshape(WIDTH, 256))
        m += nn(olg_low, oac[:, cols])
        ngt[cols, :] = m.T.astype(BF)
        return carry

    lax.fori_loop(0, 4, mixed_columns, 0)
    for k in range(4):
        sig[k] = jnp.zeros((AUG, 128), F32)

    def states_four(n, carry):
        g = n // 2
        rows = [pl.ds(pl.multiple_of(n * 256 + k * HEAD, HEAD), HEAD) for k in range(4)]
        for p in range(2):
            cols = slice(p * 128, (p + 1) * 128)
            left, right = [], []
            for k in range(4):
                h = (n * 4 + k) * 2 + p
                rden = den[h, :1]
                m = ngt[rows[k], cols].astype(F32)
                ng = (m * rden).astype(BF)
                dg = -jnp.sum(m * mixf[rows[k], cols], 0, keepdims=True) * rden
                ngt[rows[k], cols] = ng
                dgr[h, :1] = dg
                dq = (qfeat[rows[k], cols] * damp[h, :1]).astype(BF)
                right.append(jnp.concatenate([jnp.where(low_lane, dq, zero_low), jnp.where(low_lane, zero_low, dq)], 0))
                tail = jnp.where(lax.broadcasted_iota(jnp.int32, (AUG - HEAD, 128), 0) == 0, dg, 0.0).astype(BF)
                left.append(jnp.concatenate([ng, tail], 0))
            sig[g * 2 + p] = sig[g * 2 + p] + nt(lanes(left), lanes(right))
        return carry

    lax.fori_loop(0, 4, states_four, 0)
    sg_states = []
    for p in range(2):
        a, b = sig[p], sig[2 + p]
        sg_states.append(jnp.where(low_lane, a, pltpu.roll(b, 64, 1)))
        sg_states.append(jnp.where(low_lane, pltpu.roll(a, 64, 1), b))
    for s in range(4):
        st[s] = sg_states[s]
    folded = sg_states[3]
    for s in (2, 1, 0):
        folded = sg_states[s] + gates[s + 1] * folded
    fly = gather_plane(1, folded)
    blk_fly += give_back(ht, rbb, pl.ds(HALF, HALF))

    for k in range(4):
        kacc[k] = jnp.zeros((HEAD, 128), F32)
        vacc[k] = jnp.zeros((HEAD, 128), F32)

    def back_four(n, carry):
        g = n // 2
        rows = [pl.ds(pl.multiple_of(n * 256 + k * HEAD, HEAD), HEAD) for k in range(4)]
        for p in range(2):
            cols = slice(p * 128, (p + 1) * 128)
            ngs = lanes([ngt[r, cols] for r in rows])
            dgs = [dgr[(n * 4 + k) * 2 + p, :1] for k in range(4)]
            dg = lanes(dgs)
            ws = lanes([wts[(n * 4 + k) * 2 + p] for k in range(4)])
            pt = nn(vnat[g, cols, :], jnp.concatenate([ngs, ngs], 0)) + dg
            sgr = (ws.astype(F32) * pt).astype(BF)
            tail = jnp.where(lax.broadcasted_iota(jnp.int32, (HEAD, 512), 0) == 0, dg, 0.0).astype(BF)
            both = split(nn(comb_t[g * 2 + p], jnp.concatenate([ngs, tail], 0)))
            for k in range(4):
                qg = jnp.where(low_lane, both[k][:HEAD], both[k][HEAD:]) * damp[(n * 4 + k) * 2 + p, :1]
                f = qfeat[rows[k], cols]
                qlg[rows[k], cols] = (f * (qg - jnp.sum(f * qg, 0, keepdims=True))).astype(BF)
            near = split(nn(kt[g, :, cols], sgr))
            for k in range(4):
                far = nn(fq[c * 16 + n * 4 + k], qlg[rows[k], cols])
                gt[rows[k], cols] = (near[k] * 0.125 + far).astype(BF)
            kacc[g * 2 + p] = kacc[g * 2 + p] + nt(lanes([qt[r, cols] for r in rows]), sgr)
            vacc[g * 2 + p] = vacc[g * 2 + p] + nt(ngs, ws)
        return carry

    lax.fori_loop(0, 4, back_four, 0)
    lowo_t = lowo[...].astype(F32).T.astype(BF)
    olg_t = olg.T.astype(BF)
    apart[24:32] = 2.0 * nn(lowo_t[:16], bg[...].reshape(CHIP, WIDTH))[:8]
    red[72:80, :HALF] = nn(olg_t[:16], mixn[...])[:8]


    def grad_rows(n, carry):
        rows = pl.ds(pl.multiple_of(n * 256, 256), 256)
        gnat[:, rows] = gt[rows, :].astype(F32).T.astype(BF)
        return carry

    lax.fori_loop(0, 4, grad_rows, 0)

    def feat_pairs(n, carry):
        rows = pl.ds(pl.multiple_of(n * 128, 128), 128)
        r = nt(qt[rows, :], qlg[rows, :])
        red[0:64, rows] = jnp.where(low_lane, r[:HEAD], r[HEAD:])
        return carry

    lax.fori_loop(0, 8, feat_pairs, 0)

    part, fly = fold_plane(1, fly)

    def one_queries(n, carry):
        w = wa[n // 2, pl.ds(pl.multiple_of(lax.rem(n, 2) * 2, 2), 2), :, :, :, 0:HALF].reshape(256, HALF)
        o = nt(gnat[:, :HALF], w)
        rows = pl.ds(pl.multiple_of(lax.rem(n, 4) * 256, 256), 256)

        @pl.when(n < 4)
        def _():
            qfeat[rows, :] = o

        @pl.when(n >= 4)
        def _():
            mixf[rows, :] = o

        return carry

    lax.fori_loop(0, 8, one_queries, 0)
    suffix = fold_line(1, part, fly)
    states = [None, None, None, suffix]
    for s in (2, 1, 0):
        states[s] = gates[s + 1] * (states[s + 1] + st[s + 1])
    put_states(states, 4)

    for g in range(2):
        f_rows = slice(g * HEAD, (g + 1) * HEAD)
        for p in range(2):
            k = g * 2 + p
            cols = slice(p * 128, (p + 1) * 128)
            f = kfeat[f_rows, cols]
            both = nn(comb_t[4 + k], vt[g, :, cols])
            fg = jnp.where(low_lane, both[:HEAD], both[HEAD:]) * valid[:, cols]
            kl = (f * (fg - jnp.sum(f * fg, 0, keepdims=True))).astype(BF)
            qlg[HALF + g * HEAD : HALF + (g + 1) * HEAD, cols] = kl
            gt[HALF + g * HEAD : HALF + (g + 1) * HEAD, cols] = (kacc[k] * 0.125 + nn(fk[c * 2 + g], kl)).astype(BF)
            fl = f.astype(BF)
            stack = jnp.concatenate([jnp.where(low_lane, fl, zero_low), jnp.where(low_lane, zero_low, fl)], 0)
            gt[HALF + NARROW + g * HEAD : HALF + NARROW + (g + 1) * HEAD, cols] = (
                vacc[k] + nn(comb[4 + k, :HEAD], stack)
            ).astype(BF)

    lowg_t = nn(ball[...], gt[...])
    lowg[...] = lowg_t.T.astype(BF)
    lowg_t = lowg_t.astype(BF)

    grad_rows(4, 0)

    def one_columns(n, had):
        cols = pl.ds(pl.multiple_of(n * 256, 256), 256)
        w = wa[n // 2, pl.ds(pl.multiple_of(lax.rem(n, 2) * 2, 2), 2), :, :, :, HALF:QKV].reshape(256, 2 * NARROW)
        o = had[pl.ds(pl.multiple_of(lax.rem(n, 4) * 256, 256), 256), :]
        o = o + nt(gnat[:, HALF:], w) + nn(lowg[...], aall[:, cols])
        normed = [tok2[side, :, cols].astype(F32) * r1[side, :, :1] for side in range(2)]
        gain = jnp.sum(o[:ROWS] * normed[0] + o[ROWS:] * normed[1], 0, keepdims=True)
        gsum[0, pl.ds(2 * n, 1), :] = gain[:, :128]
        gsum[0, pl.ds(2 * n + 1, 1), :] = gain[:, 128:]
        ones[:, cols] = jnp.where(c == 0, o[:ROWS], o[ROWS:])
        outs[:, cols] = jnp.where(c == 0, o[ROWS:], o[:ROWS]).astype(BF)

    def one_first(n, carry):
        one_columns(n, qfeat)
        return carry

    def one_second(n, carry):
        one_columns(n, mixf)
        return carry

    apart[0:24] = nn(lowg_t[:32], hid1[...])[:24]
    for k in range(16):
        gsum[1, k : k + 1, :] = gain_mlp[:, k * 128 : (k + 1) * 128]
    theirs = pl.ds(pl.multiple_of((1 - c) * HALF, HALF), HALF)
    mine = pl.ds(pl.multiple_of(c * HALF, HALF), HALF)
    a_copy = copies.start(apart.at[:, theirs], asib, sibling)
    copies.sent(out_copy)
    lax.fori_loop(0, 4, one_first, 0)
    lax.fori_loop(4, 8, one_second, 0)
    one_copy = copies.start(outs, outr, sibling)

    r = nt(kt[...].reshape(128, CHIP), qlg[HALF:, :])
    red[0:64, HALF : HALF + 128] = jnp.where(low_lane, r[:HEAD], r[HEAD:])

    low_t = low[...].astype(F32).T.astype(BF)
    up = 2.0 * nt(low_t[:32], gt[...])
    red[64:72, :HALF] = up[0:8, :HALF]
    red[64:72, HALF : HALF + NARROW] = up[8:16, HALF : HALF + NARROW]
    red[64:72, HALF + NARROW :] = up[16:24, HALF + NARROW :]

    def block(k, value):
        redb[k // 4, :, (k % 4) * 128 : (k % 4 + 1) * 128] = value.astype(BF)

    def feat_blocks(k, carry):
        rows = pl.ds(pl.multiple_of(k * 16, 16), 16)
        for j in range(8):
            redb[2 * k + j // 4, :, (j % 4) * 128 : (j % 4 + 1) * 128] = red[rows, j * 128 : (j + 1) * 128].astype(BF)
        redb[8, :, pl.ds(pl.multiple_of(k * 128, 128), 128)] = red[rows, HALF : HALF + 128].astype(BF)
        return carry

    lax.fori_loop(0, 4, feat_blocks, 0)
    for j in range(8):
        block(36 + j, red[64:80, j * 128 : (j + 1) * 128])
    block(44, jnp.concatenate([red[64:72, HALF : HALF + NARROW], red[64:72, HALF + NARROW :]], 0))
    a_copy.wait_recv()
    summed = apart[:, mine] + asib[...]
    for j in range(8):
        block(45 + j, summed[:16, j * 128 : (j + 1) * 128])
        block(53 + j, summed[16:, j * 128 : (j + 1) * 128])
    block(61, gsum[0])
    block(62, gsum[1])
    block(63, jnp.zeros((16, 128), F32))
    fly = []
    for i in range(4):
        for j in range(4):
            if i + j > 0:
                to = wrap(x + i) * 4 + wrap(y + j)
                fly.append(copies.start(redb.at[to], rr.at[plane], device({"x": i, "y": j})))
    rr[plane] = redb[plane]
    for copy in blk_fly:
        copy.wait_recv()

    def block_rows(i, carry):
        rows = pl.ds(i * 16, 16)
        t = mid[rows, :] + ht[rows, :].astype(F32)
        for k in range(3):
            t += rbb[k, rows, :].astype(F32)
        ht[rows, :] = t.astype(BF)
        return carry

    copies.sent(blk_fly)
    lax.fori_loop(0, ROWS // 16, block_rows, 0)
    here(ht.at[pl.ds(0, ROWS)], blk_out)
    for copy in fly:
        copy.wait_recv()
    total = rr[0].astype(F32)
    for k in range(1, 16):
        total += rr[k].astype(F32)
    rz[z] = total.astype(BF)
    line = [copies.start(rz.at[z], rz.at[z], device({"z": i})) for i in (1, 2, 3)]
    one_copy.wait_recv()
    copies.sent([one_copy])

    def token_rows(i, carry):
        rows = pl.ds(i * 16, 16)
        o = ones[rows, :] + outr[rows, :].astype(F32)
        t = tok2[c, rows, :].astype(F32)
        r = r1[c, rows, :1]
        n = t * r
        o = o * gain1[...]
        outs[rows, :] = (mgrad[rows, :] + r * (o - n * jnp.mean(o * n, -1, keepdims=True))).astype(BF)
        return carry

    lax.fori_loop(0, ROWS // 32, token_rows, 0)
    for copy in line:
        copy.wait_recv()
    total = sum((rz[k].astype(F32) for k in range(1, 4)), rz[0].astype(F32))
    fin[c, plane] = total.astype(BF)
    piece = fin.at[c, plane]
    fly = [
        copies.start(piece, piece, device({"x": i, "y": j})) for i in range(4) for j in range(4) if i + j > 0
    ]
    lax.fori_loop(ROWS // 32, ROWS // 16, token_rows, 0)
    here(outs, gtok_out)
    for copy in fly:
        copy.wait_recv()
    f_copy = copies.start(fin.at[c], fin.at[c], sibling)
    here(fin.at[c], red_out.at[c])
    f_copy.wait_recv()

    here(fin.at[1 - c], red_out.at[1 - c])
    for copy in local[-4:]:
        copy.wait()
    copies.drain()


def finish(
    blk, gtok, fin,
    blk_out, gtok_out, gain_a_out, qa_out, qb_out, ka_out, kb_out, va_out, vb_out, oa_out, ob_out, fq_out, fk_out,
    gain_b_out, sem,
):
    copies = [pltpu.make_async_copy(a, b, sem.at[k]) for k, (a, b) in enumerate(((blk, blk_out), (gtok, gtok_out)))]
    for copy in copies:
        copy.start()

    def block(side, k):
        return fin[side, k // 4, :, (k % 4) * 128 : (k % 4 + 1) * 128].astype(F32)

    for side in range(2):
        at = side * HALF
        for k in range(4):
            rows = slice(k * 16, (k + 1) * 16)
            for j in range(9):
                v = block(side, k * 8 + j if j < 8 else 32 + k)
                out, head = (fq_out, side * 16 + 2 * j) if j < 8 else (fk_out, side * 2)
                out[head, rows, :] = v[:, :64]
                out[head + 1, rows, :] = pltpu.roll(v, 64, 1)[:, :64]
        for j in range(8):
            cols = slice(at + j * 128, at + (j + 1) * 128)
            for k, over, under in ((36, qb_out, oa_out), (45, qa_out, ka_out), (53, va_out, ob_out)):
                v = block(side, k + j)
                over[:, cols] = v[:8]
                under[:, cols] = v[8:]
        v = block(side, 44)
        kb_out[:, side * NARROW : (side + 1) * NARROW] = v[:8]
        vb_out[:, side * NARROW : (side + 1) * NARROW] = v[8:]
    gain_a_out[...] = block(0, 61) + block(1, 61)
    gain_b_out[...] = block(0, 62) + block(1, 62)
    for copy in copies:
        copy.wait()


N_COPIES = 193
N_SENDS = 64


def scratch():
    v = pltpu.VMEM
    return [
        v((4, 4, 4, 2, 16, ATT), BF),
        v((4, 2, 2, 2, 2, 2, 16, 3 * SLICE), BF),
        v((2, 2, 16, 3 * SLICE), BF),
        v((2, ROWS, WIDTH), BF),
        v((ROWS, WIDTH), BF),
        v((8, WIDTH), F32),
        v((2, ROWS, 128), F32),
        v((128, WIDTH), BF),
        v((128, QKV), BF),
        v((128, HALF), BF),
        v((128, WIDTH), BF),
        v((4, 16, 128), F32),
        v((2, 8, 128), F32),
        v((2, 128, 128), F32),
        v((CHIP, WIDTH), BF),
        v((CHIP, 128), BF),
        v((HALF, CHIP), BF),
        v((2, HEAD, CHIP), BF),
        v((2, 128, CHIP), BF),
        v((2, CHIP, 128), BF),
        v((2, CHIP, 128), BF),
        v((128, CHIP), F32),
        v((4, AUG, 128), F32),
        v((8, AUG, 128), BF),
        v((8, 128, 128), BF),
        v((32, 128, 128), BF),
        v((HALF, CHIP), F32),
        v((HALF, CHIP), F32),
        v((32, 8, 128), F32),
        v((32, 8, 128), F32),
        v((CHIP, HALF), BF),
        v((CHIP, 128), BF),
        v((ROWS, WIDTH), BF),
        v((ROWS, WIDTH), BF),
        v((ROWS, WIDTH), F32),
        v((512, WIDTH), BF),
        v((512, WIDTH), BF),
        v((512, SLICE), BF),
        v((512, SLICE), BF),
        v((512, SLICE), BF),
        v((3, ROWS, WIDTH), BF),
        v((3, ROWS, WIDTH), BF),
        v((ROWS, WIDTH), F32),
        v((2, ROWS, WIDTH), BF),
        v((HALF, CHIP), BF),
        v((32, 8, 128), F32),
        v((4, AUG, 128), F32),
        v((HALF + 128, CHIP), BF),
        v((QKV, CHIP), BF),
        v((CHIP, QKV), BF),
        v((CHIP, 128), BF),
        v((ROWS, WIDTH), F32),
        v((4, HEAD, 128), F32),
        v((4, HEAD, 128), F32),
        v((2, AUG, 128), BF),
        v((2, 16, AUG, 128), BF),
        v((2, AUG, 128), BF),
        v((2, 3, AUG, 128), BF),
        v((80, QKV), F32),
        v((16, 16, PIECE), BF),
        v((16, 16, PIECE), BF),
        v((4, 16, PIECE), BF),
        v((2, 16, 16, PIECE), BF),
        v((32, WIDTH), F32),
        v((32, HALF), F32),
        v((2, 16, 128), F32),
        pltpu.SemaphoreType.DMA((N_SENDS,)),
        pltpu.SemaphoreType.DMA((N_COPIES,)),
        pltpu.SemaphoreType.DMA((19,)),
    ]


def body(
    tokens, sequence_lengths, attention_gain, query_weight, key_weight, value_weight, output_weight_flipped,
    query_adapter_down, query_adapter_up, key_adapter_down, key_adapter_up, value_adapter_down, value_adapter_up,
    output_adapter_down, output_adapter_up, query_feature_map, key_feature_map, feedforward_gain,
    gate_weight, up_weight, down_weight_flipped, output_gradient,
):
    vmem = pl.BlockSpec(memory_space=pltpu.VMEM)
    smem = pl.BlockSpec(memory_space=pltpu.SMEM)
    anywhere = pl.BlockSpec(memory_space=pl.ANY)

    def array(*shape, dtype=F32):
        return jax.ShapeDtypeStruct(shape, dtype)

    parts = pl.pallas_call(
        kernel,
        out_shape=(
            array(ROWS, WIDTH, dtype=BF), array(ROWS, WIDTH, dtype=BF), array(2, 16, 16, PIECE, dtype=BF),
        ),
        in_specs=[anywhere, smem, vmem] + [anywhere] * 4 + [vmem] * 11 + [anywhere] * 4,
        out_specs=(anywhere,) * 3,
        scratch_shapes=scratch(),
        compiler_params=pltpu.CompilerParams(
            collective_id=0, has_side_effects=True, vmem_limit_bytes=64 * 1024 * 1024
        ),
    )(
        tokens, sequence_lengths, attention_gain.reshape(16, 128),
        query_weight, key_weight, value_weight, output_weight_flipped,
        query_adapter_down.T, query_adapter_up, key_adapter_down.T, key_adapter_up, value_adapter_down.T,
        value_adapter_up, output_adapter_down.T, output_adapter_up, query_feature_map, key_feature_map,
        feedforward_gain.reshape(16, 128), gate_weight, up_weight, down_weight_flipped, output_gradient,
    )
    out = pl.pallas_call(
        finish,
        out_shape=(
            array(ROWS, WIDTH, dtype=BF), array(ROWS, WIDTH, dtype=BF), array(16, 128),
            array(RANK, WIDTH), array(RANK, WIDTH), array(RANK, WIDTH), array(RANK, 2 * NARROW),
            array(RANK, WIDTH), array(RANK, 2 * NARROW), array(RANK, WIDTH), array(RANK, WIDTH),
            array(QUERY_HEADS, HEAD, HEAD), array(KEY_VALUE_HEADS, HEAD, HEAD), array(16, 128),
        ),
        in_specs=[vmem] * 3,
        out_specs=(anywhere,) * 2 + (vmem,) * 12,
        scratch_shapes=[pltpu.SemaphoreType.DMA((2,))],
    )(*parts)
    (
        block_out, grad_tokens, gain_attn, qa, qb, ka, kb, va, vb, oa, ob, feat_q, feat_k, gain_mlp,
    ) = out
    return (
        block_out, grad_tokens, gain_attn.reshape(WIDTH), qa.T, qb, ka.T, kb, va.T, vb, oa.T, ob, feat_q, feat_k,
        gain_mlp.reshape(WIDTH),
    )


def solution(mesh):
    split, whole = P("seq", None), P()
    return jax.shard_map(
        body,
        mesh=mesh,
        in_specs=(
            (split, whole, whole) + (split,) * 4 + (whole,) * 11 + (split,) * 4
        ),
        out_specs=(split, split) + (whole,) * 12,
        check_vma=False,
    )
```

```python
import math

import jax
import jax.numpy as jnp
from jax import lax
from jax.experimental import pallas as pl
from jax.experimental.pallas import tpu as pltpu
from jax.sharding import PartitionSpec as P

QUERY_HEADS = 32
KEY_VALUE_HEADS = 4
HEAD = 64
STRETCH = 64
WIDTH = 2048
FF = 5632
ROWS = 128
CHIP = 256
HALF = 1024
NARROW = 128
QKV = HALF + 2 * NARROW
ATT = QKV + HALF
SLICE = FF // 4
AUG = 80
RANK = 8
EARLY_BLOCKS = 4
LATE_BLOCKS = 2
EPSILON = 1e-05
MESH = pl.DeviceIdType.MESH
F32 = jnp.float32
BF = jnp.bfloat16

SHARES = (
    (1, 0, 0, 64, 128),
    (3, 0, 64, 64, 192),
    (0, 1, 0, 64, 256),
    (0, 3, 64, 64, 320),
    (1, 1, 0, 32, 384),
    (1, 3, 32, 32, 416),
    (3, 1, 64, 32, 448),
    (3, 3, 96, 32, 480),
)


def nn(left, right):
    return jnp.dot(left, right, preferred_element_type=F32)


def tn(left, right):
    return lax.dot_general(left, right, (((0,), (0,)), ((), ())), preferred_element_type=F32)


def nt(left, right):
    return lax.dot_general(left, right, (((1,), (1,)), ((), ())), preferred_element_type=F32)


def wrap(value):
    return lax.rem(value, 4)


class Copy:
    def __init__(self, copy, index):
        self.copy, self.index, self.landed = copy, index, False
        self.wait_send = copy.wait_send

    def wait_recv(self):
        self.copy.wait_recv()
        self.landed = True


class Copies:
    def __init__(self, send, recv):
        self.send, self.recv, self.count, self.open = send, recv, 0, {}
        self.all, self.heard, self.free, self.indices = [], [], [], 0

    def start(self, src, dst, device):
        slot = self.count % N_SENDS
        if slot in self.open:
            self.open.pop(slot).wait_send()
        if self.free:
            index = self.free.pop()
        else:
            index = self.indices
            self.indices += 1
        copy = pltpu.make_async_remote_copy(
            src_ref=src,
            dst_ref=dst,
            send_sem=self.send.at[slot],
            recv_sem=self.recv.at[index],
            device_id=(device,),
            device_id_type=MESH,
        )
        self.count += 1
        copy.start()
        copy = Copy(copy, index)
        self.open[slot] = copy
        self.all.append(copy)
        return copy

    def note(self):
        last = {copy.index: copy for copy in self.all}
        self.heard = [index for index, copy in last.items() if copy.landed]

    def reuse(self):
        self.free = self.heard

    def sent(self, copies):
        for slot in [k for k, copy in self.open.items() if any(copy is other for other in copies)]:
            self.open.pop(slot).wait_send()

    def drain(self):
        for copy in self.open.values():
            copy.wait_send()


class Heads:
    def __init__(self, copies, wa, where, device, settled, parts):
        self.copies, self.wa, self.where, self.device = copies, wa, where, device
        self.settled, self.parts = settled, parts
        self.flying = {}

    def block(self, order, phase, at, cols, core=slice(None)):
        index = []
        for axis in "zxy":
            k = order.index(axis)
            index.append(slice(None) if k < phase else at if k == phase else self.where[axis])
        return self.wa.at[index[0], index[1], index[2], core, :, cols]

    def begin(self, phase):
        c = self.where["c"]
        for part, (order, src, at, first, count) in enumerate(self.parts):
            axis = order[phase]
            cols = pl.ds(first, count)
            fly = []
            if phase == 0:
                for step in (1, 3, 2):
                    for cross in (0, 1):
                        core = 1 - c if cross else c
                        piece = src.at[:, pl.ds(pl.multiple_of(core * (src.shape[1] // 2) + at, 128), count)]
                        dst = self.wa.at[self.where["z"], self.where["x"], self.where["y"], c, :, cols]
                        fly.append(self.copies.start(piece, dst, self.device({axis: step}, cross)))
            else:
                own = self.block(order, phase, self.where[axis], cols)
                fly = [self.copies.start(own, own, self.device({axis: step})) for step in (1, 3)]
            self.flying[phase, part] = fly

    def middle(self, phase):
        for part, (order, src, at, first, count) in enumerate(self.parts):
            axis = order[phase]
            for copy in self.flying[phase, part]:
                copy.wait_recv()
            here = self.where[axis]
            left = self.block(order, phase, wrap(here + 3), pl.ds(first, count), 0)
            right = self.block(order, phase, wrap(here + 1), pl.ds(first, count), 1)
            self.flying[phase, part] = [
                self.copies.start(left, left, self.device({axis: 1})),
                self.copies.start(right, right, self.device({axis: 3})),
            ]

    def end(self, phase):
        self.settled()
        for part in range(len(self.parts)):
            for copy in self.flying[phase, part]:
                copy.wait_recv()


class Units:
    def __init__(self, copies, here, wf, stage, where, device, sibling, parts):
        self.copies, self.here, self.wf, self.stage = copies, here, wf, stage
        self.where, self.device, self.sibling, self.parts = where, device, sibling, parts
        self.flying, self.handed, self.own = {}, [], []

    def rows(self, order, along, across, cols):
        w = self.where
        a = (slice(None), slice(None)) if along is None else (along // 2, lax.rem(along, 2))
        b = (across // 2, lax.rem(across, 2))
        x, y = (a, b) if order == "xy" else (b, a)
        return self.wf.at[w["z"], x[0], x[1], y[0], y[1], w["c"], :, cols]

    def line(self, z, cols):
        return self.wf.at[z, :, :, :, :, self.where["c"], :, cols]

    def hand_on(self, block):
        self.handed.append(self.copies.start(block, block, self.sibling))

    def begin(self, phase):
        w = self.where
        for part, (order, src, at, first, count) in enumerate(self.parts):
            cols = pl.ds(first, count)
            a, b = order
            fly = []
            if phase == 0:
                for d in (1, 3, 2, 0):
                    for e in (0, 1):
                        pa, pb = lax.rem(w[a] + d, 2), lax.rem(w[b] + e, 2)
                        slot = pa * 2 + pb if order == "xy" else pb * 2 + pa
                        piece = src.at[:, pl.ds(pl.multiple_of(slot * SLICE + at, 128), count)]
                        if e == 0:
                            dst = self.rows(order, w[a], w[b], cols)
                        else:
                            dst = self.stage.at[w[a] // 2, lax.rem(w[a], 2), :, cols]
                        if d == 0:
                            self.own.append(self.here(piece, dst))
                        else:
                            fly.append(self.copies.start(piece, dst, self.device({a: d})))
            elif phase == 1:
                mine = self.rows(order, None, w[b], cols)
                other = self.stage.at[:, :, :, cols]
                fly = [
                    self.copies.start(other, mine, self.device({b: 1})),
                    self.copies.start(other, mine, self.device({b: 3})),
                    self.copies.start(mine, mine, self.device({b: 2})),
                ]
            else:
                block = self.line(w["z"], cols)
                self.hand_on(block)
                fly = [self.copies.start(block, block, self.device({"z": step})) for step in (1, 3)]
            self.flying[phase, part] = fly

    def middle(self, phase):
        z = self.where["z"]
        for part, (order, src, at, first, count) in enumerate(self.parts):
            for copy in self.flying[phase, part]:
                copy.wait_recv()
            one = (count // 256) * 128
            before, after = wrap(z + 3), wrap(z + 1)
            left = self.line(before, pl.ds(first, one))
            right = self.line(after, pl.ds(first + one, count - one))
            self.flying[phase, part] = [
                self.copies.start(left, left, self.device({"z": 1})),
                self.copies.start(right, right, self.device({"z": 3})),
            ]
            self.hand_on(self.line(before, pl.ds(first, count)))
            self.hand_on(self.line(after, pl.ds(first, count)))

    def end(self, phase):
        if phase == 0:
            for copy in self.own:
                copy.wait()
        for part, (order, src, at, first, count) in enumerate(self.parts):
            for copy in self.flying[phase, part]:
                copy.wait_recv()
            if phase == 2:
                self.hand_on(self.line(wrap(self.where["z"] + 2), pl.ds(first, count)))

    def settle(self):
        for copy in self.handed:
            copy.wait_recv()


class Sums:
    def __init__(self, copies, device, at, sibling, buffers, share):
        self.copies, self.device, self.sibling, self.share = copies, device, sibling, share
        self.x, self.y, self.z, self.c = at
        self.plane = self.x * 4 + self.y
        self.own, self.got, self.line, self.all = buffers

    def put(self, k, value):
        self.own[k // self.share, :, (k % self.share) * 128 : (k % self.share + 1) * 128] = value.astype(BF)

    def round(self, send):
        return [send(i, j) for i in range(4) for j in range(4) if i + j > 0]

    def scatter(self):
        def send(i, j):
            to = wrap(self.x + i) * 4 + wrap(self.y + j)
            return self.copies.start(self.own.at[to], self.got.at[self.plane], self.device({"x": i, "y": j}))

        self.fly = self.round(send)
        self.got[self.plane] = self.own[self.plane]

    def along(self):
        for copy in self.fly:
            copy.wait_recv()
        total = self.got[0].astype(F32)
        for k in range(1, 16):
            total += self.got[k].astype(F32)
        self.line[self.z] = total.astype(BF)
        mine = self.line.at[self.z]
        self.fly = [self.copies.start(mine, mine, self.device({"z": i})) for i in (1, 2, 3)]

    def gather(self):
        for copy in self.fly:
            copy.wait_recv()
        total = self.line[0].astype(F32)
        for k in range(1, 4):
            total += self.line[k].astype(F32)
        self.all[self.c, self.plane] = total.astype(BF)
        piece = self.all.at[self.c, self.plane]
        self.fly = self.round(lambda i, j: self.copies.start(piece, piece, self.device({"x": i, "y": j})))

    def cross(self):
        for copy in self.fly:
            copy.wait_recv()
        half = self.all.at[self.c]
        self.fly = [self.copies.start(half, half, self.sibling)]

    def finish(self):
        self.fly[0].wait_recv()


EARLY = ("kv.b0", "q.b0", "o.b0", "d.b0", "kv.e0", "u.b0", "g.b0", "kv.b1",)
PLAN = (
    "o.e0", "q.e0", "q.b1", "d.e0", "kv.m1", "d.b1", "o.b1", "q.m1", "kv.e1", "g.e0", "u.e0", "kv.b2",
    "d.e1", "d.b2", "q.e1", "o.m1", "g.b1", "u.b1", "kv.m2", "q.b2", "g.e1", "g.b2", "o.e1", "kv.e2",
    "low", "d.m2", "u.e1", "kvc", "pls", "o.b2", "lns", "q.m2", "u.b2", "o.m2", "g.m2", "d.e2",
    "lnw", "q.e2", "qc", "ogs", "att", "o.e2", "oproj", "mid", "u.m2", "hts", "g.e2", "ogw",
    "ds", "ig", "u.e2", "gs", "us", "htw",
)


def kernel(
    tok, lens, gain_a, qw, kw, vw, ow, qa, qb, ka, kb, va, vb, oa, ob, maps, fk, gain_b, gw, uw, dw, og,
    blk_out, gtok_out, early_out, late_out, gain_out,
    wa, wf, stage, tok2, fq, ogo, gains, r1, aall, ball, oac, ob2, masks, far_masks, bias, hid1, low, qt, kt, vt, knat, vnat,
    kfeat, st, comb, comb_t, wts, qfeat, mixf, damp, den, mixn, lowo, outs, outr, mid, ht, ogx, gg, inner, ug, rbt, rbb,
    mgrad, bg, ngt, dgr, sig, qlg, gt, gnat, lowg, ones, kacc, vacc, fsend, frecv, hsend, hrecv,
    e_own, e_got, e_line, e_all, l_own, l_got, l_line, l_all, gsum, gplane, gline, gain_all, send, recv, loc,
):
    me = lax.axis_index("seq")
    c = lax.rem(me, 2)
    y = lax.rem(me // 2, 4)
    x = lax.rem(me // 8, 4)
    z = me // 32

    def device(steps, cross=0):
        zz, xx, yy = (wrap(v + steps.get(n, 0)) for n, v in (("z", z), ("x", x), ("y", y)))
        return ((zz * 4 + xx) * 4 + yy) * 2 + (1 - c if cross else c)

    sibling = me + 1 - 2 * c
    plane = x * 4 + y
    xl, yl = lax.rem(x, 2), lax.rem(y, 2)
    xh, yh = x // 2, y // 2

    barrier = pltpu.get_barrier_semaphore()
    peers = [sibling]
    peers += [device({"x": i, "y": j}) for i in range(4) for j in range(4) if i + j > 0]
    peers += [device({"z": i}) for i in (1, 2, 3)]
    peers += [device({axis: i}, 1) for axis in "xyz" for i in (1, 2, 3)]
    for peer in peers:
        pl.semaphore_signal(barrier, inc=1, device_id=(peer,), device_id_type=MESH)
    copies = Copies(send, recv)
    local = []

    def here(src, dst):
        copy = pltpu.make_async_copy(src, dst, loc.at[len(local)])
        copy.start()
        local.append(copy)
        return copy

    own = wa.at[z, x, y, c]
    pieces = ((kw, HALF, NARROW), (vw, HALF + NARROW, NARROW), (qw, 0, HALF), (ow, QKV, HALF))
    for src, at, count in pieces:
        mine = src.at[:, pl.ds(pl.multiple_of(c * count, count), count)]
        here(mine, own.at[:, pl.ds(at, count)])
    here(tok, tok2.at[c])
    here(maps.at[pl.ds(c * 16, 16)], fq)
    here(og, ogx.at[pl.ds(0, ROWS)])
    here(og, ogo)

    pl.semaphore_wait(barrier, len(peers))
    first = []
    for src, at, count in pieces:
        other = src.at[:, pl.ds(pl.multiple_of((1 - c) * count, count), count)]
        first.append(copies.start(other, own.at[:, pl.ds(at, count)], sibling))
    tok_copy = copies.start(tok, tok2.at[c], sibling)
    where = {"z": z, "x": x, "y": y, "c": c}
    pending = [local[:4] + first]

    def settled():
        if pending:
            done = pending.pop()
            for copy in done[:4]:
                copy.wait()
            for copy in done[4:]:
                copy.wait_recv()

    streams = {
        "kv": Heads(copies, wa, where, device, settled, (("xzy", kw, 0, HALF, NARROW), ("yzx", vw, 0, HALF + NARROW, NARROW))),
        "q": Heads(copies, wa, where, device, settled, (("xzy", qw, 0, 0, 512), ("yzx", qw, 512, 0 + 512, 512))),
        "o": Heads(copies, wa, where, device, settled, (("zxy", ow, 0, QKV, 512), ("zyx", ow, 512, QKV + 512, 512))),
        "d": Units(
            copies, here, wf, stage, where, device, sibling,
            (("xy", dw, 0, 2 * SLICE, 768), ("yx", dw, 768, 2 * SLICE + 768, 640)),
        ),
        "g": Units(copies, here, wf, stage, where, device, sibling, (("xy", gw, 0, 0, SLICE),)),
        "u": Units(copies, here, wf, stage, where, device, sibling, (("yx", uw, 0, SLICE, SLICE),)),
    }
    waiting = {}

    def advance(name):
        stream, step = name.split(".")
        stream = streams[stream]
        {"b": stream.begin, "m": stream.middle, "e": stream.end}[step[0]](int(step[1]))

    for name in EARLY:
        advance(name)

    for k, src in enumerate((gain_a, gain_b)):
        g = src[...].astype(F32)
        gains[k : k + 1, :] = jnp.concatenate([g[i : i + 1] for i in range(16)], 1)
    gain1, gain2 = gains.at[pl.ds(0, 1)], gains.at[pl.ds(1, 1)]

    def below(parts, rows, count):
        got = [part.astype(F32) for part in parts]
        used = RANK * len(parts)
        return jnp.concatenate(got + [jnp.zeros((rows - used, count), F32)], 0).astype(BF)

    aall[...] = below([qa[...], ka[...], va[...]], 128, WIDTH)
    half = pl.ds(pl.multiple_of(c * HALF, HALF), HALF)
    narrow = pl.ds(pl.multiple_of(c * NARROW, NARROW), NARROW)
    none = jnp.zeros((RANK, NARROW), F32)
    ball[:, :HALF] = below([2.0 * qb[:, half].astype(F32)], 128, HALF)
    ball[:, HALF : HALF + NARROW] = below([none, 2.0 * kb[:, narrow].astype(F32)], 128, NARROW)
    ball[:, HALF + NARROW :] = below([none, none, 2.0 * vb[:, narrow].astype(F32)], 128, NARROW)
    oac[...] = below([oa[:, half]], 128, HALF)
    ob2[...] = below([2.0 * ob[...].astype(F32)], 128, WIDTH)

    chip = me // 2
    starts, ends, total = [], [], jnp.int32(0)
    for k in range(8):
        starts.append(total)
        total = total + ((lens[k] + (STRETCH - 1)) >> 6)
        ends.append(total)

    def sequence(stretch):
        found = jnp.where(stretch >= ends[0], 1, 0)
        for k in range(1, 7):
            found = found + jnp.where(stretch >= ends[k], 1, 0)
        return found

    counts, gates = [], []
    for s in range(4):
        stretch = chip * 4 + s
        begin, length = starts[0], lens[0]
        for k in range(1, 8):
            inside = stretch >= starts[k]
            begin = jnp.where(inside, starts[k], begin)
            length = jnp.where(inside, lens[k], length)
        counts.append(length - (stretch - begin) * STRETCH)
        gates.append(jnp.where(stretch != begin, 1.0, 0.0))
    first_own, last_own = sequence(chip * 4), sequence(chip * 4 + 3)
    k16 = lax.broadcasted_iota(jnp.int32, (16, 128), 0)
    firsts = sequence((z * 16 + k16) * 4)
    lasts = sequence((z * 16 + k16) * 4 + 3)
    masks[0] = jnp.where((k16 < plane) & (lasts == first_own), 1.0, 0.0)
    masks[1] = jnp.where(lasts == sequence(z * 64 + 63), 1.0, 0.0)
    masks[2] = jnp.where((k16 > plane) & (firsts == last_own), 1.0, 0.0)
    masks[3] = jnp.where(firsts == sequence(z * 64), 1.0, 0.0)
    k8 = lax.broadcasted_iota(jnp.int32, (8, 128), 0)
    far_masks[0] = jnp.where((k8 < z) & (sequence(k8 * 64 + 63) == first_own), 1.0, 0.0)
    far_masks[1] = jnp.where((k8 > z) & (sequence(k8 * 64) == last_own), 1.0, 0.0)
    lane = lax.broadcasted_iota(jnp.int32, (1, 128), 1)
    low_lane = lane < 64
    in_stretch = lax.rem(lane, STRETCH)
    valid = jnp.concatenate(
        [jnp.where(in_stretch < jnp.where(low_lane, counts[2 * p], counts[2 * p + 1]), 1.0, 0.0) for p in range(2)], 1
    )
    iu = lax.broadcasted_iota(jnp.int32, (128, 128), 0)
    it = lax.broadcasted_iota(jnp.int32, (128, 128), 1)
    for p in range(2):
        room = jnp.where(iu < 64, counts[2 * p], counts[2 * p + 1])
        seen = (iu <= it) & ((iu < 64) == (it < 64)) & (lax.rem(iu, STRETCH) < room)
        bias[p] = jnp.where(seen, 0.0, -1e30)

    for copy in local[4:8]:
        copy.wait()
    tok_copy.wait_recv()

    def norm_rows(i, carry):
        rows = pl.ds(i * 32, 32)
        for side in range(2):
            t = tok2[side, rows, :].astype(F32)
            r = lax.rsqrt(jnp.mean(t * t, -1, keepdims=True) + EPSILON)
            r1[side, rows, :] = jnp.broadcast_to(r, (32, 128))
            hid1[pl.ds(side * ROWS + i * 32, 32), :] = (t * r * gain1[...]).astype(BF)
        return carry

    lax.fori_loop(0, ROWS // 32, norm_rows, 0)

    zero_low = jnp.zeros((), BF)

    def softmax_rows(logits):
        e = jnp.exp(logits - jnp.max(logits, 0, keepdims=True))
        return e / jnp.sum(e, 0, keepdims=True)

    def gather_plane(base, folded):
        fsend[base] = folded.astype(BF)
        fly = []
        for i in range(4):
            for j in range(4):
                if i + j > 0:
                    fly.append(copies.start(fsend.at[base], frecv.at[base, plane], device({"x": i, "y": j})))
        frecv[base, plane] = folded.astype(BF)
        return fly

    def fold_plane(base, fly):
        for copy in fly:
            copy.wait_recv()
        part = jnp.zeros((AUG, 128), F32)
        whole = jnp.zeros((AUG, 128), F32)
        for k in range(16):
            f = frecv[base, k].astype(F32)
            part += masks[2 * base, k : k + 1, :] * f
            whole += masks[2 * base + 1, k : k + 1, :] * f
        hsend[base] = whole.astype(BF)
        fly = [copies.start(hsend.at[base], hrecv.at[base, i - 1], device({"z": i})) for i in (1, 2, 3)]
        return part, fly

    def fold_line(base, part, fly):
        for i, copy in zip((1, 2, 3), fly):
            copy.wait_recv()
            part += far_masks[base, pl.ds(wrap(z + 4 - i), 1), :] * hrecv[base, i - 1].astype(F32)
        return part

    def combine(states):
        for g in range(2):
            for p in range(2):
                one, two = states[2 * p], states[2 * p + 1]
                if g == 0:
                    both = jnp.where(low_lane, one, pltpu.roll(two, 64, 1))
                else:
                    both = jnp.where(low_lane, pltpu.roll(one, 64, 1), two)
                yield g * 2 + p, both

    def put_states(states, base):
        for k, both in combine(states):
            comb[base + k] = both.astype(BF)
            tall = jnp.concatenate([both, jnp.zeros((128 - AUG, 128), F32)], 0)
            comb_t[base + k] = tall.T.astype(BF)

    def share(src, dst):
        return [
            copies.start(src.at[pl.ds(r, n)], dst.at[pl.ds(at, n)], device({"x": i, "y": j}))
            for i, j, r, n, at in SHARES
        ]

    def lower():
        low[...] = nt(hid1[...], aall[...]).astype(BF)

    def keys():
        kv = nn(hid1[...], wa[:, :, :, :, :, HALF:QKV].reshape(WIDTH, 2 * NARROW))
        kv = (kv + nn(low[...], ball[:, HALF:QKV])).astype(BF)
        kv_t = kv.astype(F32).T.astype(BF)
        for g in range(2):
            keep = low_lane if g == 0 else ~low_lane
            knat[g] = jnp.where(keep, kv[:, :NARROW], jnp.zeros((), BF))
            vnat[g] = jnp.where(keep, kv[:, NARROW:], jnp.zeros((), BF))
            kt[g] = kv_t[g * HEAD : (g + 1) * HEAD]
            tail = lax.broadcasted_iota(jnp.int32, (64, CHIP), 0) == 0
            vt[g, :HEAD] = kv_t[NARROW + g * HEAD : NARROW + (g + 1) * HEAD]
            vt[g, HEAD:] = tail.astype(F32).astype(BF)
        lanes4 = lax.broadcasted_iota(jnp.int32, (1, CHIP), 1) // STRETCH

        for g in range(2):
            kfeat[g * HEAD : (g + 1) * HEAD] = softmax_rows(tn(fk[c * 2 + g], kt[g])) * valid
        kf = kfeat[...]
        kf_high = kf.astype(BF)
        kf_rest = (kf - kf_high.astype(F32)).astype(BF)
        for s in range(4):
            got = []
            for g in range(2):
                va = jnp.where(lanes4 == s, vt[g, :AUG], jnp.zeros((), BF))
                got.append(nt(va, kf_high) + nt(va, kf_rest))
            st[s] = jnp.where(low_lane, got[0], got[1])


    def send_plane():
        folded = st[0]
        for s in (1, 2, 3):
            folded = st[s] + gates[s] * folded
        copies.note()
        waiting["plane"] = gather_plane(0, folded)

    def send_line():
        waiting["part"], waiting["line"] = fold_plane(0, waiting["plane"])

    def take_line():
        prefix = fold_line(0, waiting["part"], waiting["line"])
        states = [prefix]
        for s in (1, 2, 3):
            states.append(gates[s] * (states[s - 1] + st[s - 1]))
        put_states(states, 0)

    def queries():
        def query_columns(n, carry):
            cols = pl.ds(pl.multiple_of(n * 256, 256), 256)
            q = nn(hid1[...], wa[:, :, :, :, :, cols].reshape(WIDTH, 256)) + nn(low[...], ball[:, cols])
            qt[cols, :] = q.T.astype(BF)
            return carry

        lax.fori_loop(0, 4, query_columns, 0)

    def lanes(parts):
        return jnp.concatenate(parts, 1)

    def split(wide):
        return [wide[:, k * 128 : (k + 1) * 128] for k in range(4)]

    def attend_four(n, carry):
        g = n // 2
        rows = [pl.ds(pl.multiple_of(n * 256 + k * HEAD, HEAD), HEAD) for k in range(4)]
        for k in range(4):
            qfeat[rows[k], :] = softmax_rows(tn(fq[n * 4 + k], qt[rows[k], :]))
        for p in range(2):
            cols = slice(p * 128, (p + 1) * 128)
            q = lanes([qt[r, cols] for r in rows])
            scores = split(nn(knat[g, cols, :], jnp.concatenate([q, q], 0)))
            stacks = []
            for k in range(4):
                sc = scores[k] * 0.125 + bias[p]
                peak = jnp.max(sc, 0, keepdims=True)
                w = jnp.exp(sc - peak).astype(BF)
                wts[(n * 4 + k) * 2 + p] = w
                dm = jnp.exp(-peak)
                damp[(n * 4 + k) * 2 + p, :1] = dm
                dq = (qfeat[rows[k], cols] * dm).astype(BF)
                stacks.append(
                    jnp.concatenate([w, jnp.where(low_lane, dq, zero_low), jnp.where(low_lane, zero_low, dq)], 0)
                )
            lhs = jnp.concatenate([vt[g, :AUG, cols], comb[g * 2 + p]], 1)
            both = split(nn(lhs, lanes(stacks)))
            for k in range(4):
                rden = 1.0 / both[k][HEAD : HEAD + 1]
                den[(n * 4 + k) * 2 + p, :1] = rden
                mixf[rows[k], cols] = both[k][:HEAD] * rden
        return carry

    def attend():
        lax.fori_loop(0, 4, attend_four, 0)


    def project():
        def mix_rows(n, carry):
            cols = pl.ds(pl.multiple_of(n * 256, 256), 256)
            mixn[:, cols] = mixf[cols, :].T.astype(BF)
            return carry

        lax.fori_loop(0, 4, mix_rows, 0)
        lowo[...] = nt(mixn[...], oac[...]).astype(BF)

        def out_columns(n, carry):
            cols = pl.ds(pl.multiple_of(n * 256, 256), 256)
            w = wa[n // 2, pl.ds(pl.multiple_of(lax.rem(n, 2) * 2, 2), 2), :, :, :, QKV:ATT].reshape(256, HALF)
            o = nt(mixn[...], w) + nn(lowo[...], ob2[:, cols])
            mine = jnp.where(c == 0, o[:ROWS], o[ROWS:])
            other = jnp.where(c == 0, o[ROWS:], o[:ROWS])
            mid[:, cols] = mine + tok2[c, :, cols].astype(F32)
            outs[:, cols] = other.astype(BF)
            return carry

        waiting["out"] = []
        for at in (0, 4):
            lax.fori_loop(at, at + 4, out_columns, 0)
            cols = pl.ds(at * 256, HALF)
            waiting["out"].append(copies.start(outs.at[:, cols], outr.at[:, cols], sibling))

    def middle():
        arrived("out")

        def middle_rows(i, carry):
            rows = pl.ds(i * 32, 32)
            m = mid[rows, :] + outr[rows, :].astype(F32)
            mid[rows, :] = m
            r = lax.rsqrt(jnp.mean(m * m, -1, keepdims=True) + EPSILON)
            ht[rows, :] = (m * r * gain2[...]).astype(BF)
            return carry

        lax.fori_loop(0, ROWS // 32, middle_rows, 0)

    def send_hidden():
        waiting["ht"] = share(ht, ht)

    def send_gradient():
        waiting["og"] = share(ogo, ogx)

    def arrived(name):
        for copy in waiting[name]:
            copy.wait_recv()

    def ff_cols(first, count):
        return wf[:, :, :, :, :, :, :, pl.ds(first, count)].reshape(WIDTH, count)

    def inner_gradient():
        gg[...] = nn(ogx[...], ff_cols(2 * SLICE, SLICE)).astype(BF)

    steps = {
        "low": lower,
        "kvc": keys,
        "pls": send_plane,
        "lns": send_line,
        "lnw": take_line,
        "qc": queries,
        "att": attend,
        "oproj": project,
        "mid": middle,
        "hts": send_hidden,
        "htw": lambda: arrived("ht"),
        "ogs": send_gradient,
        "ogw": lambda: arrived("og"),
        "ds": streams["d"].settle,
        "gs": streams["g"].settle,
        "us": streams["u"].settle,
        "ig": inner_gradient,
    }
    for name in PLAN:
        if "." in name:
            advance(name)
        else:
            steps[name]()
    copies.reuse()
    og_fly, ht_fly, out_copy = waiting["og"], waiting["ht"], waiting["out"]

    def activate(gate, up, cols):
        s = 0.5 * jnp.tanh(0.5 * gate) + 0.5
        swish = gate * s
        inner[:, cols] = (swish * up).astype(BF)
        d = gg[:, cols].astype(F32)
        gg[:, cols] = (d * up * s * (1.0 + gate * (1.0 - s))).astype(BF)
        ug[:, cols] = (d * swish).astype(BF)

    for at, count in ((0, 512), (512, 512), (1024, 256)):
        cols = slice(at, at + count)
        activate(nn(ht[...], ff_cols(at, count)), nn(ht[...], ff_cols(SLICE + at, count)), cols)
    both = nn(ht[...], jnp.concatenate([ff_cols(1280, 128), ff_cols(SLICE + 1280, 128)], 1))
    activate(both[:, :128], both[:, 128:], slice(1280, SLICE))

    def ff_rows(n, at):
        return wf[n // 2, lax.rem(n, 2), :, :, :, :, :, pl.ds(at, SLICE)].reshape(256, SLICE)

    copies.sent(ht_fly)
    copies.sent(og_fly)

    def two_columns(n, carry):
        cols = pl.ds(pl.multiple_of(n * 256, 256), 256)
        ogx[:, cols] = (nt(gg[...], ff_rows(n, 0)) + nt(ug[...], ff_rows(n, SLICE))).astype(BF)
        return carry

    def give_back(src, dst, cols):
        return [
            copies.start(src.at[pl.ds(at, n), cols], dst.at[k // 2 - (k > 5), pl.ds(r, n), cols], device({"x": (4 - i) % 4, "y": (4 - j) % 4}))
            for k, (i, j, r, n, at) in enumerate(SHARES)
        ]

    two_fly = []
    for at, end in ((0, 2), (2, 4), (4, 6), (6, 8)):
        lax.fori_loop(at, end, two_columns, 0)
        two_fly += give_back(ogx, rbt, pl.ds(at * 256, (end - at) * 256))

    def block_columns(n, carry):
        cols = pl.ds(pl.multiple_of(n * 256, 256), 256)
        ht[:, cols] = nt(inner[...], ff_rows(n, 2 * SLICE)).astype(BF)
        return carry

    lax.fori_loop(0, 6, block_columns, 0)
    blk_fly = give_back(ht, rbb, pl.ds(0, 1536))
    lax.fori_loop(6, 8, block_columns, 0)
    for copy in two_fly:
        copy.wait_recv()

    def middle_back(i, acc):
        rows = pl.ds(i * 16, 16)
        t = ogx[rows, :].astype(F32)
        for k in range(3):
            t += rbt[k, rows, :].astype(F32)
        m = mid[rows, :]
        r = lax.rsqrt(jnp.mean(m * m, -1, keepdims=True) + EPSILON)
        n = m * r
        acc += jnp.sum(t * n, 0, keepdims=True)
        t = t * gain2[...]
        g = ogo[rows, :].astype(F32) + r * (t - n * jnp.mean(t * n, -1, keepdims=True))
        mgrad[rows, :] = g
        bg[c, rows, :] = g.astype(BF)
        return acc

    gain_mlp = jnp.zeros((1, WIDTH), F32)
    bg_fly = []
    for at in (0, ROWS // 2):
        gain_mlp = lax.fori_loop(at // 16, at // 16 + ROWS // 32, middle_back, gain_mlp)
        part = bg.at[c, pl.ds(at, ROWS // 2)]
        bg_fly.append(copies.start(part, part, sibling))
    for copy in bg_fly:
        copy.wait_recv()
    bgv = bg.at[:, :, :]
    olg = nt(bgv[...].reshape(CHIP, WIDTH), ob2[...])
    olg_low = olg.astype(BF)

    def mixed_columns(n, carry):
        cols = pl.ds(pl.multiple_of(n * 256, 256), 256)
        wcols = pl.ds(pl.multiple_of(QKV + n * 256, 256), 256)
        m = nn(bg[...].reshape(CHIP, WIDTH), wa[:, :, :, :, :, wcols].reshape(WIDTH, 256))
        m += nn(olg_low, oac[:, cols])
        ngt[cols, :] = m.T.astype(BF)
        return carry

    lax.fori_loop(0, 4, mixed_columns, 0)
    for k in range(4):
        sig[k] = jnp.zeros((AUG, 128), F32)

    def states_four(n, carry):
        g = n // 2
        rows = [pl.ds(pl.multiple_of(n * 256 + k * HEAD, HEAD), HEAD) for k in range(4)]
        for p in range(2):
            cols = slice(p * 128, (p + 1) * 128)
            left, right = [], []
            for k in range(4):
                h = (n * 4 + k) * 2 + p
                rden = den[h, :1]
                m = ngt[rows[k], cols].astype(F32)
                ng = (m * rden).astype(BF)
                dg = -jnp.sum(m * mixf[rows[k], cols], 0, keepdims=True) * rden
                ngt[rows[k], cols] = ng
                dgr[h, :1] = dg
                dq = (qfeat[rows[k], cols] * damp[h, :1]).astype(BF)
                right.append(jnp.concatenate([jnp.where(low_lane, dq, zero_low), jnp.where(low_lane, zero_low, dq)], 0))
                tail = jnp.where(lax.broadcasted_iota(jnp.int32, (AUG - HEAD, 128), 0) == 0, dg, 0.0).astype(BF)
                left.append(jnp.concatenate([ng, tail], 0))
            sig[g * 2 + p] = sig[g * 2 + p] + nt(lanes(left), lanes(right))
        return carry

    lax.fori_loop(0, 4, states_four, 0)
    sg_states = []
    for p in range(2):
        a, b = sig[p], sig[2 + p]
        sg_states.append(jnp.where(low_lane, a, pltpu.roll(b, 64, 1)))
        sg_states.append(jnp.where(low_lane, pltpu.roll(a, 64, 1), b))
    for s in range(4):
        st[s] = sg_states[s]
    folded = sg_states[3]
    for s in (2, 1, 0):
        folded = sg_states[s] + gates[s + 1] * folded
    copies.note()
    fly = gather_plane(1, folded)
    blk_fly += give_back(ht, rbb, pl.ds(1536, 512))

    for k in range(4):
        kacc[k] = jnp.zeros((HEAD, 128), F32)
        vacc[k] = jnp.zeros((HEAD, 128), F32)

    def back_four(n, carry):
        g = n // 2
        rows = [pl.ds(pl.multiple_of(n * 256 + k * HEAD, HEAD), HEAD) for k in range(4)]
        for p in range(2):
            cols = slice(p * 128, (p + 1) * 128)
            ngs = lanes([ngt[r, cols] for r in rows])
            dgs = [dgr[(n * 4 + k) * 2 + p, :1] for k in range(4)]
            dg = lanes(dgs)
            ws = lanes([wts[(n * 4 + k) * 2 + p] for k in range(4)])
            pt = nn(vnat[g, cols, :], jnp.concatenate([ngs, ngs], 0)) + dg
            sgr = (ws.astype(F32) * pt).astype(BF)
            tail = jnp.where(lax.broadcasted_iota(jnp.int32, (HEAD, 512), 0) == 0, dg, 0.0).astype(BF)
            both = split(nn(comb_t[g * 2 + p], jnp.concatenate([ngs, tail], 0)))
            for k in range(4):
                qg = jnp.where(low_lane, both[k][:HEAD], both[k][HEAD:]) * damp[(n * 4 + k) * 2 + p, :1]
                f = qfeat[rows[k], cols]
                qlg[rows[k], cols] = (f * (qg - jnp.sum(f * qg, 0, keepdims=True))).astype(BF)
            near = split(nn(kt[g, :, cols], sgr))
            for k in range(4):
                far = nn(fq[n * 4 + k], qlg[rows[k], cols])
                gt[rows[k], cols] = (near[k] * 0.125 + far).astype(BF)
            kacc[g * 2 + p] = kacc[g * 2 + p] + nt(lanes([qt[r, cols] for r in rows]), sgr)
            vacc[g * 2 + p] = vacc[g * 2 + p] + nt(ngs, ws)
        return carry

    lax.fori_loop(0, 4, back_four, 0)
    early = Sums(copies, device, (x, y, z, c), sibling, (e_own, e_got, e_line, e_all), EARLY_BLOCKS)
    late = Sums(copies, device, (x, y, z, c), sibling, (l_own, l_got, l_line, l_all), LATE_BLOCKS)
    lowo_t = lowo[...].astype(F32).T.astype(BF)
    olg_t = olg.T.astype(BF)
    low_t = low[...].astype(F32).T.astype(BF)
    lowg_q = nn(ball[:16, :HALF], gt[:HALF, :]).astype(BF)
    grads = jnp.concatenate(
        [nn(lowg_q, hid1[...])[:8], 2.0 * nn(lowo_t[:16], bg[...].reshape(CHIP, WIDTH))[:8]], 0
    )
    for j in range(16):
        early.put(40 + j, grads[:, j * 128 : (j + 1) * 128])
    grads = jnp.concatenate([2.0 * nt(low_t[:16], gt[:HALF, :])[:8], nn(olg_t[:16], mixn[...])[:8]], 0)
    for j in range(8):
        early.put(32 + j, grads[:, j * 128 : (j + 1) * 128])
    early.put(56, jnp.concatenate([gain_mlp[:, k * 128 : (k + 1) * 128] for k in range(16)], 0))
    for k in range(57, 64):
        early.put(k, jnp.zeros((16, 128), F32))

    def grad_rows(n, carry):
        rows = pl.ds(pl.multiple_of(n * 256, 256), 256)
        gnat[:, rows] = gt[rows, :].astype(F32).T.astype(BF)
        return carry

    lax.fori_loop(0, 4, grad_rows, 0)

    def feat_pairs(n, carry):
        rows = pl.ds(pl.multiple_of(n * 128, 128), 128)
        r = nt(qt[rows, :], qlg[rows, :])
        r = jnp.where(low_lane, r[:HEAD], r[HEAD:]).astype(BF)
        for k in range(4):
            e_own[2 * k + n // 4, :, pl.ds(pl.multiple_of(lax.rem(n, 4) * 128, 128), 128)] = r[k * 16 : (k + 1) * 16]
        return carry

    lax.fori_loop(0, 8, feat_pairs, 0)

    early.scatter()
    part, fly = fold_plane(1, fly)

    def one_queries(n, carry):
        w = wa[n // 2, pl.ds(pl.multiple_of(lax.rem(n, 2) * 2, 2), 2), :, :, :, 0:HALF].reshape(256, HALF)
        o = nt(gnat[:, :HALF], w)
        rows = pl.ds(pl.multiple_of(lax.rem(n, 4) * 256, 256), 256)

        @pl.when(n < 4)
        def _():
            qfeat[rows, :] = o

        @pl.when(n >= 4)
        def _():
            mixf[rows, :] = o

        return carry

    lax.fori_loop(0, 8, one_queries, 0)
    suffix = fold_line(1, part, fly)
    used = {copy.index for copy in copies.all if not copy.landed}
    copies.heard = [index for index in copies.heard if index not in used]
    copies.reuse()
    states = [None, None, None, suffix]
    for s in (2, 1, 0):
        states[s] = gates[s + 1] * (states[s + 1] + st[s + 1])
    put_states(states, 4)

    for g in range(2):
        f_rows = slice(g * HEAD, (g + 1) * HEAD)
        for p in range(2):
            k = g * 2 + p
            cols = slice(p * 128, (p + 1) * 128)
            f = kfeat[f_rows, cols]
            both = nn(comb_t[4 + k], vt[g, :, cols])
            fg = jnp.where(low_lane, both[:HEAD], both[HEAD:]) * valid[:, cols]
            kl = (f * (fg - jnp.sum(f * fg, 0, keepdims=True))).astype(BF)
            qlg[HALF + g * HEAD : HALF + (g + 1) * HEAD, cols] = kl
            gt[HALF + g * HEAD : HALF + (g + 1) * HEAD, cols] = (kacc[k] * 0.125 + nn(fk[c * 2 + g], kl)).astype(BF)
            fl = f.astype(BF)
            stack = jnp.concatenate([jnp.where(low_lane, fl, zero_low), jnp.where(low_lane, zero_low, fl)], 0)
            gt[HALF + NARROW + g * HEAD : HALF + NARROW + (g + 1) * HEAD, cols] = (
                vacc[k] + nn(comb[4 + k, :HEAD], stack)
            ).astype(BF)

    lowg_t = nn(ball[...], gt[...])
    lowg[...] = lowg_t.T.astype(BF)
    lowg_t = lowg_t.astype(BF)

    grad_rows(4, 0)

    def one_columns(n, had):
        cols = pl.ds(pl.multiple_of(n * 256, 256), 256)
        w = wa[n // 2, pl.ds(pl.multiple_of(lax.rem(n, 2) * 2, 2), 2), :, :, :, HALF:QKV].reshape(256, 2 * NARROW)
        o = had[pl.ds(pl.multiple_of(lax.rem(n, 4) * 256, 256), 256), :]
        o = o + nt(gnat[:, HALF:], w) + nn(lowg[...], aall[:, cols])
        normed = [tok2[side, :, cols].astype(F32) * r1[side, :, :1] for side in range(2)]
        gain = jnp.sum(o[:ROWS] * normed[0] + o[ROWS:] * normed[1], 0, keepdims=True)
        gsum[pl.ds(2 * n, 1), :] = gain[:, :128]
        gsum[pl.ds(2 * n + 1, 1), :] = gain[:, 128:]
        ones[:, cols] = jnp.where(c == 0, o[:ROWS], o[ROWS:])
        outs[:, cols] = jnp.where(c == 0, o[ROWS:], o[:ROWS]).astype(BF)

    def one_first(n, carry):
        one_columns(n, qfeat)
        return carry

    def one_second(n, carry):
        one_columns(n, mixf)
        return carry

    r = nt(kt[...].reshape(128, CHIP), qlg[HALF:, :])
    r = jnp.where(low_lane, r[:HEAD], r[HEAD:])
    for k in range(4):
        late.put(k, r[k * 16 : (k + 1) * 16])
    up = 2.0 * nt(low_t[:32], gt[HALF:, :])
    late.put(4, jnp.concatenate([up[8:16, :NARROW], up[16:24, NARROW:]], 0))
    down = nn(lowg_t[:32], hid1[...])
    for j in range(16):
        late.put(5 + j, down[8:24, j * 128 : (j + 1) * 128])
    for k in range(21, 32):
        late.put(k, jnp.zeros((16, 128), F32))
    late.scatter()

    copies.sent(out_copy)
    lax.fori_loop(0, 4, one_first, 0)
    lax.fori_loop(4, 8, one_second, 0)
    one_copy = copies.start(outs, outr, sibling)

    gplane[plane] = gsum[...]
    gain_fly = [
        copies.start(gsum, gplane.at[plane], device({"x": i, "y": j}))
        for i in range(4)
        for j in range(4)
        if i + j > 0
    ]
    early.along()
    late.along()
    one_copy.wait_recv()
    copies.sent([one_copy])

    def token_rows(i, carry):
        rows = pl.ds(i * 16, 16)
        o = ones[rows, :] + outr[rows, :].astype(F32)
        t = tok2[c, rows, :].astype(F32)
        r = r1[c, rows, :1]
        n = t * r
        o = o * gain1[...]
        outs[rows, :] = (mgrad[rows, :] + r * (o - n * jnp.mean(o * n, -1, keepdims=True))).astype(BF)
        return carry

    lax.fori_loop(0, ROWS // 32, token_rows, 0)
    early.gather()
    for copy in gain_fly:
        copy.wait_recv()
    total = gplane[0]
    for k in range(1, 16):
        total += gplane[k]
    gline[z, c] = total
    mine = gline.at[z, c]
    gain_fly = [copies.start(mine, mine, device({"z": i}, cross)) for cross in (0, 1) for i in range(4) if i + cross > 0]
    late.gather()
    for copy in blk_fly:
        copy.wait_recv()

    def block_rows(i, carry):
        rows = pl.ds(i * 16, 16)
        t = mid[rows, :] + ht[rows, :].astype(F32)
        for k in range(3):
            t += rbb[k, rows, :].astype(F32)
        ht[rows, :] = t.astype(BF)
        return carry

    copies.sent(blk_fly)
    lax.fori_loop(0, ROWS // 16, block_rows, 0)
    here(ht.at[pl.ds(0, ROWS)], blk_out)
    lax.fori_loop(ROWS // 32, ROWS // 16, token_rows, 0)
    here(outs, gtok_out)
    for copy in gain_fly:
        copy.wait_recv()
    total = gline[0, 0] + gline[0, 1]
    for k in range(1, 4):
        total += gline[k, 0] + gline[k, 1]
    gain_all[...] = total
    here(gain_all, gain_out)
    early.cross()
    here(e_all.at[c], early_out.at[c])
    late.cross()
    here(l_all.at[c], late_out.at[c])
    early.finish()
    here(e_all.at[1 - c], early_out.at[1 - c])
    late.finish()
    here(l_all.at[1 - c], late_out.at[1 - c])
    for copy in local[-7:]:
        copy.wait()
    copies.drain()


def finish(
    blk, gtok, early, late, gain,
    blk_out, gtok_out, gain_a_out, qa_out, qb_out, ka_out, kb_out, va_out, vb_out, oa_out, ob_out, fq_out, fk_out,
    gain_b_out, sem,
):
    copies = [pltpu.make_async_copy(a, b, sem.at[k]) for k, (a, b) in enumerate(((blk, blk_out), (gtok, gtok_out)))]
    for copy in copies:
        copy.start()

    def block(sums, share, side, k):
        return sums[side, k // share, :, (k % share) * 128 : (k % share + 1) * 128].astype(F32)

    def first(side, k):
        return block(early, EARLY_BLOCKS, side, k)

    def second(side, k):
        return block(late, LATE_BLOCKS, side, k)

    for side in range(2):
        at = side * HALF
        for k in range(4):
            rows = slice(k * 16, (k + 1) * 16)
            for j in range(9):
                v = first(side, k * 8 + j) if j < 8 else second(side, k)
                out, head = (fq_out, side * 16 + 2 * j) if j < 8 else (fk_out, side * 2)
                out[head, rows, :] = v[:, :64]
                out[head + 1, rows, :] = pltpu.roll(v, 64, 1)[:, :64]
        for j in range(8):
            cols = slice(at + j * 128, at + (j + 1) * 128)
            v = first(side, 32 + j)
            qb_out[:, cols] = v[:8]
            oa_out[:, cols] = v[8:]
        v = second(side, 4)
        kb_out[:, side * NARROW : (side + 1) * NARROW] = v[:8]
        vb_out[:, side * NARROW : (side + 1) * NARROW] = v[8:]
    for j in range(16):
        cols = slice(j * 128, (j + 1) * 128)
        v = first(0, 40 + j) + first(1, 40 + j)
        qa_out[:, cols] = v[:8]
        ob_out[:, cols] = v[8:]
        v = second(0, 5 + j) + second(1, 5 + j)
        ka_out[:, cols] = v[:8]
        va_out[:, cols] = v[8:]
    gain_a_out[...] = gain[...]
    gain_b_out[...] = first(0, 56) + first(1, 56)
    for copy in copies:
        copy.wait()


N_COPIES = 193
N_SENDS = 48


def scratch():
    v = pltpu.VMEM
    return [
        v((4, 4, 4, 2, 16, ATT), BF),
        v((4, 2, 2, 2, 2, 2, 16, 3 * SLICE), BF),
        v((2, 2, 16, 3 * SLICE), BF),
        v((2, ROWS, WIDTH), BF),
        v((QUERY_HEADS // 2, HEAD, HEAD), BF),
        v((ROWS, WIDTH), BF),
        v((8, WIDTH), F32),
        v((2, ROWS, 128), F32),
        v((128, WIDTH), BF),
        v((128, QKV), BF),
        v((128, HALF), BF),
        v((128, WIDTH), BF),
        v((4, 16, 128), F32),
        v((2, 8, 128), F32),
        v((2, 128, 128), F32),
        v((CHIP, WIDTH), BF),
        v((CHIP, 128), BF),
        v((HALF, CHIP), BF),
        v((2, HEAD, CHIP), BF),
        v((2, 128, CHIP), BF),
        v((2, CHIP, 128), BF),
        v((2, CHIP, 128), BF),
        v((128, CHIP), F32),
        v((4, AUG, 128), F32),
        v((8, AUG, 128), BF),
        v((8, 128, 128), BF),
        v((32, 128, 128), BF),
        v((HALF, CHIP), F32),
        v((HALF, CHIP), F32),
        v((32, 8, 128), F32),
        v((32, 8, 128), F32),
        v((CHIP, HALF), BF),
        v((CHIP, 128), BF),
        v((ROWS, WIDTH), BF),
        v((ROWS, WIDTH), BF),
        v((ROWS, WIDTH), F32),
        v((512, WIDTH), BF),
        v((512, WIDTH), BF),
        v((512, SLICE), BF),
        v((512, SLICE), BF),
        v((512, SLICE), BF),
        v((3, ROWS, WIDTH), BF),
        v((3, ROWS, WIDTH), BF),
        v((ROWS, WIDTH), F32),
        v((2, ROWS, WIDTH), BF),
        v((HALF, CHIP), BF),
        v((32, 8, 128), F32),
        v((4, AUG, 128), F32),
        v((HALF + 128, CHIP), BF),
        v((QKV, CHIP), BF),
        v((CHIP, QKV), BF),
        v((CHIP, 128), BF),
        v((ROWS, WIDTH), F32),
        v((4, HEAD, 128), F32),
        v((4, HEAD, 128), F32),
        v((2, AUG, 128), BF),
        v((2, 16, AUG, 128), BF),
        v((2, AUG, 128), BF),
        v((2, 3, AUG, 128), BF),
        v((16, 16, EARLY_BLOCKS * 128), BF),
        v((16, 16, EARLY_BLOCKS * 128), BF),
        v((4, 16, EARLY_BLOCKS * 128), BF),
        v((2, 16, 16, EARLY_BLOCKS * 128), BF),
        v((16, 16, LATE_BLOCKS * 128), BF),
        v((16, 16, LATE_BLOCKS * 128), BF),
        v((4, 16, LATE_BLOCKS * 128), BF),
        v((2, 16, 16, LATE_BLOCKS * 128), BF),
        v((16, 128), F32),
        v((16, 16, 128), F32),
        v((4, 2, 16, 128), F32),
        v((16, 128), F32),
        pltpu.SemaphoreType.DMA((N_SENDS,)),
        pltpu.SemaphoreType.DMA((N_COPIES,)),
        pltpu.SemaphoreType.DMA((23,)),
    ]


def body(
    tokens, sequence_lengths, attention_gain, query_weight, key_weight, value_weight, output_weight_flipped,
    query_adapter_down, query_adapter_up, key_adapter_down, key_adapter_up, value_adapter_down, value_adapter_up,
    output_adapter_down, output_adapter_up, query_feature_map, key_feature_map, feedforward_gain,
    gate_weight, up_weight, down_weight_flipped, output_gradient,
):
    vmem = pl.BlockSpec(memory_space=pltpu.VMEM)
    smem = pl.BlockSpec(memory_space=pltpu.SMEM)
    anywhere = pl.BlockSpec(memory_space=pl.ANY)

    def array(*shape, dtype=F32):
        return jax.ShapeDtypeStruct(shape, dtype)

    parts = pl.pallas_call(
        kernel,
        out_shape=(
            array(ROWS, WIDTH, dtype=BF), array(ROWS, WIDTH, dtype=BF), array(2, 16, 16, EARLY_BLOCKS * 128, dtype=BF),
            array(2, 16, 16, LATE_BLOCKS * 128, dtype=BF),
            array(16, 128),
        ),
        in_specs=[anywhere, smem, vmem] + [anywhere] * 4 + [vmem] * 8 + [anywhere] + [vmem] * 2 + [anywhere] * 4,
        out_specs=(anywhere,) * 5,
        scratch_shapes=scratch(),
        compiler_params=pltpu.CompilerParams(
            collective_id=0, has_side_effects=True, vmem_limit_bytes=64 * 1024 * 1024
        ),
    )(
        tokens, sequence_lengths, attention_gain.reshape(16, 128),
        query_weight, key_weight, value_weight, output_weight_flipped,
        query_adapter_down.T, query_adapter_up, key_adapter_down.T, key_adapter_up, value_adapter_down.T,
        value_adapter_up, output_adapter_down.T, output_adapter_up, query_feature_map, key_feature_map,
        feedforward_gain.reshape(16, 128), gate_weight, up_weight, down_weight_flipped, output_gradient,
    )
    out = pl.pallas_call(
        finish,
        out_shape=(
            array(ROWS, WIDTH, dtype=BF), array(ROWS, WIDTH, dtype=BF), array(16, 128),
            array(RANK, WIDTH), array(RANK, WIDTH), array(RANK, WIDTH), array(RANK, 2 * NARROW),
            array(RANK, WIDTH), array(RANK, 2 * NARROW), array(RANK, WIDTH), array(RANK, WIDTH),
            array(QUERY_HEADS, HEAD, HEAD), array(KEY_VALUE_HEADS, HEAD, HEAD), array(16, 128),
        ),
        in_specs=[vmem] * 5,
        out_specs=(anywhere,) * 2 + (vmem,) * 12,
        scratch_shapes=[pltpu.SemaphoreType.DMA((2,))],
    )(*parts)
    (
        block_out, grad_tokens, gain_attn, qa, qb, ka, kb, va, vb, oa, ob, feat_q, feat_k, gain_mlp,
    ) = out
    return (
        block_out, grad_tokens, gain_attn.reshape(WIDTH), qa.T, qb, ka.T, kb, va.T, vb, oa.T, ob, feat_q, feat_k,
        gain_mlp.reshape(WIDTH),
    )


def solution(mesh):
    split, whole = P("seq", None), P()
    return jax.shard_map(
        body,
        mesh=mesh,
        in_specs=(
            (split, whole, whole) + (split,) * 4 + (whole,) * 11 + (split,) * 4
        ),
        out_specs=(split, split) + (whole,) * 12,
        check_vma=False,
    )
```

```python
import math

import jax
import jax.numpy as jnp
from jax import lax
from jax.experimental import pallas as pl
from jax.experimental.pallas import tpu as pltpu
from jax.sharding import PartitionSpec as P

QUERY_HEADS = 32
KEY_VALUE_HEADS = 4
HEAD = 64
STRETCH = 64
WIDTH = 2048
FF = 5632
ROWS = 128
CHIP = 256
HALF = 1024
NARROW = 128
QKV = HALF + 2 * NARROW
ATT = QKV + HALF
SLICE = FF // 4
AUG = 80
RANK = 8
EARLY_BLOCKS = 4
LATE_BLOCKS = 2
EPSILON = 1e-05
MESH = pl.DeviceIdType.MESH
F32 = jnp.float32
BF = jnp.bfloat16

SHARES = (
    (1, 0, 0, 64, 128),
    (3, 0, 64, 64, 192),
    (0, 1, 0, 64, 256),
    (0, 3, 64, 64, 320),
    (1, 1, 0, 32, 384),
    (1, 3, 32, 32, 416),
    (3, 1, 64, 32, 448),
    (3, 3, 96, 32, 480),
)


def nn(left, right):
    return jnp.dot(left, right, preferred_element_type=F32)


def tn(left, right):
    return lax.dot_general(left, right, (((0,), (0,)), ((), ())), preferred_element_type=F32)


def nt(left, right):
    return lax.dot_general(left, right, (((1,), (1,)), ((), ())), preferred_element_type=F32)


def wrap(value):
    return lax.rem(value, 4)


class Group:
    def __init__(self, copies, index):
        self.copies, self.index, self.members = copies, index, []

    def start(self, src, dst, device):
        self.members.append(self.copies.start(src, dst, device, self.index))

    def wait(self, ref):
        pltpu.make_async_copy(ref, ref, self.copies.recv.at[self.index]).wait()


class Copies:
    def __init__(self, send, recv):
        self.send, self.recv, self.count, self.open, self.indices = send, recv, 0, {}, 0

    def index(self):
        self.indices += 1
        return self.indices - 1

    def group(self):
        return Group(self, self.index())

    def start(self, src, dst, device, index=None):
        slot = self.count % N_SENDS
        if slot in self.open:
            self.open.pop(slot).wait_send()
        copy = pltpu.make_async_remote_copy(
            src_ref=src,
            dst_ref=dst,
            send_sem=self.send.at[slot],
            recv_sem=self.recv.at[self.index() if index is None else index],
            device_id=(device,),
            device_id_type=MESH,
        )
        self.count += 1
        copy.start()
        self.open[slot] = copy
        return copy

    def sent(self, copies):
        for slot in [k for k, copy in self.open.items() if any(copy is other for other in copies)]:
            self.open.pop(slot).wait_send()

    def drain(self):
        for copy in self.open.values():
            copy.wait_send()


class Heads:
    def __init__(self, copies, wa, where, device, settled, parts):
        self.copies, self.wa, self.where, self.device = copies, wa, where, device
        self.settled, self.parts = settled, parts
        self.flying = {}

    def block(self, order, phase, at, cols, core=slice(None)):
        index = []
        for axis in "zxy":
            k = order.index(axis)
            index.append(slice(None) if k < phase else at if k == phase else self.where[axis])
        return self.wa.at[index[0], index[1], index[2], core, :, cols]

    def begin(self, phase):
        c = self.where["c"]
        for part, (order, src, at, first, count) in enumerate(self.parts):
            axis = order[phase]
            cols = pl.ds(first, count)
            group = self.flying[phase, part] = self.copies.group()
            if phase == 0:
                for step in (1, 3, 2):
                    for cross in (0, 1):
                        core = 1 - c if cross else c
                        piece = src.at[:, pl.ds(pl.multiple_of(core * (src.shape[1] // 2) + at, 128), count)]
                        dst = self.wa.at[self.where["z"], self.where["x"], self.where["y"], c, :, cols]
                        group.start(piece, dst, self.device({axis: step}, cross))
            else:
                own = self.block(order, phase, self.where[axis], cols)
                for step in (1, 3):
                    group.start(own, own, self.device({axis: step}))

    def middle(self, phase):
        for part, (order, src, at, first, count) in enumerate(self.parts):
            axis = order[phase]
            cols = pl.ds(first, count)
            self.flying[phase, part].wait(self.block(order, phase, pl.ds(0, 2), cols))
            here = self.where[axis]
            left = self.block(order, phase, wrap(here + 3), cols, 0)
            right = self.block(order, phase, wrap(here + 1), cols, 1)
            group = self.flying[phase, part] = self.copies.group()
            group.start(left, left, self.device({axis: 1}))
            group.start(right, right, self.device({axis: 3}))

    def end(self, phase):
        self.settled()
        for part, (order, src, at, first, count) in enumerate(self.parts):
            at = pl.ds(0, 3) if phase == 0 else 0
            self.flying[phase, part].wait(self.block(order, phase, at, pl.ds(first, count)))


class Units:
    def __init__(self, copies, here, wf, stage, where, device, sibling, parts):
        self.copies, self.here, self.wf, self.stage = copies, here, wf, stage
        self.where, self.device, self.sibling, self.parts = where, device, sibling, parts
        self.flying, self.own = {}, []
        self.handed = [copies.group() for _ in parts]

    def rows(self, order, along, across, cols):
        w = self.where
        a = (slice(None), slice(None)) if along is None else (along // 2, lax.rem(along, 2))
        b = (across // 2, lax.rem(across, 2))
        x, y = (a, b) if order == "xy" else (b, a)
        return self.wf.at[w["z"], x[0], x[1], y[0], y[1], w["c"], :, cols]

    def line(self, z, cols):
        return self.wf.at[z, :, :, :, :, self.where["c"], :, cols]

    def hand_on(self, part, block):
        self.handed[part].start(block, block, self.sibling)

    def begin(self, phase):
        w = self.where
        for part, (order, src, at, first, count) in enumerate(self.parts):
            cols = pl.ds(first, count)
            a, b = order
            group = self.flying[phase, part] = self.copies.group()
            if phase == 0:
                for d in (1, 3, 2, 0):
                    for e in (0, 1):
                        pa, pb = lax.rem(w[a] + d, 2), lax.rem(w[b] + e, 2)
                        slot = pa * 2 + pb if order == "xy" else pb * 2 + pa
                        piece = src.at[:, pl.ds(pl.multiple_of(slot * SLICE + at, 128), count)]
                        if e == 0:
                            dst = self.rows(order, w[a], w[b], cols)
                        else:
                            dst = self.stage.at[w[a] // 2, lax.rem(w[a], 2), :, cols]
                        if d == 0:
                            self.own.append(self.here(piece, dst))
                        else:
                            group.start(piece, dst, self.device({a: d}))
            elif phase == 1:
                mine = self.rows(order, None, w[b], cols)
                other = self.stage.at[:, :, :, cols]
                group.start(other, mine, self.device({b: 1}))
                group.start(other, mine, self.device({b: 3}))
                group.start(mine, mine, self.device({b: 2}))
            else:
                block = self.line(w["z"], cols)
                self.hand_on(part, block)
                for step in (1, 3):
                    group.start(block, block, self.device({"z": step}))

    def some(self, phase, cols):
        if phase == 0:
            return self.wf.at[pl.ds(0, 3), 0, 0, 0, 0, :, :, cols]
        if phase == 1:
            return self.wf.at[pl.ds(0, 3), :, :, 0, 0, 0, :, cols]
        return self.wf.at[pl.ds(0, 2), :, :, :, :, 0, :, cols]

    def middle(self, phase):
        z = self.where["z"]
        for part, (order, src, at, first, count) in enumerate(self.parts):
            cols = pl.ds(first, count)
            self.flying[phase, part].wait(self.some(2, cols))
            one = (count // 256) * 128
            before, after = wrap(z + 3), wrap(z + 1)
            left = self.line(before, pl.ds(first, one))
            right = self.line(after, pl.ds(first + one, count - one))
            group = self.flying[phase, part] = self.copies.group()
            group.start(left, left, self.device({"z": 1}))
            group.start(right, right, self.device({"z": 3}))
            self.hand_on(part, self.line(before, cols))
            self.hand_on(part, self.line(after, cols))

    def end(self, phase):
        if phase == 0:
            for copy in self.own:
                copy.wait()
        for part, (order, src, at, first, count) in enumerate(self.parts):
            cols = pl.ds(first, count)
            self.flying[phase, part].wait(self.line(0, cols) if phase == 2 else self.some(phase, cols))
            if phase == 2:
                self.hand_on(part, self.line(wrap(self.where["z"] + 2), cols))

    def settle(self):
        for part, (order, src, at, first, count) in enumerate(self.parts):
            self.handed[part].wait(self.wf.at[:, :, :, :, :, 0, :, pl.ds(first, count)])


class Sums:
    def __init__(self, copies, device, at, sibling, buffers, share):
        self.copies, self.device, self.sibling, self.share = copies, device, sibling, share
        self.x, self.y, self.z, self.c = at
        self.plane = self.x * 4 + self.y
        self.own, self.got, self.line, self.all = buffers

    def put(self, k, value):
        self.own[k // self.share, :, (k % self.share) * 128 : (k % self.share + 1) * 128] = value.astype(BF)

    def others(self):
        return [(i, j) for i in range(4) for j in range(4) if i + j > 0]

    def scatter(self):
        self.fly = self.copies.group()
        for i, j in self.others():
            to = wrap(self.x + i) * 4 + wrap(self.y + j)
            self.fly.start(self.own.at[to], self.got.at[self.plane], self.device({"x": i, "y": j}))
        self.got[self.plane] = self.own[self.plane]

    def along(self):
        self.fly.wait(self.got.at[pl.ds(0, 15)])
        total = self.got[0].astype(F32)
        for k in range(1, 16):
            total += self.got[k].astype(F32)
        self.line[self.z] = total.astype(BF)
        mine = self.line.at[self.z]
        self.fly = self.copies.group()
        for i in (1, 2, 3):
            self.fly.start(mine, mine, self.device({"z": i}))

    def gather(self):
        self.fly.wait(self.line.at[pl.ds(0, 3)])
        total = self.line[0].astype(F32)
        for k in range(1, 4):
            total += self.line[k].astype(F32)
        self.all[self.c, self.plane] = total.astype(BF)
        piece = self.all.at[self.c, self.plane]
        self.fly = self.copies.group()
        for i, j in self.others():
            self.fly.start(piece, piece, self.device({"x": i, "y": j}))

    def cross(self):
        self.fly.wait(self.all.at[0, pl.ds(0, 15)])
        half = self.all.at[self.c]
        self.fly = self.copies.start(half, half, self.sibling)

    def finish(self):
        self.fly.wait_recv()


EARLY = ("kv.b0", "q.b0", "o.b0", "d.b0", "kv.e0", "u.b0", "g.b0", "kv.b1",)
PLAN = (
    "o.e0", "q.e0", "q.b1", "d.e0", "kv.m1", "d.b1", "o.b1", "q.m1", "kv.e1", "g.e0", "u.e0", "kv.b2",
    "d.e1", "d.b2", "q.e1", "o.m1", "g.b1", "u.b1", "kv.m2", "q.b2", "g.e1", "g.b2", "o.e1", "kv.e2",
    "low", "d.m2", "u.e1", "kvc", "pls", "o.b2", "lns", "q.m2", "u.b2", "o.m2", "g.m2", "d.e2",
    "lnw", "q.e2", "qc", "ogs", "att", "o.e2", "oproj", "mid", "u.m2", "hts", "g.e2", "ogw",
    "ds", "ig", "u.e2", "gs", "us", "htw",
)


def kernel(
    tok, lens, gain_a, qw, kw, vw, ow, qa, qb, ka, kb, va, vb, oa, ob, maps, fk, gain_b, gw, uw, dw, og,
    blk_out, gtok_out, early_out, late_out, gain_out,
    wa, wf, stage, tok2, fq, ogo, gains, r1, aall, ball, oac, ob2, masks, far_masks, bias, hid1, low, qt, kt, vt, knat, vnat,
    kfeat, st, comb, comb_t, wts, qfeat, mixf, damp, den, mixn, lowo, outs, outr, mid, ht, ogx, gg, inner, ug, rbt, rbb,
    mgrad, bg, ngt, dgr, sig, qlg, gt, gnat, lowg, ones, kacc, vacc, fsend, frecv, hsend, hrecv,
    e_own, e_got, e_line, e_all, l_own, l_got, l_line, l_all, gsum, gplane, gline, gain_all, send, recv, loc, two_send, two_recv,
):
    me = lax.axis_index("seq")
    c = lax.rem(me, 2)
    y = lax.rem(me // 2, 4)
    x = lax.rem(me // 8, 4)
    z = me // 32

    def device(steps, cross=0):
        zz, xx, yy = (wrap(v + steps.get(n, 0)) for n, v in (("z", z), ("x", x), ("y", y)))
        return ((zz * 4 + xx) * 4 + yy) * 2 + (1 - c if cross else c)

    sibling = me + 1 - 2 * c
    plane = x * 4 + y
    xl, yl = lax.rem(x, 2), lax.rem(y, 2)
    xh, yh = x // 2, y // 2

    barrier = pltpu.get_barrier_semaphore()
    peers = [sibling]
    peers += [device({"x": i, "y": j}) for i in range(4) for j in range(4) if i + j > 0]
    peers += [device({"z": i}) for i in (1, 2, 3)]
    peers += [device({axis: i}, 1) for axis in "xyz" for i in (1, 2, 3)]
    for peer in peers:
        pl.semaphore_signal(barrier, inc=1, device_id=(peer,), device_id_type=MESH)
    copies = Copies(send, recv)
    local = []

    def here(src, dst):
        copy = pltpu.make_async_copy(src, dst, loc.at[len(local)])
        copy.start()
        local.append(copy)
        return copy

    own = wa.at[z, x, y, c]
    pieces = ((kw, HALF, NARROW), (vw, HALF + NARROW, NARROW), (qw, 0, HALF), (ow, QKV, HALF))
    for src, at, count in pieces:
        mine = src.at[:, pl.ds(pl.multiple_of(c * count, count), count)]
        here(mine, own.at[:, pl.ds(at, count)])
    here(tok, tok2.at[c])
    here(maps.at[pl.ds(c * 16, 16)], fq)
    here(og, ogx.at[pl.ds(0, ROWS)])
    here(og, ogo)

    pl.semaphore_wait(barrier, len(peers))
    first = []
    for src, at, count in pieces:
        other = src.at[:, pl.ds(pl.multiple_of((1 - c) * count, count), count)]
        first.append(copies.start(other, own.at[:, pl.ds(at, count)], sibling))
    tok_copy = copies.start(tok, tok2.at[c], sibling)
    where = {"z": z, "x": x, "y": y, "c": c}
    pending = [local[:4] + first]

    def settled():
        if pending:
            done = pending.pop()
            for copy in done[:4]:
                copy.wait()
            for copy in done[4:]:
                copy.wait_recv()

    streams = {
        "kv": Heads(copies, wa, where, device, settled, (("xzy", kw, 0, HALF, NARROW), ("yzx", vw, 0, HALF + NARROW, NARROW))),
        "q": Heads(copies, wa, where, device, settled, (("xzy", qw, 0, 0, 512), ("yzx", qw, 512, 0 + 512, 512))),
        "o": Heads(copies, wa, where, device, settled, (("zxy", ow, 0, QKV, 512), ("zyx", ow, 512, QKV + 512, 512))),
        "d": Units(
            copies, here, wf, stage, where, device, sibling,
            (("xy", dw, 0, 2 * SLICE, 768), ("yx", dw, 768, 2 * SLICE + 768, 640)),
        ),
        "g": Units(copies, here, wf, stage, where, device, sibling, (("xy", gw, 0, 0, SLICE),)),
        "u": Units(copies, here, wf, stage, where, device, sibling, (("yx", uw, 0, SLICE, SLICE),)),
    }
    waiting = {}

    def advance(name):
        stream, step = name.split(".")
        stream = streams[stream]
        {"b": stream.begin, "m": stream.middle, "e": stream.end}[step[0]](int(step[1]))

    for name in EARLY:
        advance(name)

    for k, src in enumerate((gain_a, gain_b)):
        g = src[...].astype(F32)
        gains[k : k + 1, :] = jnp.concatenate([g[i : i + 1] for i in range(16)], 1)
    gain1, gain2 = gains.at[pl.ds(0, 1)], gains.at[pl.ds(1, 1)]

    def below(parts, rows, count):
        got = [part.astype(F32) for part in parts]
        used = RANK * len(parts)
        return jnp.concatenate(got + [jnp.zeros((rows - used, count), F32)], 0).astype(BF)

    aall[...] = below([qa[...], ka[...], va[...]], 128, WIDTH)
    half = pl.ds(pl.multiple_of(c * HALF, HALF), HALF)
    narrow = pl.ds(pl.multiple_of(c * NARROW, NARROW), NARROW)
    none = jnp.zeros((RANK, NARROW), F32)
    ball[:, :HALF] = below([2.0 * qb[:, half].astype(F32)], 128, HALF)
    ball[:, HALF : HALF + NARROW] = below([none, 2.0 * kb[:, narrow].astype(F32)], 128, NARROW)
    ball[:, HALF + NARROW :] = below([none, none, 2.0 * vb[:, narrow].astype(F32)], 128, NARROW)
    oac[...] = below([oa[:, half]], 128, HALF)
    ob2[...] = below([2.0 * ob[...].astype(F32)], 128, WIDTH)

    chip = me // 2
    starts, ends, total = [], [], jnp.int32(0)
    for k in range(8):
        starts.append(total)
        total = total + ((lens[k] + (STRETCH - 1)) >> 6)
        ends.append(total)

    def sequence(stretch):
        found = jnp.where(stretch >= ends[0], 1, 0)
        for k in range(1, 7):
            found = found + jnp.where(stretch >= ends[k], 1, 0)
        return found

    counts, gates = [], []
    for s in range(4):
        stretch = chip * 4 + s
        begin, length = starts[0], lens[0]
        for k in range(1, 8):
            inside = stretch >= starts[k]
            begin = jnp.where(inside, starts[k], begin)
            length = jnp.where(inside, lens[k], length)
        counts.append(length - (stretch - begin) * STRETCH)
        gates.append(jnp.where(stretch != begin, 1.0, 0.0))
    first_own, last_own = sequence(chip * 4), sequence(chip * 4 + 3)
    k16 = lax.broadcasted_iota(jnp.int32, (16, 128), 0)
    firsts = sequence((z * 16 + k16) * 4)
    lasts = sequence((z * 16 + k16) * 4 + 3)
    masks[0] = jnp.where((k16 < plane) & (lasts == first_own), 1.0, 0.0)
    masks[1] = jnp.where(lasts == sequence(z * 64 + 63), 1.0, 0.0)
    masks[2] = jnp.where((k16 > plane) & (firsts == last_own), 1.0, 0.0)
    masks[3] = jnp.where(firsts == sequence(z * 64), 1.0, 0.0)
    k8 = lax.broadcasted_iota(jnp.int32, (8, 128), 0)
    far_masks[0] = jnp.where((k8 < z) & (sequence(k8 * 64 + 63) == first_own), 1.0, 0.0)
    far_masks[1] = jnp.where((k8 > z) & (sequence(k8 * 64) == last_own), 1.0, 0.0)
    lane = lax.broadcasted_iota(jnp.int32, (1, 128), 1)
    low_lane = lane < 64
    in_stretch = lax.rem(lane, STRETCH)
    valid = jnp.concatenate(
        [jnp.where(in_stretch < jnp.where(low_lane, counts[2 * p], counts[2 * p + 1]), 1.0, 0.0) for p in range(2)], 1
    )
    iu = lax.broadcasted_iota(jnp.int32, (128, 128), 0)
    it = lax.broadcasted_iota(jnp.int32, (128, 128), 1)
    for p in range(2):
        room = jnp.where(iu < 64, counts[2 * p], counts[2 * p + 1])
        seen = (iu <= it) & ((iu < 64) == (it < 64)) & (lax.rem(iu, STRETCH) < room)
        bias[p] = jnp.where(seen, 0.0, -1e30)

    for copy in local[4:8]:
        copy.wait()
    tok_copy.wait_recv()

    def norm_rows(i, carry):
        rows = pl.ds(i * 32, 32)
        for side in range(2):
            t = tok2[side, rows, :].astype(F32)
            r = lax.rsqrt(jnp.mean(t * t, -1, keepdims=True) + EPSILON)
            r1[side, rows, :] = jnp.broadcast_to(r, (32, 128))
            hid1[pl.ds(side * ROWS + i * 32, 32), :] = (t * r * gain1[...]).astype(BF)
        return carry

    lax.fori_loop(0, ROWS // 32, norm_rows, 0)

    zero_low = jnp.zeros((), BF)

    def softmax_rows(logits):
        e = jnp.exp(logits - jnp.max(logits, 0, keepdims=True))
        return e / jnp.sum(e, 0, keepdims=True)

    def gather_plane(base, folded):
        fsend[base] = folded.astype(BF)
        frecv[base, plane] = folded.astype(BF)
        fly = copies.group()
        for i in range(4):
            for j in range(4):
                if i + j > 0:
                    fly.start(fsend.at[base], frecv.at[base, plane], device({"x": i, "y": j}))
        return fly

    def fold_plane(base, fly):
        fly.wait(frecv.at[base, pl.ds(0, 15)])
        whole = jnp.zeros((AUG, 128), F32)
        for k in range(16):
            whole += masks[2 * base + 1, k : k + 1, :] * frecv[base, k].astype(F32)
        hsend[base] = whole.astype(BF)
        fly = copies.group()
        for i in (1, 2, 3):
            fly.start(hsend.at[base], hrecv.at[base, i - 1], device({"z": i}))
        part = jnp.zeros((AUG, 128), F32)
        for k in range(16):
            part += masks[2 * base, k : k + 1, :] * frecv[base, k].astype(F32)
        return part, fly

    def fold_line(base, part, fly):
        fly.wait(hrecv.at[base])
        for i in (1, 2, 3):
            part += far_masks[base, pl.ds(wrap(z + 4 - i), 1), :] * hrecv[base, i - 1].astype(F32)
        return part

    def combine(states):
        for g in range(2):
            for p in range(2):
                one, two = states[2 * p], states[2 * p + 1]
                if g == 0:
                    both = jnp.where(low_lane, one, pltpu.roll(two, 64, 1))
                else:
                    both = jnp.where(low_lane, pltpu.roll(one, 64, 1), two)
                yield g * 2 + p, both

    def put_states(states, base):
        for k, both in combine(states):
            comb[base + k] = both.astype(BF)
            tall = jnp.concatenate([both, jnp.zeros((128 - AUG, 128), F32)], 0)
            comb_t[base + k] = tall.T.astype(BF)

    def share(src, dst):
        fly = copies.group()
        for i, j, r, n, at in SHARES:
            fly.start(src.at[pl.ds(r, n)], dst.at[pl.ds(at, n)], device({"x": i, "y": j}))
        return fly

    def lower():
        low[...] = nt(hid1[...], aall[...]).astype(BF)

    def keys():
        kv = nn(hid1[...], wa[:, :, :, :, :, HALF:QKV].reshape(WIDTH, 2 * NARROW))
        kv = (kv + nn(low[...], ball[:, HALF:QKV])).astype(BF)
        kv_t = kv.astype(F32).T.astype(BF)
        for g in range(2):
            keep = low_lane if g == 0 else ~low_lane
            knat[g] = jnp.where(keep, kv[:, :NARROW], jnp.zeros((), BF))
            vnat[g] = jnp.where(keep, kv[:, NARROW:], jnp.zeros((), BF))
            kt[g] = kv_t[g * HEAD : (g + 1) * HEAD]
            tail = lax.broadcasted_iota(jnp.int32, (64, CHIP), 0) == 0
            vt[g, :HEAD] = kv_t[NARROW + g * HEAD : NARROW + (g + 1) * HEAD]
            vt[g, HEAD:] = tail.astype(F32).astype(BF)
        lanes4 = lax.broadcasted_iota(jnp.int32, (1, CHIP), 1) // STRETCH

        for g in range(2):
            kfeat[g * HEAD : (g + 1) * HEAD] = softmax_rows(tn(fk[c * 2 + g], kt[g])) * valid
        kf = kfeat[...]
        kf_high = kf.astype(BF)
        kf_rest = (kf - kf_high.astype(F32)).astype(BF)
        for s in range(4):
            got = []
            for g in range(2):
                va = jnp.where(lanes4 == s, vt[g, :AUG], jnp.zeros((), BF))
                got.append(nt(va, kf_high) + nt(va, kf_rest))
            st[s] = jnp.where(low_lane, got[0], got[1])


    def send_plane():
        folded = st[0]
        for s in (1, 2, 3):
            folded = st[s] + gates[s] * folded
        waiting["plane"] = gather_plane(0, folded)

    def send_line():
        waiting["part"], waiting["line"] = fold_plane(0, waiting["plane"])

    def take_line():
        prefix = fold_line(0, waiting["part"], waiting["line"])
        states = [prefix]
        for s in (1, 2, 3):
            states.append(gates[s] * (states[s - 1] + st[s - 1]))
        put_states(states, 0)

    def queries():
        def query_columns(n, carry):
            cols = pl.ds(pl.multiple_of(n * 256, 256), 256)
            q = nn(hid1[...], wa[:, :, :, :, :, cols].reshape(WIDTH, 256)) + nn(low[...], ball[:, cols])
            qt[cols, :] = q.T.astype(BF)
            return carry

        lax.fori_loop(0, 4, query_columns, 0)

    def lanes(parts):
        return jnp.concatenate(parts, 1)

    def split(wide):
        return [wide[:, k * 128 : (k + 1) * 128] for k in range(4)]

    def attend_four(n, carry):
        g = n // 2
        rows = [pl.ds(pl.multiple_of(n * 256 + k * HEAD, HEAD), HEAD) for k in range(4)]
        for k in range(4):
            qfeat[rows[k], :] = softmax_rows(tn(fq[n * 4 + k], qt[rows[k], :]))
        for p in range(2):
            cols = slice(p * 128, (p + 1) * 128)
            q = lanes([qt[r, cols] for r in rows])
            scores = split(nn(knat[g, cols, :], jnp.concatenate([q, q], 0)))
            stacks = []
            for k in range(4):
                sc = scores[k] * 0.125 + bias[p]
                peak = jnp.max(sc, 0, keepdims=True)
                w = jnp.exp(sc - peak).astype(BF)
                wts[(n * 4 + k) * 2 + p] = w
                dm = jnp.exp(-peak)
                damp[(n * 4 + k) * 2 + p, :1] = dm
                dq = (qfeat[rows[k], cols] * dm).astype(BF)
                stacks.append(
                    jnp.concatenate([w, jnp.where(low_lane, dq, zero_low), jnp.where(low_lane, zero_low, dq)], 0)
                )
            lhs = jnp.concatenate([vt[g, :AUG, cols], comb[g * 2 + p]], 1)
            both = split(nn(lhs, lanes(stacks)))
            for k in range(4):
                rden = 1.0 / both[k][HEAD : HEAD + 1]
                den[(n * 4 + k) * 2 + p, :1] = rden
                mixf[rows[k], cols] = both[k][:HEAD] * rden
        return carry

    def attend():
        lax.fori_loop(0, 4, attend_four, 0)


    def project():
        def mix_rows(n, carry):
            cols = pl.ds(pl.multiple_of(n * 256, 256), 256)
            mixn[:, cols] = mixf[cols, :].T.astype(BF)
            return carry

        lax.fori_loop(0, 4, mix_rows, 0)
        lowo[...] = nt(mixn[...], oac[...]).astype(BF)

        def out_columns(n, carry):
            cols = pl.ds(pl.multiple_of(n * 256, 256), 256)
            w = wa[n // 2, pl.ds(pl.multiple_of(lax.rem(n, 2) * 2, 2), 2), :, :, :, QKV:ATT].reshape(256, HALF)
            o = nt(mixn[...], w) + nn(lowo[...], ob2[:, cols])
            mine = jnp.where(c == 0, o[:ROWS], o[ROWS:])
            other = jnp.where(c == 0, o[ROWS:], o[:ROWS])
            mid[:, cols] = mine + tok2[c, :, cols].astype(F32)
            outs[:, cols] = other.astype(BF)
            return carry

        waiting["out"] = []
        for at in (0, 4):
            lax.fori_loop(at, at + 4, out_columns, 0)
            cols = pl.ds(at * 256, HALF)
            waiting["out"].append(copies.start(outs.at[:, cols], outr.at[:, cols], sibling))

    def middle():
        for copy in waiting["out"]:
            copy.wait_recv()

        def middle_rows(i, carry):
            rows = pl.ds(i * 32, 32)
            m = mid[rows, :] + outr[rows, :].astype(F32)
            mid[rows, :] = m
            r = lax.rsqrt(jnp.mean(m * m, -1, keepdims=True) + EPSILON)
            ht[rows, :] = (m * r * gain2[...]).astype(BF)
            return carry

        lax.fori_loop(0, ROWS // 32, middle_rows, 0)

    def send_hidden():
        waiting["ht"] = share(ht, ht)

    def send_gradient():
        waiting["og"] = share(ogo, ogx)

    def arrived(name):
        waiting[name].wait(ogx.at[pl.ds(ROWS, 384)])

    def ff_cols(first, count):
        return wf[:, :, :, :, :, :, :, pl.ds(first, count)].reshape(WIDTH, count)

    def inner_gradient():
        gg[...] = nn(ogx[...], ff_cols(2 * SLICE, SLICE)).astype(BF)

    steps = {
        "low": lower,
        "kvc": keys,
        "pls": send_plane,
        "lns": send_line,
        "lnw": take_line,
        "qc": queries,
        "att": attend,
        "oproj": project,
        "mid": middle,
        "hts": send_hidden,
        "htw": lambda: arrived("ht"),
        "ogs": send_gradient,
        "ogw": lambda: arrived("og"),
        "ds": streams["d"].settle,
        "gs": streams["g"].settle,
        "us": streams["u"].settle,
        "ig": inner_gradient,
    }
    for name in PLAN:
        if "." in name:
            advance(name)
        else:
            steps[name]()
    og_fly, ht_fly, out_copy = waiting["og"], waiting["ht"], waiting["out"]

    def activate(gate, up, cols):
        s = 0.5 * jnp.tanh(0.5 * gate) + 0.5
        swish = gate * s
        inner[:, cols] = (swish * up).astype(BF)
        d = gg[:, cols].astype(F32)
        gg[:, cols] = (d * up * s * (1.0 + gate * (1.0 - s))).astype(BF)
        ug[:, cols] = (d * swish).astype(BF)

    for at, count in ((0, 512), (512, 512), (1024, 256)):
        cols = slice(at, at + count)
        activate(nn(ht[...], ff_cols(at, count)), nn(ht[...], ff_cols(SLICE + at, count)), cols)
    both = nn(ht[...], jnp.concatenate([ff_cols(1280, 128), ff_cols(SLICE + 1280, 128)], 1))
    activate(both[:, :128], both[:, 128:], slice(1280, SLICE))

    def ff_rows(n, at):
        return wf[n // 2, lax.rem(n, 2), :, :, :, :, :, pl.ds(at, SLICE)].reshape(256, SLICE)

    copies.sent(ht_fly.members)
    copies.sent(og_fly.members)

    def two_columns(n, carry):
        cols = pl.ds(pl.multiple_of(n * 256, 256), 256)
        ogx[:, cols] = (nt(gg[...], ff_rows(n, 0)) + nt(ug[...], ff_rows(n, SLICE))).astype(BF)
        return carry

    def give_back(src, dst, cols):
        fly = copies.group()
        for k, (i, j, r, n, at) in enumerate(SHARES):
            there = dst.at[k // 2 - (k > 5), pl.ds(r, n), cols]
            fly.start(src.at[pl.ds(at, n), cols], there, device({"x": (4 - i) % 4, "y": (4 - j) % 4}))
        return [(fly, dst.at[:, :, cols])]

    def two_step(n, carry):
        two_columns(n, carry)
        cols = pl.ds(pl.multiple_of(n * 256, 256), 256)
        for k, (i, j, r, count, at) in enumerate(SHARES):
            pltpu.make_async_remote_copy(
                src_ref=ogx.at[pl.ds(at, count), cols],
                dst_ref=rbt.at[k // 2 - (k > 5), pl.ds(r, count), cols],
                send_sem=two_send.at[n],
                recv_sem=two_recv.at[n],
                device_id=(device({"x": (4 - i) % 4, "y": (4 - j) % 4}),),
                device_id_type=MESH,
            ).start()
        return carry

    lax.fori_loop(0, 8, two_step, 0)

    def two_wait(n, carry):
        cols = pl.ds(pl.multiple_of(n * 256, 256), 256)
        here_to = ogx.at[pl.ds(ROWS, 384), cols]
        pltpu.make_async_copy(here_to, here_to, two_send.at[n]).wait()
        come = rbt.at[:, :, cols]
        pltpu.make_async_copy(come, come, two_recv.at[n]).wait()
        return carry

    def block_columns(n, carry):
        cols = pl.ds(pl.multiple_of(n * 256, 256), 256)
        ht[:, cols] = nt(inner[...], ff_rows(n, 2 * SLICE)).astype(BF)
        return carry

    lax.fori_loop(0, 6, block_columns, 0)
    blk_fly = give_back(ht, rbb, pl.ds(0, 1536))
    lax.fori_loop(6, 8, block_columns, 0)
    lax.fori_loop(0, 8, two_wait, 0)

    def middle_back(i, acc):
        rows = pl.ds(i * 16, 16)
        t = ogx[rows, :].astype(F32)
        for k in range(3):
            t += rbt[k, rows, :].astype(F32)
        m = mid[rows, :]
        r = lax.rsqrt(jnp.mean(m * m, -1, keepdims=True) + EPSILON)
        n = m * r
        acc += jnp.sum(t * n, 0, keepdims=True)
        t = t * gain2[...]
        g = ogo[rows, :].astype(F32) + r * (t - n * jnp.mean(t * n, -1, keepdims=True))
        mgrad[rows, :] = g
        bg[c, rows, :] = g.astype(BF)
        return acc

    gain_mlp = jnp.zeros((1, WIDTH), F32)
    bg_fly = []
    for at in (0, ROWS // 2):
        gain_mlp = lax.fori_loop(at // 16, at // 16 + ROWS // 32, middle_back, gain_mlp)
        part = bg.at[c, pl.ds(at, ROWS // 2)]
        bg_fly.append(copies.start(part, part, sibling))
    for copy in bg_fly:
        copy.wait_recv()
    bgv = bg.at[:, :, :]
    olg = nt(bgv[...].reshape(CHIP, WIDTH), ob2[...])
    olg_low = olg.astype(BF)

    def mixed_columns(n, carry):
        cols = pl.ds(pl.multiple_of(n * 256, 256), 256)
        wcols = pl.ds(pl.multiple_of(QKV + n * 256, 256), 256)
        m = nn(bg[...].reshape(CHIP, WIDTH), wa[:, :, :, :, :, wcols].reshape(WIDTH, 256))
        m += nn(olg_low, oac[:, cols])
        ngt[cols, :] = m.T.astype(BF)
        return carry

    lax.fori_loop(0, 4, mixed_columns, 0)
    for k in range(4):
        sig[k] = jnp.zeros((AUG, 128), F32)

    def states_four(n, carry):
        g = n // 2
        rows = [pl.ds(pl.multiple_of(n * 256 + k * HEAD, HEAD), HEAD) for k in range(4)]
        for p in range(2):
            cols = slice(p * 128, (p + 1) * 128)
            left, right = [], []
            for k in range(4):
                h = (n * 4 + k) * 2 + p
                rden = den[h, :1]
                m = ngt[rows[k], cols].astype(F32)
                ng = (m * rden).astype(BF)
                dg = -jnp.sum(m * mixf[rows[k], cols], 0, keepdims=True) * rden
                ngt[rows[k], cols] = ng
                dgr[h, :1] = dg
                dq = (qfeat[rows[k], cols] * damp[h, :1]).astype(BF)
                right.append(jnp.concatenate([jnp.where(low_lane, dq, zero_low), jnp.where(low_lane, zero_low, dq)], 0))
                tail = jnp.where(lax.broadcasted_iota(jnp.int32, (AUG - HEAD, 128), 0) == 0, dg, 0.0).astype(BF)
                left.append(jnp.concatenate([ng, tail], 0))
            sig[g * 2 + p] = sig[g * 2 + p] + nt(lanes(left), lanes(right))
        return carry

    lax.fori_loop(0, 4, states_four, 0)
    sg_states = []
    for p in range(2):
        a, b = sig[p], sig[2 + p]
        sg_states.append(jnp.where(low_lane, a, pltpu.roll(b, 64, 1)))
        sg_states.append(jnp.where(low_lane, pltpu.roll(a, 64, 1), b))
    for s in range(4):
        st[s] = sg_states[s]
    folded = sg_states[3]
    for s in (2, 1, 0):
        folded = sg_states[s] + gates[s + 1] * folded
    fly = gather_plane(1, folded)
    blk_fly += give_back(ht, rbb, pl.ds(1536, 512))

    for k in range(4):
        kacc[k] = jnp.zeros((HEAD, 128), F32)
        vacc[k] = jnp.zeros((HEAD, 128), F32)

    def back_four(n, carry):
        g = n // 2
        rows = [pl.ds(pl.multiple_of(n * 256 + k * HEAD, HEAD), HEAD) for k in range(4)]
        for p in range(2):
            cols = slice(p * 128, (p + 1) * 128)
            ngs = lanes([ngt[r, cols] for r in rows])
            dgs = [dgr[(n * 4 + k) * 2 + p, :1] for k in range(4)]
            dg = lanes(dgs)
            ws = lanes([wts[(n * 4 + k) * 2 + p] for k in range(4)])
            pt = nn(vnat[g, cols, :], jnp.concatenate([ngs, ngs], 0)) + dg
            sgr = (ws.astype(F32) * pt).astype(BF)
            tail = jnp.where(lax.broadcasted_iota(jnp.int32, (HEAD, 512), 0) == 0, dg, 0.0).astype(BF)
            both = split(nn(comb_t[g * 2 + p], jnp.concatenate([ngs, tail], 0)))
            for k in range(4):
                qg = jnp.where(low_lane, both[k][:HEAD], both[k][HEAD:]) * damp[(n * 4 + k) * 2 + p, :1]
                f = qfeat[rows[k], cols]
                qlg[rows[k], cols] = (f * (qg - jnp.sum(f * qg, 0, keepdims=True))).astype(BF)
            near = split(nn(kt[g, :, cols], sgr))
            for k in range(4):
                far = nn(fq[n * 4 + k], qlg[rows[k], cols])
                gt[rows[k], cols] = (near[k] * 0.125 + far).astype(BF)
            kacc[g * 2 + p] = kacc[g * 2 + p] + nt(lanes([qt[r, cols] for r in rows]), sgr)
            vacc[g * 2 + p] = vacc[g * 2 + p] + nt(ngs, ws)
        return carry

    lax.fori_loop(0, 4, back_four, 0)
    early = Sums(copies, device, (x, y, z, c), sibling, (e_own, e_got, e_line, e_all), EARLY_BLOCKS)
    late = Sums(copies, device, (x, y, z, c), sibling, (l_own, l_got, l_line, l_all), LATE_BLOCKS)
    lowo_t = lowo[...].astype(F32).T.astype(BF)
    olg_t = olg.T.astype(BF)
    low_t = low[...].astype(F32).T.astype(BF)
    lowg_q = nn(ball[:16, :HALF], gt[:HALF, :]).astype(BF)
    grads = jnp.concatenate(
        [nn(lowg_q, hid1[...])[:8], 2.0 * nn(lowo_t[:16], bg[...].reshape(CHIP, WIDTH))[:8]], 0
    )
    for j in range(16):
        early.put(40 + j, grads[:, j * 128 : (j + 1) * 128])
    grads = jnp.concatenate([2.0 * nt(low_t[:16], gt[:HALF, :])[:8], nn(olg_t[:16], mixn[...])[:8]], 0)
    for j in range(8):
        early.put(32 + j, grads[:, j * 128 : (j + 1) * 128])
    early.put(56, jnp.concatenate([gain_mlp[:, k * 128 : (k + 1) * 128] for k in range(16)], 0))
    for k in range(57, 64):
        early.put(k, jnp.zeros((16, 128), F32))

    def grad_rows(n, carry):
        rows = pl.ds(pl.multiple_of(n * 256, 256), 256)
        gnat[:, rows] = gt[rows, :].astype(F32).T.astype(BF)
        return carry

    lax.fori_loop(0, 4, grad_rows, 0)

    def feat_pairs(n, carry):
        rows = pl.ds(pl.multiple_of(n * 128, 128), 128)
        r = nt(qt[rows, :], qlg[rows, :])
        r = jnp.where(low_lane, r[:HEAD], r[HEAD:]).astype(BF)
        for k in range(4):
            e_own[2 * k + n // 4, :, pl.ds(pl.multiple_of(lax.rem(n, 4) * 128, 128), 128)] = r[k * 16 : (k + 1) * 16]
        return carry

    lax.fori_loop(0, 8, feat_pairs, 0)

    early.scatter()
    part, fly = fold_plane(1, fly)

    def one_queries(n, carry):
        w = wa[n // 2, pl.ds(pl.multiple_of(lax.rem(n, 2) * 2, 2), 2), :, :, :, 0:HALF].reshape(256, HALF)
        o = nt(gnat[:, :HALF], w)
        rows = pl.ds(pl.multiple_of(lax.rem(n, 4) * 256, 256), 256)

        @pl.when(n < 4)
        def _():
            qfeat[rows, :] = o

        @pl.when(n >= 4)
        def _():
            mixf[rows, :] = o

        return carry

    lax.fori_loop(0, 8, one_queries, 0)
    suffix = fold_line(1, part, fly)
    states = [None, None, None, suffix]
    for s in (2, 1, 0):
        states[s] = gates[s + 1] * (states[s + 1] + st[s + 1])
    put_states(states, 4)

    for g in range(2):
        f_rows = slice(g * HEAD, (g + 1) * HEAD)
        for p in range(2):
            k = g * 2 + p
            cols = slice(p * 128, (p + 1) * 128)
            f = kfeat[f_rows, cols]
            both = nn(comb_t[4 + k], vt[g, :, cols])
            fg = jnp.where(low_lane, both[:HEAD], both[HEAD:]) * valid[:, cols]
            kl = (f * (fg - jnp.sum(f * fg, 0, keepdims=True))).astype(BF)
            qlg[HALF + g * HEAD : HALF + (g + 1) * HEAD, cols] = kl
            gt[HALF + g * HEAD : HALF + (g + 1) * HEAD, cols] = (kacc[k] * 0.125 + nn(fk[c * 2 + g], kl)).astype(BF)
            fl = f.astype(BF)
            stack = jnp.concatenate([jnp.where(low_lane, fl, zero_low), jnp.where(low_lane, zero_low, fl)], 0)
            gt[HALF + NARROW + g * HEAD : HALF + NARROW + (g + 1) * HEAD, cols] = (
                vacc[k] + nn(comb[4 + k, :HEAD], stack)
            ).astype(BF)

    lowg_t = nn(ball[...], gt[...])
    lowg[...] = lowg_t.T.astype(BF)
    lowg_t = lowg_t.astype(BF)

    grad_rows(4, 0)

    def one_columns(n, had):
        cols = pl.ds(pl.multiple_of(n * 256, 256), 256)
        w = wa[n // 2, pl.ds(pl.multiple_of(lax.rem(n, 2) * 2, 2), 2), :, :, :, HALF:QKV].reshape(256, 2 * NARROW)
        o = had[pl.ds(pl.multiple_of(lax.rem(n, 4) * 256, 256), 256), :]
        o = o + nt(gnat[:, HALF:], w) + nn(lowg[...], aall[:, cols])
        normed = [tok2[side, :, cols].astype(F32) * r1[side, :, :1] for side in range(2)]
        gain = jnp.sum(o[:ROWS] * normed[0] + o[ROWS:] * normed[1], 0, keepdims=True)
        gsum[pl.ds(2 * n, 1), :] = gain[:, :128]
        gsum[pl.ds(2 * n + 1, 1), :] = gain[:, 128:]
        ones[:, cols] = jnp.where(c == 0, o[:ROWS], o[ROWS:])
        outs[:, cols] = jnp.where(c == 0, o[ROWS:], o[:ROWS]).astype(BF)

    def one_first(n, carry):
        one_columns(n, qfeat)
        return carry

    def one_second(n, carry):
        one_columns(n, mixf)
        return carry

    r = nt(kt[...].reshape(128, CHIP), qlg[HALF:, :])
    r = jnp.where(low_lane, r[:HEAD], r[HEAD:])
    for k in range(4):
        late.put(k, r[k * 16 : (k + 1) * 16])
    up = 2.0 * nt(low_t[:32], gt[HALF:, :])
    late.put(4, jnp.concatenate([up[8:16, :NARROW], up[16:24, NARROW:]], 0))
    down = nn(lowg_t[:32], hid1[...])
    for j in range(16):
        late.put(5 + j, down[8:24, j * 128 : (j + 1) * 128])
    for k in range(21, 32):
        late.put(k, jnp.zeros((16, 128), F32))
    late.scatter()

    copies.sent(out_copy)
    lax.fori_loop(0, 4, one_first, 0)
    lax.fori_loop(4, 8, one_second, 0)
    one_copy = copies.start(outs, outr, sibling)

    gplane[plane] = gsum[...]
    gain_fly = copies.group()
    for i, j in early.others():
        gain_fly.start(gsum, gplane.at[plane], device({"x": i, "y": j}))
    early.along()
    late.along()
    one_copy.wait_recv()
    copies.sent([one_copy])

    def token_rows(i, carry):
        rows = pl.ds(i * 16, 16)
        o = ones[rows, :] + outr[rows, :].astype(F32)
        t = tok2[c, rows, :].astype(F32)
        r = r1[c, rows, :1]
        n = t * r
        o = o * gain1[...]
        outs[rows, :] = (mgrad[rows, :] + r * (o - n * jnp.mean(o * n, -1, keepdims=True))).astype(BF)
        return carry

    lax.fori_loop(0, ROWS // 32, token_rows, 0)
    early.gather()
    gain_fly.wait(gplane.at[pl.ds(0, 15)])
    total = gplane[0]
    for k in range(1, 16):
        total += gplane[k]
    gline[z, c] = total
    mine = gline.at[z, c]
    same, cross = copies.group(), copies.group()
    for i in (1, 2, 3):
        same.start(mine, mine, device({"z": i}))
    for i in range(4):
        cross.start(mine, mine, device({"z": i}, 1))
    late.gather()
    for fly, ref in blk_fly:
        fly.wait(ref)

    def block_rows(i, carry):
        rows = pl.ds(i * 16, 16)
        t = mid[rows, :] + ht[rows, :].astype(F32)
        for k in range(3):
            t += rbb[k, rows, :].astype(F32)
        ht[rows, :] = t.astype(BF)
        return carry

    copies.sent([copy for fly, ref in blk_fly for copy in fly.members])
    lax.fori_loop(0, ROWS // 16, block_rows, 0)
    here(ht.at[pl.ds(0, ROWS)], blk_out)
    lax.fori_loop(ROWS // 32, ROWS // 16, token_rows, 0)
    here(outs, gtok_out)
    same.wait(gline.at[pl.ds(0, 3), 0])
    cross.wait(gline.at[:, 0])
    total = gline[0, 0] + gline[0, 1]
    for k in range(1, 4):
        total += gline[k, 0] + gline[k, 1]
    gain_all[...] = total
    here(gain_all, gain_out)
    early.cross()
    here(e_all.at[c], early_out.at[c])
    late.cross()
    here(l_all.at[c], late_out.at[c])
    early.finish()
    here(e_all.at[1 - c], early_out.at[1 - c])
    late.finish()
    here(l_all.at[1 - c], late_out.at[1 - c])
    for copy in local[-7:]:
        copy.wait()
    copies.drain()


def finish(
    blk, gtok, early, late, gain,
    blk_out, gtok_out, gain_a_out, qa_out, qb_out, ka_out, kb_out, va_out, vb_out, oa_out, ob_out, fq_out, fk_out,
    gain_b_out, sem,
):
    copies = [pltpu.make_async_copy(a, b, sem.at[k]) for k, (a, b) in enumerate(((blk, blk_out), (gtok, gtok_out)))]
    for copy in copies:
        copy.start()

    def block(sums, share, side, k):
        return sums[side, k // share, :, (k % share) * 128 : (k % share + 1) * 128].astype(F32)

    def first(side, k):
        return block(early, EARLY_BLOCKS, side, k)

    def second(side, k):
        return block(late, LATE_BLOCKS, side, k)

    for side in range(2):
        at = side * HALF
        for k in range(4):
            rows = slice(k * 16, (k + 1) * 16)
            for j in range(9):
                v = first(side, k * 8 + j) if j < 8 else second(side, k)
                out, head = (fq_out, side * 16 + 2 * j) if j < 8 else (fk_out, side * 2)
                out[head, rows, :] = v[:, :64]
                out[head + 1, rows, :] = pltpu.roll(v, 64, 1)[:, :64]
        for j in range(8):
            cols = slice(at + j * 128, at + (j + 1) * 128)
            v = first(side, 32 + j)
            qb_out[:, cols] = v[:8]
            oa_out[:, cols] = v[8:]
        v = second(side, 4)
        kb_out[:, side * NARROW : (side + 1) * NARROW] = v[:8]
        vb_out[:, side * NARROW : (side + 1) * NARROW] = v[8:]
    for j in range(16):
        cols = slice(j * 128, (j + 1) * 128)
        v = first(0, 40 + j) + first(1, 40 + j)
        qa_out[:, cols] = v[:8]
        ob_out[:, cols] = v[8:]
        v = second(0, 5 + j) + second(1, 5 + j)
        ka_out[:, cols] = v[:8]
        va_out[:, cols] = v[8:]
    gain_a_out[...] = gain[...]
    gain_b_out[...] = first(0, 56) + first(1, 56)
    for copy in copies:
        copy.wait()


N_COPIES = 79
N_SENDS = 48


def scratch():
    v = pltpu.VMEM
    return [
        v((4, 4, 4, 2, 16, ATT), BF),
        v((4, 2, 2, 2, 2, 2, 16, 3 * SLICE), BF),
        v((2, 2, 16, 3 * SLICE), BF),
        v((2, ROWS, WIDTH), BF),
        v((QUERY_HEADS // 2, HEAD, HEAD), BF),
        v((ROWS, WIDTH), BF),
        v((8, WIDTH), F32),
        v((2, ROWS, 128), F32),
        v((128, WIDTH), BF),
        v((128, QKV), BF),
        v((128, HALF), BF),
        v((128, WIDTH), BF),
        v((4, 16, 128), F32),
        v((2, 8, 128), F32),
        v((2, 128, 128), F32),
        v((CHIP, WIDTH), BF),
        v((CHIP, 128), BF),
        v((HALF, CHIP), BF),
        v((2, HEAD, CHIP), BF),
        v((2, 128, CHIP), BF),
        v((2, CHIP, 128), BF),
        v((2, CHIP, 128), BF),
        v((128, CHIP), F32),
        v((4, AUG, 128), F32),
        v((8, AUG, 128), BF),
        v((8, 128, 128), BF),
        v((32, 128, 128), BF),
        v((HALF, CHIP), F32),
        v((HALF, CHIP), F32),
        v((32, 8, 128), F32),
        v((32, 8, 128), F32),
        v((CHIP, HALF), BF),
        v((CHIP, 128), BF),
        v((ROWS, WIDTH), BF),
        v((ROWS, WIDTH), BF),
        v((ROWS, WIDTH), F32),
        v((512, WIDTH), BF),
        v((512, WIDTH), BF),
        v((512, SLICE), BF),
        v((512, SLICE), BF),
        v((512, SLICE), BF),
        v((3, ROWS, WIDTH), BF),
        v((3, ROWS, WIDTH), BF),
        v((ROWS, WIDTH), F32),
        v((2, ROWS, WIDTH), BF),
        v((HALF, CHIP), BF),
        v((32, 8, 128), F32),
        v((4, AUG, 128), F32),
        v((HALF + 128, CHIP), BF),
        v((QKV, CHIP), BF),
        v((CHIP, QKV), BF),
        v((CHIP, 128), BF),
        v((ROWS, WIDTH), F32),
        v((4, HEAD, 128), F32),
        v((4, HEAD, 128), F32),
        v((2, AUG, 128), BF),
        v((2, 16, AUG, 128), BF),
        v((2, AUG, 128), BF),
        v((2, 3, AUG, 128), BF),
        v((16, 16, EARLY_BLOCKS * 128), BF),
        v((16, 16, EARLY_BLOCKS * 128), BF),
        v((4, 16, EARLY_BLOCKS * 128), BF),
        v((2, 16, 16, EARLY_BLOCKS * 128), BF),
        v((16, 16, LATE_BLOCKS * 128), BF),
        v((16, 16, LATE_BLOCKS * 128), BF),
        v((4, 16, LATE_BLOCKS * 128), BF),
        v((2, 16, 16, LATE_BLOCKS * 128), BF),
        v((16, 128), F32),
        v((16, 16, 128), F32),
        v((4, 2, 16, 128), F32),
        v((16, 128), F32),
        pltpu.SemaphoreType.DMA((N_SENDS,)),
        pltpu.SemaphoreType.DMA((N_COPIES,)),
        pltpu.SemaphoreType.DMA((23,)),
        pltpu.SemaphoreType.DMA((8,)),
        pltpu.SemaphoreType.DMA((8,)),
    ]


def body(
    tokens, sequence_lengths, attention_gain, query_weight, key_weight, value_weight, output_weight_flipped,
    query_adapter_down, query_adapter_up, key_adapter_down, key_adapter_up, value_adapter_down, value_adapter_up,
    output_adapter_down, output_adapter_up, query_feature_map, key_feature_map, feedforward_gain,
    gate_weight, up_weight, down_weight_flipped, output_gradient,
):
    vmem = pl.BlockSpec(memory_space=pltpu.VMEM)
    smem = pl.BlockSpec(memory_space=pltpu.SMEM)
    anywhere = pl.BlockSpec(memory_space=pl.ANY)

    def array(*shape, dtype=F32):
        return jax.ShapeDtypeStruct(shape, dtype)

    parts = pl.pallas_call(
        kernel,
        out_shape=(
            array(ROWS, WIDTH, dtype=BF), array(ROWS, WIDTH, dtype=BF), array(2, 16, 16, EARLY_BLOCKS * 128, dtype=BF),
            array(2, 16, 16, LATE_BLOCKS * 128, dtype=BF),
            array(16, 128),
        ),
        in_specs=[anywhere, smem, vmem] + [anywhere] * 4 + [vmem] * 8 + [anywhere] + [vmem] * 2 + [anywhere] * 4,
        out_specs=(anywhere,) * 5,
        scratch_shapes=scratch(),
        compiler_params=pltpu.CompilerParams(
            collective_id=0, has_side_effects=True, vmem_limit_bytes=64 * 1024 * 1024
        ),
    )(
        tokens, sequence_lengths, attention_gain.reshape(16, 128),
        query_weight, key_weight, value_weight, output_weight_flipped,
        query_adapter_down.T, query_adapter_up, key_adapter_down.T, key_adapter_up, value_adapter_down.T,
        value_adapter_up, output_adapter_down.T, output_adapter_up, query_feature_map, key_feature_map,
        feedforward_gain.reshape(16, 128), gate_weight, up_weight, down_weight_flipped, output_gradient,
    )
    out = pl.pallas_call(
        finish,
        out_shape=(
            array(ROWS, WIDTH, dtype=BF), array(ROWS, WIDTH, dtype=BF), array(16, 128),
            array(RANK, WIDTH), array(RANK, WIDTH), array(RANK, WIDTH), array(RANK, 2 * NARROW),
            array(RANK, WIDTH), array(RANK, 2 * NARROW), array(RANK, WIDTH), array(RANK, WIDTH),
            array(QUERY_HEADS, HEAD, HEAD), array(KEY_VALUE_HEADS, HEAD, HEAD), array(16, 128),
        ),
        in_specs=[vmem] * 5,
        out_specs=(anywhere,) * 2 + (vmem,) * 12,
        scratch_shapes=[pltpu.SemaphoreType.DMA((2,))],
    )(*parts)
    (
        block_out, grad_tokens, gain_attn, qa, qb, ka, kb, va, vb, oa, ob, feat_q, feat_k, gain_mlp,
    ) = out
    return (
        block_out, grad_tokens, gain_attn.reshape(WIDTH), qa.T, qb, ka.T, kb, va.T, vb, oa.T, ob, feat_q, feat_k,
        gain_mlp.reshape(WIDTH),
    )


def solution(mesh):
    split, whole = P("seq", None), P()
    return jax.shard_map(
        body,
        mesh=mesh,
        in_specs=(
            (split, whole, whole) + (split,) * 4 + (whole,) * 11 + (split,) * 4
        ),
        out_specs=(split, split) + (whole,) * 12,
        check_vma=False,
    )
```

```python
import math

import jax
import jax.numpy as jnp
from jax import lax
from jax.experimental import pallas as pl
from jax.experimental.pallas import tpu as pltpu
from jax.sharding import PartitionSpec as P

QUERY_HEADS = 32
KEY_VALUE_HEADS = 4
HEAD = 64
STRETCH = 64
WIDTH = 2048
FF = 5632
ROWS = 128
CHIP = 256
HALF = 1024
NARROW = 128
QKV = HALF + 2 * NARROW
ATT = QKV + HALF
SLICE = FF // 4
AUG = 80
RANK = 8
EARLY_BLOCKS = 4
LATE_BLOCKS = 2
EPSILON = 1e-05
MESH = pl.DeviceIdType.MESH
F32 = jnp.float32
BF = jnp.bfloat16

SHARES = (
    (1, 0, 0, 64, 128),
    (3, 0, 64, 64, 192),
    (0, 1, 0, 64, 256),
    (0, 3, 64, 64, 320),
    (1, 1, 0, 32, 384),
    (1, 3, 32, 32, 416),
    (3, 1, 64, 32, 448),
    (3, 3, 96, 32, 480),
)


def nn(left, right):
    return jnp.dot(left, right, preferred_element_type=F32)


def tn(left, right):
    return lax.dot_general(left, right, (((0,), (0,)), ((), ())), preferred_element_type=F32)


def nt(left, right):
    return lax.dot_general(left, right, (((1,), (1,)), ((), ())), preferred_element_type=F32)


def wrap(value):
    return lax.rem(value, 4)


class Group:
    def __init__(self, copies, index):
        self.copies, self.index, self.members = copies, index, []

    def start(self, src, dst, device):
        self.members.append(self.copies.start(src, dst, device, self.index))

    def wait(self, ref):
        pltpu.make_async_copy(ref, ref, self.copies.recv.at[self.index]).wait()


class Copies:
    def __init__(self, send, recv):
        self.send, self.recv, self.count, self.open, self.indices = send, recv, 0, {}, 0

    def index(self):
        self.indices += 1
        return self.indices - 1

    def group(self):
        return Group(self, self.index())

    def start(self, src, dst, device, index=None):
        slot = self.count % N_SENDS
        if slot in self.open:
            self.open.pop(slot).wait_send()
        copy = pltpu.make_async_remote_copy(
            src_ref=src,
            dst_ref=dst,
            send_sem=self.send.at[slot],
            recv_sem=self.recv.at[self.index() if index is None else index],
            device_id=(device,),
            device_id_type=MESH,
        )
        self.count += 1
        copy.start()
        self.open[slot] = copy
        return copy

    def sent(self, copies):
        for slot in [k for k, copy in self.open.items() if any(copy is other for other in copies)]:
            self.open.pop(slot).wait_send()

    def drain(self):
        for copy in self.open.values():
            copy.wait_send()


class Heads:
    def __init__(self, copies, wa, where, device, settled, parts):
        self.copies, self.wa, self.where, self.device = copies, wa, where, device
        self.settled, self.parts = settled, parts
        self.flying = {}

    def block(self, order, phase, at, cols, core=slice(None)):
        index = []
        for axis in "zxy":
            k = order.index(axis)
            index.append(slice(None) if k < phase else at if k == phase else self.where[axis])
        return self.wa.at[index[0], index[1], index[2], core, :, cols]

    def begin(self, phase):
        c = self.where["c"]
        for part, (order, src, at, first, count) in enumerate(self.parts):
            axis = order[phase]
            cols = pl.ds(first, count)
            group = self.flying[phase, part] = self.copies.group()
            if phase == 0:
                for step in (1, 3, 2):
                    for cross in (0, 1):
                        core = 1 - c if cross else c
                        piece = src.at[:, pl.ds(pl.multiple_of(core * (src.shape[1] // 2) + at, 128), count)]
                        dst = self.wa.at[self.where["z"], self.where["x"], self.where["y"], c, :, cols]
                        group.start(piece, dst, self.device({axis: step}, cross))
            else:
                own = self.block(order, phase, self.where[axis], cols)
                for step in (1, 3):
                    group.start(own, own, self.device({axis: step}))

    def middle(self, phase):
        for part, (order, src, at, first, count) in enumerate(self.parts):
            axis = order[phase]
            cols = pl.ds(first, count)
            self.flying[phase, part].wait(self.block(order, phase, pl.ds(0, 2), cols))
            here = self.where[axis]
            left = self.block(order, phase, wrap(here + 3), cols, 0)
            right = self.block(order, phase, wrap(here + 1), cols, 1)
            group = self.flying[phase, part] = self.copies.group()
            group.start(left, left, self.device({axis: 1}))
            group.start(right, right, self.device({axis: 3}))

    def end(self, phase):
        self.settled()
        for part, (order, src, at, first, count) in enumerate(self.parts):
            at = pl.ds(0, 3) if phase == 0 else 0
            self.flying[phase, part].wait(self.block(order, phase, at, pl.ds(first, count)))


class Units:
    def __init__(self, copies, here, wf, stage, where, device, sibling, parts):
        self.copies, self.here, self.wf, self.stage = copies, here, wf, stage
        self.where, self.device, self.sibling, self.parts = where, device, sibling, parts
        self.flying, self.own = {}, []
        self.handed = [copies.group() for _ in parts]

    def rows(self, order, along, across, cols):
        w = self.where
        a = (slice(None), slice(None)) if along is None else (along // 2, lax.rem(along, 2))
        b = (across // 2, lax.rem(across, 2))
        x, y = (a, b) if order == "xy" else (b, a)
        return self.wf.at[w["z"], x[0], x[1], y[0], y[1], w["c"], :, cols]

    def line(self, z, cols):
        return self.wf.at[z, :, :, :, :, self.where["c"], :, cols]

    def hand_on(self, part, block):
        self.handed[part].start(block, block, self.sibling)

    def begin(self, phase):
        w = self.where
        for part, (order, src, at, first, count) in enumerate(self.parts):
            cols = pl.ds(first, count)
            a, b = order
            group = self.flying[phase, part] = self.copies.group()
            if phase == 0:
                for d in (1, 3, 2, 0):
                    for e in (0, 1):
                        pa, pb = lax.rem(w[a] + d, 2), lax.rem(w[b] + e, 2)
                        slot = pa * 2 + pb if order == "xy" else pb * 2 + pa
                        piece = src.at[:, pl.ds(pl.multiple_of(slot * SLICE + at, 128), count)]
                        if e == 0:
                            dst = self.rows(order, w[a], w[b], cols)
                        else:
                            dst = self.stage.at[w[a] // 2, lax.rem(w[a], 2), :, cols]
                        if d == 0:
                            self.own.append(self.here(piece, dst))
                        else:
                            group.start(piece, dst, self.device({a: d}))
            elif phase == 1:
                mine = self.rows(order, None, w[b], cols)
                other = self.stage.at[:, :, :, cols]
                group.start(other, mine, self.device({b: 1}))
                group.start(other, mine, self.device({b: 3}))
                group.start(mine, mine, self.device({b: 2}))
            else:
                block = self.line(w["z"], cols)
                self.hand_on(part, block)
                for step in (1, 3):
                    group.start(block, block, self.device({"z": step}))

    def some(self, phase, cols):
        if phase == 0:
            return self.wf.at[pl.ds(0, 3), 0, 0, 0, 0, :, :, cols]
        if phase == 1:
            return self.wf.at[pl.ds(0, 3), :, :, 0, 0, 0, :, cols]
        return self.wf.at[pl.ds(0, 2), :, :, :, :, 0, :, cols]

    def middle(self, phase):
        z = self.where["z"]
        for part, (order, src, at, first, count) in enumerate(self.parts):
            cols = pl.ds(first, count)
            self.flying[phase, part].wait(self.some(2, cols))
            one = (count // 256) * 128
            before, after = wrap(z + 3), wrap(z + 1)
            left = self.line(before, pl.ds(first, one))
            right = self.line(after, pl.ds(first + one, count - one))
            group = self.flying[phase, part] = self.copies.group()
            group.start(left, left, self.device({"z": 1}))
            group.start(right, right, self.device({"z": 3}))
            self.hand_on(part, self.line(before, cols))
            self.hand_on(part, self.line(after, cols))

    def end(self, phase):
        if phase == 0:
            for copy in self.own:
                copy.wait()
        for part, (order, src, at, first, count) in enumerate(self.parts):
            cols = pl.ds(first, count)
            self.flying[phase, part].wait(self.line(0, cols) if phase == 2 else self.some(phase, cols))
            if phase == 2:
                self.hand_on(part, self.line(wrap(self.where["z"] + 2), cols))

    def settle(self):
        for part, (order, src, at, first, count) in enumerate(self.parts):
            self.handed[part].wait(self.wf.at[:, :, :, :, :, 0, :, pl.ds(first, count)])


class Sums:
    def __init__(self, copies, device, at, sibling, buffers, share):
        self.copies, self.device, self.sibling, self.share = copies, device, sibling, share
        self.x, self.y, self.z, self.c = at
        self.plane = self.x * 4 + self.y
        self.own, self.got, self.line, self.all = buffers

    def put(self, k, value):
        self.own[k // self.share, :, (k % self.share) * 128 : (k % self.share + 1) * 128] = value.astype(BF)

    def others(self):
        return [(i, j) for i in range(4) for j in range(4) if i + j > 0]

    def scatter(self):
        self.fly = self.copies.group()
        for i, j in self.others():
            to = wrap(self.x + i) * 4 + wrap(self.y + j)
            self.fly.start(self.own.at[to], self.got.at[self.plane], self.device({"x": i, "y": j}))
        self.got[self.plane] = self.own[self.plane]

    def along(self):
        self.fly.wait(self.got.at[pl.ds(0, 15)])
        total = self.got[0].astype(F32)
        for k in range(1, 16):
            total += self.got[k].astype(F32)
        self.line[self.z] = total.astype(BF)
        mine = self.line.at[self.z]
        self.fly = self.copies.group()
        for i in (1, 2, 3):
            self.fly.start(mine, mine, self.device({"z": i}))

    def gather(self):
        self.fly.wait(self.line.at[pl.ds(0, 3)])
        total = self.line[0].astype(F32)
        for k in range(1, 4):
            total += self.line[k].astype(F32)
        self.all[self.c, self.plane] = total.astype(BF)
        piece = self.all.at[self.c, self.plane]
        self.fly = self.copies.group()
        for i, j in self.others():
            self.fly.start(piece, piece, self.device({"x": i, "y": j}))

    def cross(self):
        self.fly.wait(self.all.at[0, pl.ds(0, 15)])
        half = self.all.at[self.c]
        self.fly = self.copies.start(half, half, self.sibling)

    def finish(self):
        self.fly.wait_recv()


EARLY = ("kv.b0", "q.b0", "o.b0", "d.b0", "kv.e0", "u.b0", "g.b0", "kv.b1",)
PLAN = (
    "o.e0", "q.e0", "q.b1", "d.e0", "kv.m1", "d.b1", "o.b1", "q.m1", "kv.e1", "g.e0", "u.e0", "kv.b2",
    "d.e1", "d.b2", "q.e1", "o.m1", "g.b1", "u.b1", "kv.m2", "q.b2", "g.e1", "g.b2", "o.e1", "kv.e2",
    "low", "d.m2", "u.e1", "kvc", "pls", "o.b2", "lns", "q.m2", "u.b2", "o.m2", "g.m2", "d.e2",
    "lnw", "q.e2", "qc", "ogs", "att", "o.e2", "oproj", "mid", "u.m2", "hts", "g.e2", "ogw",
    "ds", "ig", "gs", "go", "u.e2", "us", "uo", "htw",
)


def kernel(
    tok, lens, gain_a, qw, kw, vw, ow, qa, qb, ka, kb, va, vb, oa, ob, maps, fk, gain_b, gw, uw, dw, og,
    blk_out, gtok_out, early_out, late_out, gain_out,
    wa, wf, stage, tok2, fq, ogo, gains, r1, aall, ball, oac, ob2, masks, far_masks, bias, hid1, low, qt, kt, vt, knat, vnat,
    kfeat, st, comb, comb_t, wts, qfeat, mixf, damp, den, mixn, lowo, outs, outr, mid, ht, ogx, gg, inner, ug, rbt, rbb,
    mgrad, bg, ngt, dgr, sig, qlg, gt, gnat, lowg, ones, kacc, vacc, fsend, frecv, hsend, hrecv,
    gown, e_own, e_got, e_line, e_all, l_own, l_got, l_line, l_all, gsum, gplane, gline, gain_all, send, recv, loc, two_send, two_recv,
):
    me = lax.axis_index("seq")
    c = lax.rem(me, 2)
    y = lax.rem(me // 2, 4)
    x = lax.rem(me // 8, 4)
    z = me // 32

    def device(steps, cross=0):
        zz, xx, yy = (wrap(v + steps.get(n, 0)) for n, v in (("z", z), ("x", x), ("y", y)))
        return ((zz * 4 + xx) * 4 + yy) * 2 + (1 - c if cross else c)

    sibling = me + 1 - 2 * c
    plane = x * 4 + y
    xl, yl = lax.rem(x, 2), lax.rem(y, 2)
    xh, yh = x // 2, y // 2

    barrier = pltpu.get_barrier_semaphore()
    peers = [sibling]
    peers += [device({"x": i, "y": j}) for i in range(4) for j in range(4) if i + j > 0]
    peers += [device({"z": i}) for i in (1, 2, 3)]
    peers += [device({axis: i}, 1) for axis in "xyz" for i in (1, 2, 3)]
    for peer in peers:
        pl.semaphore_signal(barrier, inc=1, device_id=(peer,), device_id_type=MESH)
    copies = Copies(send, recv)
    local = []

    def here(src, dst):
        copy = pltpu.make_async_copy(src, dst, loc.at[len(local)])
        copy.start()
        local.append(copy)
        return copy

    own = wa.at[z, x, y, c]
    pieces = ((kw, HALF, NARROW), (vw, HALF + NARROW, NARROW), (qw, 0, HALF), (ow, QKV, HALF))
    for src, at, count in pieces:
        mine = src.at[:, pl.ds(pl.multiple_of(c * count, count), count)]
        here(mine, own.at[:, pl.ds(at, count)])
    here(tok, tok2.at[c])
    here(maps.at[pl.ds(c * 16, 16)], fq)
    here(og, ogx.at[pl.ds(0, ROWS)])
    here(og, ogo)

    pl.semaphore_wait(barrier, len(peers))
    first = []
    for src, at, count in pieces:
        other = src.at[:, pl.ds(pl.multiple_of((1 - c) * count, count), count)]
        first.append(copies.start(other, own.at[:, pl.ds(at, count)], sibling))
    tok_copy = copies.start(tok, tok2.at[c], sibling)
    where = {"z": z, "x": x, "y": y, "c": c}
    pending = [local[:4] + first]

    def settled():
        if pending:
            done = pending.pop()
            for copy in done[:4]:
                copy.wait()
            for copy in done[4:]:
                copy.wait_recv()

    streams = {
        "kv": Heads(copies, wa, where, device, settled, (("xzy", kw, 0, HALF, NARROW), ("yzx", vw, 0, HALF + NARROW, NARROW))),
        "q": Heads(copies, wa, where, device, settled, (("xzy", qw, 0, 0, 512), ("yzx", qw, 512, 0 + 512, 512))),
        "o": Heads(copies, wa, where, device, settled, (("zxy", ow, 0, QKV, 512), ("zyx", ow, 512, QKV + 512, 512))),
        "d": Units(
            copies, here, wf, stage, where, device, sibling,
            (("xy", dw, 0, 2 * SLICE, 768), ("yx", dw, 768, 2 * SLICE + 768, 640)),
        ),
        "g": Units(copies, here, wf, stage, where, device, sibling, (("xy", gw, 0, 0, SLICE),)),
        "u": Units(copies, here, wf, stage, where, device, sibling, (("yx", uw, 0, SLICE, SLICE),)),
    }
    waiting = {}

    def advance(name):
        stream, step = name.split(".")
        stream = streams[stream]
        {"b": stream.begin, "m": stream.middle, "e": stream.end}[step[0]](int(step[1]))

    for name in EARLY:
        advance(name)

    for k, src in enumerate((gain_a, gain_b)):
        g = src[...].astype(F32)
        gains[k : k + 1, :] = jnp.concatenate([g[i : i + 1] for i in range(16)], 1)
    gain1, gain2 = gains.at[pl.ds(0, 1)], gains.at[pl.ds(1, 1)]

    def below(parts, rows, count):
        got = [part.astype(F32) for part in parts]
        used = RANK * len(parts)
        return jnp.concatenate(got + [jnp.zeros((rows - used, count), F32)], 0).astype(BF)

    aall[...] = below([qa[...], ka[...], va[...]], 128, WIDTH)
    half = pl.ds(pl.multiple_of(c * HALF, HALF), HALF)
    narrow = pl.ds(pl.multiple_of(c * NARROW, NARROW), NARROW)
    none = jnp.zeros((RANK, NARROW), F32)
    ball[:, :HALF] = below([2.0 * qb[:, half].astype(F32)], 128, HALF)
    ball[:, HALF : HALF + NARROW] = below([none, 2.0 * kb[:, narrow].astype(F32)], 128, NARROW)
    ball[:, HALF + NARROW :] = below([none, none, 2.0 * vb[:, narrow].astype(F32)], 128, NARROW)
    oac[...] = below([oa[:, half]], 128, HALF)
    ob2[...] = below([2.0 * ob[...].astype(F32)], 128, WIDTH)

    chip = me // 2
    starts, ends, total = [], [], jnp.int32(0)
    for k in range(8):
        starts.append(total)
        total = total + ((lens[k] + (STRETCH - 1)) >> 6)
        ends.append(total)

    def sequence(stretch):
        found = jnp.where(stretch >= ends[0], 1, 0)
        for k in range(1, 7):
            found = found + jnp.where(stretch >= ends[k], 1, 0)
        return found

    counts, gates = [], []
    for s in range(4):
        stretch = chip * 4 + s
        begin, length = starts[0], lens[0]
        for k in range(1, 8):
            inside = stretch >= starts[k]
            begin = jnp.where(inside, starts[k], begin)
            length = jnp.where(inside, lens[k], length)
        counts.append(length - (stretch - begin) * STRETCH)
        gates.append(jnp.where(stretch != begin, 1.0, 0.0))
    first_own, last_own = sequence(chip * 4), sequence(chip * 4 + 3)
    k16 = lax.broadcasted_iota(jnp.int32, (16, 128), 0)
    firsts = sequence((z * 16 + k16) * 4)
    lasts = sequence((z * 16 + k16) * 4 + 3)
    masks[0] = jnp.where((k16 < plane) & (lasts == first_own), 1.0, 0.0)
    masks[1] = jnp.where(lasts == sequence(z * 64 + 63), 1.0, 0.0)
    masks[2] = jnp.where((k16 > plane) & (firsts == last_own), 1.0, 0.0)
    masks[3] = jnp.where(firsts == sequence(z * 64), 1.0, 0.0)
    k8 = lax.broadcasted_iota(jnp.int32, (8, 128), 0)
    far_masks[0] = jnp.where((k8 < z) & (sequence(k8 * 64 + 63) == first_own), 1.0, 0.0)
    far_masks[1] = jnp.where((k8 > z) & (sequence(k8 * 64) == last_own), 1.0, 0.0)
    lane = lax.broadcasted_iota(jnp.int32, (1, 128), 1)
    low_lane = lane < 64
    in_stretch = lax.rem(lane, STRETCH)
    valid = jnp.concatenate(
        [jnp.where(in_stretch < jnp.where(low_lane, counts[2 * p], counts[2 * p + 1]), 1.0, 0.0) for p in range(2)], 1
    )
    iu = lax.broadcasted_iota(jnp.int32, (128, 128), 0)
    it = lax.broadcasted_iota(jnp.int32, (128, 128), 1)
    for p in range(2):
        room = jnp.where(iu < 64, counts[2 * p], counts[2 * p + 1])
        seen = (iu <= it) & ((iu < 64) == (it < 64)) & (lax.rem(iu, STRETCH) < room)
        bias[p] = jnp.where(seen, 0.0, -1e30)

    for copy in local[4:8]:
        copy.wait()
    tok_copy.wait_recv()

    def norm_rows(i, carry):
        rows = pl.ds(i * 32, 32)
        for side in range(2):
            t = tok2[side, rows, :].astype(F32)
            r = lax.rsqrt(jnp.mean(t * t, -1, keepdims=True) + EPSILON)
            r1[side, rows, :] = jnp.broadcast_to(r, (32, 128))
            hid1[pl.ds(side * ROWS + i * 32, 32), :] = (t * r * gain1[...]).astype(BF)
        return carry

    lax.fori_loop(0, ROWS // 32, norm_rows, 0)

    zero_low = jnp.zeros((), BF)

    def softmax_rows(logits):
        e = jnp.exp(logits - jnp.max(logits, 0, keepdims=True))
        return e / jnp.sum(e, 0, keepdims=True)

    def gather_plane(base, folded):
        fsend[base] = folded.astype(BF)
        frecv[base, plane] = folded.astype(BF)
        fly = copies.group()
        for i in range(4):
            for j in range(4):
                if i + j > 0:
                    fly.start(fsend.at[base], frecv.at[base, plane], device({"x": i, "y": j}))
        return fly

    def fold_plane(base, fly):
        fly.wait(frecv.at[base, pl.ds(0, 15)])
        whole = jnp.zeros((AUG, 128), F32)
        for k in range(16):
            whole += masks[2 * base + 1, k : k + 1, :] * frecv[base, k].astype(F32)
        hsend[base] = whole.astype(BF)
        fly = copies.group()
        for i in (1, 2, 3):
            fly.start(hsend.at[base], hrecv.at[base, i - 1], device({"z": i}))
        part = jnp.zeros((AUG, 128), F32)
        for k in range(16):
            part += masks[2 * base, k : k + 1, :] * frecv[base, k].astype(F32)
        return part, fly

    def fold_line(base, part, fly):
        fly.wait(hrecv.at[base])
        for i in (1, 2, 3):
            part += far_masks[base, pl.ds(wrap(z + 4 - i), 1), :] * hrecv[base, i - 1].astype(F32)
        return part

    def combine(states):
        for g in range(2):
            for p in range(2):
                one, two = states[2 * p], states[2 * p + 1]
                if g == 0:
                    both = jnp.where(low_lane, one, pltpu.roll(two, 64, 1))
                else:
                    both = jnp.where(low_lane, pltpu.roll(one, 64, 1), two)
                yield g * 2 + p, both

    def put_states(states, base):
        for k, both in combine(states):
            comb[base + k] = both.astype(BF)
            tall = jnp.concatenate([both, jnp.zeros((128 - AUG, 128), F32)], 0)
            comb_t[base + k] = tall.T.astype(BF)

    def share(src, dst):
        fly = copies.group()
        for i, j, r, n, at in SHARES:
            fly.start(src.at[pl.ds(r, n)], dst.at[pl.ds(at, n)], device({"x": i, "y": j}))
        return fly

    def lower():
        low[...] = nt(hid1[...], aall[...]).astype(BF)

    def keys():
        kv = nn(hid1[...], wa[:, :, :, :, :, HALF:QKV].reshape(WIDTH, 2 * NARROW))
        kv = (kv + nn(low[...], ball[:, HALF:QKV])).astype(BF)
        kv_t = kv.astype(F32).T.astype(BF)
        for g in range(2):
            keep = low_lane if g == 0 else ~low_lane
            knat[g] = jnp.where(keep, kv[:, :NARROW], jnp.zeros((), BF))
            vnat[g] = jnp.where(keep, kv[:, NARROW:], jnp.zeros((), BF))
            kt[g] = kv_t[g * HEAD : (g + 1) * HEAD]
            tail = lax.broadcasted_iota(jnp.int32, (64, CHIP), 0) == 0
            vt[g, :HEAD] = kv_t[NARROW + g * HEAD : NARROW + (g + 1) * HEAD]
            vt[g, HEAD:] = tail.astype(F32).astype(BF)
        lanes4 = lax.broadcasted_iota(jnp.int32, (1, CHIP), 1) // STRETCH

        for g in range(2):
            kfeat[g * HEAD : (g + 1) * HEAD] = softmax_rows(tn(fk[c * 2 + g], kt[g])) * valid
        kf = kfeat[...]
        kf_high = kf.astype(BF)
        kf_rest = (kf - kf_high.astype(F32)).astype(BF)
        for s in range(4):
            got = []
            for g in range(2):
                va = jnp.where(lanes4 == s, vt[g, :AUG], jnp.zeros((), BF))
                got.append(nt(va, kf_high) + nt(va, kf_rest))
            st[s] = jnp.where(low_lane, got[0], got[1])


    def send_plane():
        folded = st[0]
        for s in (1, 2, 3):
            folded = st[s] + gates[s] * folded
        waiting["plane"] = gather_plane(0, folded)

    def send_line():
        waiting["part"], waiting["line"] = fold_plane(0, waiting["plane"])

    def take_line():
        prefix = fold_line(0, waiting["part"], waiting["line"])
        states = [prefix]
        for s in (1, 2, 3):
            states.append(gates[s] * (states[s - 1] + st[s - 1]))
        put_states(states, 0)

    def queries():
        def query_columns(n, carry):
            cols = pl.ds(pl.multiple_of(n * 256, 256), 256)
            q = nn(hid1[...], wa[:, :, :, :, :, cols].reshape(WIDTH, 256)) + nn(low[...], ball[:, cols])
            qt[cols, :] = q.T.astype(BF)
            return carry

        lax.fori_loop(0, 4, query_columns, 0)

    def lanes(parts):
        return jnp.concatenate(parts, 1)

    def split(wide):
        return [wide[:, k * 128 : (k + 1) * 128] for k in range(4)]

    def attend_four(n, carry):
        g = n // 2
        rows = [pl.ds(pl.multiple_of(n * 256 + k * HEAD, HEAD), HEAD) for k in range(4)]
        for k in range(4):
            qfeat[rows[k], :] = softmax_rows(tn(fq[n * 4 + k], qt[rows[k], :]))
        for p in range(2):
            cols = slice(p * 128, (p + 1) * 128)
            q = lanes([qt[r, cols] for r in rows])
            scores = split(nn(knat[g, cols, :], jnp.concatenate([q, q], 0)))
            stacks = []
            for k in range(4):
                sc = scores[k] * 0.125 + bias[p]
                peak = jnp.max(sc, 0, keepdims=True)
                w = jnp.exp(sc - peak).astype(BF)
                wts[(n * 4 + k) * 2 + p] = w
                dm = jnp.exp(-peak)
                damp[(n * 4 + k) * 2 + p, :1] = dm
                dq = (qfeat[rows[k], cols] * dm).astype(BF)
                stacks.append(
                    jnp.concatenate([w, jnp.where(low_lane, dq, zero_low), jnp.where(low_lane, zero_low, dq)], 0)
                )
            lhs = jnp.concatenate([vt[g, :AUG, cols], comb[g * 2 + p]], 1)
            both = split(nn(lhs, lanes(stacks)))
            for k in range(4):
                rden = 1.0 / both[k][HEAD : HEAD + 1]
                den[(n * 4 + k) * 2 + p, :1] = rden
                mixf[rows[k], cols] = both[k][:HEAD] * rden
        return carry

    def attend():
        lax.fori_loop(0, 4, attend_four, 0)


    def project():
        def mix_rows(n, carry):
            cols = pl.ds(pl.multiple_of(n * 256, 256), 256)
            mixn[:, cols] = mixf[cols, :].T.astype(BF)
            return carry

        lax.fori_loop(0, 4, mix_rows, 0)
        lowo[...] = nt(mixn[...], oac[...]).astype(BF)

        def out_columns(n, carry):
            cols = pl.ds(pl.multiple_of(n * 256, 256), 256)
            w = wa[n // 2, pl.ds(pl.multiple_of(lax.rem(n, 2) * 2, 2), 2), :, :, :, QKV:ATT].reshape(256, HALF)
            o = nt(mixn[...], w) + nn(lowo[...], ob2[:, cols])
            mine = jnp.where(c == 0, o[:ROWS], o[ROWS:])
            other = jnp.where(c == 0, o[ROWS:], o[:ROWS])
            mid[:, cols] = mine + tok2[c, :, cols].astype(F32)
            outs[:, cols] = other.astype(BF)
            return carry

        waiting["out"] = []
        for at in (0, 4):
            lax.fori_loop(at, at + 4, out_columns, 0)
            cols = pl.ds(at * 256, HALF)
            waiting["out"].append(copies.start(outs.at[:, cols], outr.at[:, cols], sibling))

    def middle():
        for copy in waiting["out"]:
            copy.wait_recv()

        def middle_rows(i, carry):
            rows = pl.ds(i * 32, 32)
            m = mid[rows, :] + outr[rows, :].astype(F32)
            mid[rows, :] = m
            r = lax.rsqrt(jnp.mean(m * m, -1, keepdims=True) + EPSILON)
            ht[rows, :] = (m * r * gain2[...]).astype(BF)
            return carry

        lax.fori_loop(0, ROWS // 32, middle_rows, 0)

    def send_hidden():
        waiting["ht"] = share(ht, ht)

    def send_gradient():
        waiting["og"] = share(ogo, ogx)

    def arrived(name):
        waiting[name].wait(ogx.at[pl.ds(ROWS, 384)])

    def ff_cols(first, count):
        return wf[:, :, :, :, :, :, :, pl.ds(first, count)].reshape(WIDTH, count)

    def inner_gradient():
        gg[...] = nn(ogx[...], ff_cols(2 * SLICE, SLICE)).astype(BF)

    def activate(gate, up, rows, cols):
        s = 0.5 * jnp.tanh(0.5 * gate) + 0.5
        swish = gate * s
        inner[rows, cols] = (swish * up).astype(BF)
        d = gg[rows, cols].astype(F32)
        gg[rows, cols] = (d * up * s * (1.0 + gate * (1.0 - s))).astype(BF)
        ug[rows, cols] = (d * swish).astype(BF)

    owned, own_chunks = slice(0, ROWS), ((0, 512), (512, 512), (1024, 384))

    def own_gate():
        for at, count in own_chunks:
            gown[:, at : at + count] = nn(ht[owned, :], ff_cols(at, count))

    def own_up():
        for at, count in own_chunks:
            cols = slice(at, at + count)
            activate(gown[:, cols], nn(ht[owned, :], ff_cols(SLICE + at, count)), owned, cols)

    steps = {
        "low": lower,
        "kvc": keys,
        "pls": send_plane,
        "lns": send_line,
        "lnw": take_line,
        "qc": queries,
        "att": attend,
        "oproj": project,
        "mid": middle,
        "hts": send_hidden,
        "htw": lambda: arrived("ht"),
        "ogs": send_gradient,
        "ogw": lambda: arrived("og"),
        "ds": streams["d"].settle,
        "gs": streams["g"].settle,
        "us": streams["u"].settle,
        "ig": inner_gradient,
        "go": own_gate,
        "uo": own_up,
    }
    for name in PLAN:
        if "." in name:
            advance(name)
        else:
            steps[name]()
    og_fly, ht_fly, out_copy = waiting["og"], waiting["ht"], waiting["out"]

    others = slice(ROWS, 512)
    for at, count in ((0, 512), (512, 512), (1024, 256)):
        cols = slice(at, at + count)
        gate, up = nn(ht[others, :], ff_cols(at, count)), nn(ht[others, :], ff_cols(SLICE + at, count))
        activate(gate, up, others, cols)
    both = nn(ht[others, :], jnp.concatenate([ff_cols(1280, 128), ff_cols(SLICE + 1280, 128)], 1))
    activate(both[:, :128], both[:, 128:], others, slice(1280, SLICE))

    def ff_rows(n, at):
        return wf[n // 2, lax.rem(n, 2), :, :, :, :, :, pl.ds(at, SLICE)].reshape(256, SLICE)

    copies.sent(ht_fly.members)
    copies.sent(og_fly.members)

    def two_columns(n, carry):
        cols = pl.ds(pl.multiple_of(n * 256, 256), 256)
        ogx[:, cols] = (nt(gg[...], ff_rows(n, 0)) + nt(ug[...], ff_rows(n, SLICE))).astype(BF)
        return carry

    def give_back(src, dst, cols):
        fly = copies.group()
        for k, (i, j, r, n, at) in enumerate(SHARES):
            there = dst.at[k // 2 - (k > 5), pl.ds(r, n), cols]
            fly.start(src.at[pl.ds(at, n), cols], there, device({"x": (4 - i) % 4, "y": (4 - j) % 4}))
        return [(fly, dst.at[:, :, cols])]

    def two_step(n, carry):
        two_columns(n, carry)
        cols = pl.ds(pl.multiple_of(n * 256, 256), 256)
        for k, (i, j, r, count, at) in enumerate(SHARES):
            pltpu.make_async_remote_copy(
                src_ref=ogx.at[pl.ds(at, count), cols],
                dst_ref=rbt.at[k // 2 - (k > 5), pl.ds(r, count), cols],
                send_sem=two_send.at[n],
                recv_sem=two_recv.at[n],
                device_id=(device({"x": (4 - i) % 4, "y": (4 - j) % 4}),),
                device_id_type=MESH,
            ).start()
        return carry

    lax.fori_loop(0, 8, two_step, 0)

    def two_wait(n, carry):
        cols = pl.ds(pl.multiple_of(n * 256, 256), 256)
        here_to = ogx.at[pl.ds(ROWS, 384), cols]
        pltpu.make_async_copy(here_to, here_to, two_send.at[n]).wait()
        come = rbt.at[:, :, cols]
        pltpu.make_async_copy(come, come, two_recv.at[n]).wait()
        return carry

    def block_columns(n, carry):
        cols = pl.ds(pl.multiple_of(n * 256, 256), 256)
        ht[:, cols] = nt(inner[...], ff_rows(n, 2 * SLICE)).astype(BF)
        return carry

    lax.fori_loop(0, 6, block_columns, 0)
    blk_fly = give_back(ht, rbb, pl.ds(0, 1536))
    lax.fori_loop(6, 8, block_columns, 0)
    lax.fori_loop(0, 8, two_wait, 0)

    def middle_back(i, acc):
        rows = pl.ds(i * 16, 16)
        t = ogx[rows, :].astype(F32)
        for k in range(3):
            t += rbt[k, rows, :].astype(F32)
        m = mid[rows, :]
        r = lax.rsqrt(jnp.mean(m * m, -1, keepdims=True) + EPSILON)
        n = m * r
        acc += jnp.sum(t * n, 0, keepdims=True)
        t = t * gain2[...]
        g = ogo[rows, :].astype(F32) + r * (t - n * jnp.mean(t * n, -1, keepdims=True))
        mgrad[rows, :] = g
        bg[c, rows, :] = g.astype(BF)
        return acc

    gain_mlp = jnp.zeros((1, WIDTH), F32)
    bg_fly = []
    for at in (0, ROWS // 2):
        gain_mlp = lax.fori_loop(at // 16, at // 16 + ROWS // 32, middle_back, gain_mlp)
        part = bg.at[c, pl.ds(at, ROWS // 2)]
        bg_fly.append(copies.start(part, part, sibling))
    for copy in bg_fly:
        copy.wait_recv()
    bgv = bg.at[:, :, :]
    olg = nt(bgv[...].reshape(CHIP, WIDTH), ob2[...])
    olg_low = olg.astype(BF)

    def mixed_columns(n, carry):
        cols = pl.ds(pl.multiple_of(n * 256, 256), 256)
        wcols = pl.ds(pl.multiple_of(QKV + n * 256, 256), 256)
        m = nn(bg[...].reshape(CHIP, WIDTH), wa[:, :, :, :, :, wcols].reshape(WIDTH, 256))
        m += nn(olg_low, oac[:, cols])
        ngt[cols, :] = m.T.astype(BF)
        return carry

    lax.fori_loop(0, 4, mixed_columns, 0)
    for k in range(4):
        sig[k] = jnp.zeros((AUG, 128), F32)

    def states_four(n, carry):
        g = n // 2
        rows = [pl.ds(pl.multiple_of(n * 256 + k * HEAD, HEAD), HEAD) for k in range(4)]
        for p in range(2):
            cols = slice(p * 128, (p + 1) * 128)
            left, right = [], []
            for k in range(4):
                h = (n * 4 + k) * 2 + p
                rden = den[h, :1]
                m = ngt[rows[k], cols].astype(F32)
                ng = (m * rden).astype(BF)
                dg = -jnp.sum(m * mixf[rows[k], cols], 0, keepdims=True) * rden
                ngt[rows[k], cols] = ng
                dgr[h, :1] = dg
                dq = (qfeat[rows[k], cols] * damp[h, :1]).astype(BF)
                right.append(jnp.concatenate([jnp.where(low_lane, dq, zero_low), jnp.where(low_lane, zero_low, dq)], 0))
                tail = jnp.where(lax.broadcasted_iota(jnp.int32, (AUG - HEAD, 128), 0) == 0, dg, 0.0).astype(BF)
                left.append(jnp.concatenate([ng, tail], 0))
            sig[g * 2 + p] = sig[g * 2 + p] + nt(lanes(left), lanes(right))
        return carry

    lax.fori_loop(0, 4, states_four, 0)
    sg_states = []
    for p in range(2):
        a, b = sig[p], sig[2 + p]
        sg_states.append(jnp.where(low_lane, a, pltpu.roll(b, 64, 1)))
        sg_states.append(jnp.where(low_lane, pltpu.roll(a, 64, 1), b))
    for s in range(4):
        st[s] = sg_states[s]
    folded = sg_states[3]
    for s in (2, 1, 0):
        folded = sg_states[s] + gates[s + 1] * folded
    fly = gather_plane(1, folded)
    blk_fly += give_back(ht, rbb, pl.ds(1536, 512))

    for k in range(4):
        kacc[k] = jnp.zeros((HEAD, 128), F32)
        vacc[k] = jnp.zeros((HEAD, 128), F32)

    def back_four(n, carry):
        g = n // 2
        rows = [pl.ds(pl.multiple_of(n * 256 + k * HEAD, HEAD), HEAD) for k in range(4)]
        for p in range(2):
            cols = slice(p * 128, (p + 1) * 128)
            ngs = lanes([ngt[r, cols] for r in rows])
            dgs = [dgr[(n * 4 + k) * 2 + p, :1] for k in range(4)]
            dg = lanes(dgs)
            ws = lanes([wts[(n * 4 + k) * 2 + p] for k in range(4)])
            pt = nn(vnat[g, cols, :], jnp.concatenate([ngs, ngs], 0)) + dg
            sgr = (ws.astype(F32) * pt).astype(BF)
            tail = jnp.where(lax.broadcasted_iota(jnp.int32, (HEAD, 512), 0) == 0, dg, 0.0).astype(BF)
            both = split(nn(comb_t[g * 2 + p], jnp.concatenate([ngs, tail], 0)))
            for k in range(4):
                qg = jnp.where(low_lane, both[k][:HEAD], both[k][HEAD:]) * damp[(n * 4 + k) * 2 + p, :1]
                f = qfeat[rows[k], cols]
                qlg[rows[k], cols] = (f * (qg - jnp.sum(f * qg, 0, keepdims=True))).astype(BF)
            near = split(nn(kt[g, :, cols], sgr))
            for k in range(4):
                far = nn(fq[n * 4 + k], qlg[rows[k], cols])
                gt[rows[k], cols] = (near[k] * 0.125 + far).astype(BF)
            kacc[g * 2 + p] = kacc[g * 2 + p] + nt(lanes([qt[r, cols] for r in rows]), sgr)
            vacc[g * 2 + p] = vacc[g * 2 + p] + nt(ngs, ws)
        return carry

    lax.fori_loop(0, 4, back_four, 0)
    early = Sums(copies, device, (x, y, z, c), sibling, (e_own, e_got, e_line, e_all), EARLY_BLOCKS)
    late = Sums(copies, device, (x, y, z, c), sibling, (l_own, l_got, l_line, l_all), LATE_BLOCKS)
    lowo_t = lowo[...].astype(F32).T.astype(BF)
    olg_t = olg.T.astype(BF)
    low_t = low[...].astype(F32).T.astype(BF)
    lowg_q = nn(ball[:16, :HALF], gt[:HALF, :]).astype(BF)
    grads = jnp.concatenate(
        [nn(lowg_q, hid1[...])[:8], 2.0 * nn(lowo_t[:16], bg[...].reshape(CHIP, WIDTH))[:8]], 0
    )
    for j in range(16):
        early.put(40 + j, grads[:, j * 128 : (j + 1) * 128])
    grads = jnp.concatenate([2.0 * nt(low_t[:16], gt[:HALF, :])[:8], nn(olg_t[:16], mixn[...])[:8]], 0)
    for j in range(8):
        early.put(32 + j, grads[:, j * 128 : (j + 1) * 128])
    early.put(56, jnp.concatenate([gain_mlp[:, k * 128 : (k + 1) * 128] for k in range(16)], 0))
    for k in range(57, 64):
        early.put(k, jnp.zeros((16, 128), F32))

    def grad_rows(n, carry):
        rows = pl.ds(pl.multiple_of(n * 256, 256), 256)
        gnat[:, rows] = gt[rows, :].astype(F32).T.astype(BF)
        return carry

    lax.fori_loop(0, 4, grad_rows, 0)

    def feat_pairs(n, carry):
        rows = pl.ds(pl.multiple_of(n * 128, 128), 128)
        r = nt(qt[rows, :], qlg[rows, :])
        r = jnp.where(low_lane, r[:HEAD], r[HEAD:]).astype(BF)
        for k in range(4):
            e_own[2 * k + n // 4, :, pl.ds(pl.multiple_of(lax.rem(n, 4) * 128, 128), 128)] = r[k * 16 : (k + 1) * 16]
        return carry

    lax.fori_loop(0, 8, feat_pairs, 0)

    early.scatter()
    part, fly = fold_plane(1, fly)

    def one_queries(n, carry):
        w = wa[n // 2, pl.ds(pl.multiple_of(lax.rem(n, 2) * 2, 2), 2), :, :, :, 0:HALF].reshape(256, HALF)
        o = nt(gnat[:, :HALF], w)
        rows = pl.ds(pl.multiple_of(lax.rem(n, 4) * 256, 256), 256)

        @pl.when(n < 4)
        def _():
            qfeat[rows, :] = o

        @pl.when(n >= 4)
        def _():
            mixf[rows, :] = o

        return carry

    lax.fori_loop(0, 8, one_queries, 0)
    suffix = fold_line(1, part, fly)
    states = [None, None, None, suffix]
    for s in (2, 1, 0):
        states[s] = gates[s + 1] * (states[s + 1] + st[s + 1])
    put_states(states, 4)

    for g in range(2):
        f_rows = slice(g * HEAD, (g + 1) * HEAD)
        for p in range(2):
            k = g * 2 + p
            cols = slice(p * 128, (p + 1) * 128)
            f = kfeat[f_rows, cols]
            both = nn(comb_t[4 + k], vt[g, :, cols])
            fg = jnp.where(low_lane, both[:HEAD], both[HEAD:]) * valid[:, cols]
            kl = (f * (fg - jnp.sum(f * fg, 0, keepdims=True))).astype(BF)
            qlg[HALF + g * HEAD : HALF + (g + 1) * HEAD, cols] = kl
            gt[HALF + g * HEAD : HALF + (g + 1) * HEAD, cols] = (kacc[k] * 0.125 + nn(fk[c * 2 + g], kl)).astype(BF)
            fl = f.astype(BF)
            stack = jnp.concatenate([jnp.where(low_lane, fl, zero_low), jnp.where(low_lane, zero_low, fl)], 0)
            gt[HALF + NARROW + g * HEAD : HALF + NARROW + (g + 1) * HEAD, cols] = (
                vacc[k] + nn(comb[4 + k, :HEAD], stack)
            ).astype(BF)

    lowg_t = nn(ball[...], gt[...])
    lowg[...] = lowg_t.T.astype(BF)
    lowg_t = lowg_t.astype(BF)

    grad_rows(4, 0)

    def one_columns(n, had):
        cols = pl.ds(pl.multiple_of(n * 256, 256), 256)
        w = wa[n // 2, pl.ds(pl.multiple_of(lax.rem(n, 2) * 2, 2), 2), :, :, :, HALF:QKV].reshape(256, 2 * NARROW)
        o = had[pl.ds(pl.multiple_of(lax.rem(n, 4) * 256, 256), 256), :]
        o = o + nt(gnat[:, HALF:], w) + nn(lowg[...], aall[:, cols])
        normed = [tok2[side, :, cols].astype(F32) * r1[side, :, :1] for side in range(2)]
        gain = jnp.sum(o[:ROWS] * normed[0] + o[ROWS:] * normed[1], 0, keepdims=True)
        gsum[pl.ds(2 * n, 1), :] = gain[:, :128]
        gsum[pl.ds(2 * n + 1, 1), :] = gain[:, 128:]
        ones[:, cols] = jnp.where(c == 0, o[:ROWS], o[ROWS:])
        outs[:, cols] = jnp.where(c == 0, o[ROWS:], o[:ROWS]).astype(BF)

    def one_first(n, carry):
        one_columns(n, qfeat)
        return carry

    def one_second(n, carry):
        one_columns(n, mixf)
        return carry

    r = nt(kt[...].reshape(128, CHIP), qlg[HALF:, :])
    r = jnp.where(low_lane, r[:HEAD], r[HEAD:])
    for k in range(4):
        late.put(k, r[k * 16 : (k + 1) * 16])
    up = 2.0 * nt(low_t[:32], gt[HALF:, :])
    late.put(4, jnp.concatenate([up[8:16, :NARROW], up[16:24, NARROW:]], 0))
    down = nn(lowg_t[:32], hid1[...])
    for j in range(16):
        late.put(5 + j, down[8:24, j * 128 : (j + 1) * 128])
    for k in range(21, 32):
        late.put(k, jnp.zeros((16, 128), F32))
    late.scatter()

    copies.sent(out_copy)
    lax.fori_loop(0, 4, one_first, 0)
    lax.fori_loop(4, 8, one_second, 0)
    one_copy = copies.start(outs, outr, sibling)

    gplane[plane] = gsum[...]
    gain_fly = copies.group()
    for i, j in early.others():
        gain_fly.start(gsum, gplane.at[plane], device({"x": i, "y": j}))
    early.along()
    late.along()
    one_copy.wait_recv()
    copies.sent([one_copy])

    def token_rows(i, carry):
        rows = pl.ds(i * 16, 16)
        o = ones[rows, :] + outr[rows, :].astype(F32)
        t = tok2[c, rows, :].astype(F32)
        r = r1[c, rows, :1]
        n = t * r
        o = o * gain1[...]
        outs[rows, :] = (mgrad[rows, :] + r * (o - n * jnp.mean(o * n, -1, keepdims=True))).astype(BF)
        return carry

    lax.fori_loop(0, ROWS // 32, token_rows, 0)
    early.gather()
    gain_fly.wait(gplane.at[pl.ds(0, 15)])
    total = gplane[0]
    for k in range(1, 16):
        total += gplane[k]
    gline[z, c] = total
    mine = gline.at[z, c]
    same, cross = copies.group(), copies.group()
    for i in (1, 2, 3):
        same.start(mine, mine, device({"z": i}))
    for i in range(4):
        cross.start(mine, mine, device({"z": i}, 1))
    late.gather()
    for fly, ref in blk_fly:
        fly.wait(ref)

    def block_rows(i, carry):
        rows = pl.ds(i * 16, 16)
        t = mid[rows, :] + ht[rows, :].astype(F32)
        for k in range(3):
            t += rbb[k, rows, :].astype(F32)
        ht[rows, :] = t.astype(BF)
        return carry

    copies.sent([copy for fly, ref in blk_fly for copy in fly.members])
    lax.fori_loop(0, ROWS // 16, block_rows, 0)
    here(ht.at[pl.ds(0, ROWS)], blk_out)
    lax.fori_loop(ROWS // 32, ROWS // 16, token_rows, 0)
    here(outs, gtok_out)
    same.wait(gline.at[pl.ds(0, 3), 0])
    cross.wait(gline.at[:, 0])
    total = gline[0, 0] + gline[0, 1]
    for k in range(1, 4):
        total += gline[k, 0] + gline[k, 1]
    gain_all[...] = total
    here(gain_all, gain_out)
    early.cross()
    here(e_all.at[c], early_out.at[c])
    late.cross()
    here(l_all.at[c], late_out.at[c])
    early.finish()
    here(e_all.at[1 - c], early_out.at[1 - c])
    late.finish()
    here(l_all.at[1 - c], late_out.at[1 - c])
    for copy in local[-7:]:
        copy.wait()
    copies.drain()


def finish(
    blk, gtok, early, late, gain,
    blk_out, gtok_out, gain_a_out, qa_out, qb_out, ka_out, kb_out, va_out, vb_out, oa_out, ob_out, fq_out, fk_out,
    gain_b_out, sem,
):
    copies = [pltpu.make_async_copy(a, b, sem.at[k]) for k, (a, b) in enumerate(((blk, blk_out), (gtok, gtok_out)))]
    for copy in copies:
        copy.start()

    def block(sums, share, side, k):
        return sums[side, k // share, :, (k % share) * 128 : (k % share + 1) * 128].astype(F32)

    def first(side, k):
        return block(early, EARLY_BLOCKS, side, k)

    def second(side, k):
        return block(late, LATE_BLOCKS, side, k)

    for side in range(2):
        at = side * HALF
        for k in range(4):
            rows = slice(k * 16, (k + 1) * 16)
            for j in range(9):
                v = first(side, k * 8 + j) if j < 8 else second(side, k)
                out, head = (fq_out, side * 16 + 2 * j) if j < 8 else (fk_out, side * 2)
                out[head, rows, :] = v[:, :64]
                out[head + 1, rows, :] = pltpu.roll(v, 64, 1)[:, :64]
        for j in range(8):
            cols = slice(at + j * 128, at + (j + 1) * 128)
            v = first(side, 32 + j)
            qb_out[:, cols] = v[:8]
            oa_out[:, cols] = v[8:]
        v = second(side, 4)
        kb_out[:, side * NARROW : (side + 1) * NARROW] = v[:8]
        vb_out[:, side * NARROW : (side + 1) * NARROW] = v[8:]
    for j in range(16):
        cols = slice(j * 128, (j + 1) * 128)
        v = first(0, 40 + j) + first(1, 40 + j)
        qa_out[:, cols] = v[:8]
        ob_out[:, cols] = v[8:]
        v = second(0, 5 + j) + second(1, 5 + j)
        ka_out[:, cols] = v[:8]
        va_out[:, cols] = v[8:]
    gain_a_out[...] = gain[...]
    gain_b_out[...] = first(0, 56) + first(1, 56)
    for copy in copies:
        copy.wait()


N_COPIES = 79
N_SENDS = 48


def scratch():
    v = pltpu.VMEM
    return [
        v((4, 4, 4, 2, 16, ATT), BF),
        v((4, 2, 2, 2, 2, 2, 16, 3 * SLICE), BF),
        v((2, 2, 16, 3 * SLICE), BF),
        v((2, ROWS, WIDTH), BF),
        v((QUERY_HEADS // 2, HEAD, HEAD), BF),
        v((ROWS, WIDTH), BF),
        v((8, WIDTH), F32),
        v((2, ROWS, 128), F32),
        v((128, WIDTH), BF),
        v((128, QKV), BF),
        v((128, HALF), BF),
        v((128, WIDTH), BF),
        v((4, 16, 128), F32),
        v((2, 8, 128), F32),
        v((2, 128, 128), F32),
        v((CHIP, WIDTH), BF),
        v((CHIP, 128), BF),
        v((HALF, CHIP), BF),
        v((2, HEAD, CHIP), BF),
        v((2, 128, CHIP), BF),
        v((2, CHIP, 128), BF),
        v((2, CHIP, 128), BF),
        v((128, CHIP), F32),
        v((4, AUG, 128), F32),
        v((8, AUG, 128), BF),
        v((8, 128, 128), BF),
        v((32, 128, 128), BF),
        v((HALF, CHIP), F32),
        v((HALF, CHIP), F32),
        v((32, 8, 128), F32),
        v((32, 8, 128), F32),
        v((CHIP, HALF), BF),
        v((CHIP, 128), BF),
        v((ROWS, WIDTH), BF),
        v((ROWS, WIDTH), BF),
        v((ROWS, WIDTH), F32),
        v((512, WIDTH), BF),
        v((512, WIDTH), BF),
        v((512, SLICE), BF),
        v((512, SLICE), BF),
        v((512, SLICE), BF),
        v((3, ROWS, WIDTH), BF),
        v((3, ROWS, WIDTH), BF),
        v((ROWS, WIDTH), F32),
        v((2, ROWS, WIDTH), BF),
        v((HALF, CHIP), BF),
        v((32, 8, 128), F32),
        v((4, AUG, 128), F32),
        v((HALF + 128, CHIP), BF),
        v((QKV, CHIP), BF),
        v((CHIP, QKV), BF),
        v((CHIP, 128), BF),
        v((ROWS, WIDTH), F32),
        v((4, HEAD, 128), F32),
        v((4, HEAD, 128), F32),
        v((2, AUG, 128), BF),
        v((2, 16, AUG, 128), BF),
        v((2, AUG, 128), BF),
        v((2, 3, AUG, 128), BF),
        v((ROWS, SLICE), F32),
        v((16, 16, EARLY_BLOCKS * 128), BF),
        v((16, 16, EARLY_BLOCKS * 128), BF),
        v((4, 16, EARLY_BLOCKS * 128), BF),
        v((2, 16, 16, EARLY_BLOCKS * 128), BF),
        v((16, 16, LATE_BLOCKS * 128), BF),
        v((16, 16, LATE_BLOCKS * 128), BF),
        v((4, 16, LATE_BLOCKS * 128), BF),
        v((2, 16, 16, LATE_BLOCKS * 128), BF),
        v((16, 128), F32),
        v((16, 16, 128), F32),
        v((4, 2, 16, 128), F32),
        v((16, 128), F32),
        pltpu.SemaphoreType.DMA((N_SENDS,)),
        pltpu.SemaphoreType.DMA((N_COPIES,)),
        pltpu.SemaphoreType.DMA((23,)),
        pltpu.SemaphoreType.DMA((8,)),
        pltpu.SemaphoreType.DMA((8,)),
    ]


def body(
    tokens, sequence_lengths, attention_gain, query_weight, key_weight, value_weight, output_weight_flipped,
    query_adapter_down, query_adapter_up, key_adapter_down, key_adapter_up, value_adapter_down, value_adapter_up,
    output_adapter_down, output_adapter_up, query_feature_map, key_feature_map, feedforward_gain,
    gate_weight, up_weight, down_weight_flipped, output_gradient,
):
    vmem = pl.BlockSpec(memory_space=pltpu.VMEM)
    smem = pl.BlockSpec(memory_space=pltpu.SMEM)
    anywhere = pl.BlockSpec(memory_space=pl.ANY)

    def array(*shape, dtype=F32):
        return jax.ShapeDtypeStruct(shape, dtype)

    parts = pl.pallas_call(
        kernel,
        out_shape=(
            array(ROWS, WIDTH, dtype=BF), array(ROWS, WIDTH, dtype=BF), array(2, 16, 16, EARLY_BLOCKS * 128, dtype=BF),
            array(2, 16, 16, LATE_BLOCKS * 128, dtype=BF),
            array(16, 128),
        ),
        in_specs=[anywhere, smem, vmem] + [anywhere] * 4 + [vmem] * 8 + [anywhere] + [vmem] * 2 + [anywhere] * 4,
        out_specs=(anywhere,) * 5,
        scratch_shapes=scratch(),
        compiler_params=pltpu.CompilerParams(
            collective_id=0, has_side_effects=True, vmem_limit_bytes=64 * 1024 * 1024
        ),
    )(
        tokens, sequence_lengths, attention_gain.reshape(16, 128),
        query_weight, key_weight, value_weight, output_weight_flipped,
        query_adapter_down.T, query_adapter_up, key_adapter_down.T, key_adapter_up, value_adapter_down.T,
        value_adapter_up, output_adapter_down.T, output_adapter_up, query_feature_map, key_feature_map,
        feedforward_gain.reshape(16, 128), gate_weight, up_weight, down_weight_flipped, output_gradient,
    )
    out = pl.pallas_call(
        finish,
        out_shape=(
            array(ROWS, WIDTH, dtype=BF), array(ROWS, WIDTH, dtype=BF), array(16, 128),
            array(RANK, WIDTH), array(RANK, WIDTH), array(RANK, WIDTH), array(RANK, 2 * NARROW),
            array(RANK, WIDTH), array(RANK, 2 * NARROW), array(RANK, WIDTH), array(RANK, WIDTH),
            array(QUERY_HEADS, HEAD, HEAD), array(KEY_VALUE_HEADS, HEAD, HEAD), array(16, 128),
        ),
        in_specs=[vmem] * 5,
        out_specs=(anywhere,) * 2 + (vmem,) * 12,
        scratch_shapes=[pltpu.SemaphoreType.DMA((2,))],
    )(*parts)
    (
        block_out, grad_tokens, gain_attn, qa, qb, ka, kb, va, vb, oa, ob, feat_q, feat_k, gain_mlp,
    ) = out
    return (
        block_out, grad_tokens, gain_attn.reshape(WIDTH), qa.T, qb, ka.T, kb, va.T, vb, oa.T, ob, feat_q, feat_k,
        gain_mlp.reshape(WIDTH),
    )


def solution(mesh):
    split, whole = P("seq", None), P()
    return jax.shard_map(
        body,
        mesh=mesh,
        in_specs=(
            (split, whole, whole) + (split,) * 4 + (whole,) * 11 + (split,) * 4
        ),
        out_specs=(split, split) + (whole,) * 12,
        check_vma=False,
    )
```

```python
import math

import jax
import jax.numpy as jnp
from jax import lax
from jax.experimental import pallas as pl
from jax.experimental.pallas import tpu as pltpu
from jax.sharding import PartitionSpec as P

QUERY_HEADS = 32
KEY_VALUE_HEADS = 4
HEAD = 64
STRETCH = 64
WIDTH = 2048
FF = 5632
ROWS = 128
CHIP = 256
HALF = 1024
NARROW = 128
QKV = HALF + 2 * NARROW
ATT = QKV + HALF
SLICE = FF // 4
AUG = 80
RANK = 8
EARLY_BLOCKS = 4
LATE_BLOCKS = 2
EPSILON = 1e-05
MESH = pl.DeviceIdType.MESH
F32 = jnp.float32
BF = jnp.bfloat16

SHARES = (
    (1, 0, 0, 64, 128),
    (3, 0, 64, 64, 192),
    (0, 1, 0, 64, 256),
    (0, 3, 64, 64, 320),
    (1, 1, 0, 32, 384),
    (1, 3, 32, 32, 416),
    (3, 1, 64, 32, 448),
    (3, 3, 96, 32, 480),
)


def nn(left, right):
    return jnp.dot(left, right, preferred_element_type=F32)


def tn(left, right):
    return lax.dot_general(left, right, (((0,), (0,)), ((), ())), preferred_element_type=F32)


def nt(left, right):
    return lax.dot_general(left, right, (((1,), (1,)), ((), ())), preferred_element_type=F32)


def wrap(value):
    return lax.rem(value, 4)


class Group:
    def __init__(self, copies, index):
        self.copies, self.index, self.members = copies, index, []

    def start(self, src, dst, device):
        self.members.append(self.copies.start(src, dst, device, self.index))

    def wait(self, ref):
        pltpu.make_async_copy(ref, ref, self.copies.recv.at[self.index]).wait()


class Copies:
    def __init__(self, send, recv):
        self.send, self.recv, self.count, self.open, self.indices = send, recv, 0, {}, 0

    def index(self):
        self.indices += 1
        return self.indices - 1

    def group(self):
        return Group(self, self.index())

    def start(self, src, dst, device, index=None):
        slot = self.count % N_SENDS
        if slot in self.open:
            self.open.pop(slot).wait_send()
        copy = pltpu.make_async_remote_copy(
            src_ref=src,
            dst_ref=dst,
            send_sem=self.send.at[slot],
            recv_sem=self.recv.at[self.index() if index is None else index],
            device_id=(device,),
            device_id_type=MESH,
        )
        self.count += 1
        copy.start()
        self.open[slot] = copy
        return copy

    def sent(self, copies):
        for slot in [k for k, copy in self.open.items() if any(copy is other for other in copies)]:
            self.open.pop(slot).wait_send()

    def drain(self):
        for copy in self.open.values():
            copy.wait_send()


class Heads:
    def __init__(self, copies, wa, where, device, settled, parts):
        self.copies, self.wa, self.where, self.device = copies, wa, where, device
        self.settled, self.parts = settled, parts
        self.flying = {}

    def block(self, order, phase, at, cols, core=slice(None)):
        index = []
        for axis in "zxy":
            k = order.index(axis)
            index.append(slice(None) if k < phase else at if k == phase else self.where[axis])
        return self.wa.at[index[0], index[1], index[2], core, :, cols]

    def begin(self, phase):
        c = self.where["c"]
        for part, (order, src, at, first, count) in enumerate(self.parts):
            axis = order[phase]
            cols = pl.ds(first, count)
            group = self.flying[phase, part] = self.copies.group()
            if phase == 0:
                for step in (1, 3, 2):
                    for cross in (0, 1):
                        core = 1 - c if cross else c
                        piece = src.at[:, pl.ds(pl.multiple_of(core * (src.shape[1] // 2) + at, 128), count)]
                        dst = self.wa.at[self.where["z"], self.where["x"], self.where["y"], c, :, cols]
                        group.start(piece, dst, self.device({axis: step}, cross))
            else:
                own = self.block(order, phase, self.where[axis], cols)
                for step in (1, 3):
                    group.start(own, own, self.device({axis: step}))

    def middle(self, phase):
        for part, (order, src, at, first, count) in enumerate(self.parts):
            axis = order[phase]
            cols = pl.ds(first, count)
            self.flying[phase, part].wait(self.block(order, phase, pl.ds(0, 2), cols))
            here = self.where[axis]
            left = self.block(order, phase, wrap(here + 3), cols, 0)
            right = self.block(order, phase, wrap(here + 1), cols, 1)
            group = self.flying[phase, part] = self.copies.group()
            group.start(left, left, self.device({axis: 1}))
            group.start(right, right, self.device({axis: 3}))

    def end(self, phase):
        self.settled()
        for part, (order, src, at, first, count) in enumerate(self.parts):
            at = pl.ds(0, 3) if phase == 0 else 0
            self.flying[phase, part].wait(self.block(order, phase, at, pl.ds(first, count)))


class Units:
    def __init__(self, copies, here, wf, stage, where, device, sibling, parts):
        self.copies, self.here, self.wf, self.stage = copies, here, wf, stage
        self.where, self.device, self.sibling, self.parts = where, device, sibling, parts
        self.flying, self.own = {}, []
        self.handed = [copies.group() for _ in parts]

    def rows(self, order, along, across, cols):
        w = self.where
        a = (slice(None), slice(None)) if along is None else (along // 2, lax.rem(along, 2))
        b = (across // 2, lax.rem(across, 2))
        x, y = (a, b) if order == "xy" else (b, a)
        return self.wf.at[w["z"], x[0], x[1], y[0], y[1], w["c"], :, cols]

    def line(self, z, cols):
        return self.wf.at[z, :, :, :, :, self.where["c"], :, cols]

    def hand_on(self, part, block):
        self.handed[part].start(block, block, self.sibling)

    def begin(self, phase):
        w = self.where
        for part, (order, src, at, first, count) in enumerate(self.parts):
            cols = pl.ds(first, count)
            a, b = order
            group = self.flying[phase, part] = self.copies.group()
            if phase == 0:
                for d in (1, 3, 2, 0):
                    for e in (0, 1):
                        pa, pb = lax.rem(w[a] + d, 2), lax.rem(w[b] + e, 2)
                        slot = pa * 2 + pb if order == "xy" else pb * 2 + pa
                        piece = src.at[:, pl.ds(pl.multiple_of(slot * SLICE + at, 128), count)]
                        if e == 0:
                            dst = self.rows(order, w[a], w[b], cols)
                        else:
                            dst = self.stage.at[w[a] // 2, lax.rem(w[a], 2), :, cols]
                        if d == 0:
                            self.own.append(self.here(piece, dst))
                        else:
                            group.start(piece, dst, self.device({a: d}))
            elif phase == 1:
                mine = self.rows(order, None, w[b], cols)
                other = self.stage.at[:, :, :, cols]
                group.start(other, mine, self.device({b: 1}))
                group.start(other, mine, self.device({b: 3}))
                group.start(mine, mine, self.device({b: 2}))
            else:
                block = self.line(w["z"], cols)
                self.hand_on(part, block)
                for step in (1, 3):
                    group.start(block, block, self.device({"z": step}))

    def some(self, phase, cols):
        if phase == 0:
            return self.wf.at[pl.ds(0, 3), 0, 0, 0, 0, :, :, cols]
        if phase == 1:
            return self.wf.at[pl.ds(0, 3), :, :, 0, 0, 0, :, cols]
        return self.wf.at[pl.ds(0, 2), :, :, :, :, 0, :, cols]

    def middle(self, phase):
        z = self.where["z"]
        for part, (order, src, at, first, count) in enumerate(self.parts):
            cols = pl.ds(first, count)
            self.flying[phase, part].wait(self.some(2, cols))
            one = (count // 256) * 128
            before, after = wrap(z + 3), wrap(z + 1)
            left = self.line(before, pl.ds(first, one))
            right = self.line(after, pl.ds(first + one, count - one))
            group = self.flying[phase, part] = self.copies.group()
            group.start(left, left, self.device({"z": 1}))
            group.start(right, right, self.device({"z": 3}))
            self.hand_on(part, self.line(before, cols))
            self.hand_on(part, self.line(after, cols))

    def end(self, phase):
        if phase == 0:
            for copy in self.own:
                copy.wait()
        for part, (order, src, at, first, count) in enumerate(self.parts):
            cols = pl.ds(first, count)
            self.flying[phase, part].wait(self.line(0, cols) if phase == 2 else self.some(phase, cols))
            if phase == 2:
                self.hand_on(part, self.line(wrap(self.where["z"] + 2), cols))

    def settle(self):
        for part, (order, src, at, first, count) in enumerate(self.parts):
            self.handed[part].wait(self.wf.at[:, :, :, :, :, 0, :, pl.ds(first, count)])


class Sums:
    def __init__(self, copies, device, at, sibling, buffers, share):
        self.copies, self.device, self.sibling, self.share = copies, device, sibling, share
        self.x, self.y, self.z, self.c = at
        self.plane = self.x * 4 + self.y
        self.own, self.got, self.line, self.all = buffers

    def put(self, k, value):
        self.own[k // self.share, :, (k % self.share) * 128 : (k % self.share + 1) * 128] = value.astype(BF)

    def others(self):
        return [(i, j) for i in range(4) for j in range(4) if i + j > 0]

    def scatter(self):
        self.fly = self.copies.group()
        for i, j in self.others():
            to = wrap(self.x + i) * 4 + wrap(self.y + j)
            self.fly.start(self.own.at[to], self.got.at[self.plane], self.device({"x": i, "y": j}))
        self.got[self.plane] = self.own[self.plane]

    def along(self):
        self.fly.wait(self.got.at[pl.ds(0, 15)])
        total = self.got[0].astype(F32)
        for k in range(1, 16):
            total += self.got[k].astype(F32)
        self.line[self.z] = total.astype(BF)
        mine = self.line.at[self.z]
        self.fly = self.copies.group()
        for i in (1, 2, 3):
            self.fly.start(mine, mine, self.device({"z": i}))

    def gather(self):
        self.fly.wait(self.line.at[pl.ds(0, 3)])
        total = self.line[0].astype(F32)
        for k in range(1, 4):
            total += self.line[k].astype(F32)
        self.all[self.c, self.plane] = total.astype(BF)
        piece = self.all.at[self.c, self.plane]
        self.fly = self.copies.group()
        for i, j in self.others():
            self.fly.start(piece, piece, self.device({"x": i, "y": j}))

    def cross(self):
        self.fly.wait(self.all.at[0, pl.ds(0, 15)])
        half = self.all.at[self.c]
        self.fly = self.copies.start(half, half, self.sibling)

    def finish(self):
        self.fly.wait_recv()


EARLY = ("kv.b0", "q.b0", "o.b0", "d.b0", "kv.e0", "u.b0", "g.b0", "kv.b1",)
PLAN = (
    "o.e0", "q.e0", "q.b1", "d.e0", "kv.m1", "d.b1", "o.b1", "q.m1", "kv.e1", "g.e0", "u.e0", "kv.b2",
    "d.e1", "d.b2", "q.e1", "o.m1", "g.b1", "u.b1", "kv.m2", "q.b2", "g.e1", "g.b2", "o.e1", "kv.e2",
    "low", "d.m2", "u.e1", "kvc", "pls", "o.b2", "lns", "q.m2", "u.b2", "o.m2", "g.m2", "d.e2",
    "lnw", "q.e2", "qc", "ogs", "att", "o.e2", "oproj", "mid", "u.m2", "hts", "g.e2", "ogw",
    "ds", "ig", "gs", "go", "u.e2", "us", "uo", "htw",
)


def kernel(
    tok, lens, gain_a, qw, kw, vw, ow, qa, qb, ka, kb, va, vb, oa, ob, maps, fk, gain_b, gw, uw, dw, og,
    blk_out, gtok_out, early_out, late_out, gain_out,
    wa, wf, stage, tok2, fq, ogo, gains, r1, aall, ball, oac, ob2, masks, far_masks, bias, hid1, low, qt, kt, vt, knat, vnat,
    kfeat, st, comb, comb_t, wts, qfeat, mixf, damp, den, mixn, lowo, outs, outr, mid, ht, ogx, gg, inner, ug, rbt, rbb,
    mgrad, bg, ngt, dgr, sig, qlg, gt, gnat, lowg, ones, kacc, vacc, fsend, frecv, hsend, hrecv,
    gown, e_own, e_got, e_line, e_all, l_own, l_got, l_line, l_all, gsum, gplane, gline, gain_all, send, recv, loc, two_send, two_recv,
):
    me = lax.axis_index("seq")
    c = lax.rem(me, 2)
    y = lax.rem(me // 2, 4)
    x = lax.rem(me // 8, 4)
    z = me // 32

    def device(steps, cross=0):
        zz, xx, yy = (wrap(v + steps.get(n, 0)) for n, v in (("z", z), ("x", x), ("y", y)))
        return ((zz * 4 + xx) * 4 + yy) * 2 + (1 - c if cross else c)

    sibling = me + 1 - 2 * c
    plane = x * 4 + y
    xl, yl = lax.rem(x, 2), lax.rem(y, 2)
    xh, yh = x // 2, y // 2

    barrier = pltpu.get_barrier_semaphore()
    peers = [sibling]
    peers += [device({"x": i, "y": j}) for i in range(4) for j in range(4) if i + j > 0]
    peers += [device({"z": i}) for i in (1, 2, 3)]
    peers += [device({axis: i}, 1) for axis in "xyz" for i in (1, 2, 3)]
    for peer in peers:
        pl.semaphore_signal(barrier, inc=1, device_id=(peer,), device_id_type=MESH)
    copies = Copies(send, recv)
    local = []

    def here(src, dst):
        copy = pltpu.make_async_copy(src, dst, loc.at[len(local)])
        copy.start()
        local.append(copy)
        return copy

    own = wa.at[z, x, y, c]
    pieces = ((kw, HALF, NARROW), (vw, HALF + NARROW, NARROW), (qw, 0, HALF), (ow, QKV, HALF))
    for src, at, count in pieces:
        mine = src.at[:, pl.ds(pl.multiple_of(c * count, count), count)]
        here(mine, own.at[:, pl.ds(at, count)])
    here(tok, tok2.at[c])
    here(maps.at[pl.ds(c * 16, 16)], fq)
    here(og, ogx.at[pl.ds(0, ROWS)])
    here(og, ogo)

    pl.semaphore_wait(barrier, len(peers))
    first = []
    for src, at, count in pieces:
        other = src.at[:, pl.ds(pl.multiple_of((1 - c) * count, count), count)]
        first.append(copies.start(other, own.at[:, pl.ds(at, count)], sibling))
    tok_copy = copies.start(tok, tok2.at[c], sibling)
    where = {"z": z, "x": x, "y": y, "c": c}
    pending = [local[:4] + first]

    def settled():
        if pending:
            done = pending.pop()
            for copy in done[:4]:
                copy.wait()
            for copy in done[4:]:
                copy.wait_recv()

    streams = {
        "kv": Heads(copies, wa, where, device, settled, (("xzy", kw, 0, HALF, NARROW), ("yzx", vw, 0, HALF + NARROW, NARROW))),
        "q": Heads(copies, wa, where, device, settled, (("xzy", qw, 0, 0, 512), ("yzx", qw, 512, 0 + 512, 512))),
        "o": Heads(copies, wa, where, device, settled, (("zxy", ow, 0, QKV, 512), ("zyx", ow, 512, QKV + 512, 512))),
        "d": Units(
            copies, here, wf, stage, where, device, sibling,
            (("xy", dw, 0, 2 * SLICE, 768), ("yx", dw, 768, 2 * SLICE + 768, 640)),
        ),
        "g": Units(copies, here, wf, stage, where, device, sibling, (("xy", gw, 0, 0, SLICE),)),
        "u": Units(copies, here, wf, stage, where, device, sibling, (("yx", uw, 0, SLICE, SLICE),)),
    }
    waiting = {}

    def advance(name):
        stream, step = name.split(".")
        stream = streams[stream]
        {"b": stream.begin, "m": stream.middle, "e": stream.end}[step[0]](int(step[1]))

    for name in EARLY:
        advance(name)

    for k, src in enumerate((gain_a, gain_b)):
        g = src[...].astype(F32)
        gains[k : k + 1, :] = jnp.concatenate([g[i : i + 1] for i in range(16)], 1)
    gain1, gain2 = gains.at[pl.ds(0, 1)], gains.at[pl.ds(1, 1)]

    def below(parts, rows, count):
        got = [part.astype(F32) for part in parts]
        used = RANK * len(parts)
        return jnp.concatenate(got + [jnp.zeros((rows - used, count), F32)], 0).astype(BF)

    aall[...] = below([qa[...], ka[...], va[...]], 128, WIDTH)
    half = pl.ds(pl.multiple_of(c * HALF, HALF), HALF)
    narrow = pl.ds(pl.multiple_of(c * NARROW, NARROW), NARROW)
    none = jnp.zeros((RANK, NARROW), F32)
    ball[:, :HALF] = below([2.0 * qb[:, half].astype(F32)], 128, HALF)
    ball[:, HALF : HALF + NARROW] = below([none, 2.0 * kb[:, narrow].astype(F32)], 128, NARROW)
    ball[:, HALF + NARROW :] = below([none, none, 2.0 * vb[:, narrow].astype(F32)], 128, NARROW)
    oac[...] = below([oa[:, half]], 128, HALF)
    ob2[...] = below([2.0 * ob[...].astype(F32)], 128, WIDTH)

    chip = me // 2
    starts, ends, total = [], [], jnp.int32(0)
    for k in range(8):
        starts.append(total)
        total = total + ((lens[k] + (STRETCH - 1)) >> 6)
        ends.append(total)

    def sequence(stretch):
        found = jnp.where(stretch >= ends[0], 1, 0)
        for k in range(1, 7):
            found = found + jnp.where(stretch >= ends[k], 1, 0)
        return found

    counts, gates = [], []
    for s in range(4):
        stretch = chip * 4 + s
        begin, length = starts[0], lens[0]
        for k in range(1, 8):
            inside = stretch >= starts[k]
            begin = jnp.where(inside, starts[k], begin)
            length = jnp.where(inside, lens[k], length)
        counts.append(length - (stretch - begin) * STRETCH)
        gates.append(jnp.where(stretch != begin, 1.0, 0.0))
    first_own, last_own = sequence(chip * 4), sequence(chip * 4 + 3)
    k16 = lax.broadcasted_iota(jnp.int32, (16, 128), 0)
    firsts = sequence((z * 16 + k16) * 4)
    lasts = sequence((z * 16 + k16) * 4 + 3)
    masks[0] = jnp.where((k16 < plane) & (lasts == first_own), 1.0, 0.0)
    masks[1] = jnp.where(lasts == sequence(z * 64 + 63), 1.0, 0.0)
    masks[2] = jnp.where((k16 > plane) & (firsts == last_own), 1.0, 0.0)
    masks[3] = jnp.where(firsts == sequence(z * 64), 1.0, 0.0)
    k8 = lax.broadcasted_iota(jnp.int32, (8, 128), 0)
    far_masks[0] = jnp.where((k8 < z) & (sequence(k8 * 64 + 63) == first_own), 1.0, 0.0)
    far_masks[1] = jnp.where((k8 > z) & (sequence(k8 * 64) == last_own), 1.0, 0.0)
    lane = lax.broadcasted_iota(jnp.int32, (1, 128), 1)
    low_lane = lane < 64
    in_stretch = lax.rem(lane, STRETCH)
    valid = jnp.concatenate(
        [jnp.where(in_stretch < jnp.where(low_lane, counts[2 * p], counts[2 * p + 1]), 1.0, 0.0) for p in range(2)], 1
    )
    iu = lax.broadcasted_iota(jnp.int32, (128, 128), 0)
    it = lax.broadcasted_iota(jnp.int32, (128, 128), 1)
    for p in range(2):
        room = jnp.where(iu < 64, counts[2 * p], counts[2 * p + 1])
        seen = (iu <= it) & ((iu < 64) == (it < 64)) & (lax.rem(iu, STRETCH) < room)
        bias[p] = jnp.where(seen, 0.0, -1e30)

    for copy in local[4:8]:
        copy.wait()
    tok_copy.wait_recv()

    def norm_rows(i, carry):
        rows = pl.ds(i * 32, 32)
        for side in range(2):
            t = tok2[side, rows, :].astype(F32)
            r = lax.rsqrt(jnp.mean(t * t, -1, keepdims=True) + EPSILON)
            r1[side, rows, :] = jnp.broadcast_to(r, (32, 128))
            hid1[pl.ds(side * ROWS + i * 32, 32), :] = (t * r * gain1[...]).astype(BF)
        return carry

    lax.fori_loop(0, ROWS // 32, norm_rows, 0)

    zero_low = jnp.zeros((), BF)

    def softmax_rows(logits):
        e = jnp.exp(logits - jnp.max(logits, 0, keepdims=True))
        return e / jnp.sum(e, 0, keepdims=True)

    def gather_plane(base, folded):
        fsend[base] = folded.astype(BF)
        frecv[base, plane] = folded.astype(BF)
        fly = copies.group()
        for i in range(4):
            for j in range(4):
                if i + j > 0:
                    fly.start(fsend.at[base], frecv.at[base, plane], device({"x": i, "y": j}))
        return fly

    def fold_plane(base, fly):
        fly.wait(frecv.at[base, pl.ds(0, 15)])
        whole = jnp.zeros((AUG, 128), F32)
        for k in range(16):
            whole += masks[2 * base + 1, k : k + 1, :] * frecv[base, k].astype(F32)
        hsend[base] = whole.astype(BF)
        fly = copies.group()
        for i in (1, 2, 3):
            fly.start(hsend.at[base], hrecv.at[base, i - 1], device({"z": i}))
        part = jnp.zeros((AUG, 128), F32)
        for k in range(16):
            part += masks[2 * base, k : k + 1, :] * frecv[base, k].astype(F32)
        return part, fly

    def fold_line(base, part, fly):
        fly.wait(hrecv.at[base])
        for i in (1, 2, 3):
            part += far_masks[base, pl.ds(wrap(z + 4 - i), 1), :] * hrecv[base, i - 1].astype(F32)
        return part

    def combine(states):
        for g in range(2):
            for p in range(2):
                one, two = states[2 * p], states[2 * p + 1]
                if g == 0:
                    both = jnp.where(low_lane, one, pltpu.roll(two, 64, 1))
                else:
                    both = jnp.where(low_lane, pltpu.roll(one, 64, 1), two)
                yield g * 2 + p, both

    def put_states(states, base):
        for k, both in combine(states):
            comb[base + k] = both.astype(BF)
            tall = jnp.concatenate([both, jnp.zeros((128 - AUG, 128), F32)], 0)
            comb_t[base + k] = tall.T.astype(BF)

    def share(src, dst):
        fly = copies.group()
        for i, j, r, n, at in SHARES:
            fly.start(src.at[pl.ds(r, n)], dst.at[pl.ds(at, n)], device({"x": i, "y": j}))
        return fly

    def lower():
        low[...] = nt(hid1[...], aall[...]).astype(BF)

    def keys():
        kv = nn(hid1[...], wa[:, :, :, :, :, HALF:QKV].reshape(WIDTH, 2 * NARROW))
        kv = (kv + nn(low[...], ball[:, HALF:QKV])).astype(BF)
        kv_t = kv.astype(F32).T.astype(BF)
        for g in range(2):
            keep = low_lane if g == 0 else ~low_lane
            knat[g] = jnp.where(keep, kv[:, :NARROW], jnp.zeros((), BF))
            vnat[g] = jnp.where(keep, kv[:, NARROW:], jnp.zeros((), BF))
            kt[g] = kv_t[g * HEAD : (g + 1) * HEAD]
            tail = lax.broadcasted_iota(jnp.int32, (64, CHIP), 0) == 0
            vt[g, :HEAD] = kv_t[NARROW + g * HEAD : NARROW + (g + 1) * HEAD]
            vt[g, HEAD:] = tail.astype(F32).astype(BF)
        lanes4 = lax.broadcasted_iota(jnp.int32, (1, CHIP), 1) // STRETCH

        for g in range(2):
            kfeat[g * HEAD : (g + 1) * HEAD] = softmax_rows(tn(fk[c * 2 + g], kt[g])) * valid
        kf = kfeat[...]
        kf_high = kf.astype(BF)
        kf_rest = (kf - kf_high.astype(F32)).astype(BF)
        for s in range(4):
            got = []
            for g in range(2):
                va = jnp.where(lanes4 == s, vt[g, :AUG], jnp.zeros((), BF))
                got.append(nt(va, kf_high) + nt(va, kf_rest))
            st[s] = jnp.where(low_lane, got[0], got[1])


    def send_plane():
        folded = st[0]
        for s in (1, 2, 3):
            folded = st[s] + gates[s] * folded
        waiting["plane"] = gather_plane(0, folded)

    def send_line():
        waiting["part"], waiting["line"] = fold_plane(0, waiting["plane"])

    def take_line():
        prefix = fold_line(0, waiting["part"], waiting["line"])
        states = [prefix]
        for s in (1, 2, 3):
            states.append(gates[s] * (states[s - 1] + st[s - 1]))
        put_states(states, 0)

    def queries():
        def query_columns(n, carry):
            cols = pl.ds(pl.multiple_of(n * 256, 256), 256)
            q = nn(hid1[...], wa[:, :, :, :, :, cols].reshape(WIDTH, 256)) + nn(low[...], ball[:, cols])
            qt[cols, :] = q.T.astype(BF)
            return carry

        lax.fori_loop(0, 4, query_columns, 0)

    def lanes(parts):
        return jnp.concatenate(parts, 1)

    def split(wide):
        return [wide[:, k * 128 : (k + 1) * 128] for k in range(4)]

    def attend_four(n, carry):
        g = n // 2
        rows = [pl.ds(pl.multiple_of(n * 256 + k * HEAD, HEAD), HEAD) for k in range(4)]
        for k in range(4):
            qfeat[rows[k], :] = softmax_rows(tn(fq[n * 4 + k], qt[rows[k], :]))
        for p in range(2):
            cols = slice(p * 128, (p + 1) * 128)
            q = lanes([qt[r, cols] for r in rows])
            scores = split(nn(knat[g, cols, :], jnp.concatenate([q, q], 0)))
            stacks = []
            for k in range(4):
                sc = scores[k] * 0.125 + bias[p]
                peak = jnp.max(sc, 0, keepdims=True)
                w = jnp.exp(sc - peak).astype(BF)
                wts[(n * 4 + k) * 2 + p] = w
                dm = jnp.exp(-peak)
                damp[(n * 4 + k) * 2 + p, :1] = dm
                dq = (qfeat[rows[k], cols] * dm).astype(BF)
                stacks.append(
                    jnp.concatenate([w, jnp.where(low_lane, dq, zero_low), jnp.where(low_lane, zero_low, dq)], 0)
                )
            lhs = jnp.concatenate([vt[g, :AUG, cols], comb[g * 2 + p]], 1)
            both = split(nn(lhs, lanes(stacks)))
            for k in range(4):
                rden = 1.0 / both[k][HEAD : HEAD + 1]
                den[(n * 4 + k) * 2 + p, :1] = rden
                mixf[rows[k], cols] = both[k][:HEAD] * rden
        return carry

    def attend():
        lax.fori_loop(0, 4, attend_four, 0)


    def project():
        def mix_rows(n, carry):
            cols = pl.ds(pl.multiple_of(n * 256, 256), 256)
            mixn[:, cols] = mixf[cols, :].T.astype(BF)
            return carry

        lax.fori_loop(0, 4, mix_rows, 0)
        lowo[...] = nt(mixn[...], oac[...]).astype(BF)

        def out_columns(n, carry):
            cols = pl.ds(pl.multiple_of(n * 256, 256), 256)
            w = wa[n // 2, pl.ds(pl.multiple_of(lax.rem(n, 2) * 2, 2), 2), :, :, :, QKV:ATT].reshape(256, HALF)
            o = nt(mixn[...], w) + nn(lowo[...], ob2[:, cols])
            mine = jnp.where(c == 0, o[:ROWS], o[ROWS:])
            other = jnp.where(c == 0, o[ROWS:], o[:ROWS])
            mid[:, cols] = mine + tok2[c, :, cols].astype(F32)
            outs[:, cols] = other.astype(BF)
            return carry

        waiting["out"] = []
        for at in (0, 4):
            lax.fori_loop(at, at + 4, out_columns, 0)
            cols = pl.ds(at * 256, HALF)
            waiting["out"].append(copies.start(outs.at[:, cols], outr.at[:, cols], sibling))

    def middle():
        for copy in waiting["out"]:
            copy.wait_recv()

        def middle_rows(i, carry):
            rows = pl.ds(i * 32, 32)
            m = mid[rows, :] + outr[rows, :].astype(F32)
            mid[rows, :] = m
            r = lax.rsqrt(jnp.mean(m * m, -1, keepdims=True) + EPSILON)
            ht[rows, :] = (m * r * gain2[...]).astype(BF)
            return carry

        lax.fori_loop(0, ROWS // 32, middle_rows, 0)

    def send_hidden():
        waiting["ht"] = share(ht, ht)

    def send_gradient():
        waiting["og"] = share(ogo, ogx)

    def arrived(name):
        waiting[name].wait(ogx.at[pl.ds(ROWS, 384)])

    def ff_cols(first, count):
        return wf[:, :, :, :, :, :, :, pl.ds(first, count)].reshape(WIDTH, count)

    def inner_gradient():
        gg[...] = nn(ogx[...], ff_cols(2 * SLICE, SLICE)).astype(BF)

    def activate(gate, up, rows, cols):
        s = 0.5 * jnp.tanh(0.5 * gate) + 0.5
        swish = gate * s
        inner[rows, cols] = (swish * up).astype(BF)
        d = gg[rows, cols].astype(F32)
        gg[rows, cols] = (d * up * s * (1.0 + gate * (1.0 - s))).astype(BF)
        ug[rows, cols] = (d * swish).astype(BF)

    owned, own_chunks = slice(0, ROWS), ((0, 512), (512, 512), (1024, 384))

    def own_gate():
        for at, count in own_chunks:
            gown[:, at : at + count] = nn(ht[owned, :], ff_cols(at, count))

    def own_up():
        for at, count in own_chunks:
            cols = slice(at, at + count)
            activate(gown[:, cols], nn(ht[owned, :], ff_cols(SLICE + at, count)), owned, cols)

    steps = {
        "low": lower,
        "kvc": keys,
        "pls": send_plane,
        "lns": send_line,
        "lnw": take_line,
        "qc": queries,
        "att": attend,
        "oproj": project,
        "mid": middle,
        "hts": send_hidden,
        "htw": lambda: arrived("ht"),
        "ogs": send_gradient,
        "ogw": lambda: arrived("og"),
        "ds": streams["d"].settle,
        "gs": streams["g"].settle,
        "us": streams["u"].settle,
        "ig": inner_gradient,
        "go": own_gate,
        "uo": own_up,
    }
    for name in PLAN:
        if "." in name:
            advance(name)
        else:
            steps[name]()
    og_fly, ht_fly, out_copy = waiting["og"], waiting["ht"], waiting["out"]

    others = slice(ROWS, 512)
    for at, count in ((0, 512), (512, 512), (1024, 256)):
        cols = slice(at, at + count)
        gate, up = nn(ht[others, :], ff_cols(at, count)), nn(ht[others, :], ff_cols(SLICE + at, count))
        activate(gate, up, others, cols)
    both = nn(ht[others, :], jnp.concatenate([ff_cols(1280, 128), ff_cols(SLICE + 1280, 128)], 1))
    activate(both[:, :128], both[:, 128:], others, slice(1280, SLICE))

    def ff_rows(n, at):
        return wf[n // 2, lax.rem(n, 2), :, :, :, :, :, pl.ds(at, SLICE)].reshape(256, SLICE)

    copies.sent(ht_fly.members)
    copies.sent(og_fly.members)

    def two_columns(n, carry):
        cols = pl.ds(pl.multiple_of(n * 256, 256), 256)
        ogx[:, cols] = (nt(gg[...], ff_rows(n, 0)) + nt(ug[...], ff_rows(n, SLICE))).astype(BF)
        return carry

    def give_back(src, dst, cols):
        fly = copies.group()
        for k, (i, j, r, n, at) in enumerate(SHARES):
            there = dst.at[k // 2 - (k > 5), pl.ds(r, n), cols]
            fly.start(src.at[pl.ds(at, n), cols], there, device({"x": (4 - i) % 4, "y": (4 - j) % 4}))
        return [(fly, dst.at[:, :, cols])]

    def two_step(n, carry):
        two_columns(n, carry)
        cols = pl.ds(pl.multiple_of(n * 256, 256), 256)
        for k, (i, j, r, count, at) in enumerate(SHARES):
            pltpu.make_async_remote_copy(
                src_ref=ogx.at[pl.ds(at, count), cols],
                dst_ref=rbt.at[k // 2 - (k > 5), pl.ds(r, count), cols],
                send_sem=two_send.at[n],
                recv_sem=two_recv.at[n],
                device_id=(device({"x": (4 - i) % 4, "y": (4 - j) % 4}),),
                device_id_type=MESH,
            ).start()
        return carry

    lax.fori_loop(0, 8, two_step, 0)

    def two_wait(n, carry):
        cols = pl.ds(pl.multiple_of(n * 256, 256), 256)
        here_to = ogx.at[pl.ds(ROWS, 384), cols]
        pltpu.make_async_copy(here_to, here_to, two_send.at[n]).wait()
        come = rbt.at[:, :, cols]
        pltpu.make_async_copy(come, come, two_recv.at[n]).wait()
        return carry

    def block_columns(n, carry):
        cols = pl.ds(pl.multiple_of(n * 256, 256), 256)
        ht[:, cols] = nt(inner[...], ff_rows(n, 2 * SLICE)).astype(BF)
        return carry

    lax.fori_loop(0, 6, block_columns, 0)
    blk_fly = give_back(ht, rbb, pl.ds(0, 1536))
    lax.fori_loop(6, 8, block_columns, 0)
    lax.fori_loop(0, 8, two_wait, 0)

    def middle_back(i, acc):
        rows = pl.ds(i * 16, 16)
        t = ogx[rows, :].astype(F32)
        for k in range(3):
            t += rbt[k, rows, :].astype(F32)
        m = mid[rows, :]
        r = lax.rsqrt(jnp.mean(m * m, -1, keepdims=True) + EPSILON)
        n = m * r
        acc += jnp.sum(t * n, 0, keepdims=True)
        t = t * gain2[...]
        g = ogo[rows, :].astype(F32) + r * (t - n * jnp.mean(t * n, -1, keepdims=True))
        mgrad[rows, :] = g
        bg[c, rows, :] = g.astype(BF)
        return acc

    gain_mlp = jnp.zeros((1, WIDTH), F32)
    bg_fly = []
    for at in (0, ROWS // 2):
        gain_mlp = lax.fori_loop(at // 16, at // 16 + ROWS // 32, middle_back, gain_mlp)
        part = bg.at[c, pl.ds(at, ROWS // 2)]
        bg_fly.append(copies.start(part, part, sibling))
    for copy in bg_fly:
        copy.wait_recv()
    bgv = bg.at[:, :, :]
    olg = nt(bgv[...].reshape(CHIP, WIDTH), ob2[...])
    olg_low = olg.astype(BF)

    def mixed_columns(n, carry):
        cols = pl.ds(pl.multiple_of(n * 256, 256), 256)
        wcols = pl.ds(pl.multiple_of(QKV + n * 256, 256), 256)
        m = nn(bg[...].reshape(CHIP, WIDTH), wa[:, :, :, :, :, wcols].reshape(WIDTH, 256))
        m += nn(olg_low, oac[:, cols])
        ngt[cols, :] = m.T.astype(BF)
        return carry

    lax.fori_loop(0, 4, mixed_columns, 0)
    for k in range(4):
        sig[k] = jnp.zeros((AUG, 128), F32)

    def states_four(n, carry):
        g = n // 2
        rows = [pl.ds(pl.multiple_of(n * 256 + k * HEAD, HEAD), HEAD) for k in range(4)]
        for p in range(2):
            cols = slice(p * 128, (p + 1) * 128)
            left, right = [], []
            for k in range(4):
                h = (n * 4 + k) * 2 + p
                rden = den[h, :1]
                m = ngt[rows[k], cols].astype(F32)
                ng = (m * rden).astype(BF)
                dg = -jnp.sum(m * mixf[rows[k], cols], 0, keepdims=True) * rden
                ngt[rows[k], cols] = ng
                dgr[h, :1] = dg
                dq = (qfeat[rows[k], cols] * damp[h, :1]).astype(BF)
                right.append(jnp.concatenate([jnp.where(low_lane, dq, zero_low), jnp.where(low_lane, zero_low, dq)], 0))
                tail = jnp.where(lax.broadcasted_iota(jnp.int32, (AUG - HEAD, 128), 0) == 0, dg, 0.0).astype(BF)
                left.append(jnp.concatenate([ng, tail], 0))
            sig[g * 2 + p] = sig[g * 2 + p] + nt(lanes(left), lanes(right))
        return carry

    lax.fori_loop(0, 4, states_four, 0)
    sg_states = []
    for p in range(2):
        a, b = sig[p], sig[2 + p]
        sg_states.append(jnp.where(low_lane, a, pltpu.roll(b, 64, 1)))
        sg_states.append(jnp.where(low_lane, pltpu.roll(a, 64, 1), b))
    for s in range(4):
        st[s] = sg_states[s]
    folded = sg_states[3]
    for s in (2, 1, 0):
        folded = sg_states[s] + gates[s + 1] * folded
    fly = gather_plane(1, folded)
    blk_fly += give_back(ht, rbb, pl.ds(1536, 512))

    for k in range(4):
        kacc[k] = jnp.zeros((HEAD, 128), F32)
        vacc[k] = jnp.zeros((HEAD, 128), F32)

    def back_four(n, carry):
        g = n // 2
        rows = [pl.ds(pl.multiple_of(n * 256 + k * HEAD, HEAD), HEAD) for k in range(4)]
        for p in range(2):
            cols = slice(p * 128, (p + 1) * 128)
            ngs = lanes([ngt[r, cols] for r in rows])
            dgs = [dgr[(n * 4 + k) * 2 + p, :1] for k in range(4)]
            dg = lanes(dgs)
            ws = lanes([wts[(n * 4 + k) * 2 + p] for k in range(4)])
            pt = nn(vnat[g, cols, :], jnp.concatenate([ngs, ngs], 0)) + dg
            sgr = (ws.astype(F32) * pt).astype(BF)
            tail = jnp.where(lax.broadcasted_iota(jnp.int32, (HEAD, 512), 0) == 0, dg, 0.0).astype(BF)
            both = split(nn(comb_t[g * 2 + p], jnp.concatenate([ngs, tail], 0)))
            for k in range(4):
                qg = jnp.where(low_lane, both[k][:HEAD], both[k][HEAD:]) * damp[(n * 4 + k) * 2 + p, :1]
                f = qfeat[rows[k], cols]
                qlg[rows[k], cols] = (f * (qg - jnp.sum(f * qg, 0, keepdims=True))).astype(BF)
            near = split(nn(kt[g, :, cols], sgr))
            for k in range(4):
                far = nn(fq[n * 4 + k], qlg[rows[k], cols])
                gt[rows[k], cols] = (near[k] * 0.125 + far).astype(BF)
            kacc[g * 2 + p] = kacc[g * 2 + p] + nt(lanes([qt[r, cols] for r in rows]), sgr)
            vacc[g * 2 + p] = vacc[g * 2 + p] + nt(ngs, ws)
        return carry

    lax.fori_loop(0, 4, back_four, 0)
    early = Sums(copies, device, (x, y, z, c), sibling, (e_own, e_got, e_line, e_all), EARLY_BLOCKS)
    late = Sums(copies, device, (x, y, z, c), sibling, (l_own, l_got, l_line, l_all), LATE_BLOCKS)
    for k in range(21, 32):
        late.put(k, jnp.zeros((16, 128), F32))
    lowo_t = lowo[...].astype(F32).T.astype(BF)
    olg_t = olg.T.astype(BF)
    low_t = low[...].astype(F32).T.astype(BF)
    lowg_q = nn(ball[:16, :HALF], gt[:HALF, :]).astype(BF)
    grads = jnp.concatenate(
        [nn(lowg_q, hid1[...])[:8], 2.0 * nn(lowo_t[:16], bg[...].reshape(CHIP, WIDTH))[:8]], 0
    )
    for j in range(16):
        early.put(40 + j, grads[:, j * 128 : (j + 1) * 128])
    grads = jnp.concatenate([2.0 * nt(low_t[:16], gt[:HALF, :])[:8], nn(olg_t[:16], mixn[...])[:8]], 0)
    for j in range(8):
        early.put(32 + j, grads[:, j * 128 : (j + 1) * 128])
    early.put(56, jnp.concatenate([gain_mlp[:, k * 128 : (k + 1) * 128] for k in range(16)], 0))
    for k in range(57, 64):
        early.put(k, jnp.zeros((16, 128), F32))

    def grad_rows(n, carry):
        rows = pl.ds(pl.multiple_of(n * 256, 256), 256)
        gnat[:, rows] = gt[rows, :].astype(F32).T.astype(BF)
        return carry

    lax.fori_loop(0, 4, grad_rows, 0)

    def feat_pairs(n, carry):
        rows = pl.ds(pl.multiple_of(n * 128, 128), 128)
        r = nt(qt[rows, :], qlg[rows, :])
        r = jnp.where(low_lane, r[:HEAD], r[HEAD:]).astype(BF)
        for k in range(4):
            e_own[2 * k + n // 4, :, pl.ds(pl.multiple_of(lax.rem(n, 4) * 128, 128), 128)] = r[k * 16 : (k + 1) * 16]
        return carry

    lax.fori_loop(0, 8, feat_pairs, 0)

    early.scatter()
    part, fly = fold_plane(1, fly)

    def one_queries(n, carry):
        w = wa[n // 2, pl.ds(pl.multiple_of(lax.rem(n, 2) * 2, 2), 2), :, :, :, 0:HALF].reshape(256, HALF)
        o = nt(gnat[:, :HALF], w)
        rows = pl.ds(pl.multiple_of(lax.rem(n, 4) * 256, 256), 256)

        @pl.when(n < 4)
        def _():
            qfeat[rows, :] = o

        @pl.when(n >= 4)
        def _():
            mixf[rows, :] = o

        return carry

    lax.fori_loop(0, 8, one_queries, 0)
    suffix = fold_line(1, part, fly)
    states = [None, None, None, suffix]
    for s in (2, 1, 0):
        states[s] = gates[s + 1] * (states[s + 1] + st[s + 1])
    put_states(states, 4)

    for g in range(2):
        f_rows = slice(g * HEAD, (g + 1) * HEAD)
        for p in range(2):
            k = g * 2 + p
            cols = slice(p * 128, (p + 1) * 128)
            f = kfeat[f_rows, cols]
            both = nn(comb_t[4 + k], vt[g, :, cols])
            fg = jnp.where(low_lane, both[:HEAD], both[HEAD:]) * valid[:, cols]
            kl = (f * (fg - jnp.sum(f * fg, 0, keepdims=True))).astype(BF)
            qlg[HALF + g * HEAD : HALF + (g + 1) * HEAD, cols] = kl
            gt[HALF + g * HEAD : HALF + (g + 1) * HEAD, cols] = (kacc[k] * 0.125 + nn(fk[c * 2 + g], kl)).astype(BF)
            fl = f.astype(BF)
            stack = jnp.concatenate([jnp.where(low_lane, fl, zero_low), jnp.where(low_lane, zero_low, fl)], 0)
            gt[HALF + NARROW + g * HEAD : HALF + NARROW + (g + 1) * HEAD, cols] = (
                vacc[k] + nn(comb[4 + k, :HEAD], stack)
            ).astype(BF)

    lowg_t = nn(ball[...], gt[...])
    lowg_low = lowg_t.astype(BF)


    def one_columns(n, had):
        cols = pl.ds(pl.multiple_of(n * 256, 256), 256)
        w = wa[n // 2, pl.ds(pl.multiple_of(lax.rem(n, 2) * 2, 2), 2), :, :, :, HALF:QKV].reshape(256, 2 * NARROW)
        o = had[pl.ds(pl.multiple_of(lax.rem(n, 4) * 256, 256), 256), :]
        o = o + nt(gnat[:, HALF:], w) + nn(lowg[...], aall[:, cols])
        normed = [tok2[side, :, cols].astype(F32) * r1[side, :, :1] for side in range(2)]
        gain = jnp.sum(o[:ROWS] * normed[0] + o[ROWS:] * normed[1], 0, keepdims=True)
        gsum[pl.ds(2 * n, 1), :] = gain[:, :128]
        gsum[pl.ds(2 * n + 1, 1), :] = gain[:, 128:]
        ones[:, cols] = jnp.where(c == 0, o[:ROWS], o[ROWS:])
        outs[:, cols] = jnp.where(c == 0, o[ROWS:], o[:ROWS]).astype(BF)

    def one_first(n, carry):
        one_columns(n, qfeat)
        return carry

    def one_second(n, carry):
        one_columns(n, mixf)
        return carry

    r = nt(kt[...].reshape(128, CHIP), qlg[HALF:, :])
    r = jnp.where(low_lane, r[:HEAD], r[HEAD:])
    for k in range(4):
        late.put(k, r[k * 16 : (k + 1) * 16])
    up = 2.0 * nt(low_t[:32], gt[HALF:, :])
    late.put(4, jnp.concatenate([up[8:16, :NARROW], up[16:24, NARROW:]], 0))
    down = nn(lowg_low[:32], hid1[...])
    for j in range(16):
        late.put(5 + j, down[8:24, j * 128 : (j + 1) * 128])
    late.scatter()
    lowg[...] = lowg_t.T.astype(BF)
    grad_rows(4, 0)

    copies.sent(out_copy)
    lax.fori_loop(0, 4, one_first, 0)
    lax.fori_loop(4, 8, one_second, 0)
    one_copy = copies.start(outs, outr, sibling)

    gplane[plane] = gsum[...]
    gain_fly = copies.group()
    for i, j in early.others():
        gain_fly.start(gsum, gplane.at[plane], device({"x": i, "y": j}))
    early.along()
    late.along()
    one_copy.wait_recv()
    copies.sent([one_copy])

    def token_rows(i, carry):
        rows = pl.ds(i * 16, 16)
        o = ones[rows, :] + outr[rows, :].astype(F32)
        t = tok2[c, rows, :].astype(F32)
        r = r1[c, rows, :1]
        n = t * r
        o = o * gain1[...]
        outs[rows, :] = (mgrad[rows, :] + r * (o - n * jnp.mean(o * n, -1, keepdims=True))).astype(BF)
        return carry

    lax.fori_loop(0, ROWS // 32, token_rows, 0)
    early.gather()
    gain_fly.wait(gplane.at[pl.ds(0, 15)])
    total = gplane[0]
    for k in range(1, 16):
        total += gplane[k]
    gline[z, c] = total
    mine = gline.at[z, c]
    same, cross = copies.group(), copies.group()
    for i in (1, 2, 3):
        same.start(mine, mine, device({"z": i}))
    for i in range(4):
        cross.start(mine, mine, device({"z": i}, 1))
    late.gather()
    for fly, ref in blk_fly:
        fly.wait(ref)

    def block_rows(i, carry):
        rows = pl.ds(i * 16, 16)
        t = mid[rows, :] + ht[rows, :].astype(F32)
        for k in range(3):
            t += rbb[k, rows, :].astype(F32)
        ht[rows, :] = t.astype(BF)
        return carry

    copies.sent([copy for fly, ref in blk_fly for copy in fly.members])
    lax.fori_loop(0, ROWS // 16, block_rows, 0)
    here(ht.at[pl.ds(0, ROWS)], blk_out)
    lax.fori_loop(ROWS // 32, ROWS // 16, token_rows, 0)
    here(outs, gtok_out)
    same.wait(gline.at[pl.ds(0, 3), 0])
    cross.wait(gline.at[:, 0])
    total = gline[0, 0] + gline[0, 1]
    for k in range(1, 4):
        total += gline[k, 0] + gline[k, 1]
    gain_all[...] = total
    here(gain_all, gain_out)
    early.cross()
    here(e_all.at[c], early_out.at[c])
    late.cross()
    here(l_all.at[c], late_out.at[c])
    early.finish()
    here(e_all.at[1 - c], early_out.at[1 - c])
    late.finish()
    here(l_all.at[1 - c], late_out.at[1 - c])
    for copy in local[-7:]:
        copy.wait()
    copies.drain()


def finish(
    blk, gtok, early, late, gain,
    blk_out, gtok_out, gain_a_out, qa_out, qb_out, ka_out, kb_out, va_out, vb_out, oa_out, ob_out, fq_out, fk_out,
    gain_b_out, sem,
):
    copies = [pltpu.make_async_copy(a, b, sem.at[k]) for k, (a, b) in enumerate(((blk, blk_out), (gtok, gtok_out)))]
    for copy in copies:
        copy.start()

    def block(sums, share, side, k):
        return sums[side, k // share, :, (k % share) * 128 : (k % share + 1) * 128].astype(F32)

    def first(side, k):
        return block(early, EARLY_BLOCKS, side, k)

    def second(side, k):
        return block(late, LATE_BLOCKS, side, k)

    for side in range(2):
        at = side * HALF
        for k in range(4):
            rows = slice(k * 16, (k + 1) * 16)
            for j in range(9):
                v = first(side, k * 8 + j) if j < 8 else second(side, k)
                out, head = (fq_out, side * 16 + 2 * j) if j < 8 else (fk_out, side * 2)
                out[head, rows, :] = v[:, :64]
                out[head + 1, rows, :] = pltpu.roll(v, 64, 1)[:, :64]
        for j in range(8):
            cols = slice(at + j * 128, at + (j + 1) * 128)
            v = first(side, 32 + j)
            qb_out[:, cols] = v[:8]
            oa_out[:, cols] = v[8:]
        v = second(side, 4)
        kb_out[:, side * NARROW : (side + 1) * NARROW] = v[:8]
        vb_out[:, side * NARROW : (side + 1) * NARROW] = v[8:]
    for j in range(16):
        cols = slice(j * 128, (j + 1) * 128)
        v = first(0, 40 + j) + first(1, 40 + j)
        qa_out[:, cols] = v[:8]
        ob_out[:, cols] = v[8:]
        v = second(0, 5 + j) + second(1, 5 + j)
        ka_out[:, cols] = v[:8]
        va_out[:, cols] = v[8:]
    gain_a_out[...] = gain[...]
    gain_b_out[...] = first(0, 56) + first(1, 56)
    for copy in copies:
        copy.wait()


N_COPIES = 79
N_SENDS = 48


def scratch():
    v = pltpu.VMEM
    return [
        v((4, 4, 4, 2, 16, ATT), BF),
        v((4, 2, 2, 2, 2, 2, 16, 3 * SLICE), BF),
        v((2, 2, 16, 3 * SLICE), BF),
        v((2, ROWS, WIDTH), BF),
        v((QUERY_HEADS // 2, HEAD, HEAD), BF),
        v((ROWS, WIDTH), BF),
        v((8, WIDTH), F32),
        v((2, ROWS, 128), F32),
        v((128, WIDTH), BF),
        v((128, QKV), BF),
        v((128, HALF), BF),
        v((128, WIDTH), BF),
        v((4, 16, 128), F32),
        v((2, 8, 128), F32),
        v((2, 128, 128), F32),
        v((CHIP, WIDTH), BF),
        v((CHIP, 128), BF),
        v((HALF, CHIP), BF),
        v((2, HEAD, CHIP), BF),
        v((2, 128, CHIP), BF),
        v((2, CHIP, 128), BF),
        v((2, CHIP, 128), BF),
        v((128, CHIP), F32),
        v((4, AUG, 128), F32),
        v((8, AUG, 128), BF),
        v((8, 128, 128), BF),
        v((32, 128, 128), BF),
        v((HALF, CHIP), F32),
        v((HALF, CHIP), F32),
        v((32, 8, 128), F32),
        v((32, 8, 128), F32),
        v((CHIP, HALF), BF),
        v((CHIP, 128), BF),
        v((ROWS, WIDTH), BF),
        v((ROWS, WIDTH), BF),
        v((ROWS, WIDTH), F32),
        v((512, WIDTH), BF),
        v((512, WIDTH), BF),
        v((512, SLICE), BF),
        v((512, SLICE), BF),
        v((512, SLICE), BF),
        v((3, ROWS, WIDTH), BF),
        v((3, ROWS, WIDTH), BF),
        v((ROWS, WIDTH), F32),
        v((2, ROWS, WIDTH), BF),
        v((HALF, CHIP), BF),
        v((32, 8, 128), F32),
        v((4, AUG, 128), F32),
        v((HALF + 128, CHIP), BF),
        v((QKV, CHIP), BF),
        v((CHIP, QKV), BF),
        v((CHIP, 128), BF),
        v((ROWS, WIDTH), F32),
        v((4, HEAD, 128), F32),
        v((4, HEAD, 128), F32),
        v((2, AUG, 128), BF),
        v((2, 16, AUG, 128), BF),
        v((2, AUG, 128), BF),
        v((2, 3, AUG, 128), BF),
        v((ROWS, SLICE), F32),
        v((16, 16, EARLY_BLOCKS * 128), BF),
        v((16, 16, EARLY_BLOCKS * 128), BF),
        v((4, 16, EARLY_BLOCKS * 128), BF),
        v((2, 16, 16, EARLY_BLOCKS * 128), BF),
        v((16, 16, LATE_BLOCKS * 128), BF),
        v((16, 16, LATE_BLOCKS * 128), BF),
        v((4, 16, LATE_BLOCKS * 128), BF),
        v((2, 16, 16, LATE_BLOCKS * 128), BF),
        v((16, 128), F32),
        v((16, 16, 128), F32),
        v((4, 2, 16, 128), F32),
        v((16, 128), F32),
        pltpu.SemaphoreType.DMA((N_SENDS,)),
        pltpu.SemaphoreType.DMA((N_COPIES,)),
        pltpu.SemaphoreType.DMA((23,)),
        pltpu.SemaphoreType.DMA((8,)),
        pltpu.SemaphoreType.DMA((8,)),
    ]


def body(
    tokens, sequence_lengths, attention_gain, query_weight, key_weight, value_weight, output_weight_flipped,
    query_adapter_down, query_adapter_up, key_adapter_down, key_adapter_up, value_adapter_down, value_adapter_up,
    output_adapter_down, output_adapter_up, query_feature_map, key_feature_map, feedforward_gain,
    gate_weight, up_weight, down_weight_flipped, output_gradient,
):
    vmem = pl.BlockSpec(memory_space=pltpu.VMEM)
    smem = pl.BlockSpec(memory_space=pltpu.SMEM)
    anywhere = pl.BlockSpec(memory_space=pl.ANY)

    def array(*shape, dtype=F32):
        return jax.ShapeDtypeStruct(shape, dtype)

    parts = pl.pallas_call(
        kernel,
        out_shape=(
            array(ROWS, WIDTH, dtype=BF), array(ROWS, WIDTH, dtype=BF), array(2, 16, 16, EARLY_BLOCKS * 128, dtype=BF),
            array(2, 16, 16, LATE_BLOCKS * 128, dtype=BF),
            array(16, 128),
        ),
        in_specs=[anywhere, smem, vmem] + [anywhere] * 4 + [vmem] * 8 + [anywhere] + [vmem] * 2 + [anywhere] * 4,
        out_specs=(anywhere,) * 5,
        scratch_shapes=scratch(),
        compiler_params=pltpu.CompilerParams(
            collective_id=0, has_side_effects=True, vmem_limit_bytes=64 * 1024 * 1024
        ),
    )(
        tokens, sequence_lengths, attention_gain.reshape(16, 128),
        query_weight, key_weight, value_weight, output_weight_flipped,
        query_adapter_down.T, query_adapter_up, key_adapter_down.T, key_adapter_up, value_adapter_down.T,
        value_adapter_up, output_adapter_down.T, output_adapter_up, query_feature_map, key_feature_map,
        feedforward_gain.reshape(16, 128), gate_weight, up_weight, down_weight_flipped, output_gradient,
    )
    out = pl.pallas_call(
        finish,
        out_shape=(
            array(ROWS, WIDTH, dtype=BF), array(ROWS, WIDTH, dtype=BF), array(16, 128),
            array(RANK, WIDTH), array(RANK, WIDTH), array(RANK, WIDTH), array(RANK, 2 * NARROW),
            array(RANK, WIDTH), array(RANK, 2 * NARROW), array(RANK, WIDTH), array(RANK, WIDTH),
            array(QUERY_HEADS, HEAD, HEAD), array(KEY_VALUE_HEADS, HEAD, HEAD), array(16, 128),
        ),
        in_specs=[vmem] * 5,
        out_specs=(anywhere,) * 2 + (vmem,) * 12,
        scratch_shapes=[pltpu.SemaphoreType.DMA((2,))],
    )(*parts)
    (
        block_out, grad_tokens, gain_attn, qa, qb, ka, kb, va, vb, oa, ob, feat_q, feat_k, gain_mlp,
    ) = out
    return (
        block_out, grad_tokens, gain_attn.reshape(WIDTH), qa.T, qb, ka.T, kb, va.T, vb, oa.T, ob, feat_q, feat_k,
        gain_mlp.reshape(WIDTH),
    )


def solution(mesh):
    split, whole = P("seq", None), P()
    return jax.shard_map(
        body,
        mesh=mesh,
        in_specs=(
            (split, whole, whole) + (split,) * 4 + (whole,) * 11 + (split,) * 4
        ),
        out_specs=(split, split) + (whole,) * 12,
        check_vma=False,
    )
```
